32 devices in a mesh: tok: 8 (over z, x), head: 4 (over y, core).
Axes of the slice: x: 2, y: 2, z: 4, core: 2. Of those that a mesh axis runs over, the one named last changes fastest.
Arguments:
- tokens_in: bfloat16 [12288, 1024], P(('tok', 'head')), may hold values from -6 to 6
- seq_starts: int32 [2], replicated, may hold values from 0 to 11776, as said below
- block_sizes: int32 [2], replicated, may hold values from 128 to 512, as said below
- norm1_gain: float32 [1024], replicated, may hold values from 0.5 to 1.5
- norm1_bias: float32 [1024], replicated, may hold values from -1.75 to 1.75
- w_query: bfloat16 [1024, 1024], replicated, may hold values from -0.1875 to 0.1875
- w_key: bfloat16 [1024, 1024], replicated, may hold values from -0.1875 to 0.1875
- w_value: bfloat16 [1024, 1024], replicated, may hold values from -0.1875 to 0.1875
- w_output: bfloat16 [1024, 1024], replicated, may hold values from -0.75 to 0.75
- ssm_rate: float32 [1024, 16], P('head'), may hold values from 0.2 to 614
- ssm_input: float32 [1024, 16], P('head'), may hold values from -6 to 6
- ssm_output: float32 [1024, 16], P('head'), may hold values from -1.5 to 1.5
- ssm_skip: float32 [1024], P('head'), may hold values from -3 to 3
- norm2_gain: float32 [1024], replicated, may hold values from 0.5 to 1.5
- norm2_bias: float32 [1024], replicated, may hold values from -1.75 to 1.75
- w_up: bfloat16 [1024, 4096], replicated, may hold values from -0.1875 to 0.1875
- up_bias: float32 [4096], replicated, may hold values from -1.75 to 1.75
- w_down: bfloat16 [4096, 1024], replicated, may hold values from -0.09375 to 0.09375
- down_bias: float32 [1024], replicated, may hold values from -1.75 to 1.75
- out_grad: bfloat16 [12288, 1024], P(('tok', 'head')), may hold values from -6 to 6
Outputs:
- layer_out: bfloat16 [12288, 1024], P(('tok', 'head'))
- input_grad: float32 [12288, 1024], P(('tok', 'head'))
- grad_norm1_gain: float32 [1024], P(('tok', 'head'))
- grad_norm1_bias: float32 [1024], P(('tok', 'head'))
- grad_w_query: float32 [1024, 1024], P(('tok', 'head'))
- grad_w_key: float32 [1024, 1024], P(('tok', 'head'))
- grad_w_value: float32 [1024, 1024], P(('tok', 'head'))
- grad_w_output: float32 [1024, 1024], P(('tok', 'head'))
- grad_ssm_rate: float32 [1024, 16], P('head')
- grad_ssm_input: float32 [1024, 16], P('head')
- grad_ssm_output: float32 [1024, 16], P('head')
- grad_ssm_skip: float32 [1024], P('head')
- grad_norm2_gain: float32 [1024], P(('tok', 'head'))
- grad_norm2_bias: float32 [1024], P(('tok', 'head'))
- grad_w_up: float32 [1024, 4096], P(('tok', 'head'))
- grad_up_bias: float32 [4096], P(('tok', 'head'))
- grad_w_down: float32 [4096, 1024], P(('tok', 'head'))
- grad_down_bias: float32 [1024], P(('tok', 'head'))
The draws below stay inside these ranges and needn't reach their ends.
Inputs may be any that keep to these rules, and one draw needn't show every extreme that they name: seq_starts[0] is 0; the second sequence begins 12288 - L or L positions in, for a length L of 512 to 1535. `block_sizes`: one sequence has blocks of exactly 512 positions.
All inputs are finite; a program needn't handle non-finite values.
Results may differ from the reference program's by a relative error of at most 0.02.
Values may be sent and summed in bfloat16 or wider, within the bound.
A program may use at most 320 MiB of HBM per device.

```python
import math
import jax
import jax.numpy as jnp
from jax import lax

HD = 128
D = 1024
FF = 4096
NS = 16
CTX = 128
BLOCK = 256
QB = 512
SB = 128
SPAN = 1536
TOKENS = 12288


def draw_seq_starts(key, part):
    key = jax.random.fold_in(key, 11)
    first_key, second_key = jax.random.split(key)
    short_len = jax.random.randint(first_key, (), SPAN // 3, SPAN)
    leading = jax.random.randint(second_key, (), 0, 2)
    second = leading * short_len + (1 - leading) * (TOKENS - short_len)
    return jnp.stack([jnp.zeros((), jnp.int32), second.astype(jnp.int32)]).astype(jnp.int32)


def draw_block_sizes(key, part):
    key = jax.random.fold_in(key, 12)
    pick_key, other_key = jax.random.split(key)
    larger = jax.random.randint(pick_key, (), 0, 2)
    other = jax.random.randint(other_key, (), BLOCK // 2, 2 * BLOCK + 1)
    first = larger * (2 * BLOCK) + (1 - larger) * other
    second = larger * other + (1 - larger) * (2 * BLOCK)
    return jnp.stack([first, second]).astype(jnp.int32)


def draw_ssm_rate(key, part):
    key = jax.random.fold_in(key, 13)
    pick_key, slow_key, fast_key = jax.random.split(key, 3)
    share = 0.5
    slow_rate = jnp.exp(jax.random.uniform(slow_key, (D, NS), jnp.float32, math.log(0.2), math.log(2.0)))
    fast_rate = float(TOKENS // 20) * jnp.exp(jax.random.uniform(fast_key, (D, NS), jnp.float32, math.log(1.0 / 20.0), 0.0))
    chosen = jax.random.uniform(pick_key, (D, NS), jnp.float32) < share
    return jnp.minimum(jnp.where(chosen, slow_rate, fast_rate), float(TOKENS // 20)).astype(jnp.float32)


def block_levels(stream_key, shape, cuts, low, largest):
    level, own = 1.0, jax.random.fold_in(stream_key, 6)
    for axis_at, blocks in cuts:
        steps = jnp.exp(jax.random.uniform(jax.random.fold_in(own, axis_at), (blocks,), jnp.float32, low / len(cuts), largest / len(cuts)))
        level = level * jnp.repeat(steps, shape[axis_at] // blocks).reshape([-1 if axis == axis_at else 1 for axis in range(len(shape))])
    return level


def noise(key, shape, width, limit, cuts=(), kind=jnp.bfloat16):
    factor_of = block_levels(key, shape, cuts, -0.22, 0.18) if cuts else 1.0
    values = jax.random.normal(key, shape, jnp.float32) * width * factor_of
    return jnp.minimum(jnp.maximum(values, -limit), limit).astype(kind)


def setup_inputs(seed: int = 0) -> dict:
    key_of = jax.random.split(jax.random.key(seed), 21)
    return {
        "tokens_in": noise(key_of[0], (TOKENS, D), 1.0, 6.0, ((0, 32),)),
        "seq_starts": draw_seq_starts(jax.random.fold_in(key_of[20], 71), 0),
        "block_sizes": draw_block_sizes(jax.random.fold_in(key_of[20], 71), 0),
        "norm1_gain": jnp.clip(1.0 + 0.1 * jax.random.normal(key_of[3], (D,), jnp.float32), 0.5, 1.5),
        "norm1_bias": noise(key_of[4], (D,), 0.3, 1.75, (), jnp.float32),
        "w_query": noise(key_of[5], (D, D), D ** -0.5, 0.1875),
        "w_key": noise(key_of[6], (D, D), D ** -0.5, 0.1875),
        "w_value": noise(key_of[7], (D, D), D ** -0.5, 0.1875),
        "w_output": noise(key_of[8], (D, D), (D // 16) ** -0.5, 0.75),
        "ssm_rate": draw_ssm_rate(jax.random.fold_in(key_of[20], 71), 0),
        "ssm_input": noise(key_of[10], (D, NS), 1.0, 6.0, ((0, 4),), jnp.float32),
        "ssm_output": noise(key_of[11], (D, NS), NS ** -0.5, 1.5, ((0, 4),), jnp.float32),
        "ssm_skip": noise(key_of[12], (D,), 0.5, 3.0, ((0, 4),), jnp.float32),
        "norm2_gain": jnp.clip(1.0 + 0.1 * jax.random.normal(key_of[13], (D,), jnp.float32), 0.5, 1.5),
        "norm2_bias": noise(key_of[14], (D,), 0.3, 1.75, (), jnp.float32),
        "w_up": noise(key_of[15], (D, FF), D ** -0.5, 0.1875),
        "up_bias": noise(key_of[16], (FF,), 0.3, 1.75, (), jnp.float32),
        "w_down": noise(key_of[17], (FF, D), FF ** -0.5, 0.09375),
        "down_bias": noise(key_of[18], (D,), 0.3, 1.75, (), jnp.float32),
        "out_grad": noise(key_of[19], (TOKENS, D), 1.0, 6.0, ((0, 32),)),
    }


epsilon = 1e-05
highest = lax.Precision.HIGHEST

@jax.custom_vjp
def low(v):
    return lax.optimization_barrier(v.astype(jnp.bfloat16)).astype(jnp.float32)

@jax.custom_vjp
def low_back(v):
    return v

def low_keep(v):
    return (low(v), None)

def low_pass(kept, grad):
    return (grad,)

def back_keep(v):
    return (v, None)

def back_low(kept, grad):
    return (low(grad),)
low.defvjp(low_keep, low_pass)
low_back.defvjp(back_keep, back_low)

def layer_norm(row_block, gain, bias):
    centre = lax.optimization_barrier(jnp.mean(row_block, axis=-1, keepdims=True))
    centred = row_block - centre
    spread = lax.optimization_barrier(jnp.mean(centred * centred, axis=-1, keepdims=True))
    return centred * lax.rsqrt(spread + epsilon) * gain + bias

def matmul(left, right):
    return jnp.dot(left, right, precision=highest, preferred_element_type=jnp.float32)

def seq_index(positions, seq_starts):
    return lax.optimization_barrier(jnp.sum((positions[:, None] >= seq_starts[None, 1:]).astype(jnp.int32), axis=1)).astype(jnp.int32)

def seq_place(positions, seq_starts, block_sizes):
    number = seq_index(positions, seq_starts)
    onehot = number[:, None] == jnp.arange(seq_starts.shape[0], dtype=jnp.int32)[None, :]
    opening = lax.optimization_barrier(jnp.sum(jnp.where(onehot, seq_starts[None, :], 0), axis=1)).astype(jnp.int32)
    length = lax.optimization_barrier(jnp.sum(jnp.where(onehot, block_sizes[None, :], 0), axis=1)).astype(jnp.int32)
    block_first = opening + (positions - opening) // length * length
    return (opening, block_first.astype(jnp.int32))

def ssm_tables(decay_rate, drive_in, read_out, total_len, block_len):
    step_lags = jnp.arange(block_len + 1, dtype=jnp.float32)
    powers = jnp.exp(-(decay_rate / total_len)[None, :, :] * step_lags[:, None, None])
    driving = jnp.sqrt(-jnp.expm1(-2.0 * decay_rate / total_len)) * drive_in
    kernel = lax.optimization_barrier(jnp.sum(powers[:block_len] * (read_out * driving)[None, :, :], axis=2))
    offsets = jnp.arange(block_len, dtype=jnp.int32)
    toeplitz = jnp.take(kernel, jnp.maximum(offsets[:, None] - offsets[None, :], 0), axis=0)
    return (powers, driving, toeplitz)

def ssm_block(state_now, feed_rows, seq_rows, seq_before, powers, driving, toeplitz, read_out, skip_gain):
    block_len = feed_rows.shape[0]
    offsets = jnp.arange(block_len, dtype=jnp.int32)
    linked = ((seq_rows[:, None] == seq_rows[None, :]) & (offsets[:, None] >= offsets[None, :])).astype(jnp.float32)
    carried = (seq_rows == seq_before).astype(jnp.float32)
    mixed = jnp.einsum('ijc,jc->ic', toeplitz * linked[:, :, None], feed_rows, precision=highest)
    entering = carried[:, None] * jnp.einsum('icn,cn->ic', powers[1:], read_out * state_now, precision=highest)
    result = mixed + entering + skip_gain * feed_rows
    reaching = powers[:block_len][::-1] * linked[block_len - 1][:, None, None]
    leaving = carried[block_len - 1] * powers[block_len] * state_now + driving * jnp.einsum('jcn,jc->cn', reaching, feed_rows, precision=highest)
    return (leaving, result)

def ssm_chain(feed_all, decay_rate, drive_in, read_out, skip_gain, seq_starts):
    row_count, col_count = feed_all.shape
    tiles = row_count // SB
    seq_rows = seq_index(jnp.arange(row_count, dtype=jnp.int32), seq_starts)
    seq_before = seq_index(jnp.arange(tiles, dtype=jnp.int32) * SB - 1, seq_starts)
    powers, driving, toeplitz = ssm_tables(decay_rate, drive_in, read_out, TOKENS, SB)

    def advance(state_now, pieces):
        return ssm_block(state_now, pieces[0], pieces[1], pieces[2], powers, driving, toeplitz, read_out, skip_gain)
    anchor_state = jnp.zeros((col_count, NS), jnp.float32)
    _, outputs = lax.scan(jax.checkpoint(advance), anchor_state, (feed_all.reshape(tiles, SB, col_count), seq_rows.reshape(tiles, SB), seq_before))
    return outputs.reshape(row_count, col_count)

def to_heads(rows_in):
    return rows_in.reshape(rows_in.shape[0], rows_in.shape[1] // HD, HD)

def attend_tile(query_rows, key_rows, value_rows, context_rows, query_pos, key_pos, seq_starts, block_sizes):
    opening, block_first = seq_place(query_pos, seq_starts, block_sizes)
    see_local = (key_pos[None, :] >= block_first[:, None]) & (key_pos[None, :] <= query_pos[:, None])
    see_context = (key_pos[None, :] >= jnp.maximum(block_first - CTX, opening)[:, None]) & (key_pos[None, :] < block_first[:, None])
    factor = HD ** (-0.5)
    query_heads = to_heads(query_rows)
    context_heads = to_heads(context_rows)
    score_local = low_back(factor * jnp.einsum('qhd,khd->hqk', query_heads, to_heads(key_rows), precision=highest))
    score_context = low_back(factor * jnp.einsum('qhd,khd->hqk', query_heads, context_heads, precision=highest))
    score_local = jnp.where(see_local[None], score_local, -jnp.inf)
    score_context = jnp.where(see_context[None], score_context, -jnp.inf)
    top_score = jnp.maximum(lax.optimization_barrier(jnp.max(score_local, axis=-1)), lax.optimization_barrier(jnp.max(score_context, axis=-1)))
    exp_local = jnp.exp(score_local - top_score[..., None])
    exp_context = jnp.exp(score_context - top_score[..., None])
    mass = lax.optimization_barrier(jnp.sum(exp_local, axis=-1)) + lax.optimization_barrier(jnp.sum(exp_context, axis=-1))
    weight_local = low(exp_local / mass[..., None])
    weight_context = low(exp_context / mass[..., None])
    mixed = jnp.einsum('hqk,khd->qhd', weight_local, to_heads(value_rows), precision=highest)
    mixed = mixed + jnp.einsum('hqk,khd->qhd', weight_context, context_heads, precision=highest)
    return mixed.reshape(query_rows.shape)

def attend_stream(query, key, value, context, seq_starts, block_sizes):
    row_count, col_count = query.shape
    window = 2 * BLOCK + CTX
    reach = window + QB
    front = jnp.zeros((window, col_count), jnp.float32)
    key_pad = jnp.concatenate([front, key], axis=0)
    value_pad = jnp.concatenate([front, value], axis=0)
    context_pad = jnp.concatenate([front, context], axis=0)

    def one_tile(number):
        offset = number * QB
        query_pos = offset + jnp.arange(QB, dtype=jnp.int32)
        key_pos = offset - window + jnp.arange(reach, dtype=jnp.int32)
        return attend_tile(lax.dynamic_slice_in_dim(query, offset, QB, 0), lax.dynamic_slice_in_dim(key_pad, offset, reach, 0), lax.dynamic_slice_in_dim(value_pad, offset, reach, 0), lax.dynamic_slice_in_dim(context_pad, offset, reach, 0), query_pos, key_pos, seq_starts, block_sizes)
    outputs = lax.map(jax.checkpoint(one_tile), jnp.arange(row_count // QB, dtype=jnp.int32))
    return outputs.reshape(row_count, col_count)

def reference(tokens_in, seq_starts, block_sizes, norm1_gain, norm1_bias, w_query, w_key, w_value, w_output, ssm_rate, ssm_input, ssm_output, ssm_skip, norm2_gain, norm2_bias, w_up, up_bias, w_down, down_bias, out_grad):

    def layer(tokens, gain_one, bias_one, wq_full, wk_full, wv_full, wo_full, decay_rate, drive_in, read_out, skip_gain, gain_two, bias_two, wup_full, bias_up, wdown_full, bias_down):
        hid = low(layer_norm(tokens, gain_one, bias_one))
        query = low_back(low(matmul(hid, wq_full)))
        key = low_back(low(matmul(hid, wk_full)))
        value = low_back(low(matmul(hid, wv_full)))
        feed_all = low_back(hid)
        context = low(ssm_chain(feed_all, decay_rate, drive_in, read_out, skip_gain, seq_starts))
        attended = low_back(low(attend_stream(query, key, value, context, seq_starts, block_sizes)))
        middle = tokens + low_back(matmul(attended, wo_full))
        normed = low(layer_norm(middle, gain_two, bias_two))
        before = low_back(matmul(normed, wup_full) + bias_up)
        active = low(jax.nn.gelu(before))
        return middle + matmul(active, wdown_full) + bias_down
    floats = tuple((arg.astype(jnp.float32) for arg in (tokens_in, norm1_gain, norm1_bias, w_query, w_key, w_value, w_output, ssm_rate, ssm_input, ssm_output, ssm_skip, norm2_gain, norm2_bias, w_up, up_bias, w_down, down_bias)))
    result, pullback = jax.vjp(layer, *floats)
    grads = pullback(out_grad.astype(jnp.float32))
    return (result.astype(jnp.bfloat16), grads[0], grads[1], grads[2], grads[3], grads[4], grads[5], grads[6], grads[7], grads[8], grads[9], grads[10], grads[11], grads[12], grads[13], grads[14], grads[15], grads[16])
```

```python
import functools
import math

import jax
import jax.numpy as jnp
from jax import lax
from jax.experimental import pallas as pl
from jax.experimental.pallas import tpu as pltpu
from jax.sharding import PartitionSpec as P

HD = 128
CTX = 128
BLOCK = 256
NS = 16
SUB = 8
UNROLL = 8
HALF = 8
TILE = 256
MIB = 1 << 20
LOWEST = -1e30
FACTOR = HD ** (-0.5)
FACTOR2 = FACTOR * math.log2(math.e)


def spread(table, n):
    return jnp.broadcast_to(table[n : n + 1, :], (SUB, table.shape[1]))


def stepped(length, chunk, step, body, carry):
    blocks = length // UNROLL
    hit = jnp.where(step < 0, blocks, step // UNROLL)

    def plain(block, now):
        for inner in range(UNROLL):
            now = body(block * UNROLL + inner, now, None)
        return now

    def masked(block, now):
        rows = lax.broadcasted_iota(jnp.int32, (SUB, HD), 0)
        for inner in range(UNROLL):
            t = block * UNROLL + inner
            live = jnp.where((rows == chunk) & (t == step), 0.0, 1.0)
            now = body(t, now, live)
        return now

    carry = lax.fori_loop(0, hit, plain, carry)
    carry = lax.fori_loop(hit, jnp.minimum(hit + 1, blocks), masked, carry)
    return lax.fori_loop(hit + 1, blocks, plain, carry)


def ssm_ends_kernel(brk, feed, decay, ends, rows):
    length = rows.shape[0] // SUB
    rows[...] = feed[...].astype(jnp.float32)
    table = decay[...]
    factors = [spread(table, n) for n in range(NS)]

    def body(t, states, live):
        drive = rows[pl.ds(t, SUB, stride=length), :]
        if live is not None:
            states = [state * live for state in states]
        return tuple(state * factor + drive for state, factor in zip(states, factors))

    zero = jnp.zeros((SUB, HD), jnp.float32)
    states = stepped(length, brk[0], brk[1], body, (zero,) * NS)
    for n in range(NS):
        ends[n] = states[n]


def ssm_out_kernel(brk, feed, decay, mix, skip, starts, out, rows, sums):
    length = rows.shape[0] // SUB
    rows[...] = feed[...].astype(jnp.float32)
    table = decay[...]
    weights = mix[...]
    factors = [spread(table, n) for n in range(NS)]
    mixes = [spread(weights, n) for n in range(NS)]
    direct = spread(skip[...], 0)

    def body(t, states, live):
        drive = rows[pl.ds(t, SUB, stride=length), :]
        if live is not None:
            states = [state * live for state in states]
        states = tuple(state * factor + drive for state, factor in zip(states, factors))
        parts = [state * weight for state, weight in zip(states, mixes)] + [direct * drive]
        while len(parts) > 1:
            parts = [a + b for a, b in zip(parts[::2], parts[1::2])] + (
                [parts[-1]] if len(parts) % 2 else []
            )
        sums[pl.ds(t, SUB, stride=length), :] = parts[0]
        return states

    stepped(length, brk[0], brk[1], body, tuple(starts[n] for n in range(NS)))
    out[...] = sums[...].astype(out.dtype)


def ssm_back_ends_kernel(brk, slope, decay, ends, lags):
    length = slope.shape[0] // SUB
    table = decay[...]
    zero = jnp.zeros((SUB, HD), jnp.float32)
    factors = [spread(table, n) for n in range(NS)]

    def body(t, carry, live):
        drive = slope[pl.ds(length - 1 - t, SUB, stride=length), :]
        adjoint, lag = carry[:NS], carry[NS:]
        lag = [a * f + b for a, f, b in zip(lag, factors, adjoint)]
        adjoint = [a * f + drive for a, f in zip(adjoint, factors)]
        if live is not None:
            lag = [a * live for a in lag]
            adjoint = [a * live for a in adjoint]
        return tuple(adjoint) + tuple(lag)

    back = jnp.where(brk[1] < 0, -1, length - 1 - brk[1])
    done = stepped(length, brk[0], back, body, (zero,) * (2 * NS))
    for n in range(NS):
        ends[n] = done[n]
        lags[n] = done[NS + n]


def ssm_back_kernel(
    brk, slope, feed, decay, mix, skip, starts, lag_starts, back, sums, lag_sums, skip_sum, rows, total
):
    length = rows.shape[0] // SUB
    rows[...] = feed[...].astype(jnp.float32)
    table = decay[...]
    weights = mix[...]
    zero = jnp.zeros((SUB, HD), jnp.float32)
    total[...] = slope[...] * skip[...]
    skip_sum[...] = jnp.sum(slope[...] * rows[...], axis=0, keepdims=True)
    reversed_step = jnp.where(brk[1] < 0, -1, length - 1 - brk[1])
    for base in range(0, NS, HALF):
        factors = [spread(table, base + n) for n in range(HALF)]
        mixes = [spread(weights, base + n) for n in range(HALF)]

        def body(t, carry, live):
            at = pl.ds(length - 1 - t, SUB, stride=length)
            drive, source = slope[at, :], rows[at, :]
            adjoint, lag = carry[:HALF], carry[HALF : 2 * HALF]
            direct, late = carry[2 * HALF : 3 * HALF], carry[3 * HALF :]
            lag = [a * f + b for a, f, b in zip(lag, factors, adjoint)]
            adjoint = [a * f + drive for a, f in zip(adjoint, factors)]
            direct = [a + b * source for a, b in zip(direct, adjoint)]
            late = [a + b * source for a, b in zip(late, lag)]
            parts = [a * b for a, b in zip(adjoint, mixes)]
            while len(parts) > 1:
                parts = [a + b for a, b in zip(parts[::2], parts[1::2])]
            total[at, :] = total[at, :] + parts[0]
            if live is not None:
                lag = [a * live for a in lag]
                adjoint = [a * live for a in adjoint]
            return tuple(adjoint) + tuple(lag) + tuple(direct) + tuple(late)

        first = tuple(starts[base + n] for n in range(HALF)) + tuple(
            lag_starts[base + n] for n in range(HALF)
        )
        done = stepped(length, brk[0], reversed_step, body, first + (zero,) * (2 * HALF))
        for n in range(HALF):
            sums[base + n : base + n + 1, :] = jnp.sum(done[2 * HALF + n], axis=0, keepdims=True)
            lag_sums[base + n : base + n + 1, :] = jnp.sum(
                done[3 * HALF + n], axis=0, keepdims=True
            )
    back[...] = total[...].astype(back.dtype)


def columns(rows):
    return pl.BlockSpec((rows, HD), lambda g: (0, g))


def chunked():
    return pl.BlockSpec((NS, SUB, HD), lambda g: (0, 0, g))


SCALARS = pl.BlockSpec(memory_space=pltpu.SMEM)


def wide(limit=48):
    return pltpu.CompilerParams(vmem_limit_bytes=limit * MIB)


def ssm_ends(brk, feed, decay):
    rows, width = feed.shape
    return pl.pallas_call(
        ssm_ends_kernel,
        grid=(width // HD,),
        in_specs=[SCALARS, columns(rows), columns(NS)],
        out_specs=chunked(),
        out_shape=jax.ShapeDtypeStruct((NS, SUB, width), jnp.float32),
        scratch_shapes=[pltpu.VMEM((rows, HD), jnp.float32)],
        compiler_params=wide(),
        name="ssm_ends",
    )(brk, feed, decay)


def ssm_out(brk, feed, decay, mix, skip, starts):
    rows, width = feed.shape
    return pl.pallas_call(
        ssm_out_kernel,
        grid=(width // HD,),
        in_specs=[SCALARS, columns(rows), columns(NS), columns(NS), columns(1), chunked()],
        out_specs=columns(rows),
        out_shape=jax.ShapeDtypeStruct((rows, width), jnp.bfloat16),
        scratch_shapes=[pltpu.VMEM((rows, HD), jnp.float32)] * 2,
        compiler_params=wide(),
        name="ssm_out",
    )(brk, feed, decay, mix, skip, starts)


def ssm_back_ends(brk, slope, decay):
    rows, width = slope.shape
    return pl.pallas_call(
        ssm_back_ends_kernel,
        grid=(width // HD,),
        in_specs=[SCALARS, columns(rows), columns(NS)],
        out_specs=(chunked(), chunked()),
        out_shape=(jax.ShapeDtypeStruct((NS, SUB, width), jnp.float32),) * 2,
        compiler_params=wide(),
        name="ssm_back_ends",
    )(brk, slope, decay)


def ssm_back(brk, slope, feed, decay, mix, skip, starts, lag_starts):
    rows, width = feed.shape
    table = jax.ShapeDtypeStruct((NS, width), jnp.float32)
    return pl.pallas_call(
        ssm_back_kernel,
        grid=(width // HD,),
        in_specs=[
            SCALARS,
            columns(rows),
            columns(rows),
            columns(NS),
            columns(NS),
            columns(1),
            chunked(),
            chunked(),
        ],
        out_specs=(columns(rows), columns(NS), columns(NS), columns(1)),
        out_shape=(
            jax.ShapeDtypeStruct((rows, width), jnp.bfloat16),
            table,
            table,
            jax.ShapeDtypeStruct((1, width), jnp.float32),
        ),
        scratch_shapes=[pltpu.VMEM((rows, HD), jnp.float32)] * 2,
        compiler_params=wide(),
        name="ssm_back",
    )(brk, slope, feed, decay, mix, skip, starts, lag_starts)


def across(left, right):
    return lax.dot_general(
        left, right, (((1,), (1,)), ((), ())), preferred_element_type=jnp.float32
    )


def times(left, right):
    return lax.dot_general(
        left, right, (((1,), (0,)), ((), ())), preferred_element_type=jnp.float32
    )


def turn(source, target):
    for at in range(0, source.shape[0], TILE):
        size = min(TILE, source.shape[0] - at)
        piece = source[at : at + size, :].astype(jnp.float32)
        target[:, at : at + size] = piece.T.astype(target.dtype)


def local_tiles(where_, tile):
    return (where_[4 + tile] + 2 * BLOCK) // TILE


def next_block(where_, now):
    second = where_[1]
    length = jnp.where(now >= second, where_[3], where_[2])
    after = now + length
    return jnp.where((now < second) & (after > second), second, after)


def local_mask(tile, key_tile, first):
    rows = lax.broadcasted_iota(jnp.int32, (TILE, TILE), 0) + (key_tile * TILE - 2 * BLOCK)
    cols = lax.broadcasted_iota(jnp.int32, (1, TILE), 1) + tile * TILE
    return (rows >= first) & (rows <= cols)


def context_at(now):
    return pl.multiple_of((now + 2 * BLOCK) // CTX * CTX, CTX)


def context_mask(start, now, first, opening):
    rows = lax.broadcasted_iota(jnp.int32, (TILE, TILE), 0) + (start - 2 * BLOCK - CTX)
    low = jnp.where(first == now, jnp.maximum(now - CTX, opening), 1 << 28)
    return (rows >= low) & (rows < now)


def attend_kernel(
    where_, query, key, value, context, first, opening, out, fine, level, value_t, context_t
):
    turn(value, value_t)
    turn(context, context_t)

    def one_tile(tile, _):
        rows = query[pl.ds(pl.multiple_of(tile * TILE, TILE), TILE), :]
        firsts = first[tile]
        openings = opening[tile]

        def add(carry, keys, values_t, mask):
            top, mass, low_mass, total = carry
            score = jnp.where(mask, across(keys, rows) * FACTOR2, LOWEST)
            new_top = jnp.maximum(top, jnp.max(score, axis=0, keepdims=True))
            prob = jnp.exp2(score - new_top)
            shrink = jnp.exp2(top - new_top)
            low = prob.astype(jnp.bfloat16)
            mass = mass * shrink + jnp.sum(prob, axis=0, keepdims=True)
            low_mass = low_mass * shrink + jnp.sum(
                low.astype(jnp.float32), axis=0, keepdims=True
            )
            total = total * shrink + times(values_t, low)
            return new_top, mass, low_mass, total

        def local(key_tile, carry):
            at = pl.ds(pl.multiple_of(key_tile * TILE, TILE), TILE)
            return add(carry, key[at, :], value_t[:, at], local_mask(tile, key_tile, firsts))

        def earlier(state):
            now, carry = state[0], state[1:]
            start = context_at(now)
            at = pl.ds(start, TILE)
            carry = add(
                carry,
                context[at, :],
                context_t[:, at],
                context_mask(start, now, firsts, openings),
            )
            return (next_block(where_, now),) + tuple(carry)

        carry = (
            jnp.full((1, TILE), LOWEST, jnp.float32),
            jnp.zeros((1, TILE), jnp.float32),
            jnp.zeros((1, TILE), jnp.float32),
            jnp.zeros((HD, TILE), jnp.float32),
        )
        carry = lax.fori_loop(local_tiles(where_, tile), tile + 3, local, carry)
        state = lax.while_loop(
            lambda state: state[0] < (tile + 1) * TILE, earlier, (where_[4 + tile],) + carry
        )
        _, top, mass, low_mass, total = state
        done = (total / low_mass).T
        here = pl.ds(pl.multiple_of(tile * TILE, TILE), TILE)
        fine[here, :] = done
        out[here, :] = done.astype(out.dtype)
        level[0, tile] = top + jnp.log2(mass)
        return 0

    lax.fori_loop(0, query.shape[0] // TILE, one_tile, 0)


def attend_back_kernel(
    where_,
    query,
    key,
    value,
    context,
    first,
    opening,
    attended,
    grad,
    level,
    back_query,
    key_rim,
    value_rim,
    context_rim,
    back_key,
    back_value,
    back_context,
    key_t,
    context_t,
    key_sum,
    value_sum,
    context_sum,
):
    turn(key, key_t)
    turn(context, context_t)
    key_sum[...] = jnp.zeros_like(key_sum)
    value_sum[...] = jnp.zeros_like(value_sum)
    context_sum[...] = jnp.zeros_like(context_sum)

    def one_tile(tile, _):
        here = pl.ds(pl.multiple_of(tile * TILE, TILE), TILE)
        rows = query[here, :]
        grads = grad[here, :]
        firsts = first[tile]
        openings = opening[tile]
        levels = level[0, tile]
        joint = grads.astype(jnp.float32) * attended[here, :]
        centre = jnp.sum(joint.T, axis=0, keepdims=True)

        def slopes(keys, values, mask):
            prob = jnp.exp2(jnp.where(mask, across(keys, rows) * FACTOR2 - levels, LOWEST))
            slope = prob * (across(values, grads) - centre)
            return prob.astype(jnp.bfloat16), slope.astype(jnp.bfloat16)

        def local(key_tile, total):
            at = pl.ds(pl.multiple_of(key_tile * TILE, TILE), TILE)
            prob, slope = slopes(key[at, :], value[at, :], local_mask(tile, key_tile, firsts))
            key_sum[at, :] += times(slope, rows)
            value_sum[at, :] += times(prob, grads)
            return total + times(key_t[:, at], slope)

        def earlier(state):
            now, total = state
            start = context_at(now)
            at = pl.ds(start, TILE)
            near = context[at, :]
            prob, slope = slopes(near, near, context_mask(start, now, firsts, openings))
            context_sum[at, :] += FACTOR * times(slope, rows) + times(prob, grads)
            return next_block(where_, now), total + times(context_t[:, at], slope)

        total = jnp.zeros((HD, TILE), jnp.float32)
        total = lax.fori_loop(local_tiles(where_, tile), tile + 3, local, total)
        _, total = lax.while_loop(
            lambda state: state[0] < (tile + 1) * TILE, earlier, (where_[4 + tile], total)
        )
        back_query[here, :] = (FACTOR * total).T.astype(back_query.dtype)
        return 0

    lax.fori_loop(0, query.shape[0] // TILE, one_tile, 0)
    window = 2 * BLOCK
    key_rim[...] = (FACTOR * key_sum[:window, :]).astype(key_rim.dtype)
    value_rim[...] = value_sum[:window, :].astype(value_rim.dtype)
    context_rim[...] = context_sum[: window + CTX, :].astype(context_rim.dtype)
    back_key[...] = FACTOR * key_sum[window:, :]
    back_value[...] = value_sum[window:, :]
    back_context[...] = context_sum[window + CTX :, :]


def attend(where_, query, key, value, context, first, opening):
    rows, width = query.shape
    heads, tiles = width // HD, rows // TILE
    near, far = key.shape[0], context.shape[0]
    whole = pl.BlockSpec((tiles, 1, TILE), lambda g: (0, 0, 0))
    return pl.pallas_call(
        attend_kernel,
        grid=(heads,),
        in_specs=[
            SCALARS,
            columns(rows),
            columns(near),
            columns(near),
            columns(far),
            whole,
            whole,
        ],
        out_specs=(
            columns(rows),
            columns(rows),
            pl.BlockSpec((1, tiles, 1, TILE), lambda g: (g, 0, 0, 0)),
        ),
        out_shape=(
            jax.ShapeDtypeStruct((rows, width), jnp.bfloat16),
            jax.ShapeDtypeStruct((rows, width), jnp.float32),
            jax.ShapeDtypeStruct((heads, tiles, 1, TILE), jnp.float32),
        ),
        scratch_shapes=[
            pltpu.VMEM((HD, near), jnp.bfloat16),
            pltpu.VMEM((HD, far), jnp.bfloat16),
        ],
        compiler_params=wide(),
        name="attend",
    )(where_, query, key, value, context, first, opening)


def attend_back(where_, query, key, value, context, first, opening, attended, grad, level):
    rows, width = query.shape
    heads, tiles = width // HD, rows // TILE
    near, far = key.shape[0], context.shape[0]
    whole = pl.BlockSpec((tiles, 1, TILE), lambda g: (0, 0, 0))
    low = lambda count: jax.ShapeDtypeStruct((count, width), jnp.bfloat16)
    full = lambda count: jax.ShapeDtypeStruct((count, width), jnp.float32)
    return pl.pallas_call(
        attend_back_kernel,
        grid=(heads,),
        in_specs=[
            SCALARS,
            columns(rows),
            columns(near),
            columns(near),
            columns(far),
            whole,
            whole,
            columns(rows),
            columns(rows),
            pl.BlockSpec((1, tiles, 1, TILE), lambda g: (g, 0, 0, 0)),
        ],
        out_specs=(
            columns(rows),
            columns(near - rows),
            columns(near - rows),
            columns(far - rows),
            columns(rows),
            columns(rows),
            columns(rows),
        ),
        out_shape=(
            low(rows),
            low(near - rows),
            low(near - rows),
            low(far - rows),
            full(rows),
            full(rows),
            full(rows),
        ),
        scratch_shapes=[
            pltpu.VMEM((HD, near), jnp.bfloat16),
            pltpu.VMEM((HD, far), jnp.bfloat16),
            pltpu.VMEM((near, HD), jnp.float32),
            pltpu.VMEM((near, HD), jnp.float32),
            pltpu.VMEM((far, HD), jnp.float32),
        ],
        compiler_params=wide(),
        name="attend_back",
    )(where_, query, key, value, context, first, opening, attended, grad, level)


MESH = pl.DeviceIdType.MESH


def bits_of(count):
    return count.bit_length() - 1


def mesh_bits():
    found = []
    tok, head = lax.axis_index("tok"), lax.axis_index("head")
    for axis in ("head", "tok"):
        for level in range(bits_of(lax.axis_size(axis))):
            at = head if axis == "head" else tok
            bit = (at // (1 << level)) % 2
            other = at + (1 - 2 * bit) * (1 << level)
            found.append((bit, (tok, other) if axis == "head" else (other, head)))
    return found


def greet(partners):
    barrier = pltpu.get_barrier_semaphore()
    for partner in partners:
        pl.semaphore_signal(barrier, inc=1, device_id=partner, device_id_type=MESH)
    pl.semaphore_wait(barrier, len(partners))


def halving_orders(bits):
    rest = list(range(1, bits))
    return [
        [0] + rest,
        [0] + [rest[1], rest[0]] + rest[2:],
        [0] + [rest[2], rest[0], rest[1]] + rest[3:],
    ]


def slot_of(block, order):
    place = 0
    for bit in order:
        place = place * 2 + (block // (1 << bit)) % 2
    return place


ROWS = 512


def products_kernel(pairs, plan, bits, *refs):
    lefts, refs = refs[:pairs], refs[pairs:]
    rights, refs = refs[:pairs], refs[pairs:]
    outs, refs = refs[:pairs], refs[pairs:]
    count = len(plan)
    grads, refs = refs[:count], refs[count:]
    arrivals, refs = refs[: count * bits], refs[count * bits :]
    send_sems, recv_sems = refs
    here = mesh_bits()
    orders = halving_orders(bits)
    greet([partner for _, partner in here])
    base = [0] * count
    started = []

    def send(number, stage):
        bit, partner = here[orders[plan[number][3]][stage]]
        half = 1 << (bits - 1 - stage)
        copy = pltpu.make_async_remote_copy(
            src_ref=grads[number].at[pl.ds(base[number] + (1 - bit) * half, half)],
            dst_ref=arrivals[number * bits + stage],
            send_sem=send_sems.at[number, stage],
            recv_sem=recv_sems.at[number, stage],
            device_id=partner,
            device_id_type=MESH,
        )
        copy.start()
        started.append(copy)
        base[number] = base[number] + bit * half
        return copy

    flying = []
    for number, (pair, start, width, order) in enumerate(plan):
        left, right, grad = lefts[pair], rights[pair], grads[number]
        block = grad.shape[1]
        each = ROWS // block

        def some_rows(chunk, _, left=left, right=right, grad=grad, block=block, each=each, start=start, width=width, order=order):
            at = pl.ds(pl.multiple_of(chunk * ROWS, ROWS), ROWS)
            found = lax.dot_general(
                left[:, at],
                right[:, start : start + width],
                (((0,), (0,)), ((), ())),
                preferred_element_type=jnp.float32,
            ).astype(jnp.bfloat16)
            for inner in range(each):
                grad[slot_of(chunk * each + inner, orders[order])] = found[
                    inner * block : (inner + 1) * block
                ]
            return 0

        lax.fori_loop(0, left.shape[1] // ROWS, some_rows, 0)
        flying.append(send(number, 0))

    for stage in range(bits):
        for number, (pair, start, width, order) in enumerate(plan):
            flying[number].wait_recv()
            grad, arrival = grads[number], arrivals[number * bits + stage]
            half = 1 << (bits - 1 - stage)
            if stage == bits - 1:
                outs[pair][:, start : start + width] = grad[base[number]].astype(
                    jnp.float32
                ) + arrival[0].astype(jnp.float32)
            else:
                place = base[number]

                def add(i, _, grad=grad, arrival=arrival, place=place):
                    grad[place + i] = grad[place + i] + arrival[i]
                    return 0

                lax.fori_loop(0, half, add, 0)
                flying[number] = send(number, stage + 1)
    for copy in started:
        copy.wait_send()


def summed_products(lefts, rights, plan, collective_id, name):
    devices = lax.axis_size("tok") * lax.axis_size("head")
    bits = bits_of(devices)
    blocks = [left.shape[1] // devices for left in lefts]
    if min(blocks) < 16:
        return [
            lax.psum_scatter(
                product_left(left, right), ("tok", "head"), scatter_dimension=0, tiled=True
            )
            for left, right in zip(lefts, rights)
        ]
    scratch = [pltpu.VMEM((devices, blocks[p], w), jnp.bfloat16) for p, _, w, _ in plan]
    for p, _, w, _ in plan:
        for stage in range(bits):
            scratch.append(pltpu.VMEM((1 << (bits - 1 - stage), blocks[p], w), jnp.bfloat16))
    flops = sum(2 * l.shape[0] * l.shape[1] * r.shape[1] for l, r in zip(lefts, rights))
    return pl.pallas_call(
        functools.partial(products_kernel, len(lefts), plan, bits),
        in_specs=[pl.BlockSpec(memory_space=pltpu.VMEM)] * (2 * len(lefts)),
        out_specs=[pl.BlockSpec(memory_space=pltpu.VMEM)] * len(lefts),
        out_shape=[
            jax.ShapeDtypeStruct((block, right.shape[1]), jnp.float32)
            for block, right in zip(blocks, rights)
        ],
        scratch_shapes=scratch
        + [pltpu.SemaphoreType.DMA((len(plan), bits)), pltpu.SemaphoreType.DMA((len(plan), bits))],
        compiler_params=pltpu.CompilerParams(
            collective_id=collective_id, has_side_effects=True, vmem_limit_bytes=60 * MIB
        ),
        cost_estimate=pl.CostEstimate(flops=flops, bytes_accessed=20 * MIB, transcendentals=0),
        name=name,
    )(*lefts, *rights)


FEED_PLAN = [
    (0, 0, 512, 0),
    (0, 512, 512, 1),
    (1, 0, 512, 2),
    (1, 512, 512, 0),
    (1, 1024, 512, 1),
    (1, 1536, 512, 2),
    (1, 2048, 512, 0),
    (1, 2560, 512, 1),
    (2, 0, 512, 2),
    (1, 3072, 512, 0),
    (1, 3584, 512, 1),
    (2, 512, 512, 2),
]
HEAD_PLAN = [
    (0, 0, 512, 0),
    (0, 512, 512, 1),
    (1, 0, 512, 2),
    (1, 512, 512, 0),
    (2, 0, 512, 1),
    (2, 512, 512, 0),
]


def tok_peers():
    count, here = lax.axis_size("tok"), lax.axis_index("tok")
    head = lax.axis_index("head")
    return [
        ((lax.rem(here + step, count), head), lax.rem(here + count - step, count))
        for step in range(1, count)
    ]


def share(mine, every, send_sems, recv_sems, place, peers):
    copies = []
    for step, (target, _) in enumerate(peers):
        copy = pltpu.make_async_remote_copy(
            src_ref=mine,
            dst_ref=every.at[place],
            send_sem=send_sems.at[step],
            recv_sem=recv_sems.at[step],
            device_id=target,
            device_id_type=MESH,
        )
        copy.start()
        copies.append(copy)
    return copies


def state_exchange_kernel(
    keep, whole, ends, chunk_decay, span_decay, starts, mine, every, send_sems, recv_sems
):
    here, count = lax.axis_index("tok"), every.shape[0]
    peers = tok_peers()
    greet([target for target, _ in peers])
    factor = chunk_decay[...]
    now = ends[:, 0, :]
    for chunk in range(1, SUB):
        now = keep[chunk] * (factor * now) + ends[:, chunk, :]
    mine[...] = now
    every[here] = now
    copies = share(mine, every, send_sems, recv_sems, here, peers)
    for copy in copies:
        copy.wait()
    over = span_decay[...]
    now = jnp.zeros_like(over)
    for place in range(count - 1):
        now = jnp.where(place < here, whole[place] * (over * now) + every[place], now)
    for chunk in range(SUB):
        starts[:, chunk, :] = now
        now = keep[chunk] * (factor * now) + ends[:, chunk, :]


def adjoint_exchange_kernel(
    keep,
    whole,
    ends,
    lags,
    chunk_decay,
    chunk_slope,
    span_decay,
    span_slope,
    starts,
    lag_starts,
    mine,
    every,
    send_sems,
    recv_sems,
):
    here, count = lax.axis_index("tok"), every.shape[0]
    peers = tok_peers()
    greet([target for target, _ in peers])
    factor, slope = chunk_decay[...], chunk_slope[...]
    now, late = ends[:, SUB - 1, :], lags[:, SUB - 1, :]
    for chunk in reversed(range(SUB - 1)):
        late = keep[chunk] * (factor * late + slope * now) + lags[:, chunk, :]
        now = keep[chunk] * (factor * now) + ends[:, chunk, :]
    mine[0] = now
    mine[1] = late
    every[here, 0] = now
    every[here, 1] = late
    copies = share(mine, every, send_sems, recv_sems, here, peers)
    for copy in copies:
        copy.wait()
    over, over_slope = span_decay[...], span_slope[...]
    now, late = jnp.zeros_like(over), jnp.zeros_like(over)
    for place in reversed(range(1, count)):
        reached = place > here
        late = jnp.where(
            reached, whole[place] * (over * late + over_slope * now) + every[place, 1], late
        )
        now = jnp.where(reached, whole[place] * (over * now) + every[place, 0], now)
    for chunk in reversed(range(SUB)):
        starts[:, chunk, :] = now
        lag_starts[:, chunk, :] = late
        late = keep[chunk] * (factor * late + slope * now) + lags[:, chunk, :]
        now = keep[chunk] * (factor * now) + ends[:, chunk, :]


VMEM = pl.BlockSpec(memory_space=pltpu.VMEM)


def state_exchange(keep, whole, ends, chunk_decay, span_decay, collective_id):
    states, _, width = ends.shape
    count = whole.shape[0]
    return pl.pallas_call(
        state_exchange_kernel,
        in_specs=[SCALARS, SCALARS, VMEM, VMEM, VMEM],
        out_specs=VMEM,
        out_shape=jax.ShapeDtypeStruct(ends.shape, jnp.float32),
        scratch_shapes=[
            pltpu.VMEM((states, width), jnp.float32),
            pltpu.VMEM((count, states, width), jnp.float32),
            pltpu.SemaphoreType.DMA((count - 1,)),
            pltpu.SemaphoreType.DMA((count - 1,)),
        ],
        compiler_params=pltpu.CompilerParams(
            collective_id=collective_id, has_side_effects=True, vmem_limit_bytes=16 * MIB
        ),
        name="state_exchange",
    )(keep, whole, ends, chunk_decay, span_decay)


def adjoint_exchange(
    keep, whole, ends, lags, chunk_decay, chunk_slope, span_decay, span_slope, collective_id
):
    states, _, width = ends.shape
    count = whole.shape[0]
    return pl.pallas_call(
        adjoint_exchange_kernel,
        in_specs=[SCALARS, SCALARS] + [VMEM] * 6,
        out_specs=(VMEM, VMEM),
        out_shape=(jax.ShapeDtypeStruct(ends.shape, jnp.float32),) * 2,
        scratch_shapes=[
            pltpu.VMEM((2, states, width), jnp.float32),
            pltpu.VMEM((count, 2, states, width), jnp.float32),
            pltpu.SemaphoreType.DMA((count - 1,)),
            pltpu.SemaphoreType.DMA((count - 1,)),
        ],
        compiler_params=pltpu.CompilerParams(
            collective_id=collective_id, has_side_effects=True, vmem_limit_bytes=16 * MIB
        ),
        name="adjoint_exchange",
    )(keep, whole, ends, lags, chunk_decay, chunk_slope, span_decay, span_slope)


def final_sums_kernel(
    rows, vectors, row_sum, vector_sum, every_row, every_vector, send_rows, recv_rows, send_v, recv_v
):
    tok, head = lax.axis_index("tok"), lax.axis_index("head")
    toks, heads = lax.axis_size("tok"), lax.axis_size("head")
    devices = toks * heads
    here = tok * heads + head
    peers = []
    for step in range(1, devices):
        other = lax.rem(here + step, devices)
        peers.append((other, (other // heads, lax.rem(other, heads))))
    greet([target for _, target in peers])
    every_row[tok] = rows[...]
    every_vector[here] = vectors[here]
    copies = share(rows, every_row, send_rows, recv_rows, tok, tok_peers())
    for step, (other, target) in enumerate(peers):
        copy = pltpu.make_async_remote_copy(
            src_ref=vectors.at[other],
            dst_ref=every_vector.at[here],
            send_sem=send_v.at[step],
            recv_sem=recv_v.at[step],
            device_id=target,
            device_id_type=MESH,
        )
        copy.start()
        copies.append(copy)
    for copy in copies:
        copy.wait()
    row_sum[...] = jnp.sum(every_row[...], axis=0)
    vector_sum[...] = jnp.sum(every_vector[...], axis=0)


def final_sums(rows, vectors, collective_id):
    toks, devices = lax.axis_size("tok"), vectors.shape[0]
    return pl.pallas_call(
        final_sums_kernel,
        in_specs=[VMEM, VMEM],
        out_specs=(VMEM, VMEM),
        out_shape=(
            jax.ShapeDtypeStruct(rows.shape, jnp.float32),
            jax.ShapeDtypeStruct(vectors.shape[1:], jnp.float32),
        ),
        scratch_shapes=[
            pltpu.VMEM((toks,) + rows.shape, jnp.float32),
            pltpu.VMEM(vectors.shape, jnp.float32),
            pltpu.SemaphoreType.DMA((toks - 1,)),
            pltpu.SemaphoreType.DMA((toks - 1,)),
            pltpu.SemaphoreType.DMA((devices - 1,)),
            pltpu.SemaphoreType.DMA((devices - 1,)),
        ],
        compiler_params=pltpu.CompilerParams(
            collective_id=collective_id, has_side_effects=True, vmem_limit_bytes=16 * MIB
        ),
        name="final_sums",
    )(rows, vectors)


epsilon = 1e-05


def layer_norm(row_block, gain, bias):
    centre = jnp.mean(row_block, axis=-1, keepdims=True)
    centred = row_block - centre
    spread = jnp.mean(centred * centred, axis=-1, keepdims=True)
    return centred * lax.rsqrt(spread + epsilon) * gain + bias


def product(left, right):
    return jnp.dot(left, right, preferred_element_type=jnp.float32)


def product_left(left, right):
    return lax.dot_general(
        left, right, (((0,), (0,)), ((), ())), preferred_element_type=jnp.float32
    )


def product_right(left, right):
    return lax.dot_general(
        left, right, (((1,), (1,)), ((), ())), preferred_element_type=jnp.float32
    )


def seq_place(positions, seq_starts, block_sizes):
    later = positions >= seq_starts[1]
    opening = jnp.where(later, seq_starts[1], seq_starts[0])
    length = jnp.where(later, block_sizes[1], block_sizes[0])
    return opening, opening + (positions - opening) // length * length


def shifted(shard, axis, by):
    devices = lax.axis_size(axis)
    pairs = [(i, i + by) for i in range(devices) if 0 <= i + by < devices]
    return lax.ppermute(shard, axis, pairs)


def per_device(
    tokens_in,
    seq_starts,
    block_sizes,
    norm1_gain,
    norm1_bias,
    w_query,
    w_key,
    w_value,
    w_output,
    ssm_rate,
    ssm_input,
    ssm_output,
    ssm_skip,
    norm2_gain,
    norm2_bias,
    w_up,
    up_bias,
    w_down,
    down_bias,
    out_grad,
):
    tok_rows = tokens_in.shape[0]
    pieces, here = lax.axis_size("tok"), lax.axis_index("tok")
    span = tok_rows * lax.axis_size("head")
    total_len = span * pieces
    anchor = here * span
    window = 2 * BLOCK
    length = span // SUB

    residual = tokens_in.astype(jnp.float32)
    normed_one, norm1_pull = jax.vjp(layer_norm, residual, norm1_gain, norm1_bias)
    hidden = normed_one.astype(jnp.bfloat16)
    query = product(hidden, w_query).astype(jnp.bfloat16)
    key_rows = product(hidden, w_key).astype(jnp.bfloat16)
    value_rows = product(hidden, w_value).astype(jnp.bfloat16)
    hidden_h, key_h, value_h, query_h = (
        lax.all_to_all(rows, "head", split_axis=1, concat_axis=0, tiled=True)
        for rows in (hidden, key_rows, value_rows, query)
    )

    second = seq_starts[1] - anchor
    inside = (second >= 0) & (second < span)
    brk = jnp.where(inside, jnp.stack([second // length, second % length]), -1).astype(jnp.int32)
    keep = 1.0 - (jnp.arange(SUB) == brk[0]).astype(jnp.float32)
    whole = 1.0 - (jnp.arange(pieces) == seq_starts[1] // span).astype(jnp.float32)
    positions = anchor + jnp.arange(span, dtype=jnp.int32)
    opening, first = seq_place(positions, seq_starts, block_sizes)
    first = first - anchor
    where_ = jnp.concatenate([jnp.stack([anchor, second]), block_sizes, first[::TILE]]).astype(
        jnp.int32
    )
    first = first.reshape(-1, 1, TILE)
    opening = (opening - anchor).reshape(-1, 1, TILE)

    rate = ssm_rate.T / total_len
    drive_in, read_out = ssm_input.T, ssm_output.T
    skip = ssm_skip[None, :]
    decay = jnp.exp(-rate)
    gain = jnp.sqrt(-jnp.expm1(-2.0 * rate))
    driving = gain * drive_in
    mix = read_out * driving
    chunk_decay = jnp.exp(-rate * length)
    chunk_slope = length * jnp.exp(-rate * (length - 1))
    span_decay = jnp.exp(-rate * span)
    span_slope = span * jnp.exp(-rate * (span - 1))

    ends = ssm_ends(brk, hidden_h, decay)
    starts = state_exchange(keep, whole, ends, chunk_decay, span_decay, 1)
    context = ssm_out(brk, hidden_h, decay, mix, skip, starts)

    rims = shifted(jnp.stack([key_h[span - window :], value_h[span - window :]]), "tok", 1)
    context_rim = shifted(context[span - window - CTX :], "tok", 1)
    key_ext = jnp.concatenate([rims[0], key_h], axis=0)
    value_ext = jnp.concatenate([rims[1], value_h], axis=0)
    context_ext = jnp.concatenate([context_rim, context], axis=0)
    attended, attended_fine, level = attend(where_, query_h, key_ext, value_ext, context_ext, first, opening)
    joined = lax.all_to_all(attended, "head", split_axis=0, concat_axis=1, tiled=True)
    middle = residual + product(joined, w_output)
    normed_two, norm2_pull = jax.vjp(layer_norm, middle, norm2_gain, norm2_bias)
    normed_low = normed_two.astype(jnp.bfloat16)
    before = product(normed_low, w_up) + up_bias
    active, gelu_pull = jax.vjp(jax.nn.gelu, before)
    active_low = active.astype(jnp.bfloat16)
    layer_out = (middle + product(active_low, w_down) + down_bias).astype(jnp.bfloat16)
    grad_top = out_grad.astype(jnp.float32)
    grad_down_bias = jnp.sum(grad_top, axis=0)
    (grad_before,) = gelu_pull(product_right(out_grad, w_down))
    grad_before_low = grad_before.astype(jnp.bfloat16)
    grad_up_bias = jnp.sum(grad_before_low.astype(jnp.float32), axis=0)
    grad_mid_norm, grad_norm2_gain, grad_norm2_bias = norm2_pull(
        product_right(grad_before_low, w_up)
    )
    grad_middle = grad_top + grad_mid_norm
    grad_branch = grad_middle.astype(jnp.bfloat16)
    grad_joined = product_right(grad_branch, w_output).astype(jnp.bfloat16)
    grad_att = lax.all_to_all(grad_joined, "head", split_axis=1, concat_axis=0, tiled=True)

    back_query_h, key_rim, value_rim, near_rim, back_key_h, back_value_h, back_context = attend_back(
        where_, query_h, key_ext, value_ext, context_ext, first, opening, attended_fine, grad_att, level
    )
    near_rim = shifted(near_rim, "tok", -1).astype(jnp.float32)
    rims = shifted(jnp.stack([key_rim, value_rim]), "tok", -1).astype(jnp.float32)
    back_context = back_context.at[span - window - CTX :].add(near_rim)
    back_key_h = back_key_h.at[span - window :].add(rims[0]).astype(jnp.bfloat16)
    back_value_h = back_value_h.at[span - window :].add(rims[1]).astype(jnp.bfloat16)

    back_ends, back_lags = ssm_back_ends(brk, back_context, decay)
    starts, lag_starts = adjoint_exchange(
        keep, whole, back_ends, back_lags, chunk_decay, chunk_slope, span_decay, span_slope, 2
    )
    back_feed_h, sums, lag_sums, skip_sum = ssm_back(
        brk, back_context, hidden_h, decay, mix, skip, starts, lag_starts
    )
    back_query, back_key, back_value, back_feed = (
        lax.all_to_all(rows, "head", split_axis=0, concat_axis=1, tiled=True)
        for rows in (back_query_h, back_key_h, back_value_h, back_feed_h)
    )
    grad_hidden = (
        product_right(back_query, w_query)
        + product_right(back_key, w_key)
        + product_right(back_value, w_value)
        + back_feed.astype(jnp.float32)
    )
    grad_res_norm, grad_norm1_gain, grad_norm1_bias = norm1_pull(grad_hidden)
    input_grad = grad_middle + grad_res_norm

    out_w_down, out_w_up, out_w_output = summed_products(
        [active_low, normed_low, joined],
        [out_grad, grad_before_low, grad_branch],
        FEED_PLAN,
        3,
        "feed_products",
    )
    out_w_query, out_w_key, out_w_value = summed_products(
        [hidden] * 3, [back_query, back_key, back_value], HEAD_PLAN, 4, "head_products"
    )
    devices = pieces * lax.axis_size("head")
    short = [grad_norm1_gain, grad_norm1_bias, grad_norm2_gain, grad_norm2_bias, grad_down_bias]
    packed = jnp.concatenate(
        [grad.reshape(devices, -1) for grad in short + [grad_up_bias]], axis=1
    )
    each = short[0].shape[0] // devices
    lanes = -packed.shape[1] % HD
    packed = jnp.pad(packed, ((0, 0), (0, lanes))).reshape(devices, 1, -1)
    rows = jnp.concatenate([sums, lag_sums, skip_sum], axis=0)
    rows = jnp.pad(rows, ((0, -rows.shape[0] % SUB), (0, 0)))
    summed, packed = final_sums(rows, packed, 5)
    short = [packed[0, at * each : (at + 1) * each] for at in range(len(short))]
    out_up_bias = packed[0, len(short) * each : len(short) * each + up_bias.shape[0] // devices]
    sums, lag_sums, skip_sum = summed[:NS], summed[NS : 2 * NS], summed[2 * NS]
    grad_ssm_output = (driving * sums).T
    grad_driving = read_out * sums
    grad_ssm_input = (gain * grad_driving).T
    grad_ssm_rate = (
        grad_driving * drive_in * jnp.exp(-2.0 * rate) / gain - mix * lag_sums * decay
    ).T / total_len

    return (
        layer_out,
        input_grad,
        short[0],
        short[1],
        out_w_query,
        out_w_key,
        out_w_value,
        out_w_output,
        grad_ssm_rate,
        grad_ssm_input,
        grad_ssm_output,
        skip_sum,
        short[2],
        short[3],
        out_w_up,
        out_up_bias,
        out_w_down,
        short[4],
    )


def solution(mesh):
    return jax.shard_map(
        per_device,
        mesh=mesh,
        in_specs=(
            P(("tok", "head"), None),
            P(),
            P(),
            P(),
            P(),
            P(),
            P(),
            P(),
            P(),
            P("head", None),
            P("head", None),
            P("head", None),
            P("head"),
            P(),
            P(),
            P(),
            P(),
            P(),
            P(),
            P(("tok", "head"), None),
        ),
        out_specs=(
            P(("tok", "head"), None),
            P(("tok", "head"), None),
            P(("tok", "head")),
            P(("tok", "head")),
            P(("tok", "head"), None),
            P(("tok", "head"), None),
            P(("tok", "head"), None),
            P(("tok", "head"), None),
            P("head", None),
            P("head", None),
            P("head", None),
            P("head"),
            P(("tok", "head")),
            P(("tok", "head")),
            P(("tok", "head"), None),
            P(("tok", "head")),
            P(("tok", "head"), None),
            P(("tok", "head")),
        ),
        check_vma=False,
    )
```

```python
import functools
import math

import jax
import jax.numpy as jnp
from jax import lax
from jax.experimental import pallas as pl
from jax.experimental.pallas import tpu as pltpu
from jax.sharding import PartitionSpec as P

epsilon = 1e-05
HD = 128
CTX = 128
BLOCK = 256
NS = 16
SUB = 8
UNROLL = 8
HALF = 8
TILE = 256
MIB = 1 << 20
LOWEST = -1e30
FACTOR = HD ** (-0.5)
FACTOR2 = FACTOR * math.log2(math.e)


def spread(table, n):
    return jnp.broadcast_to(table[n : n + 1, :], (SUB, table.shape[1]))


def stepped(length, chunk, step, body, carry):
    blocks = length // UNROLL
    hit = jnp.where(step < 0, blocks, step // UNROLL)

    def plain(block, now):
        for inner in range(UNROLL):
            now = body(block * UNROLL + inner, now, None)
        return now

    def masked(block, now):
        rows = lax.broadcasted_iota(jnp.int32, (SUB, HD), 0)
        for inner in range(UNROLL):
            t = block * UNROLL + inner
            live = jnp.where((rows == chunk) & (t == step), 0.0, 1.0)
            now = body(t, now, live)
        return now

    carry = lax.fori_loop(0, hit, plain, carry)
    carry = lax.fori_loop(hit, jnp.minimum(hit + 1, blocks), masked, carry)
    return lax.fori_loop(hit + 1, blocks, plain, carry)


def ssm_ends_kernel(brk, feed, decay, ends, rows):
    length = rows.shape[0] // SUB
    rows[...] = feed[...].astype(jnp.float32)
    table = decay[...]
    factors = [spread(table, n) for n in range(NS)]

    def body(t, states, live):
        drive = rows[pl.ds(t, SUB, stride=length), :]
        if live is not None:
            states = [state * live for state in states]
        return tuple(state * factor + drive for state, factor in zip(states, factors))

    zero = jnp.zeros((SUB, HD), jnp.float32)
    states = stepped(length, brk[0], brk[1], body, (zero,) * NS)
    for n in range(NS):
        ends[n] = states[n]


def ssm_out_kernel(brk, feed, decay, mix, skip, starts, out, rows, sums):
    length = rows.shape[0] // SUB
    rows[...] = feed[...].astype(jnp.float32)
    table = decay[...]
    weights = mix[...]
    factors = [spread(table, n) for n in range(NS)]
    mixes = [spread(weights, n) for n in range(NS)]
    direct = spread(skip[...], 0)

    def body(t, states, live):
        drive = rows[pl.ds(t, SUB, stride=length), :]
        if live is not None:
            states = [state * live for state in states]
        states = tuple(state * factor + drive for state, factor in zip(states, factors))
        parts = [state * weight for state, weight in zip(states, mixes)] + [direct * drive]
        while len(parts) > 1:
            parts = [a + b for a, b in zip(parts[::2], parts[1::2])] + (
                [parts[-1]] if len(parts) % 2 else []
            )
        sums[pl.ds(t, SUB, stride=length), :] = parts[0]
        return states

    stepped(length, brk[0], brk[1], body, tuple(starts[n] for n in range(NS)))
    out[...] = sums[...].astype(out.dtype)


def ssm_back_ends_kernel(brk, slope, decay, ends, lags):
    length = slope.shape[0] // SUB
    table = decay[...]
    zero = jnp.zeros((SUB, HD), jnp.float32)
    factors = [spread(table, n) for n in range(NS)]

    def body(t, carry, live):
        drive = slope[pl.ds(length - 1 - t, SUB, stride=length), :]
        adjoint, lag = carry[:NS], carry[NS:]
        lag = [a * f + b for a, f, b in zip(lag, factors, adjoint)]
        adjoint = [a * f + drive for a, f in zip(adjoint, factors)]
        if live is not None:
            lag = [a * live for a in lag]
            adjoint = [a * live for a in adjoint]
        return tuple(adjoint) + tuple(lag)

    back = jnp.where(brk[1] < 0, -1, length - 1 - brk[1])
    done = stepped(length, brk[0], back, body, (zero,) * (2 * NS))
    for n in range(NS):
        ends[n] = done[n]
        lags[n] = done[NS + n]


def ssm_back_kernel(
    brk, slope, feed, decay, mix, skip, starts, lag_starts, back, sums, lag_sums, skip_sum, rows, total
):
    length = rows.shape[0] // SUB
    rows[...] = feed[...].astype(jnp.float32)
    table = decay[...]
    weights = mix[...]
    zero = jnp.zeros((SUB, HD), jnp.float32)
    total[...] = slope[...] * skip[...]
    skip_sum[...] = jnp.sum(slope[...] * rows[...], axis=0, keepdims=True)
    reversed_step = jnp.where(brk[1] < 0, -1, length - 1 - brk[1])
    for base in range(0, NS, HALF):
        factors = [spread(table, base + n) for n in range(HALF)]
        mixes = [spread(weights, base + n) for n in range(HALF)]

        def body(t, carry, live):
            at = pl.ds(length - 1 - t, SUB, stride=length)
            drive, source = slope[at, :], rows[at, :]
            adjoint, lag = carry[:HALF], carry[HALF : 2 * HALF]
            direct, late = carry[2 * HALF : 3 * HALF], carry[3 * HALF :]
            lag = [a * f + b for a, f, b in zip(lag, factors, adjoint)]
            adjoint = [a * f + drive for a, f in zip(adjoint, factors)]
            direct = [a + b * source for a, b in zip(direct, adjoint)]
            late = [a + b * source for a, b in zip(late, lag)]
            parts = [a * b for a, b in zip(adjoint, mixes)]
            while len(parts) > 1:
                parts = [a + b for a, b in zip(parts[::2], parts[1::2])]
            total[at, :] = total[at, :] + parts[0]
            if live is not None:
                lag = [a * live for a in lag]
                adjoint = [a * live for a in adjoint]
            return tuple(adjoint) + tuple(lag) + tuple(direct) + tuple(late)

        first = tuple(starts[base + n] for n in range(HALF)) + tuple(
            lag_starts[base + n] for n in range(HALF)
        )
        done = stepped(length, brk[0], reversed_step, body, first + (zero,) * (2 * HALF))
        for n in range(HALF):
            sums[base + n : base + n + 1, :] = jnp.sum(done[2 * HALF + n], axis=0, keepdims=True)
            lag_sums[base + n : base + n + 1, :] = jnp.sum(
                done[3 * HALF + n], axis=0, keepdims=True
            )
    back[...] = total[...].astype(back.dtype)


def columns(rows):
    return pl.BlockSpec((rows, HD), lambda g: (0, g))


def chunked():
    return pl.BlockSpec((NS, SUB, HD), lambda g: (0, 0, g))


SCALARS = pl.BlockSpec(memory_space=pltpu.SMEM)


def wide(limit=48):
    return pltpu.CompilerParams(vmem_limit_bytes=limit * MIB)


def ssm_ends(brk, feed, decay):
    rows, width = feed.shape
    return pl.pallas_call(
        ssm_ends_kernel,
        grid=(width // HD,),
        in_specs=[SCALARS, columns(rows), columns(NS)],
        out_specs=chunked(),
        out_shape=jax.ShapeDtypeStruct((NS, SUB, width), jnp.float32),
        scratch_shapes=[pltpu.VMEM((rows, HD), jnp.float32)],
        compiler_params=wide(),
        name="ssm_ends",
    )(brk, feed, decay)


def ssm_out(brk, feed, decay, mix, skip, starts):
    rows, width = feed.shape
    return pl.pallas_call(
        ssm_out_kernel,
        grid=(width // HD,),
        in_specs=[SCALARS, columns(rows), columns(NS), columns(NS), columns(1), chunked()],
        out_specs=columns(rows),
        out_shape=jax.ShapeDtypeStruct((rows, width), jnp.bfloat16),
        scratch_shapes=[pltpu.VMEM((rows, HD), jnp.float32)] * 2,
        compiler_params=wide(),
        name="ssm_out",
    )(brk, feed, decay, mix, skip, starts)


def ssm_back_ends(brk, slope, decay):
    rows, width = slope.shape
    return pl.pallas_call(
        ssm_back_ends_kernel,
        grid=(width // HD,),
        in_specs=[SCALARS, columns(rows), columns(NS)],
        out_specs=(chunked(), chunked()),
        out_shape=(jax.ShapeDtypeStruct((NS, SUB, width), jnp.float32),) * 2,
        compiler_params=wide(),
        name="ssm_back_ends",
    )(brk, slope, decay)


def ssm_back(brk, slope, feed, decay, mix, skip, starts, lag_starts):
    rows, width = feed.shape
    table = jax.ShapeDtypeStruct((NS, width), jnp.float32)
    return pl.pallas_call(
        ssm_back_kernel,
        grid=(width // HD,),
        in_specs=[
            SCALARS,
            columns(rows),
            columns(rows),
            columns(NS),
            columns(NS),
            columns(1),
            chunked(),
            chunked(),
        ],
        out_specs=(columns(rows), columns(NS), columns(NS), columns(1)),
        out_shape=(
            jax.ShapeDtypeStruct((rows, width), jnp.bfloat16),
            table,
            table,
            jax.ShapeDtypeStruct((1, width), jnp.float32),
        ),
        scratch_shapes=[pltpu.VMEM((rows, HD), jnp.float32)] * 2,
        compiler_params=wide(),
        name="ssm_back",
    )(brk, slope, feed, decay, mix, skip, starts, lag_starts)


def across(left, right):
    return lax.dot_general(
        left, right, (((1,), (1,)), ((), ())), preferred_element_type=jnp.float32
    )


def times(left, right):
    return lax.dot_general(
        left, right, (((1,), (0,)), ((), ())), preferred_element_type=jnp.float32
    )


def turn(source, target):
    for at in range(0, source.shape[0], TILE):
        size = min(TILE, source.shape[0] - at)
        piece = source[at : at + size, :].astype(jnp.float32)
        target[:, at : at + size] = piece.T.astype(target.dtype)


def local_tiles(where_, tile):
    return (where_[4 + tile] + 2 * BLOCK) // TILE


def next_block(where_, now):
    second = where_[1]
    length = jnp.where(now >= second, where_[3], where_[2])
    after = now + length
    return jnp.where((now < second) & (after > second), second, after)


def local_mask(tile, key_tile, first):
    rows = lax.broadcasted_iota(jnp.int32, (TILE, TILE), 0) + (key_tile * TILE - 2 * BLOCK)
    cols = lax.broadcasted_iota(jnp.int32, (1, TILE), 1) + tile * TILE
    return (rows >= first) & (rows <= cols)


def context_at(now):
    return pl.multiple_of((now + 2 * BLOCK) // CTX * CTX, CTX)


def context_mask(start, now, first, opening):
    rows = lax.broadcasted_iota(jnp.int32, (TILE, TILE), 0) + (start - 2 * BLOCK - CTX)
    low = jnp.where(first == now, jnp.maximum(now - CTX, opening), 1 << 28)
    return (rows >= low) & (rows < now)


def attend_kernel(
    where_, query, key, value, context, first, opening, out, fine, level, value_t, context_t
):
    turn(value, value_t)
    turn(context, context_t)

    def one_tile(tile, _):
        rows = query[pl.ds(pl.multiple_of(tile * TILE, TILE), TILE), :]
        firsts = first[tile]
        openings = opening[tile]

        def add(carry, keys, values_t, mask):
            top, mass, low_mass, total = carry
            score = jnp.where(mask, across(keys, rows) * FACTOR2, LOWEST)
            new_top = jnp.maximum(top, jnp.max(score, axis=0, keepdims=True))
            prob = jnp.exp2(score - new_top)
            shrink = jnp.exp2(top - new_top)
            low = prob.astype(jnp.bfloat16)
            mass = mass * shrink + jnp.sum(prob, axis=0, keepdims=True)
            low_mass = low_mass * shrink + jnp.sum(
                low.astype(jnp.float32), axis=0, keepdims=True
            )
            total = total * shrink + times(values_t, low)
            return new_top, mass, low_mass, total

        def local(key_tile, carry):
            at = pl.ds(pl.multiple_of(key_tile * TILE, TILE), TILE)
            return add(carry, key[at, :], value_t[:, at], local_mask(tile, key_tile, firsts))

        def earlier(state):
            now, carry = state[0], state[1:]
            start = context_at(now)
            at = pl.ds(start, TILE)
            carry = add(
                carry,
                context[at, :],
                context_t[:, at],
                context_mask(start, now, firsts, openings),
            )
            return (next_block(where_, now),) + tuple(carry)

        carry = (
            jnp.full((1, TILE), LOWEST, jnp.float32),
            jnp.zeros((1, TILE), jnp.float32),
            jnp.zeros((1, TILE), jnp.float32),
            jnp.zeros((HD, TILE), jnp.float32),
        )
        carry = lax.fori_loop(local_tiles(where_, tile), tile + 3, local, carry)
        state = lax.while_loop(
            lambda state: state[0] < (tile + 1) * TILE, earlier, (where_[4 + tile],) + carry
        )
        _, top, mass, low_mass, total = state
        done = (total / low_mass).T
        here = pl.ds(pl.multiple_of(tile * TILE, TILE), TILE)
        fine[here, :] = done
        out[here, :] = done.astype(out.dtype)
        level[0, tile] = top + jnp.log2(mass)
        return 0

    lax.fori_loop(0, query.shape[0] // TILE, one_tile, 0)


def attend_back_kernel(
    where_,
    query,
    key,
    value,
    context,
    first,
    opening,
    attended,
    grad,
    level,
    back_query,
    key_rim,
    value_rim,
    context_rim,
    back_key,
    back_value,
    back_context,
    key_t,
    context_t,
    key_sum,
    value_sum,
    context_sum,
):
    turn(key, key_t)
    turn(context, context_t)
    key_sum[...] = jnp.zeros_like(key_sum)
    value_sum[...] = jnp.zeros_like(value_sum)
    context_sum[...] = jnp.zeros_like(context_sum)

    def one_tile(tile, _):
        here = pl.ds(pl.multiple_of(tile * TILE, TILE), TILE)
        rows = query[here, :]
        grads = grad[here, :]
        firsts = first[tile]
        openings = opening[tile]
        levels = level[0, tile]
        joint = grads.astype(jnp.float32) * attended[here, :]
        centre = jnp.sum(joint.T, axis=0, keepdims=True)

        def slopes(keys, values, mask):
            prob = jnp.exp2(jnp.where(mask, across(keys, rows) * FACTOR2 - levels, LOWEST))
            slope = prob * (across(values, grads) - centre)
            return prob.astype(jnp.bfloat16), slope.astype(jnp.bfloat16)

        def local(key_tile, total):
            at = pl.ds(pl.multiple_of(key_tile * TILE, TILE), TILE)
            prob, slope = slopes(key[at, :], value[at, :], local_mask(tile, key_tile, firsts))
            key_sum[at, :] += times(slope, rows)
            value_sum[at, :] += times(prob, grads)
            return total + times(key_t[:, at], slope)

        def earlier(state):
            now, total = state
            start = context_at(now)
            at = pl.ds(start, TILE)
            near = context[at, :]
            prob, slope = slopes(near, near, context_mask(start, now, firsts, openings))
            context_sum[at, :] += FACTOR * times(slope, rows) + times(prob, grads)
            return next_block(where_, now), total + times(context_t[:, at], slope)

        total = jnp.zeros((HD, TILE), jnp.float32)
        total = lax.fori_loop(local_tiles(where_, tile), tile + 3, local, total)
        _, total = lax.while_loop(
            lambda state: state[0] < (tile + 1) * TILE, earlier, (where_[4 + tile], total)
        )
        back_query[here, :] = (FACTOR * total).T.astype(back_query.dtype)
        return 0

    lax.fori_loop(0, query.shape[0] // TILE, one_tile, 0)
    window = 2 * BLOCK
    key_rim[...] = (FACTOR * key_sum[:window, :]).astype(key_rim.dtype)
    value_rim[...] = value_sum[:window, :].astype(value_rim.dtype)
    context_rim[...] = context_sum[: window + CTX, :].astype(context_rim.dtype)
    back_key[...] = FACTOR * key_sum[window:, :]
    back_value[...] = value_sum[window:, :]
    back_context[...] = context_sum[window + CTX :, :]


def attend(where_, query, key, value, context, first, opening):
    rows, width = query.shape
    heads, tiles = width // HD, rows // TILE
    near, far = key.shape[0], context.shape[0]
    whole = pl.BlockSpec((tiles, 1, TILE), lambda g: (0, 0, 0))
    return pl.pallas_call(
        attend_kernel,
        grid=(heads,),
        in_specs=[
            SCALARS,
            columns(rows),
            columns(near),
            columns(near),
            columns(far),
            whole,
            whole,
        ],
        out_specs=(
            columns(rows),
            columns(rows),
            pl.BlockSpec((1, tiles, 1, TILE), lambda g: (g, 0, 0, 0)),
        ),
        out_shape=(
            jax.ShapeDtypeStruct((rows, width), jnp.bfloat16),
            jax.ShapeDtypeStruct((rows, width), jnp.float32),
            jax.ShapeDtypeStruct((heads, tiles, 1, TILE), jnp.float32),
        ),
        scratch_shapes=[
            pltpu.VMEM((HD, near), jnp.bfloat16),
            pltpu.VMEM((HD, far), jnp.bfloat16),
        ],
        compiler_params=wide(),
        name="attend",
    )(where_, query, key, value, context, first, opening)


def attend_back(where_, query, key, value, context, first, opening, attended, grad, level):
    rows, width = query.shape
    heads, tiles = width // HD, rows // TILE
    near, far = key.shape[0], context.shape[0]
    whole = pl.BlockSpec((tiles, 1, TILE), lambda g: (0, 0, 0))
    low = lambda count: jax.ShapeDtypeStruct((count, width), jnp.bfloat16)
    full = lambda count: jax.ShapeDtypeStruct((count, width), jnp.float32)
    return pl.pallas_call(
        attend_back_kernel,
        grid=(heads,),
        in_specs=[
            SCALARS,
            columns(rows),
            columns(near),
            columns(near),
            columns(far),
            whole,
            whole,
            columns(rows),
            columns(rows),
            pl.BlockSpec((1, tiles, 1, TILE), lambda g: (g, 0, 0, 0)),
        ],
        out_specs=(
            columns(rows),
            columns(near - rows),
            columns(near - rows),
            columns(far - rows),
            columns(rows),
            columns(rows),
            columns(rows),
        ),
        out_shape=(
            low(rows),
            low(near - rows),
            low(near - rows),
            low(far - rows),
            full(rows),
            full(rows),
            full(rows),
        ),
        scratch_shapes=[
            pltpu.VMEM((HD, near), jnp.bfloat16),
            pltpu.VMEM((HD, far), jnp.bfloat16),
            pltpu.VMEM((near, HD), jnp.float32),
            pltpu.VMEM((near, HD), jnp.float32),
            pltpu.VMEM((far, HD), jnp.float32),
        ],
        compiler_params=wide(),
        name="attend_back",
    )(where_, query, key, value, context, first, opening, attended, grad, level)


MESH = pl.DeviceIdType.MESH


def bits_of(count):
    return count.bit_length() - 1


def mesh_bits():
    found = []
    tok, head = lax.axis_index("tok"), lax.axis_index("head")
    for axis in ("head", "tok"):
        for level in range(bits_of(lax.axis_size(axis))):
            at = head if axis == "head" else tok
            bit = (at // (1 << level)) % 2
            other = at + (1 - 2 * bit) * (1 << level)
            found.append((bit, (tok, other) if axis == "head" else (other, head)))
    return found


def greet(partners):
    barrier = pltpu.get_barrier_semaphore()
    for partner in partners:
        pl.semaphore_signal(barrier, inc=1, device_id=partner, device_id_type=MESH)
    pl.semaphore_wait(barrier, len(partners))


def halving_orders(bits):
    rest = list(range(1, bits))
    return [
        [0] + rest,
        [0] + [rest[1], rest[0]] + rest[2:],
        [0] + [rest[2], rest[0], rest[1]] + rest[3:],
    ]


def slot_of(block, order):
    place = 0
    for bit in order:
        place = place * 2 + (block // (1 << bit)) % 2
    return place


ROWS = 512


def products_kernel(pairs, plan, bits, *refs):
    lefts, refs = refs[:pairs], refs[pairs:]
    rights, refs = refs[:pairs], refs[pairs:]
    outs, refs = refs[:pairs], refs[pairs:]
    count = len(plan)
    grads, refs = refs[:count], refs[count:]
    arrivals, refs = refs[: count * bits], refs[count * bits :]
    send_sems, recv_sems = refs
    here = mesh_bits()
    orders = halving_orders(bits)
    greet([partner for _, partner in here])
    base = [0] * count
    started = []

    def send(number, stage):
        bit, partner = here[orders[plan[number][3]][stage]]
        half = 1 << (bits - 1 - stage)
        copy = pltpu.make_async_remote_copy(
            src_ref=grads[number].at[pl.ds(base[number] + (1 - bit) * half, half)],
            dst_ref=arrivals[number * bits + stage],
            send_sem=send_sems.at[number, stage],
            recv_sem=recv_sems.at[number, stage],
            device_id=partner,
            device_id_type=MESH,
        )
        copy.start()
        started.append(copy)
        base[number] = base[number] + bit * half
        return copy

    flying = []
    for number, (pair, start, width, order) in enumerate(plan):
        left, right, grad = lefts[pair], rights[pair], grads[number]
        block = grad.shape[1]
        each = ROWS // block

        def some_rows(chunk, _, left=left, right=right, grad=grad, block=block, each=each, start=start, width=width, order=order):
            at = pl.ds(pl.multiple_of(chunk * ROWS, ROWS), ROWS)
            found = lax.dot_general(
                left[:, at],
                right[:, start : start + width],
                (((0,), (0,)), ((), ())),
                preferred_element_type=jnp.float32,
            ).astype(jnp.bfloat16)
            for inner in range(each):
                grad[slot_of(chunk * each + inner, orders[order])] = found[
                    inner * block : (inner + 1) * block
                ]
            return 0

        lax.fori_loop(0, left.shape[1] // ROWS, some_rows, 0)
        flying.append(send(number, 0))

    for stage in range(bits):
        for number, (pair, start, width, order) in enumerate(plan):
            flying[number].wait_recv()
            grad, arrival = grads[number], arrivals[number * bits + stage]
            half = 1 << (bits - 1 - stage)
            if stage == bits - 1:
                outs[pair][:, start : start + width] = grad[base[number]].astype(
                    jnp.float32
                ) + arrival[0].astype(jnp.float32)
            else:
                place = base[number]

                def add(i, _, grad=grad, arrival=arrival, place=place):
                    grad[place + i] = grad[place + i] + arrival[i]
                    return 0

                lax.fori_loop(0, half, add, 0)
                flying[number] = send(number, stage + 1)
    for copy in started:
        copy.wait_send()


def summed_products(lefts, rights, plan, collective_id, name):
    devices = lax.axis_size("tok") * lax.axis_size("head")
    bits = bits_of(devices)
    blocks = [left.shape[1] // devices for left in lefts]
    if min(blocks) < 16:
        return [
            lax.psum_scatter(
                product_left(left, right), ("tok", "head"), scatter_dimension=0, tiled=True
            )
            for left, right in zip(lefts, rights)
        ]
    scratch = [pltpu.VMEM((devices, blocks[p], w), jnp.bfloat16) for p, _, w, _ in plan]
    for p, _, w, _ in plan:
        for stage in range(bits):
            scratch.append(pltpu.VMEM((1 << (bits - 1 - stage), blocks[p], w), jnp.bfloat16))
    flops = sum(2 * l.shape[0] * l.shape[1] * r.shape[1] for l, r in zip(lefts, rights))
    return pl.pallas_call(
        functools.partial(products_kernel, len(lefts), plan, bits),
        in_specs=[pl.BlockSpec(memory_space=pltpu.VMEM)] * (2 * len(lefts)),
        out_specs=[pl.BlockSpec(memory_space=pltpu.VMEM)] * len(lefts),
        out_shape=[
            jax.ShapeDtypeStruct((block, right.shape[1]), jnp.float32)
            for block, right in zip(blocks, rights)
        ],
        scratch_shapes=scratch
        + [pltpu.SemaphoreType.DMA((len(plan), bits)), pltpu.SemaphoreType.DMA((len(plan), bits))],
        compiler_params=pltpu.CompilerParams(
            collective_id=collective_id, has_side_effects=True, vmem_limit_bytes=60 * MIB
        ),
        cost_estimate=pl.CostEstimate(flops=flops, bytes_accessed=20 * MIB, transcendentals=0),
        name=name,
    )(*lefts, *rights)


FEED_PLAN = [
    (0, 0, 512, 0),
    (0, 512, 512, 1),
    (1, 0, 512, 2),
    (1, 512, 512, 0),
    (1, 1024, 512, 1),
    (1, 1536, 512, 2),
    (1, 2048, 512, 0),
    (1, 2560, 512, 1),
    (2, 0, 512, 2),
    (1, 3072, 512, 0),
    (1, 3584, 512, 1),
    (2, 512, 512, 2),
]
HEAD_PLAN = [
    (0, 0, 512, 0),
    (0, 512, 512, 1),
    (1, 0, 512, 2),
    (1, 512, 512, 0),
    (2, 0, 512, 1),
    (2, 512, 512, 0),
]


def tok_peers():
    count, here = lax.axis_size("tok"), lax.axis_index("tok")
    head = lax.axis_index("head")
    return [
        ((lax.rem(here + step, count), head), lax.rem(here + count - step, count))
        for step in range(1, count)
    ]


def share(mine, every, send_sems, recv_sems, place, peers):
    copies = []
    for step, (target, _) in enumerate(peers):
        copy = pltpu.make_async_remote_copy(
            src_ref=mine,
            dst_ref=every.at[place],
            send_sem=send_sems.at[step],
            recv_sem=recv_sems.at[step],
            device_id=target,
            device_id_type=MESH,
        )
        copy.start()
        copies.append(copy)
    return copies


def state_exchange_kernel(
    keep, whole, ends, chunk_decay, span_decay, starts, mine, every, send_sems, recv_sems
):
    here, count = lax.axis_index("tok"), every.shape[0]
    peers = tok_peers()
    greet([target for target, _ in peers])
    factor = chunk_decay[...]
    now = ends[:, 0, :]
    for chunk in range(1, SUB):
        now = keep[chunk] * (factor * now) + ends[:, chunk, :]
    mine[...] = now
    every[here] = now
    copies = share(mine, every, send_sems, recv_sems, here, peers)
    for copy in copies:
        copy.wait()
    over = span_decay[...]
    now = jnp.zeros_like(over)
    for place in range(count - 1):
        now = jnp.where(place < here, whole[place] * (over * now) + every[place], now)
    for chunk in range(SUB):
        starts[:, chunk, :] = now
        now = keep[chunk] * (factor * now) + ends[:, chunk, :]


def adjoint_exchange_kernel(
    keep,
    whole,
    ends,
    lags,
    chunk_decay,
    chunk_slope,
    span_decay,
    span_slope,
    starts,
    lag_starts,
    mine,
    every,
    send_sems,
    recv_sems,
):
    here, count = lax.axis_index("tok"), every.shape[0]
    peers = tok_peers()
    greet([target for target, _ in peers])
    factor, slope = chunk_decay[...], chunk_slope[...]
    now, late = ends[:, SUB - 1, :], lags[:, SUB - 1, :]
    for chunk in reversed(range(SUB - 1)):
        late = keep[chunk] * (factor * late + slope * now) + lags[:, chunk, :]
        now = keep[chunk] * (factor * now) + ends[:, chunk, :]
    mine[0] = now
    mine[1] = late
    every[here, 0] = now
    every[here, 1] = late
    copies = share(mine, every, send_sems, recv_sems, here, peers)
    for copy in copies:
        copy.wait()
    over, over_slope = span_decay[...], span_slope[...]
    now, late = jnp.zeros_like(over), jnp.zeros_like(over)
    for place in reversed(range(1, count)):
        reached = place > here
        late = jnp.where(
            reached, whole[place] * (over * late + over_slope * now) + every[place, 1], late
        )
        now = jnp.where(reached, whole[place] * (over * now) + every[place, 0], now)
    for chunk in reversed(range(SUB)):
        starts[:, chunk, :] = now
        lag_starts[:, chunk, :] = late
        late = keep[chunk] * (factor * late + slope * now) + lags[:, chunk, :]
        now = keep[chunk] * (factor * now) + ends[:, chunk, :]


VMEM = pl.BlockSpec(memory_space=pltpu.VMEM)


def state_exchange(keep, whole, ends, chunk_decay, span_decay, collective_id):
    states, _, width = ends.shape
    count = whole.shape[0]
    return pl.pallas_call(
        state_exchange_kernel,
        in_specs=[SCALARS, SCALARS, VMEM, VMEM, VMEM],
        out_specs=VMEM,
        out_shape=jax.ShapeDtypeStruct(ends.shape, jnp.float32),
        scratch_shapes=[
            pltpu.VMEM((states, width), jnp.float32),
            pltpu.VMEM((count, states, width), jnp.float32),
            pltpu.SemaphoreType.DMA((count - 1,)),
            pltpu.SemaphoreType.DMA((count - 1,)),
        ],
        compiler_params=pltpu.CompilerParams(
            collective_id=collective_id, has_side_effects=True, vmem_limit_bytes=16 * MIB
        ),
        name="state_exchange",
    )(keep, whole, ends, chunk_decay, span_decay)


def adjoint_exchange(
    keep, whole, ends, lags, chunk_decay, chunk_slope, span_decay, span_slope, collective_id
):
    states, _, width = ends.shape
    count = whole.shape[0]
    return pl.pallas_call(
        adjoint_exchange_kernel,
        in_specs=[SCALARS, SCALARS] + [VMEM] * 6,
        out_specs=(VMEM, VMEM),
        out_shape=(jax.ShapeDtypeStruct(ends.shape, jnp.float32),) * 2,
        scratch_shapes=[
            pltpu.VMEM((2, states, width), jnp.float32),
            pltpu.VMEM((count, 2, states, width), jnp.float32),
            pltpu.SemaphoreType.DMA((count - 1,)),
            pltpu.SemaphoreType.DMA((count - 1,)),
        ],
        compiler_params=pltpu.CompilerParams(
            collective_id=collective_id, has_side_effects=True, vmem_limit_bytes=16 * MIB
        ),
        name="adjoint_exchange",
    )(keep, whole, ends, lags, chunk_decay, chunk_slope, span_decay, span_slope)


def final_sums_kernel(
    rows, vectors, row_sum, vector_sum, every_row, every_vector, send_rows, recv_rows, send_v, recv_v
):
    tok, head = lax.axis_index("tok"), lax.axis_index("head")
    toks, heads = lax.axis_size("tok"), lax.axis_size("head")
    devices = toks * heads
    here = tok * heads + head
    peers = []
    for step in range(1, devices):
        other = lax.rem(here + step, devices)
        peers.append((other, (other // heads, lax.rem(other, heads))))
    greet([target for _, target in peers])
    every_row[tok] = rows[...]
    every_vector[here] = vectors[here]
    copies = share(rows, every_row, send_rows, recv_rows, tok, tok_peers())
    for step, (other, target) in enumerate(peers):
        copy = pltpu.make_async_remote_copy(
            src_ref=vectors.at[other],
            dst_ref=every_vector.at[here],
            send_sem=send_v.at[step],
            recv_sem=recv_v.at[step],
            device_id=target,
            device_id_type=MESH,
        )
        copy.start()
        copies.append(copy)
    for copy in copies:
        copy.wait()
    row_sum[...] = jnp.sum(every_row[...], axis=0)
    vector_sum[...] = jnp.sum(every_vector[...], axis=0)


def final_sums(rows, vectors, collective_id):
    toks, devices = lax.axis_size("tok"), vectors.shape[0]
    return pl.pallas_call(
        final_sums_kernel,
        in_specs=[VMEM, VMEM],
        out_specs=(VMEM, VMEM),
        out_shape=(
            jax.ShapeDtypeStruct(rows.shape, jnp.float32),
            jax.ShapeDtypeStruct(vectors.shape[1:], jnp.float32),
        ),
        scratch_shapes=[
            pltpu.VMEM((toks,) + rows.shape, jnp.float32),
            pltpu.VMEM(vectors.shape, jnp.float32),
            pltpu.SemaphoreType.DMA((toks - 1,)),
            pltpu.SemaphoreType.DMA((toks - 1,)),
            pltpu.SemaphoreType.DMA((devices - 1,)),
            pltpu.SemaphoreType.DMA((devices - 1,)),
        ],
        compiler_params=pltpu.CompilerParams(
            collective_id=collective_id, has_side_effects=True, vmem_limit_bytes=16 * MIB
        ),
        name="final_sums",
    )(rows, vectors)


def row_norm(rows, gain, bias):
    rows = rows.astype(jnp.float32)
    centred = rows - jnp.mean(rows, axis=-1, keepdims=True)
    spread_ = jnp.mean(centred * centred, axis=-1, keepdims=True)
    return (centred * lax.rsqrt(spread_ + epsilon) * gain + bias).astype(jnp.bfloat16)


PIECE = 128


def head_forward_kernel(
    tokens, gain, bias, weights, hid, query, key, value, gathered, send_sems, recv_sems
):
    tok, head = lax.axis_index("tok"), lax.axis_index("head")
    near = head + 1 - 2 * lax.rem(head, 2)
    far = head + 2 - 4 * (head // 2)
    across_ = near + 2 - 4 * (near // 2)
    greet([(tok, near), (tok, far)])
    rows = tokens.shape[0]
    pieces = rows // PIECE

    def copy(source, owner, target, number):
        return pltpu.make_async_remote_copy(
            src_ref=source,
            dst_ref=gathered.at[owner, pl.ds(number % pieces * PIECE, PIECE)],
            send_sem=send_sems.at[number],
            recv_sem=recv_sems.at[number],
            device_id=(tok, target),
            device_id_type=MESH,
        )

    def own(number):
        return tokens.at[pl.ds(number * PIECE, PIECE)]

    over = [copy(own(i), head, far, i) for i in range(pieces)]
    beside = [copy(own(i), head, near, pieces + i) for i in range(pieces)]
    for one in over + beside:
        one.start()

    def work(found, owner, number):
        at = pl.ds(pl.multiple_of(owner * rows + number * PIECE, PIECE), PIECE)
        low = row_norm(found, gain[...], bias[...])
        hid[at, :] = low
        mixed = jnp.dot(low, weights[...], preferred_element_type=jnp.float32).astype(
            jnp.bfloat16
        )
        width = query.shape[1]
        query[at, :] = mixed[:, :width]
        key[at, :] = mixed[:, width : 2 * width]
        value[at, :] = mixed[:, 2 * width :]

    def block(owner, number):
        return gathered[owner, number * PIECE : (number + 1) * PIECE, :]

    for i in range(pieces):
        work(tokens[i * PIECE : (i + 1) * PIECE, :], head, i)
    for i in range(pieces):
        beside[i].wait_recv()
        work(block(near, i), near, i)
    passed = []
    for i in range(pieces):
        over[i].wait_recv()
        one = copy(
            gathered.at[far, pl.ds(i * PIECE, PIECE)], far, near, 2 * pieces + i
        )
        one.start()
        passed.append(one)
        work(block(far, i), far, i)
    for i in range(pieces):
        passed[i].wait_recv()
        work(block(across_, i), across_, i)
    for one in over + beside + passed:
        one.wait_send()


def head_forward(tokens, gain, bias, weights, collective_id):
    rows, depth = tokens.shape
    heads = lax.axis_size("head")
    span, width = rows * heads, weights.shape[1] // 3
    low = lambda count: jax.ShapeDtypeStruct((span, count), jnp.bfloat16)
    return pl.pallas_call(
        head_forward_kernel,
        in_specs=[VMEM] * 4,
        out_specs=[VMEM] * 4,
        out_shape=[low(depth), low(width), low(width), low(width)],
        scratch_shapes=[
            pltpu.VMEM((heads, rows, depth), jnp.bfloat16),
            pltpu.SemaphoreType.DMA((3 * (rows // PIECE),)),
            pltpu.SemaphoreType.DMA((3 * (rows // PIECE),)),
        ],
        compiler_params=pltpu.CompilerParams(
            collective_id=collective_id, has_side_effects=True, vmem_limit_bytes=32 * MIB
        ),
        name="head_forward",
    )(tokens, gain, bias, weights)


def head_backward_kernel(
    bits,
    back_query,
    back_key,
    back_value,
    back_feed,
    hid,
    weights,
    grad_hid,
    grad_weights,
    total,
    parts,
    near_in,
    far_in,
    products,
    arrived,
    shares,
    head_sems,
    tok_sends,
    tok_recvs,
    share_sends,
    share_recvs,
):
    tok, head = lax.axis_index("tok"), lax.axis_index("head")
    heads, toks = lax.axis_size("head"), lax.axis_size("tok")
    near = head + 1 - 2 * lax.rem(head, 2)
    far = head + 2 - 4 * (head // 2)
    across_ = near + 2 - 4 * (near // 2)
    head_peers = [lax.rem(head + step, heads) for step in range(1, heads)]
    ladder = mesh_bits()[bits_of(heads) :]
    greet([(tok, other) for other in head_peers] + [partner for _, partner in ladder])
    rows = grad_hid.shape[0]
    width = back_query.shape[1]
    columns_ = pl.ds(pl.multiple_of(head * width, HD), width)

    def block_of(owner):
        return pl.ds(pl.multiple_of(owner * rows, PIECE), rows)

    def partial(owner):
        at = block_of(owner)
        found = across(back_query[at, :], weights[:, :width])
        found += across(back_key[at, :], weights[:, width : 2 * width])
        found += across(back_value[at, :], weights[:, 2 * width :])
        total[...] = found
        total[:, columns_] += back_feed[at, :].astype(jnp.float32)

    def copy(source, target, device, number):
        one = pltpu.make_async_remote_copy(
            src_ref=source,
            dst_ref=target,
            send_sem=head_sems.at[0, number],
            recv_sem=head_sems.at[1, number],
            device_id=(tok, device),
            device_id_type=MESH,
        )
        one.start()
        return one

    partial(across_)
    parts[0] = total[...].astype(jnp.bfloat16)
    first = copy(parts.at[0], near_in.at[0], near, 0)
    partial(near)
    parts[1] = total[...].astype(jnp.bfloat16)
    second = copy(parts.at[1], near_in.at[1], near, 1)
    partial(far)
    first.wait_recv()
    parts[2] = (total[...] + near_in[0].astype(jnp.float32)).astype(jnp.bfloat16)
    third = copy(parts.at[2], far_in, far, 2)

    steps = len(ladder)
    orders = [list(range(steps)), [1, 0] + list(range(2, steps))]
    each = products[0].shape[1]
    half_width = products[0].shape[2]
    depth = hid.shape[1]
    base = [0, 0]
    sent = []

    def forward(number, stage):
        bit, partner = ladder[orders[number][stage]]
        half = 1 << (steps - 1 - stage)
        one = pltpu.make_async_remote_copy(
            src_ref=products[number].at[pl.ds(base[number] + (1 - bit) * half, half)],
            dst_ref=arrived[number * steps + stage],
            send_sem=tok_sends.at[number, stage],
            recv_sem=tok_recvs.at[number, stage],
            device_id=partner,
            device_id_type=MESH,
        )
        one.start()
        sent.append(one)
        base[number] = base[number] + bit * half
        return one

    def joined(at, number):
        if number == 0:
            return jnp.concatenate([back_query[at, :], back_key[at, : half_width - width]], axis=1)
        return jnp.concatenate([back_key[at, half_width - width :], back_value[at, :]], axis=1)

    everything = pl.ds(0, hid.shape[0])
    flying = []
    for number in range(2):
        right = joined(everything, number)
        for start in range(0, depth, TILE):
            found = lax.dot_general(
                hid[:, start : start + TILE],
                right,
                (((0,), (0,)), ((), ())),
                preferred_element_type=jnp.float32,
            ).astype(jnp.bfloat16)
            for inner in range(TILE // each):
                products[number][slot_of(start // each + inner, orders[number])] = found[
                    inner * each : (inner + 1) * each
                ]
        flying.append(forward(number, 0))

    partial(head)
    second.wait_recv()
    total[...] += near_in[1].astype(jnp.float32)

    done = []
    for stage in range(steps):
        for number in range(2):
            flying[number].wait_recv()
            arrival = arrived[number * steps + stage]
            half = 1 << (steps - 1 - stage)
            if stage == steps - 1:
                done.append(
                    products[number][base[number]].astype(jnp.float32)
                    + arrival[0].astype(jnp.float32)
                )
            else:
                for i in range(half):
                    products[number][base[number] + i] = (
                        products[number][base[number] + i] + arrival[i]
                    )
                flying[number] = forward(number, stage + 1)
    small = each // heads
    ready, landed = shares
    for other in range(heads):
        for number in range(2):
            ready[other, :, number * half_width : (number + 1) * half_width] = done[number][
                other * small : (other + 1) * small
            ]
    landed[head] = ready[head]
    swaps = []
    for step, other in enumerate(head_peers):
        one = pltpu.make_async_remote_copy(
            src_ref=ready.at[other],
            dst_ref=landed.at[head],
            send_sem=share_sends.at[step],
            recv_sem=share_recvs.at[step],
            device_id=(tok, other),
            device_id_type=MESH,
        )
        one.start()
        swaps.append(one)

    third.wait_recv()
    grad_hid[...] = total[...] + far_in[...].astype(jnp.float32)
    for one in swaps:
        one.wait()
    for other in range(heads):
        for kind in range(3):
            grad_weights[kind, :, other * width : (other + 1) * width] = landed[
                other, :, kind * width : (kind + 1) * width
            ]
    for one in sent + [first, second, third]:
        one.wait_send()


def unpack_refs(function, shapes):
    def kernel(*refs):
        grouped, at = [], 0
        for size in shapes:
            grouped.append(refs[at] if size == 0 else refs[at : at + size])
            at += max(size, 1)
        function(*grouped)

    return kernel


def head_backward(back_query, back_key, back_value, back_feed, hid, weights, collective_id):
    span, width = back_query.shape
    depth = hid.shape[1]
    heads, toks = lax.axis_size("head"), lax.axis_size("tok")
    rows, each = span // heads, depth // toks
    steps, half_width = bits_of(toks), 3 * width // 2
    low = lambda *shape: pltpu.VMEM(shape, jnp.bfloat16)
    full = lambda *shape: pltpu.VMEM(shape, jnp.float32)
    sems = lambda *shape: pltpu.SemaphoreType.DMA(shape)
    kernel = functools.partial(head_backward_kernel, steps)
    sizes = [0] * 8 + [0, 0, 0, 0] + [2, 2 * steps, 2] + [0] * 5
    return pl.pallas_call(
        unpack_refs(kernel, sizes),
        in_specs=[VMEM] * 6,
        out_specs=[VMEM] * 2,
        out_shape=[
            jax.ShapeDtypeStruct((rows, depth), jnp.float32),
            jax.ShapeDtypeStruct((3, each // heads, depth), jnp.float32),
        ],
        scratch_shapes=[
            full(rows, depth),
            low(3, rows, depth),
            low(2, rows, depth),
            low(rows, depth),
        ]
        + [low(toks, each, half_width)] * 2
        + [low(1 << (steps - 1 - stage), each, half_width) for stage in range(steps)] * 2
        + [full(heads, each // heads, 3 * width)] * 2
        + [sems(2, 3), sems(2, steps), sems(2, steps), sems(heads - 1), sems(heads - 1)],
        compiler_params=pltpu.CompilerParams(
            collective_id=collective_id, has_side_effects=True, vmem_limit_bytes=40 * MIB
        ),
        name="head_backward",
    )(back_query, back_key, back_value, back_feed, hid, weights)


def layer_norm(row_block, gain, bias):
    centre = jnp.mean(row_block, axis=-1, keepdims=True)
    centred = row_block - centre
    spread = jnp.mean(centred * centred, axis=-1, keepdims=True)
    return centred * lax.rsqrt(spread + epsilon) * gain + bias


def product(left, right):
    return jnp.dot(left, right, preferred_element_type=jnp.float32)


def product_left(left, right):
    return lax.dot_general(
        left, right, (((0,), (0,)), ((), ())), preferred_element_type=jnp.float32
    )


def product_right(left, right):
    return lax.dot_general(
        left, right, (((1,), (1,)), ((), ())), preferred_element_type=jnp.float32
    )


def seq_place(positions, seq_starts, block_sizes):
    later = positions >= seq_starts[1]
    opening = jnp.where(later, seq_starts[1], seq_starts[0])
    length = jnp.where(later, block_sizes[1], block_sizes[0])
    return opening, opening + (positions - opening) // length * length


def shifted(shard, axis, by):
    devices = lax.axis_size(axis)
    pairs = [(i, i + by) for i in range(devices) if 0 <= i + by < devices]
    return lax.ppermute(shard, axis, pairs)


def per_device(
    tokens_in,
    seq_starts,
    block_sizes,
    norm1_gain,
    norm1_bias,
    w_query,
    w_key,
    w_value,
    w_output,
    ssm_rate,
    ssm_input,
    ssm_output,
    ssm_skip,
    norm2_gain,
    norm2_bias,
    w_up,
    up_bias,
    w_down,
    down_bias,
    out_grad,
):
    tok_rows = tokens_in.shape[0]
    pieces, here = lax.axis_size("tok"), lax.axis_index("tok")
    span = tok_rows * lax.axis_size("head")
    total_len = span * pieces
    anchor = here * span
    window = 2 * BLOCK
    length = span // SUB

    residual = tokens_in.astype(jnp.float32)
    _, norm1_pull = jax.vjp(layer_norm, residual, norm1_gain, norm1_bias)
    width = ssm_rate.shape[0]
    mine = lax.axis_index("head") * width
    w_own = jnp.concatenate(
        [lax.dynamic_slice_in_dim(w, mine, width, 1) for w in (w_query, w_key, w_value)], axis=1
    )
    hid, query_h, key_h, value_h = head_forward(
        tokens_in, norm1_gain[None, :], norm1_bias[None, :], w_own, 6
    )
    hidden_h = lax.dynamic_slice_in_dim(hid, mine, width, 1)

    second = seq_starts[1] - anchor
    inside = (second >= 0) & (second < span)
    brk = jnp.where(inside, jnp.stack([second // length, second % length]), -1).astype(jnp.int32)
    keep = 1.0 - (jnp.arange(SUB) == brk[0]).astype(jnp.float32)
    whole = 1.0 - (jnp.arange(pieces) == seq_starts[1] // span).astype(jnp.float32)
    positions = anchor + jnp.arange(span, dtype=jnp.int32)
    opening, first = seq_place(positions, seq_starts, block_sizes)
    first = first - anchor
    where_ = jnp.concatenate([jnp.stack([anchor, second]), block_sizes, first[::TILE]]).astype(
        jnp.int32
    )
    first = first.reshape(-1, 1, TILE)
    opening = (opening - anchor).reshape(-1, 1, TILE)

    rate = ssm_rate.T / total_len
    drive_in, read_out = ssm_input.T, ssm_output.T
    skip = ssm_skip[None, :]
    decay = jnp.exp(-rate)
    gain = jnp.sqrt(-jnp.expm1(-2.0 * rate))
    driving = gain * drive_in
    mix = read_out * driving
    chunk_decay = jnp.exp(-rate * length)
    chunk_slope = length * jnp.exp(-rate * (length - 1))
    span_decay = jnp.exp(-rate * span)
    span_slope = span * jnp.exp(-rate * (span - 1))

    ends = ssm_ends(brk, hidden_h, decay)
    starts = state_exchange(keep, whole, ends, chunk_decay, span_decay, 1)
    context = ssm_out(brk, hidden_h, decay, mix, skip, starts)

    rims = shifted(jnp.stack([key_h[span - window :], value_h[span - window :]]), "tok", 1)
    context_rim = shifted(context[span - window - CTX :], "tok", 1)
    key_ext = jnp.concatenate([rims[0], key_h], axis=0)
    value_ext = jnp.concatenate([rims[1], value_h], axis=0)
    context_ext = jnp.concatenate([context_rim, context], axis=0)
    attended, attended_fine, level = attend(where_, query_h, key_ext, value_ext, context_ext, first, opening)
    joined = lax.all_to_all(attended, "head", split_axis=0, concat_axis=1, tiled=True)
    middle = residual + product(joined, w_output)
    normed_two, norm2_pull = jax.vjp(layer_norm, middle, norm2_gain, norm2_bias)
    normed_low = normed_two.astype(jnp.bfloat16)
    before = product(normed_low, w_up) + up_bias
    active, gelu_pull = jax.vjp(jax.nn.gelu, before)
    active_low = active.astype(jnp.bfloat16)
    layer_out = (middle + product(active_low, w_down) + down_bias).astype(jnp.bfloat16)
    grad_top = out_grad.astype(jnp.float32)
    grad_down_bias = jnp.sum(grad_top, axis=0)
    (grad_before,) = gelu_pull(product_right(out_grad, w_down))
    grad_before_low = grad_before.astype(jnp.bfloat16)
    grad_up_bias = jnp.sum(grad_before_low.astype(jnp.float32), axis=0)
    grad_mid_norm, grad_norm2_gain, grad_norm2_bias = norm2_pull(
        product_right(grad_before_low, w_up)
    )
    grad_middle = grad_top + grad_mid_norm
    grad_branch = grad_middle.astype(jnp.bfloat16)
    grad_joined = product_right(grad_branch, w_output).astype(jnp.bfloat16)
    grad_att = lax.all_to_all(grad_joined, "head", split_axis=1, concat_axis=0, tiled=True)

    back_query_h, key_rim, value_rim, near_rim, back_key_h, back_value_h, back_context = attend_back(
        where_, query_h, key_ext, value_ext, context_ext, first, opening, attended_fine, grad_att, level
    )
    near_rim = shifted(near_rim, "tok", -1).astype(jnp.float32)
    rims = shifted(jnp.stack([key_rim, value_rim]), "tok", -1).astype(jnp.float32)
    back_context = back_context.at[span - window - CTX :].add(near_rim)
    back_key_h = back_key_h.at[span - window :].add(rims[0]).astype(jnp.bfloat16)
    back_value_h = back_value_h.at[span - window :].add(rims[1]).astype(jnp.bfloat16)

    back_ends, back_lags = ssm_back_ends(brk, back_context, decay)
    starts, lag_starts = adjoint_exchange(
        keep, whole, back_ends, back_lags, chunk_decay, chunk_slope, span_decay, span_slope, 2
    )
    back_feed_h, sums, lag_sums, skip_sum = ssm_back(
        brk, back_context, hidden_h, decay, mix, skip, starts, lag_starts
    )
    grad_hidden, out_w_heads = head_backward(
        back_query_h, back_key_h, back_value_h, back_feed_h, hid, w_own, 4
    )
    grad_res_norm, grad_norm1_gain, grad_norm1_bias = norm1_pull(grad_hidden)
    input_grad = grad_middle + grad_res_norm

    out_w_down, out_w_up, out_w_output = summed_products(
        [active_low, normed_low, joined],
        [out_grad, grad_before_low, grad_branch],
        FEED_PLAN,
        3,
        "feed_products",
    )
    devices = pieces * lax.axis_size("head")
    short = [grad_norm1_gain, grad_norm1_bias, grad_norm2_gain, grad_norm2_bias, grad_down_bias]
    packed = jnp.concatenate(
        [grad.reshape(devices, -1) for grad in short + [grad_up_bias]], axis=1
    )
    each = short[0].shape[0] // devices
    lanes = -packed.shape[1] % HD
    packed = jnp.pad(packed, ((0, 0), (0, lanes))).reshape(devices, 1, -1)
    rows = jnp.concatenate([sums, lag_sums, skip_sum], axis=0)
    rows = jnp.pad(rows, ((0, -rows.shape[0] % SUB), (0, 0)))
    summed, packed = final_sums(rows, packed, 5)
    short = [packed[0, at * each : (at + 1) * each] for at in range(len(short))]
    out_up_bias = packed[0, len(short) * each : len(short) * each + up_bias.shape[0] // devices]
    sums, lag_sums, skip_sum = summed[:NS], summed[NS : 2 * NS], summed[2 * NS]
    grad_ssm_output = (driving * sums).T
    grad_driving = read_out * sums
    grad_ssm_input = (gain * grad_driving).T
    grad_ssm_rate = (
        grad_driving * drive_in * jnp.exp(-2.0 * rate) / gain - mix * lag_sums * decay
    ).T / total_len

    return (
        layer_out,
        input_grad,
        short[0],
        short[1],
        out_w_heads[0],
        out_w_heads[1],
        out_w_heads[2],
        out_w_output,
        grad_ssm_rate,
        grad_ssm_input,
        grad_ssm_output,
        skip_sum,
        short[2],
        short[3],
        out_w_up,
        out_up_bias,
        out_w_down,
        short[4],
    )


def solution(mesh):
    return jax.shard_map(
        per_device,
        mesh=mesh,
        in_specs=(
            P(("tok", "head"), None),
            P(),
            P(),
            P(),
            P(),
            P(),
            P(),
            P(),
            P(),
            P("head", None),
            P("head", None),
            P("head", None),
            P("head"),
            P(),
            P(),
            P(),
            P(),
            P(),
            P(),
            P(("tok", "head"), None),
        ),
        out_specs=(
            P(("tok", "head"), None),
            P(("tok", "head"), None),
            P(("tok", "head")),
            P(("tok", "head")),
            P(("tok", "head"), None),
            P(("tok", "head"), None),
            P(("tok", "head"), None),
            P(("tok", "head"), None),
            P("head", None),
            P("head", None),
            P("head", None),
            P("head"),
            P(("tok", "head")),
            P(("tok", "head")),
            P(("tok", "head"), None),
            P(("tok", "head")),
            P(("tok", "head"), None),
            P(("tok", "head")),
        ),
        check_vma=False,
    )
```

```python
import functools
import math

import jax
import jax.numpy as jnp
from jax import lax
from jax.experimental import pallas as pl
from jax.experimental.pallas import tpu as pltpu
from jax.sharding import PartitionSpec as P

epsilon = 1e-05
HD = 128
CTX = 128
BLOCK = 256
NS = 16
SUB = 8
UNROLL = 8
HALF = 8
TILE = 256
MIB = 1 << 20
LOWEST = -1e30
FACTOR = HD ** (-0.5)
FACTOR2 = FACTOR * math.log2(math.e)


def spread(table, n):
    return jnp.broadcast_to(table[n : n + 1, :], (SUB, table.shape[1]))


def stepped(length, chunk, step, body, carry):
    blocks = length // UNROLL
    hit = jnp.where(step < 0, blocks, step // UNROLL)

    def plain(block, now):
        for inner in range(UNROLL):
            now = body(block * UNROLL + inner, now, None)
        return now

    def masked(block, now):
        rows = lax.broadcasted_iota(jnp.int32, (SUB, HD), 0)
        for inner in range(UNROLL):
            t = block * UNROLL + inner
            live = jnp.where((rows == chunk) & (t == step), 0.0, 1.0)
            now = body(t, now, live)
        return now

    carry = lax.fori_loop(0, hit, plain, carry)
    carry = lax.fori_loop(hit, jnp.minimum(hit + 1, blocks), masked, carry)
    return lax.fori_loop(hit + 1, blocks, plain, carry)


def ssm_ends_kernel(brk, feed, decay, ends, rows):
    length = rows.shape[0] // SUB
    rows[...] = feed[...].astype(jnp.float32)
    table = decay[...]
    factors = [spread(table, n) for n in range(NS)]

    def body(t, states, live):
        drive = rows[pl.ds(t, SUB, stride=length), :]
        if live is not None:
            states = [state * live for state in states]
        return tuple(state * factor + drive for state, factor in zip(states, factors))

    zero = jnp.zeros((SUB, HD), jnp.float32)
    states = stepped(length, brk[0], brk[1], body, (zero,) * NS)
    for n in range(NS):
        ends[n] = states[n]


def ssm_out_kernel(brk, feed, decay, mix, skip, starts, out, rows, sums):
    length = rows.shape[0] // SUB
    rows[...] = feed[...].astype(jnp.float32)
    table = decay[...]
    weights = mix[...]
    factors = [spread(table, n) for n in range(NS)]
    mixes = [spread(weights, n) for n in range(NS)]
    direct = spread(skip[...], 0)

    def body(t, states, live):
        drive = rows[pl.ds(t, SUB, stride=length), :]
        if live is not None:
            states = [state * live for state in states]
        states = tuple(state * factor + drive for state, factor in zip(states, factors))
        parts = [state * weight for state, weight in zip(states, mixes)] + [direct * drive]
        while len(parts) > 1:
            parts = [a + b for a, b in zip(parts[::2], parts[1::2])] + (
                [parts[-1]] if len(parts) % 2 else []
            )
        sums[pl.ds(t, SUB, stride=length), :] = parts[0]
        return states

    stepped(length, brk[0], brk[1], body, tuple(starts[n] for n in range(NS)))
    out[...] = sums[...].astype(out.dtype)


def ssm_back_ends_kernel(brk, slope, decay, ends, lags):
    length = slope.shape[0] // SUB
    table = decay[...]
    zero = jnp.zeros((SUB, HD), jnp.float32)
    factors = [spread(table, n) for n in range(NS)]

    def body(t, carry, live):
        drive = slope[pl.ds(length - 1 - t, SUB, stride=length), :]
        adjoint, lag = carry[:NS], carry[NS:]
        lag = [a * f + b for a, f, b in zip(lag, factors, adjoint)]
        adjoint = [a * f + drive for a, f in zip(adjoint, factors)]
        if live is not None:
            lag = [a * live for a in lag]
            adjoint = [a * live for a in adjoint]
        return tuple(adjoint) + tuple(lag)

    back = jnp.where(brk[1] < 0, -1, length - 1 - brk[1])
    done = stepped(length, brk[0], back, body, (zero,) * (2 * NS))
    for n in range(NS):
        ends[n] = done[n]
        lags[n] = done[NS + n]


def ssm_back_kernel(
    brk, slope, feed, decay, mix, skip, starts, lag_starts, back, sums, lag_sums, skip_sum, rows, total
):
    length = rows.shape[0] // SUB
    rows[...] = feed[...].astype(jnp.float32)
    table = decay[...]
    weights = mix[...]
    zero = jnp.zeros((SUB, HD), jnp.float32)
    total[...] = slope[...] * skip[...]
    skip_sum[...] = jnp.sum(slope[...] * rows[...], axis=0, keepdims=True)
    reversed_step = jnp.where(brk[1] < 0, -1, length - 1 - brk[1])
    for base in range(0, NS, HALF):
        factors = [spread(table, base + n) for n in range(HALF)]
        mixes = [spread(weights, base + n) for n in range(HALF)]

        def body(t, carry, live):
            at = pl.ds(length - 1 - t, SUB, stride=length)
            drive, source = slope[at, :], rows[at, :]
            adjoint, lag = carry[:HALF], carry[HALF : 2 * HALF]
            direct, late = carry[2 * HALF : 3 * HALF], carry[3 * HALF :]
            lag = [a * f + b for a, f, b in zip(lag, factors, adjoint)]
            adjoint = [a * f + drive for a, f in zip(adjoint, factors)]
            direct = [a + b * source for a, b in zip(direct, adjoint)]
            late = [a + b * source for a, b in zip(late, lag)]
            parts = [a * b for a, b in zip(adjoint, mixes)]
            while len(parts) > 1:
                parts = [a + b for a, b in zip(parts[::2], parts[1::2])]
            total[at, :] = total[at, :] + parts[0]
            if live is not None:
                lag = [a * live for a in lag]
                adjoint = [a * live for a in adjoint]
            return tuple(adjoint) + tuple(lag) + tuple(direct) + tuple(late)

        first = tuple(starts[base + n] for n in range(HALF)) + tuple(
            lag_starts[base + n] for n in range(HALF)
        )
        done = stepped(length, brk[0], reversed_step, body, first + (zero,) * (2 * HALF))
        for n in range(HALF):
            sums[base + n : base + n + 1, :] = jnp.sum(done[2 * HALF + n], axis=0, keepdims=True)
            lag_sums[base + n : base + n + 1, :] = jnp.sum(
                done[3 * HALF + n], axis=0, keepdims=True
            )
    back[...] = total[...].astype(back.dtype)


def columns(rows):
    return pl.BlockSpec((rows, HD), lambda g: (0, g))


def chunked():
    return pl.BlockSpec((NS, SUB, HD), lambda g: (0, 0, g))


SCALARS = pl.BlockSpec(memory_space=pltpu.SMEM)


def wide(limit=48):
    return pltpu.CompilerParams(vmem_limit_bytes=limit * MIB)


def ssm_ends(brk, feed, decay):
    rows, width = feed.shape
    return pl.pallas_call(
        ssm_ends_kernel,
        grid=(width // HD,),
        in_specs=[SCALARS, columns(rows), columns(NS)],
        out_specs=chunked(),
        out_shape=jax.ShapeDtypeStruct((NS, SUB, width), jnp.float32),
        scratch_shapes=[pltpu.VMEM((rows, HD), jnp.float32)],
        compiler_params=wide(),
        name="ssm_ends",
    )(brk, feed, decay)


def ssm_out(brk, feed, decay, mix, skip, starts):
    rows, width = feed.shape
    return pl.pallas_call(
        ssm_out_kernel,
        grid=(width // HD,),
        in_specs=[SCALARS, columns(rows), columns(NS), columns(NS), columns(1), chunked()],
        out_specs=columns(rows),
        out_shape=jax.ShapeDtypeStruct((rows, width), jnp.bfloat16),
        scratch_shapes=[pltpu.VMEM((rows, HD), jnp.float32)] * 2,
        compiler_params=wide(),
        name="ssm_out",
    )(brk, feed, decay, mix, skip, starts)


def ssm_back_ends(brk, slope, decay):
    rows, width = slope.shape
    return pl.pallas_call(
        ssm_back_ends_kernel,
        grid=(width // HD,),
        in_specs=[SCALARS, columns(rows), columns(NS)],
        out_specs=(chunked(), chunked()),
        out_shape=(jax.ShapeDtypeStruct((NS, SUB, width), jnp.float32),) * 2,
        compiler_params=wide(),
        name="ssm_back_ends",
    )(brk, slope, decay)


def ssm_back(brk, slope, feed, decay, mix, skip, starts, lag_starts):
    rows, width = feed.shape
    table = jax.ShapeDtypeStruct((NS, width), jnp.float32)
    return pl.pallas_call(
        ssm_back_kernel,
        grid=(width // HD,),
        in_specs=[
            SCALARS,
            columns(rows),
            columns(rows),
            columns(NS),
            columns(NS),
            columns(1),
            chunked(),
            chunked(),
        ],
        out_specs=(columns(rows), columns(NS), columns(NS), columns(1)),
        out_shape=(
            jax.ShapeDtypeStruct((rows, width), jnp.bfloat16),
            table,
            table,
            jax.ShapeDtypeStruct((1, width), jnp.float32),
        ),
        scratch_shapes=[pltpu.VMEM((rows, HD), jnp.float32)] * 2,
        compiler_params=wide(),
        name="ssm_back",
    )(brk, slope, feed, decay, mix, skip, starts, lag_starts)


def across(left, right):
    return lax.dot_general(
        left, right, (((1,), (1,)), ((), ())), preferred_element_type=jnp.float32
    )


def times(left, right):
    return lax.dot_general(
        left, right, (((1,), (0,)), ((), ())), preferred_element_type=jnp.float32
    )


def turn(source, target):
    for at in range(0, source.shape[0], TILE):
        size = min(TILE, source.shape[0] - at)
        piece = source[at : at + size, :].astype(jnp.float32)
        target[:, at : at + size] = piece.T.astype(target.dtype)


def local_tiles(where_, tile):
    return (where_[4 + tile] + 2 * BLOCK) // TILE


def next_block(where_, now):
    second = where_[1]
    length = jnp.where(now >= second, where_[3], where_[2])
    after = now + length
    return jnp.where((now < second) & (after > second), second, after)


def local_mask(tile, key_tile, first):
    rows = lax.broadcasted_iota(jnp.int32, (TILE, TILE), 0) + (key_tile * TILE - 2 * BLOCK)
    cols = lax.broadcasted_iota(jnp.int32, (1, TILE), 1) + tile * TILE
    return (rows >= first) & (rows <= cols)


def context_at(now):
    return pl.multiple_of((now + 2 * BLOCK) // CTX * CTX, CTX)


def context_mask(start, now, first, opening):
    rows = lax.broadcasted_iota(jnp.int32, (TILE, TILE), 0) + (start - 2 * BLOCK - CTX)
    low = jnp.where(first == now, jnp.maximum(now - CTX, opening), 1 << 28)
    return (rows >= low) & (rows < now)


def attend_kernel(
    where_, query, key, value, context, first, opening, out, fine, level, value_t, context_t
):
    turn(value, value_t)
    turn(context, context_t)

    def one_tile(tile, _):
        rows = query[pl.ds(pl.multiple_of(tile * TILE, TILE), TILE), :]
        firsts = first[tile]
        openings = opening[tile]

        def add(carry, keys, values_t, mask):
            top, mass, low_mass, total = carry
            score = jnp.where(mask, across(keys, rows) * FACTOR2, LOWEST)
            new_top = jnp.maximum(top, jnp.max(score, axis=0, keepdims=True))
            prob = jnp.exp2(score - new_top)
            shrink = jnp.exp2(top - new_top)
            low = prob.astype(jnp.bfloat16)
            mass = mass * shrink + jnp.sum(prob, axis=0, keepdims=True)
            low_mass = low_mass * shrink + jnp.sum(
                low.astype(jnp.float32), axis=0, keepdims=True
            )
            total = total * shrink + times(values_t, low)
            return new_top, mass, low_mass, total

        def local(key_tile, carry):
            at = pl.ds(pl.multiple_of(key_tile * TILE, TILE), TILE)
            return add(carry, key[at, :], value_t[:, at], local_mask(tile, key_tile, firsts))

        def earlier(state):
            now, carry = state[0], state[1:]
            start = context_at(now)
            at = pl.ds(start, TILE)
            carry = add(
                carry,
                context[at, :],
                context_t[:, at],
                context_mask(start, now, firsts, openings),
            )
            return (next_block(where_, now),) + tuple(carry)

        carry = (
            jnp.full((1, TILE), LOWEST, jnp.float32),
            jnp.zeros((1, TILE), jnp.float32),
            jnp.zeros((1, TILE), jnp.float32),
            jnp.zeros((HD, TILE), jnp.float32),
        )
        carry = lax.fori_loop(local_tiles(where_, tile), tile + 3, local, carry)
        state = lax.while_loop(
            lambda state: state[0] < (tile + 1) * TILE, earlier, (where_[4 + tile],) + carry
        )
        _, top, mass, low_mass, total = state
        done = (total / low_mass).T
        here = pl.ds(pl.multiple_of(tile * TILE, TILE), TILE)
        fine[here, :] = done
        out[here, :] = done.astype(out.dtype)
        level[0, tile] = top + jnp.log2(mass)
        return 0

    lax.fori_loop(0, query.shape[0] // TILE, one_tile, 0)


def attend_back_kernel(
    where_,
    query,
    key,
    value,
    context,
    first,
    opening,
    attended,
    grad,
    level,
    back_query,
    key_rim,
    value_rim,
    context_rim,
    back_key,
    back_value,
    back_context,
    key_t,
    context_t,
    key_sum,
    value_sum,
    context_sum,
):
    turn(key, key_t)
    turn(context, context_t)
    key_sum[...] = jnp.zeros_like(key_sum)
    value_sum[...] = jnp.zeros_like(value_sum)
    context_sum[...] = jnp.zeros_like(context_sum)

    def one_tile(tile, _):
        here = pl.ds(pl.multiple_of(tile * TILE, TILE), TILE)
        rows = query[here, :]
        grads = grad[here, :]
        firsts = first[tile]
        openings = opening[tile]
        levels = level[0, tile]
        joint = grads.astype(jnp.float32) * attended[here, :]
        centre = jnp.sum(joint.T, axis=0, keepdims=True)

        def slopes(keys, values, mask):
            prob = jnp.exp2(jnp.where(mask, across(keys, rows) * FACTOR2 - levels, LOWEST))
            slope = prob * (across(values, grads) - centre)
            return prob.astype(jnp.bfloat16), slope.astype(jnp.bfloat16)

        def local(key_tile, total):
            at = pl.ds(pl.multiple_of(key_tile * TILE, TILE), TILE)
            prob, slope = slopes(key[at, :], value[at, :], local_mask(tile, key_tile, firsts))
            key_sum[at, :] += times(slope, rows)
            value_sum[at, :] += times(prob, grads)
            return total + times(key_t[:, at], slope)

        def earlier(state):
            now, total = state
            start = context_at(now)
            at = pl.ds(start, TILE)
            near = context[at, :]
            prob, slope = slopes(near, near, context_mask(start, now, firsts, openings))
            context_sum[at, :] += FACTOR * times(slope, rows) + times(prob, grads)
            return next_block(where_, now), total + times(context_t[:, at], slope)

        total = jnp.zeros((HD, TILE), jnp.float32)
        total = lax.fori_loop(local_tiles(where_, tile), tile + 3, local, total)
        _, total = lax.while_loop(
            lambda state: state[0] < (tile + 1) * TILE, earlier, (where_[4 + tile], total)
        )
        back_query[here, :] = (FACTOR * total).T.astype(back_query.dtype)
        return 0

    lax.fori_loop(0, query.shape[0] // TILE, one_tile, 0)
    window = 2 * BLOCK
    key_rim[...] = (FACTOR * key_sum[:window, :]).astype(key_rim.dtype)
    value_rim[...] = value_sum[:window, :].astype(value_rim.dtype)
    context_rim[...] = context_sum[: window + CTX, :].astype(context_rim.dtype)
    back_key[...] = FACTOR * key_sum[window:, :]
    back_value[...] = value_sum[window:, :]
    back_context[...] = context_sum[window + CTX :, :]


def attend(where_, query, key, value, context, first, opening):
    rows, width = query.shape
    heads, tiles = width // HD, rows // TILE
    near, far = key.shape[0], context.shape[0]
    whole = pl.BlockSpec((tiles, 1, TILE), lambda g: (0, 0, 0))
    return pl.pallas_call(
        attend_kernel,
        grid=(heads,),
        in_specs=[
            SCALARS,
            columns(rows),
            columns(near),
            columns(near),
            columns(far),
            whole,
            whole,
        ],
        out_specs=(
            columns(rows),
            columns(rows),
            pl.BlockSpec((1, tiles, 1, TILE), lambda g: (g, 0, 0, 0)),
        ),
        out_shape=(
            jax.ShapeDtypeStruct((rows, width), jnp.bfloat16),
            jax.ShapeDtypeStruct((rows, width), jnp.float32),
            jax.ShapeDtypeStruct((heads, tiles, 1, TILE), jnp.float32),
        ),
        scratch_shapes=[
            pltpu.VMEM((HD, near), jnp.bfloat16),
            pltpu.VMEM((HD, far), jnp.bfloat16),
        ],
        compiler_params=wide(),
        name="attend",
    )(where_, query, key, value, context, first, opening)


def attend_back(where_, query, key, value, context, first, opening, attended, grad, level):
    rows, width = query.shape
    heads, tiles = width // HD, rows // TILE
    near, far = key.shape[0], context.shape[0]
    whole = pl.BlockSpec((tiles, 1, TILE), lambda g: (0, 0, 0))
    low = lambda count: jax.ShapeDtypeStruct((count, width), jnp.bfloat16)
    full = lambda count: jax.ShapeDtypeStruct((count, width), jnp.float32)
    return pl.pallas_call(
        attend_back_kernel,
        grid=(heads,),
        in_specs=[
            SCALARS,
            columns(rows),
            columns(near),
            columns(near),
            columns(far),
            whole,
            whole,
            columns(rows),
            columns(rows),
            pl.BlockSpec((1, tiles, 1, TILE), lambda g: (g, 0, 0, 0)),
        ],
        out_specs=(
            columns(rows),
            columns(near - rows),
            columns(near - rows),
            columns(far - rows),
            columns(rows),
            columns(rows),
            columns(rows),
        ),
        out_shape=(
            low(rows),
            low(near - rows),
            low(near - rows),
            low(far - rows),
            full(rows),
            full(rows),
            full(rows),
        ),
        scratch_shapes=[
            pltpu.VMEM((HD, near), jnp.bfloat16),
            pltpu.VMEM((HD, far), jnp.bfloat16),
            pltpu.VMEM((near, HD), jnp.float32),
            pltpu.VMEM((near, HD), jnp.float32),
            pltpu.VMEM((far, HD), jnp.float32),
        ],
        compiler_params=wide(),
        name="attend_back",
    )(where_, query, key, value, context, first, opening, attended, grad, level)


MESH = pl.DeviceIdType.MESH
ROWS = 512


def bits_of(count):
    return count.bit_length() - 1


def mesh_bits():
    found = []
    tok, head = lax.axis_index("tok"), lax.axis_index("head")
    for axis in ("head", "tok"):
        for level in range(bits_of(lax.axis_size(axis))):
            at = head if axis == "head" else tok
            bit = (at // (1 << level)) % 2
            other = at + (1 - 2 * bit) * (1 << level)
            found.append((bit, (tok, other) if axis == "head" else (other, head)))
    return found


def greet(partners):
    barrier = pltpu.get_barrier_semaphore()
    for partner in partners:
        pl.semaphore_signal(barrier, inc=1, device_id=partner, device_id_type=MESH)
    pl.semaphore_wait(barrier, len(partners))


def halving_orders(bits):
    rest = list(range(4, bits))
    return [[0, 1, 3, 2] + rest, [0, 2, 1, 3] + rest, [0, 3, 2, 1] + rest]


def slot_of(block, order):
    place = 0
    for bit in order:
        place = place * 2 + (block // (1 << bit)) % 2
    return place


def unpack_refs(function, sizes):
    def kernel(*refs):
        grouped, at = [], 0
        for size in sizes:
            grouped.append(refs[at] if size == 0 else refs[at : at + max(size, 0)])
            at += 1 if size == 0 else max(size, 0)
        function(*grouped)

    return kernel


class Halver:
    def __init__(self, pieces, stages, arrivals, sems, ladder):
        self.now, self.stages, self.arrivals, self.ladder = list(pieces), stages, arrivals, ladder
        self.sems, self.steps = sems, len(ladder)
        self.orders = halving_orders(self.steps)
        self.sent, self.flying = [], {}

    def half(self, stage):
        return 1 << (self.steps - 1 - stage)

    def send(self, number, stage):
        bit, partner = self.ladder[self.orders[number][stage]]
        at = number * len(self.stages) + self.stages.index(stage)
        half = self.half(stage)
        copy = pltpu.make_async_remote_copy(
            src_ref=self.now[number].at[pl.ds((1 - bit) * half, half)],
            dst_ref=self.arrivals[at],
            send_sem=self.sems.at[0, at],
            recv_sem=self.sems.at[1, at],
            device_id=partner,
            device_id_type=MESH,
        )
        copy.start()
        self.sent.append(copy)
        self.flying[number] = (copy, self.arrivals[at], bit * half)

    def absorb(self, number, stage, into=None):
        copy, arrival, keep = self.flying[number]
        copy.wait_recv()
        before = self.now[number]
        target = arrival if into is None else into

        def add(i, _):
            if target.dtype == jnp.float32:
                target[i] = before[keep + i].astype(jnp.float32) + arrival[i].astype(jnp.float32)
            else:
                target[i] = before[keep + i] + arrival[i]
            return 0

        lax.fori_loop(0, self.half(stage), add, 0)
        self.now[number] = target

    def step(self, stage, into=None):
        for number in range(len(self.now)):
            self.absorb(number, stage, None if into is None else into[number])
            if into is None:
                self.send(number, stage + 1)

    def begin(self):
        for number in range(len(self.now)):
            self.send(number, self.stages[0])

    def drain(self):
        for copy in self.sent:
            copy.wait_send()


def halver_scratch(pieces, stages, devices):
    steps = bits_of(devices)
    buffers = [
        pltpu.VMEM((1 << (steps - 1 - stage), block, width), jnp.bfloat16)
        for block, width in pieces
        for stage in stages
    ]
    sems = pltpu.SemaphoreType.DMA((2, max(len(buffers), 1)))
    return buffers, len(buffers) or -1, sems


def left_over(pieces, stages, devices, kind=jnp.bfloat16):
    slots = 1 << (bits_of(devices) - 1 - stages[-1])
    return [jax.ShapeDtypeStruct((slots, block, width), kind) for block, width in pieces]


def fill(left, right, start, stop, target, column, order):
    block = target.shape[1]
    each = ROWS // block
    for low in range(start, stop, ROWS):
        high = min(low + ROWS, stop)
        to = column + low - start

        def some_rows(chunk, _):
            at = pl.ds(pl.multiple_of(chunk * ROWS, ROWS), ROWS)
            found = lax.dot_general(
                left[:, at],
                right[:, low:high],
                (((0,), (0,)), ((), ())),
                preferred_element_type=jnp.float32,
            ).astype(jnp.bfloat16)
            for inner in range(each):
                target[slot_of(chunk * each + inner, order), :, to : to + high - low] = found[
                    inner * block : (inner + 1) * block
                ]
            return 0

        lax.fori_loop(0, left.shape[1] // ROWS, some_rows, 0)


def stage_groups(devices):
    steps = bits_of(devices)
    return [0, 1], list(range(2, steps - 1)), [steps - 1]


DOWN_PARTS = (384, 384, 256)
UP_PARTS = (
    ((0, 0, 1792),),
    ((0, 1792, 3328),),
    ((0, 3328, 4096), (1, 0, 1024)),
)
UP_WIDTHS = (1792, 1536, 1792)


def products_apart(lefts, rights):
    return [
        lax.psum_scatter(product_left(left, right), ("tok", "head"), scatter_dimension=0, tiled=True)
        for left, right in zip(lefts, rights)
    ]


def tok_peers():
    count, here = lax.axis_size("tok"), lax.axis_index("tok")
    head = lax.axis_index("head")
    return [
        ((lax.rem(here + step, count), head), lax.rem(here + count - step, count))
        for step in range(1, count)
    ]


def share(mine, every, send_sems, recv_sems, place, peers):
    copies = []
    for step, (target, _) in enumerate(peers):
        copy = pltpu.make_async_remote_copy(
            src_ref=mine,
            dst_ref=every.at[place],
            send_sem=send_sems.at[step],
            recv_sem=recv_sems.at[step],
            device_id=target,
            device_id_type=MESH,
        )
        copy.start()
        copies.append(copy)
    return copies


def state_exchange_kernel(
    keep, whole, ends, chunk_decay, span_decay, starts, mine, every, send_sems, recv_sems
):
    here, count = lax.axis_index("tok"), every.shape[0]
    peers = tok_peers()
    greet([target for target, _ in peers])
    factor = chunk_decay[...]
    now = ends[:, 0, :]
    for chunk in range(1, SUB):
        now = keep[chunk] * (factor * now) + ends[:, chunk, :]
    mine[...] = now
    every[here] = now
    copies = share(mine, every, send_sems, recv_sems, here, peers)
    for copy in copies:
        copy.wait()
    over = span_decay[...]
    now = jnp.zeros_like(over)
    for place in range(count - 1):
        now = jnp.where(place < here, whole[place] * (over * now) + every[place], now)
    for chunk in range(SUB):
        starts[:, chunk, :] = now
        now = keep[chunk] * (factor * now) + ends[:, chunk, :]


def adjoint_exchange_kernel(
    keep,
    whole,
    ends,
    lags,
    chunk_decay,
    chunk_slope,
    span_decay,
    span_slope,
    starts,
    lag_starts,
    mine,
    every,
    send_sems,
    recv_sems,
):
    here, count = lax.axis_index("tok"), every.shape[0]
    peers = tok_peers()
    greet([target for target, _ in peers])
    factor, slope = chunk_decay[...], chunk_slope[...]
    now, late = ends[:, SUB - 1, :], lags[:, SUB - 1, :]
    for chunk in reversed(range(SUB - 1)):
        late = keep[chunk] * (factor * late + slope * now) + lags[:, chunk, :]
        now = keep[chunk] * (factor * now) + ends[:, chunk, :]
    mine[0] = now
    mine[1] = late
    every[here, 0] = now
    every[here, 1] = late
    copies = share(mine, every, send_sems, recv_sems, here, peers)
    for copy in copies:
        copy.wait()
    over, over_slope = span_decay[...], span_slope[...]
    now, late = jnp.zeros_like(over), jnp.zeros_like(over)
    for place in reversed(range(1, count)):
        reached = place > here
        late = jnp.where(
            reached, whole[place] * (over * late + over_slope * now) + every[place, 1], late
        )
        now = jnp.where(reached, whole[place] * (over * now) + every[place, 0], now)
    for chunk in reversed(range(SUB)):
        starts[:, chunk, :] = now
        lag_starts[:, chunk, :] = late
        late = keep[chunk] * (factor * late + slope * now) + lags[:, chunk, :]
        now = keep[chunk] * (factor * now) + ends[:, chunk, :]


VMEM = pl.BlockSpec(memory_space=pltpu.VMEM)


def state_exchange(keep, whole, ends, chunk_decay, span_decay, collective_id):
    states, _, width = ends.shape
    count = whole.shape[0]
    return pl.pallas_call(
        state_exchange_kernel,
        in_specs=[SCALARS, SCALARS, VMEM, VMEM, VMEM],
        out_specs=VMEM,
        out_shape=jax.ShapeDtypeStruct(ends.shape, jnp.float32),
        scratch_shapes=[
            pltpu.VMEM((states, width), jnp.float32),
            pltpu.VMEM((count, states, width), jnp.float32),
            pltpu.SemaphoreType.DMA((count - 1,)),
            pltpu.SemaphoreType.DMA((count - 1,)),
        ],
        compiler_params=pltpu.CompilerParams(
            collective_id=collective_id, has_side_effects=True, vmem_limit_bytes=16 * MIB
        ),
        name="state_exchange",
    )(keep, whole, ends, chunk_decay, span_decay)


def adjoint_exchange(
    keep, whole, ends, lags, chunk_decay, chunk_slope, span_decay, span_slope, collective_id
):
    states, _, width = ends.shape
    count = whole.shape[0]
    return pl.pallas_call(
        adjoint_exchange_kernel,
        in_specs=[SCALARS, SCALARS] + [VMEM] * 6,
        out_specs=(VMEM, VMEM),
        out_shape=(jax.ShapeDtypeStruct(ends.shape, jnp.float32),) * 2,
        scratch_shapes=[
            pltpu.VMEM((2, states, width), jnp.float32),
            pltpu.VMEM((count, 2, states, width), jnp.float32),
            pltpu.SemaphoreType.DMA((count - 1,)),
            pltpu.SemaphoreType.DMA((count - 1,)),
        ],
        compiler_params=pltpu.CompilerParams(
            collective_id=collective_id, has_side_effects=True, vmem_limit_bytes=16 * MIB
        ),
        name="adjoint_exchange",
    )(keep, whole, ends, lags, chunk_decay, chunk_slope, span_decay, span_slope)


def final_sums_kernel(
    stages,
    rows,
    vectors,
    up_in,
    row_sum,
    vector_sum,
    up_out,
    every_row,
    every_vector,
    tok_sum,
    head_sums,
    row_sems,
    tok_sems,
    head_sems,
    up_arrivals,
    up_sems,
):
    tok, head = lax.axis_index("tok"), lax.axis_index("head")
    heads = lax.axis_size("head")
    peers = tok_peers()
    head_peers = [lax.rem(head + step, heads) for step in range(1, heads)]
    greet([target for target, _ in peers] + [(tok, other) for other in head_peers])
    copies = []
    for step, (target, _) in enumerate(peers):
        copy = pltpu.make_async_remote_copy(
            src_ref=vectors.at[target[0]],
            dst_ref=every_vector.at[tok],
            send_sem=tok_sems.at[0, step],
            recv_sem=tok_sems.at[1, step],
            device_id=target,
            device_id_type=MESH,
        )
        copy.start()
        copies.append(copy)
    up = Halver(up_in, stages[2], up_arrivals, up_sems, mesh_bits())
    up.begin()
    row_copies = share(rows, every_row, row_sems.at[0], row_sems.at[1], tok, peers)
    every_row[tok] = rows[...]
    every_vector[tok] = vectors[tok]
    for copy in copies:
        copy.wait()
    tok_sum[...] = jnp.sum(every_vector[...], axis=0)
    head_sums[head] = tok_sum[...]
    copies = []
    for step, other in enumerate(head_peers):
        copy = pltpu.make_async_remote_copy(
            src_ref=tok_sum,
            dst_ref=head_sums.at[head],
            send_sem=head_sems.at[0, step],
            recv_sem=head_sems.at[1, step],
            device_id=(tok, other),
            device_id_type=MESH,
        )
        copy.start()
        copies.append(copy)
    for copy in row_copies:
        copy.wait()
    row_sum[...] = jnp.sum(every_row[...], axis=0)
    for copy in copies:
        copy.wait()
    vector_sum[...] = jnp.sum(head_sums[...], axis=0)
    up.step(stages[2][-1], up_out)
    up.drain()


def final_sums(rows, vectors, up, collective_id):
    toks, heads = lax.axis_size("tok"), lax.axis_size("head")
    devices = toks * heads
    stages = stage_groups(devices)
    pieces = [piece.shape[1:] for piece in up]
    buffers, count, up_sems = halver_scratch(pieces, stages[2], devices)
    ups = len(up) or -1
    sems = lambda *shape: pltpu.SemaphoreType.DMA(shape)
    part = vectors.shape[1:]
    found = pl.pallas_call(
        unpack_refs(
            functools.partial(final_sums_kernel, stages),
            [0, 0, ups, 0, 0, ups] + [0] * 7 + [count, 0],
        ),
        in_specs=[VMEM] * (2 + len(up)),
        out_specs=[VMEM] * (2 + len(up)),
        out_shape=[
            jax.ShapeDtypeStruct(rows.shape, jnp.float32),
            jax.ShapeDtypeStruct(part, jnp.float32),
        ]
        + left_over(pieces, stages[2], devices, jnp.float32),
        scratch_shapes=[
            pltpu.VMEM((toks,) + rows.shape, jnp.float32),
            pltpu.VMEM(vectors.shape, jnp.float32),
            pltpu.VMEM(part, jnp.float32),
            pltpu.VMEM((heads,) + part, jnp.float32),
            sems(2, toks - 1),
            sems(2, toks - 1),
            sems(2, heads - 1),
        ]
        + buffers
        + [up_sems],
        compiler_params=pltpu.CompilerParams(
            collective_id=collective_id, has_side_effects=True, vmem_limit_bytes=32 * MIB
        ),
        name="final_sums",
    )(rows, vectors, *up)
    return found[0], found[1], found[2:]


def row_norm(rows, gain, bias):
    rows = rows.astype(jnp.float32)
    centred = rows - jnp.mean(rows, axis=-1, keepdims=True)
    spread_ = jnp.mean(centred * centred, axis=-1, keepdims=True)
    return (centred * lax.rsqrt(spread_ + epsilon) * gain + bias).astype(jnp.bfloat16)


PIECE = 128


def head_forward_kernel(
    tokens, gain, bias, weights, hid, query, key, value, gathered, send_sems, recv_sems
):
    tok, head = lax.axis_index("tok"), lax.axis_index("head")
    near = head + 1 - 2 * lax.rem(head, 2)
    far = head + 2 - 4 * (head // 2)
    across_ = near + 2 - 4 * (near // 2)
    greet([(tok, near), (tok, far)])
    rows = tokens.shape[0]
    pieces = rows // PIECE

    def copy(source, owner, target, number):
        return pltpu.make_async_remote_copy(
            src_ref=source,
            dst_ref=gathered.at[owner, pl.ds(number % pieces * PIECE, PIECE)],
            send_sem=send_sems.at[number],
            recv_sem=recv_sems.at[number],
            device_id=(tok, target),
            device_id_type=MESH,
        )

    def own(number):
        return tokens.at[pl.ds(number * PIECE, PIECE)]

    over = [copy(own(i), head, far, i) for i in range(pieces)]
    beside = [copy(own(i), head, near, pieces + i) for i in range(pieces)]
    for one in over + beside:
        one.start()

    def work(found, owner, number):
        at = pl.ds(pl.multiple_of(owner * rows + number * PIECE, PIECE), PIECE)
        low = row_norm(found, gain[...], bias[...])
        hid[at, :] = low
        mixed = jnp.dot(low, weights[...], preferred_element_type=jnp.float32).astype(
            jnp.bfloat16
        )
        width = query.shape[1]
        query[at, :] = mixed[:, :width]
        key[at, :] = mixed[:, width : 2 * width]
        value[at, :] = mixed[:, 2 * width :]

    def block(owner, number):
        return gathered[owner, number * PIECE : (number + 1) * PIECE, :]

    for i in range(pieces):
        work(tokens[i * PIECE : (i + 1) * PIECE, :], head, i)
    for i in range(pieces):
        beside[i].wait_recv()
        work(block(near, i), near, i)
    passed = []
    for i in range(pieces):
        over[i].wait_recv()
        one = copy(
            gathered.at[far, pl.ds(i * PIECE, PIECE)], far, near, 2 * pieces + i
        )
        one.start()
        passed.append(one)
        work(block(far, i), far, i)
    for i in range(pieces):
        passed[i].wait_recv()
        work(block(across_, i), across_, i)
    for one in over + beside + passed:
        one.wait_send()


def head_forward(tokens, gain, bias, weights, collective_id):
    rows, depth = tokens.shape
    heads = lax.axis_size("head")
    span, width = rows * heads, weights.shape[1] // 3
    low = lambda count: jax.ShapeDtypeStruct((span, count), jnp.bfloat16)
    return pl.pallas_call(
        head_forward_kernel,
        in_specs=[VMEM] * 4,
        out_specs=[VMEM] * 4,
        out_shape=[low(depth), low(width), low(width), low(width)],
        scratch_shapes=[
            pltpu.VMEM((heads, rows, depth), jnp.bfloat16),
            pltpu.SemaphoreType.DMA((3 * (rows // PIECE),)),
            pltpu.SemaphoreType.DMA((3 * (rows // PIECE),)),
        ],
        compiler_params=pltpu.CompilerParams(
            collective_id=collective_id, has_side_effects=True, vmem_limit_bytes=32 * MIB
        ),
        name="head_forward",
    )(tokens, gain, bias, weights)


def head_backward_kernel(
    stages,
    back_query,
    back_key,
    back_value,
    back_feed,
    hid,
    weights,
    down_in,
    up_in,
    grad_hid,
    grad_weights,
    down_out,
    up_out,
    total,
    parts,
    near_in,
    far_in,
    products,
    arrived,
    shares,
    head_sems,
    tok_sends,
    tok_recvs,
    share_sends,
    share_recvs,
    down_arrivals,
    down_sems,
    up_arrivals,
    up_sems,
):
    tok, head = lax.axis_index("tok"), lax.axis_index("head")
    heads, toks = lax.axis_size("head"), lax.axis_size("tok")
    near = head + 1 - 2 * lax.rem(head, 2)
    far = head + 2 - 4 * (head // 2)
    across_ = near + 2 - 4 * (near // 2)
    head_peers = [lax.rem(head + step, heads) for step in range(1, heads)]
    ladder = mesh_bits()[bits_of(heads) :]
    greet([(tok, other) for other in head_peers] + [partner for _, partner in ladder])
    rows = grad_hid.shape[0]
    width = back_query.shape[1]
    columns_ = pl.ds(pl.multiple_of(head * width, HD), width)

    def block_of(owner):
        return pl.ds(pl.multiple_of(owner * rows, PIECE), rows)

    def partial(owner):
        at = block_of(owner)
        found = across(back_query[at, :], weights[:, :width])
        found += across(back_key[at, :], weights[:, width : 2 * width])
        found += across(back_value[at, :], weights[:, 2 * width :])
        total[...] = found
        total[:, columns_] += back_feed[at, :].astype(jnp.float32)

    def copy(source, target, device, number):
        one = pltpu.make_async_remote_copy(
            src_ref=source,
            dst_ref=target,
            send_sem=head_sems.at[0, number],
            recv_sem=head_sems.at[1, number],
            device_id=(tok, device),
            device_id_type=MESH,
        )
        one.start()
        return one

    down = Halver(down_in, stages[2], down_arrivals, down_sems, mesh_bits())
    down.begin()
    up = Halver(up_in, stages[1], up_arrivals, up_sems, mesh_bits())
    up.begin()
    partial(across_)
    parts[0] = total[...].astype(jnp.bfloat16)
    first = copy(parts.at[0], near_in.at[0], near, 0)
    partial(near)
    parts[1] = total[...].astype(jnp.bfloat16)
    second = copy(parts.at[1], near_in.at[1], near, 1)
    partial(far)
    first.wait_recv()
    parts[2] = (total[...] + near_in[0].astype(jnp.float32)).astype(jnp.bfloat16)
    third = copy(parts.at[2], far_in, far, 2)

    steps = len(ladder)
    orders = [list(range(steps)), [1, 0] + list(range(2, steps))]
    each = products[0].shape[1]
    half_width = products[0].shape[2]
    depth = hid.shape[1]
    base = [0, 0]
    sent = []

    def forward(number, stage):
        bit, partner = ladder[orders[number][stage]]
        half = 1 << (steps - 1 - stage)
        one = pltpu.make_async_remote_copy(
            src_ref=products[number].at[pl.ds(base[number] + (1 - bit) * half, half)],
            dst_ref=arrived[number * steps + stage],
            send_sem=tok_sends.at[number, stage],
            recv_sem=tok_recvs.at[number, stage],
            device_id=partner,
            device_id_type=MESH,
        )
        one.start()
        sent.append(one)
        base[number] = base[number] + bit * half
        return one

    def joined(at, number):
        if number == 0:
            return jnp.concatenate([back_query[at, :], back_key[at, : half_width - width]], axis=1)
        return jnp.concatenate([back_key[at, half_width - width :], back_value[at, :]], axis=1)

    everything = pl.ds(0, hid.shape[0])
    flying = []
    for number in range(2):
        right = joined(everything, number)
        for start in range(0, depth, TILE):
            found = lax.dot_general(
                hid[:, start : start + TILE],
                right,
                (((0,), (0,)), ((), ())),
                preferred_element_type=jnp.float32,
            ).astype(jnp.bfloat16)
            for inner in range(TILE // each):
                products[number][slot_of(start // each + inner, orders[number])] = found[
                    inner * each : (inner + 1) * each
                ]
        flying.append(forward(number, 0))

    partial(head)
    if up_in:
        for stage in stages[1][:-1]:
            up.step(stage)
    second.wait_recv()
    total[...] += near_in[1].astype(jnp.float32)

    done = []
    for stage in range(steps):
        for number in range(2):
            flying[number].wait_recv()
            arrival = arrived[number * steps + stage]
            half = 1 << (steps - 1 - stage)
            if stage == steps - 1:
                done.append(
                    products[number][base[number]].astype(jnp.float32)
                    + arrival[0].astype(jnp.float32)
                )
            else:
                for i in range(half):
                    products[number][base[number] + i] = (
                        products[number][base[number] + i] + arrival[i]
                    )
                flying[number] = forward(number, stage + 1)
    small = each // heads
    ready, landed = shares
    for other in range(heads):
        for number in range(2):
            ready[other, :, number * half_width : (number + 1) * half_width] = done[number][
                other * small : (other + 1) * small
            ]
    landed[head] = ready[head]
    swaps = []
    for step, other in enumerate(head_peers):
        one = pltpu.make_async_remote_copy(
            src_ref=ready.at[other],
            dst_ref=landed.at[head],
            send_sem=share_sends.at[step],
            recv_sem=share_recvs.at[step],
            device_id=(tok, other),
            device_id_type=MESH,
        )
        one.start()
        swaps.append(one)

    third.wait_recv()
    grad_hid[...] = total[...] + far_in[...].astype(jnp.float32)
    for one in swaps:
        one.wait()
    for other in range(heads):
        for kind in range(3):
            grad_weights[kind, :, other * width : (other + 1) * width] = landed[
                other, :, kind * width : (kind + 1) * width
            ]
    down.step(stages[2][-1], down_out)
    up.step(stages[1][-1], up_out)
    down.drain()
    up.drain()
    for one in sent + [first, second, third]:
        one.wait_send()


def head_backward(
    back_query, back_key, back_value, back_feed, hid, weights, down, up, collective_id
):
    span, width = back_query.shape
    depth = hid.shape[1]
    heads, toks = lax.axis_size("head"), lax.axis_size("tok")
    rows, each = span // heads, depth // toks
    steps, half_width = bits_of(toks), 3 * width // 2
    devices = heads * toks
    stages = stage_groups(devices)
    down_pieces = [piece.shape[1:] for piece in down]
    up_pieces = [piece.shape[1:] for piece in up]
    down_buffers, down_count, down_sems = halver_scratch(down_pieces, stages[2], devices)
    up_buffers, up_count, up_sems = halver_scratch(up_pieces, stages[1], devices)
    down_shapes = left_over(down_pieces, stages[2], devices, jnp.float32)
    up_shapes = left_over(up_pieces, stages[1], devices)
    downs, ups = len(down), len(up) or -1
    low = lambda *shape: pltpu.VMEM(shape, jnp.bfloat16)
    full = lambda *shape: pltpu.VMEM(shape, jnp.float32)
    sems = lambda *shape: pltpu.SemaphoreType.DMA(shape)
    sizes = [0] * 6 + [downs, ups] + [0] * 2 + [downs, ups] + [0] * 4 + [2, 2 * steps, 2] + [0] * 5
    sizes += [down_count, 0, up_count, 0]
    found = pl.pallas_call(
        unpack_refs(functools.partial(head_backward_kernel, stages), sizes),
        in_specs=[VMEM] * (6 + len(down) + len(up)),
        out_specs=[VMEM] * (2 + len(down) + len(up)),
        out_shape=[
            jax.ShapeDtypeStruct((rows, depth), jnp.float32),
            jax.ShapeDtypeStruct((3, each // heads, depth), jnp.float32),
        ]
        + down_shapes
        + up_shapes,
        scratch_shapes=[
            full(rows, depth),
            low(3, rows, depth),
            low(2, rows, depth),
            low(rows, depth),
        ]
        + [low(toks, each, half_width)] * 2
        + [low(1 << (steps - 1 - stage), each, half_width) for stage in range(steps)] * 2
        + [full(heads, each // heads, 3 * width)] * 2
        + [sems(2, 3), sems(2, steps), sems(2, steps), sems(heads - 1), sems(heads - 1)]
        + down_buffers
        + [down_sems]
        + up_buffers
        + [up_sems],
        compiler_params=pltpu.CompilerParams(
            collective_id=collective_id, has_side_effects=True, vmem_limit_bytes=58 * MIB
        ),
        name="head_backward",
    )(back_query, back_key, back_value, back_feed, hid, weights, *down, *up)
    return found[0], found[1], found[2 : 2 + downs], found[2 + downs :]


CHUNK = 512
ROOT = math.sqrt(2.0 / math.pi)
CUBIC = 0.044715


def feed_kernel(
    stages,
    attended,
    tokens,
    out_grad,
    gain,
    bias,
    up_bias,
    down_bias,
    w_output,
    w_up,
    w_down,
    layer_out,
    grad_middle,
    normed,
    grad_before,
    joined,
    grad_branch,
    grad_att,
    down_left,
    vectors,
    grad_up_bias,
    output_w,
    up_w,
    down_w,
    split,
    active,
    bend,
    shape,
    down_sum,
    back_sum,
    grad_split,
    grads,
    arrivals,
    weight_sems,
    down_sems,
    head_sems,
    halver_sems,
):
    tok, head = lax.axis_index("tok"), lax.axis_index("head")
    heads = lax.axis_size("head")
    rows, width = tokens.shape[0], attended.shape[1]
    hidden = up_w.shape[1]
    loads = [
        pltpu.make_async_copy(source, target, weight_sems.at[number])
        for number, (source, target) in enumerate(
            ((w_output, output_w), (w_up, up_w))
        )
    ]

    def down_load(chunk):
        slot = lax.rem(chunk, 2)
        return pltpu.make_async_copy(
            w_down.at[pl.ds(pl.multiple_of(chunk * CHUNK, CHUNK), CHUNK)],
            down_w.at[slot],
            down_sems.at[slot],
        )

    for load in loads:
        load.start()
    for chunk in range(2):
        down_load(chunk).start()
    peers = [lax.rem(head + step, heads) for step in range(1, heads)]
    ladder = mesh_bits()
    greet([(tok, other) for other in peers] + [p for _, p in ladder[bits_of(heads) :]])

    def block_of(owner):
        return pl.ds(pl.multiple_of(owner * rows, PIECE), rows)

    def swap(source_of, target, kind):
        found = []
        for step, other in enumerate(peers):
            copy = pltpu.make_async_remote_copy(
                src_ref=source_of(other),
                dst_ref=target,
                send_sem=head_sems.at[kind, 0, step],
                recv_sem=head_sems.at[kind, 1, step],
                device_id=(tok, other),
                device_id_type=MESH,
            )
            copy.start()
            found.append(copy)
        return found

    first = swap(lambda other: attended.at[block_of(other)], split.at[head], 0)
    split[head] = attended[block_of(head), :]
    loads[0].wait()
    for copy in first:
        copy.wait_recv()
    total = tokens[...].astype(jnp.float32)
    for owner in range(heads):
        at = slice(owner * width, (owner + 1) * width)
        joined[:, at] = split[owner]
        total += jnp.dot(split[owner], output_w[at, :], preferred_element_type=jnp.float32)
    grad_middle[...] = total
    centred = total - jnp.mean(total, axis=-1, keepdims=True)
    scale = lax.rsqrt(jnp.mean(centred * centred, axis=-1, keepdims=True) + epsilon)
    shape[...] = centred * scale
    normed[...] = (centred * scale * gain[...] + bias[...]).astype(jnp.bfloat16)

    loads[1].wait()
    block = grads[0].shape[1]
    halver = Halver(grads, stages, arrivals, halver_sems, ladder)

    def up_chunk(chunk, _):
        at = pl.ds(pl.multiple_of(chunk * CHUNK, CHUNK), CHUNK)
        before = jnp.dot(normed[...], up_w[:, at], preferred_element_type=jnp.float32)
        before += up_bias[:, at]
        square = before * before
        bent = jnp.tanh(ROOT * before * (1.0 + CUBIC * square))
        half = 0.5 * (1.0 + bent)
        low = (before * half).astype(jnp.bfloat16)
        active[:, at] = low
        bend[:, at] = half + (0.5 * ROOT) * before * (1.0 - bent * bent) * (
            1.0 + (3.0 * CUBIC) * square
        )
        found = lax.dot_general(
            low, out_grad[...], (((0,), (0,)), ((), ())), preferred_element_type=jnp.float32
        ).astype(jnp.bfloat16)
        for inner in range(CHUNK // block):
            some = found[inner * block : (inner + 1) * block]
            at = 0
            for grad, order, part in zip(grads, halver.orders, DOWN_PARTS):
                grad[slot_of(chunk * (CHUNK // block) + inner, order)] = some[:, at : at + part]
                at += part
        return 0

    lax.fori_loop(0, hidden // CHUNK, up_chunk, 0)
    halver.begin()
    down_sum[...] = jnp.zeros_like(down_sum)
    back_sum[...] = jnp.zeros_like(back_sum)

    def down_chunk(chunk, _):
        at = pl.ds(pl.multiple_of(chunk * CHUNK, CHUNK), CHUNK)
        down_load(chunk).wait()
        some = down_w.at[lax.rem(chunk, 2)]
        low = (across(out_grad[...], some[...]) * bend[:, at]).astype(jnp.bfloat16)
        grad_before[:, at] = low
        grad_up_bias[:, at] = jnp.sum(low.astype(jnp.float32), axis=0, keepdims=True)
        down_sum[...] += jnp.dot(
            active[:, at], some[...], preferred_element_type=jnp.float32
        )
        back_sum[...] += across(low, up_w[:, at])

        @pl.when(chunk + 2 < hidden // CHUNK)
        def _():
            down_load(chunk + 2).start()

        return 0

    groups = 4
    each = hidden // CHUNK // groups
    for group in range(groups):
        lax.fori_loop(group * each, (group + 1) * each, down_chunk, 0)
        if group == groups - 2:
            halver.step(stages[0])

    layer_out[...] = (grad_middle[...] + down_sum[...] + down_bias[...]).astype(jnp.bfloat16)
    back = back_sum[...]
    shaped = shape[...]
    vectors[0:1, :] = jnp.sum(back * shaped, axis=0, keepdims=True)
    vectors[1:2, :] = jnp.sum(back, axis=0, keepdims=True)
    top = out_grad[...].astype(jnp.float32)
    vectors[2:3, :] = jnp.sum(top, axis=0, keepdims=True)
    back = back * gain[...]
    back = back - jnp.mean(back, axis=-1, keepdims=True)
    back = back - shaped * jnp.mean(back * shaped, axis=-1, keepdims=True)
    total = grad_middle[...]
    centred = total - jnp.mean(total, axis=-1, keepdims=True)
    scale = lax.rsqrt(jnp.mean(centred * centred, axis=-1, keepdims=True) + epsilon)
    top = top + back * scale
    grad_middle[...] = top
    low = top.astype(jnp.bfloat16)
    grad_branch[...] = low
    for owner in range(heads):
        at = slice(owner * width, (owner + 1) * width)
        grad_split[owner] = across(low, output_w[at, :]).astype(jnp.bfloat16)
    second = swap(lambda other: grad_split.at[other], grad_att.at[block_of(head)], 1)
    grad_att[block_of(head), :] = grad_split[head]
    halver.step(stages[1], down_left)
    for copy in second:
        copy.wait_recv()
    halver.drain()
    for copy in first + second:
        copy.wait_send()


def feed(
    attended,
    tokens,
    out_grad,
    gain,
    bias,
    up_bias,
    down_bias,
    w_output,
    w_up,
    w_down,
    collective_id,
):
    rows, depth = tokens.shape
    span, width = attended.shape
    hidden = w_up.shape[1]
    heads = lax.axis_size("head")
    devices = heads * lax.axis_size("tok")
    block = hidden // devices
    stages = stage_groups(devices)[0]
    pieces = [(block, part) for part in DOWN_PARTS]
    buffers, buffer_count, halver_sems = halver_scratch(pieces, stages, devices)
    low = lambda *shape: jax.ShapeDtypeStruct(shape, jnp.bfloat16)
    full = lambda *shape: jax.ShapeDtypeStruct(shape, jnp.float32)
    any_ = pl.BlockSpec(memory_space=pl.ANY)
    sems = lambda *shape: pltpu.SemaphoreType.DMA(shape)
    lows = lambda *shape: pltpu.VMEM(shape, jnp.bfloat16)
    fulls = lambda *shape: pltpu.VMEM(shape, jnp.float32)
    scratch = [
        lows(depth, depth),
        lows(depth, hidden),
        lows(2, CHUNK, depth),
        lows(heads, rows, width),
        lows(rows, hidden),
        fulls(rows, hidden),
        fulls(rows, depth),
        fulls(rows, depth),
        fulls(rows, depth),
        lows(heads, rows, width),
    ]
    scratch += [lows(devices, block, part) for part in DOWN_PARTS] + buffers
    scratch += [sems(2), sems(2), sems(2, 2, heads - 1), halver_sems]
    count = len(pieces)
    sizes = [0] * 17 + [count] + [0] * 12 + [count, buffer_count] + [0] * 4
    outs = [
        low(rows, depth),
        full(rows, depth),
        low(rows, depth),
        low(rows, hidden),
        low(rows, depth),
        low(rows, depth),
        low(span, width),
    ]
    outs += left_over(pieces, stages, devices) + [full(SUB, depth), full(1, hidden)]
    return pl.pallas_call(
        unpack_refs(functools.partial(feed_kernel, stages), sizes),
        in_specs=[VMEM] * 7 + [any_] * 3,
        out_specs=[VMEM] * len(outs),
        out_shape=outs,
        scratch_shapes=scratch,
        compiler_params=pltpu.CompilerParams(
            collective_id=collective_id, has_side_effects=True, vmem_limit_bytes=60 * MIB
        ),
        name="feed",
    )(
        attended, tokens, out_grad, gain, bias, up_bias, down_bias, w_output, w_up, w_down
    )


def every_step(length, chunk, step, body, carry):
    here = lax.broadcasted_iota(jnp.int32, (SUB, HD), 0) == chunk

    def some(block, now):
        for inner in range(UNROLL):
            t = block * UNROLL + inner
            now = body(t, now, jnp.where(here & (t == step), 0.0, 1.0))
        return now

    return lax.fori_loop(0, length // UNROLL, some, carry)


def recurrence_back_kernel(
    stages,
    brk,
    keep,
    whole,
    slope,
    feed_rows,
    decay,
    mix,
    skip,
    chunk_decay,
    chunk_slope,
    span_decay,
    span_slope,
    lefts,
    rights,
    down_in,
    back,
    sums,
    lag_sums,
    skip_sum,
    down_out,
    up_out,
    slopes,
    rows,
    total,
    ends,
    lags,
    mine,
    every,
    share_sends,
    share_recvs,
    down_arrivals,
    down_sems,
    grads,
    up_arrivals,
    up_sems,
):
    here, count = lax.axis_index("tok"), every.shape[0]
    peers = tok_peers()
    ladder = mesh_bits()
    heads = bits_of(lax.axis_size("head"))
    greet([target for target, _ in peers] + [partner for _, partner in ladder[:heads]])

    down = Halver(down_in, stages[1], down_arrivals, down_sems, ladder)
    down.begin()
    length = slope.shape[0] // SUB
    groups = slope.shape[1] // HD
    zero = jnp.zeros((SUB, HD), jnp.float32)
    back_step = jnp.where(brk[1] < 0, -1, length - 1 - brk[1])
    for group in range(groups):
        lanes = slice(group * HD, (group + 1) * HD)
        slopes[group] = slope[:, lanes]
        rows[group] = feed_rows[:, lanes].astype(jnp.float32)
        total[group] = slope[:, lanes] * skip[:, lanes]
        skip_sum[:, lanes] = jnp.sum(slopes[group] * rows[group], axis=0, keepdims=True)
        factors = [spread(decay[:, lanes], n) for n in range(NS)]

        def end_step(t, carry, live):
            drive = slopes[group, pl.ds(length - 1 - t, SUB, stride=length), :]
            adjoint, lag = carry[:NS], carry[NS:]
            lag = [(a * f + b) * live for a, f, b in zip(lag, factors, adjoint)]
            adjoint = [(a * f + drive) * live for a, f in zip(adjoint, factors)]
            return tuple(adjoint) + tuple(lag)

        done = every_step(length, brk[0], back_step, end_step, (zero,) * (2 * NS))
        for n in range(NS):
            ends[n, :, lanes] = done[n]
            lags[n, :, lanes] = done[NS + n]

    factor, bend = chunk_decay[...], chunk_slope[...]
    now, late = ends[:, SUB - 1, :], lags[:, SUB - 1, :]
    for chunk in reversed(range(SUB - 1)):
        late = keep[chunk] * (factor * late + bend * now) + lags[:, chunk, :]
        now = keep[chunk] * (factor * now) + ends[:, chunk, :]
    mine[0] = now
    mine[1] = late
    every[here, 0] = now
    every[here, 1] = late
    copies = share(mine, every, share_sends, share_recvs, here, peers)
    up = Halver(grads, stages[0], up_arrivals, up_sems, ladder)
    for number, parts in enumerate(UP_PARTS if grads else ()):
        column = 0
        for pair, start, stop in parts:
            fill(
                lefts[pair], rights[pair], start, stop, grads[number], column, up.orders[number]
            )
            column += stop - start
        up.send(number, stages[0][0])

    for copy in copies:
        copy.wait()
    for stage in stages[1][:-1]:
        down.step(stage)
    up.step(stages[0][0])
    over, over_slope = span_decay[...], span_slope[...]
    now, late = jnp.zeros_like(over), jnp.zeros_like(over)
    for place in reversed(range(1, count)):
        reached = place > here
        late = jnp.where(
            reached, whole[place] * (over * late + over_slope * now) + every[place, 1], late
        )
        now = jnp.where(reached, whole[place] * (over * now) + every[place, 0], now)
    for chunk in reversed(range(SUB)):
        own, own_late = ends[:, chunk, :], lags[:, chunk, :]
        ends[:, chunk, :] = now
        lags[:, chunk, :] = late
        late = keep[chunk] * (factor * late + bend * now) + own_late
        now = keep[chunk] * (factor * now) + own

    for group in range(groups):
        lanes = slice(group * HD, (group + 1) * HD)
        for base in range(0, NS, HALF):
            factors = [spread(decay[:, lanes], base + n) for n in range(HALF)]
            mixes = [spread(mix[:, lanes], base + n) for n in range(HALF)]

            def out_step(t, carry, live):
                at = pl.ds(length - 1 - t, SUB, stride=length)
                drive, source = slopes[group, at, :], rows[group, at, :]
                adjoint, lag = carry[:HALF], carry[HALF : 2 * HALF]
                direct, late_sum = carry[2 * HALF : 3 * HALF], carry[3 * HALF :]
                lag = [a * f + b for a, f, b in zip(lag, factors, adjoint)]
                adjoint = [a * f + drive for a, f in zip(adjoint, factors)]
                direct = [a + b * source for a, b in zip(direct, adjoint)]
                late_sum = [a + b * source for a, b in zip(late_sum, lag)]
                parts = [a * b for a, b in zip(adjoint, mixes)]
                while len(parts) > 1:
                    parts = [a + b for a, b in zip(parts[::2], parts[1::2])]
                total[group, at, :] = total[group, at, :] + parts[0]
                lag = [a * live for a in lag]
                adjoint = [a * live for a in adjoint]
                return tuple(adjoint) + tuple(lag) + tuple(direct) + tuple(late_sum)

            first = tuple(ends[base + n, :, lanes] for n in range(HALF)) + tuple(
                lags[base + n, :, lanes] for n in range(HALF)
            )
            done = every_step(length, brk[0], back_step, out_step, first + (zero,) * (2 * HALF))
            for n in range(HALF):
                sums[base + n : base + n + 1, lanes] = jnp.sum(
                    done[2 * HALF + n], axis=0, keepdims=True
                )
                lag_sums[base + n : base + n + 1, lanes] = jnp.sum(
                    done[3 * HALF + n], axis=0, keepdims=True
                )
        back[:, lanes] = total[group].astype(back.dtype)
    down.step(stages[1][-1], down_out)
    up.step(stages[0][1], up_out)
    down.drain()
    up.drain()


def recurrence_back(
    brk,
    keep,
    whole,
    slope,
    feed_rows,
    decay,
    mix,
    skip,
    chunk_decay,
    chunk_slope,
    span_decay,
    span_slope,
    lefts,
    rights,
    down,
    collective_id,
):
    span, width = feed_rows.shape
    toks = whole.shape[0]
    devices = toks * lax.axis_size("head")
    stages = stage_groups(devices)
    block = lefts[0].shape[1] // devices
    apart, up_pieces = None, [(block, part) for part in UP_WIDTHS]
    if block < 16:
        apart = products_apart(lefts, rights)
        lefts, rights, up_pieces = [], [], []
    down_pieces = [piece.shape[1:] for piece in down]
    down_buffers, down_count, down_sems = halver_scratch(down_pieces, stages[1], devices)
    up_buffers, up_count, up_sems = halver_scratch(up_pieces, stages[0], devices)
    down_shapes = left_over(down_pieces, stages[1], devices)
    up_shapes = left_over(up_pieces, stages[0], devices)
    full = lambda *shape: jax.ShapeDtypeStruct(shape, jnp.float32)
    fulls = lambda *shape: pltpu.VMEM(shape, jnp.float32)
    sems = lambda *shape: pltpu.SemaphoreType.DMA(shape)
    groups = width // HD
    scratch = [
        fulls(groups, span, HD),
        fulls(groups, span, HD),
        fulls(groups, span, HD),
        fulls(NS, SUB, width),
        fulls(NS, SUB, width),
        fulls(2, NS, width),
        fulls(toks, 2, NS, width),
        sems(toks - 1),
        sems(toks - 1),
    ]
    scratch += down_buffers + [down_sems]
    scratch += [pltpu.VMEM((devices,) + piece, jnp.bfloat16) for piece in up_pieces]
    scratch += up_buffers + [up_sems]
    pairs, ups, downs = len(lefts) or -1, len(up_pieces) or -1, len(down)
    sizes = [0] * 12 + [pairs, pairs, downs] + [0] * 4 + [downs, ups] + [0] * 9
    sizes += [down_count, 0, ups, up_count, 0]
    found = pl.pallas_call(
        unpack_refs(functools.partial(recurrence_back_kernel, stages), sizes),
        in_specs=[SCALARS] * 3 + [VMEM] * (9 + 2 * len(lefts) + downs),
        out_specs=[VMEM] * (4 + len(down_shapes) + len(up_shapes)),
        out_shape=[
            jax.ShapeDtypeStruct((span, width), jnp.bfloat16),
            full(NS, width),
            full(NS, width),
            full(1, width),
        ]
        + down_shapes
        + up_shapes,
        scratch_shapes=scratch,
        compiler_params=pltpu.CompilerParams(
            collective_id=collective_id, has_side_effects=True, vmem_limit_bytes=60 * MIB
        ),
        name="recurrence_back",
    )(
        brk,
        keep,
        whole,
        slope,
        feed_rows,
        decay,
        mix,
        skip,
        chunk_decay,
        chunk_slope,
        span_decay,
        span_slope,
        *lefts,
        *rights,
        *down,
    )
    return tuple(found[:4]) + (found[4 : 4 + downs], found[4 + downs :], apart)


def layer_norm(row_block, gain, bias):
    centre = jnp.mean(row_block, axis=-1, keepdims=True)
    centred = row_block - centre
    spread = jnp.mean(centred * centred, axis=-1, keepdims=True)
    return centred * lax.rsqrt(spread + epsilon) * gain + bias


def product(left, right):
    return jnp.dot(left, right, preferred_element_type=jnp.float32)


def product_left(left, right):
    return lax.dot_general(
        left, right, (((0,), (0,)), ((), ())), preferred_element_type=jnp.float32
    )


def product_right(left, right):
    return lax.dot_general(
        left, right, (((1,), (1,)), ((), ())), preferred_element_type=jnp.float32
    )


def seq_place(positions, seq_starts, block_sizes):
    later = positions >= seq_starts[1]
    opening = jnp.where(later, seq_starts[1], seq_starts[0])
    length = jnp.where(later, block_sizes[1], block_sizes[0])
    return opening, opening + (positions - opening) // length * length


def shifted(shard, axis, by):
    devices = lax.axis_size(axis)
    pairs = [(i, i + by) for i in range(devices) if 0 <= i + by < devices]
    return lax.ppermute(shard, axis, pairs)


def per_device(
    tokens_in,
    seq_starts,
    block_sizes,
    norm1_gain,
    norm1_bias,
    w_query,
    w_key,
    w_value,
    w_output,
    ssm_rate,
    ssm_input,
    ssm_output,
    ssm_skip,
    norm2_gain,
    norm2_bias,
    w_up,
    up_bias,
    w_down,
    down_bias,
    out_grad,
):
    tok_rows = tokens_in.shape[0]
    pieces, here = lax.axis_size("tok"), lax.axis_index("tok")
    span = tok_rows * lax.axis_size("head")
    total_len = span * pieces
    anchor = here * span
    window = 2 * BLOCK
    length = span // SUB

    residual = tokens_in.astype(jnp.float32)
    _, norm1_pull = jax.vjp(layer_norm, residual, norm1_gain, norm1_bias)
    width = ssm_rate.shape[0]
    mine = lax.axis_index("head") * width
    w_own = jnp.concatenate(
        [lax.dynamic_slice_in_dim(w, mine, width, 1) for w in (w_query, w_key, w_value)], axis=1
    )
    hid, query_h, key_h, value_h = head_forward(
        tokens_in, norm1_gain[None, :], norm1_bias[None, :], w_own, 6
    )
    hidden_h = lax.dynamic_slice_in_dim(hid, mine, width, 1)

    second = seq_starts[1] - anchor
    inside = (second >= 0) & (second < span)
    brk = jnp.where(inside, jnp.stack([second // length, second % length]), -1).astype(jnp.int32)
    keep = 1.0 - (jnp.arange(SUB) == brk[0]).astype(jnp.float32)
    whole = 1.0 - (jnp.arange(pieces) == seq_starts[1] // span).astype(jnp.float32)
    positions = anchor + jnp.arange(span, dtype=jnp.int32)
    opening, first = seq_place(positions, seq_starts, block_sizes)
    first = first - anchor
    where_ = jnp.concatenate([jnp.stack([anchor, second]), block_sizes, first[::TILE]]).astype(
        jnp.int32
    )
    first = first.reshape(-1, 1, TILE)
    opening = (opening - anchor).reshape(-1, 1, TILE)

    rate = ssm_rate.T / total_len
    drive_in, read_out = ssm_input.T, ssm_output.T
    skip = ssm_skip[None, :]
    decay = jnp.exp(-rate)
    gain = jnp.sqrt(-jnp.expm1(-2.0 * rate))
    driving = gain * drive_in
    mix = read_out * driving
    chunk_decay = jnp.exp(-rate * length)
    chunk_slope = length * jnp.exp(-rate * (length - 1))
    span_decay = jnp.exp(-rate * span)
    span_slope = span * jnp.exp(-rate * (span - 1))

    ends = ssm_ends(brk, hidden_h, decay)
    starts = state_exchange(keep, whole, ends, chunk_decay, span_decay, 1)
    context = ssm_out(brk, hidden_h, decay, mix, skip, starts)

    rims = shifted(jnp.stack([key_h[span - window :], value_h[span - window :]]), "tok", 1)
    context_rim = shifted(context[span - window - CTX :], "tok", 1)
    key_ext = jnp.concatenate([rims[0], key_h], axis=0)
    value_ext = jnp.concatenate([rims[1], value_h], axis=0)
    context_ext = jnp.concatenate([context_rim, context], axis=0)
    attended, attended_fine, level = attend(where_, query_h, key_ext, value_ext, context_ext, first, opening)
    (
        layer_out,
        grad_middle,
        normed_low,
        grad_before_low,
        joined,
        grad_branch,
        grad_att,
        *down,
        vectors,
        grad_up_bias,
    ) = feed(
        attended,
        tokens_in,
        out_grad,
        norm2_gain[None, :],
        norm2_bias[None, :],
        up_bias[None, :],
        down_bias[None, :],
        w_output,
        w_up,
        w_down,
        7,
    )

    back_query_h, key_rim, value_rim, near_rim, back_key_h, back_value_h, back_context = attend_back(
        where_, query_h, key_ext, value_ext, context_ext, first, opening, attended_fine, grad_att, level
    )
    near_rim = shifted(near_rim, "tok", -1).astype(jnp.float32)
    rims = shifted(jnp.stack([key_rim, value_rim]), "tok", -1).astype(jnp.float32)
    back_context = back_context.at[span - window - CTX :].add(near_rim)
    back_key_h = back_key_h.at[span - window :].add(rims[0]).astype(jnp.bfloat16)
    back_value_h = back_value_h.at[span - window :].add(rims[1]).astype(jnp.bfloat16)

    back_feed_h, sums, lag_sums, skip_sum, down, up, apart = recurrence_back(
        brk,
        keep,
        whole,
        back_context,
        hidden_h,
        decay,
        mix,
        skip,
        chunk_decay,
        chunk_slope,
        span_decay,
        span_slope,
        [normed_low, joined],
        [grad_before_low, grad_branch],
        down,
        2,
    )
    grad_hidden, out_w_heads, down, up = head_backward(
        back_query_h, back_key_h, back_value_h, back_feed_h, hid, w_own, down, up, 4
    )
    out_w_down = jnp.concatenate([piece[0] for piece in down], axis=1)
    grad_res_norm, grad_norm1_gain, grad_norm1_bias = norm1_pull(grad_hidden)
    input_grad = grad_middle + grad_res_norm

    heads, head = lax.axis_size("head"), lax.axis_index("head")
    short = jnp.stack(
        [grad_norm1_gain, grad_norm1_bias, vectors[0], vectors[1], vectors[2]]
    ).reshape(5, pieces, -1)
    packed = jnp.concatenate(
        [short.swapaxes(0, 1).reshape(pieces, -1), grad_up_bias.reshape(pieces, -1)], axis=1
    )
    used = 5 * short.shape[2]
    packed = jnp.pad(packed, ((0, 0), (0, -packed.shape[1] % HD)))[:, None, :]
    rows = jnp.concatenate([sums, lag_sums, skip_sum], axis=0)
    rows = jnp.pad(rows, ((0, -rows.shape[0] % SUB), (0, 0)))
    summed, packed, up = final_sums(rows, packed, up, 5)
    short = packed[0, :used].reshape(5, heads, -1)[:, head]
    out_up_bias = packed[0, used : used + grad_up_bias.shape[1] // pieces].reshape(heads, -1)[head]
    if apart is None:
        out_w_up = jnp.concatenate(
            [up[0][0], up[1][0], up[2][0, :, : UP_PARTS[2][0][2] - UP_PARTS[2][0][1]]], axis=1
        )
        out_w_output = up[2][0, :, UP_PARTS[2][0][2] - UP_PARTS[2][0][1] :]
    else:
        out_w_up, out_w_output = apart
    sums, lag_sums, skip_sum = summed[:NS], summed[NS : 2 * NS], summed[2 * NS]
    grad_ssm_output = (driving * sums).T
    grad_driving = read_out * sums
    grad_ssm_input = (gain * grad_driving).T
    grad_ssm_rate = (
        grad_driving * drive_in * jnp.exp(-2.0 * rate) / gain - mix * lag_sums * decay
    ).T / total_len

    return (
        layer_out,
        input_grad,
        short[0],
        short[1],
        out_w_heads[0],
        out_w_heads[1],
        out_w_heads[2],
        out_w_output,
        grad_ssm_rate,
        grad_ssm_input,
        grad_ssm_output,
        skip_sum,
        short[2],
        short[3],
        out_w_up,
        out_up_bias,
        out_w_down,
        short[4],
    )


def solution(mesh):
    return jax.shard_map(
        per_device,
        mesh=mesh,
        in_specs=(
            P(("tok", "head"), None),
            P(),
            P(),
            P(),
            P(),
            P(),
            P(),
            P(),
            P(),
            P("head", None),
            P("head", None),
            P("head", None),
            P("head"),
            P(),
            P(),
            P(),
            P(),
            P(),
            P(),
            P(("tok", "head"), None),
        ),
        out_specs=(
            P(("tok", "head"), None),
            P(("tok", "head"), None),
            P(("tok", "head")),
            P(("tok", "head")),
            P(("tok", "head"), None),
            P(("tok", "head"), None),
            P(("tok", "head"), None),
            P(("tok", "head"), None),
            P("head", None),
            P("head", None),
            P("head", None),
            P("head"),
            P(("tok", "head")),
            P(("tok", "head")),
            P(("tok", "head"), None),
            P(("tok", "head")),
            P(("tok", "head"), None),
            P(("tok", "head")),
        ),
        check_vma=False,
    )
```

```python
import functools
import math

import jax
import jax.numpy as jnp
from jax import lax
from jax.experimental import pallas as pl
from jax.experimental.pallas import tpu as pltpu
from jax.sharding import PartitionSpec as P

epsilon = 1e-05
HD = 128
CTX = 128
BLOCK = 256
NS = 16
SUB = 8
UNROLL = 8
HALF = 8
TILE = 256
MIB = 1 << 20
LOWEST = -1e30
FACTOR = HD ** (-0.5)
FACTOR2 = FACTOR * math.log2(math.e)


def spread(table, n):
    return jnp.broadcast_to(table[n : n + 1, :], (SUB, table.shape[1]))


SCALARS = pl.BlockSpec(memory_space=pltpu.SMEM)


def wide(limit=48):
    return pltpu.CompilerParams(vmem_limit_bytes=limit * MIB)


def across(left, right):
    return lax.dot_general(
        left, right, (((1,), (1,)), ((), ())), preferred_element_type=jnp.float32
    )


def times(left, right):
    return lax.dot_general(
        left, right, (((1,), (0,)), ((), ())), preferred_element_type=jnp.float32
    )


def turn(source, target):
    for at in range(0, source.shape[0], TILE):
        size = min(TILE, source.shape[0] - at)
        piece = source[at : at + size, :].astype(jnp.float32)
        target[:, at : at + size] = piece.T.astype(target.dtype)


def next_block(where_, now):
    second = where_[1]
    length = jnp.where(now >= second, where_[3], where_[2])
    after = now + length
    return jnp.where((now < second) & (after > second), second, after)


REACH = 2 * BLOCK + TILE
BLOCKS = 4


def block_facts(starts, sizes, span):
    anchor = lax.axis_index("tok") * span
    return anchor, starts[1] - anchor, sizes[0], sizes[1]


def block_begin(where_, at):
    opening = jnp.where(at >= where_[1], where_[1], -where_[0])
    length = jnp.where(at >= where_[1], where_[3], where_[2])
    return opening + lax.div(at - opening, length) * length


def block_rows(where_, tile):
    cols = lax.broadcasted_iota(jnp.int32, (1, TILE), 1) + tile * TILE
    begin = block_begin(where_, tile * TILE)
    now, firsts = begin, jnp.zeros_like(cols) + begin
    for _ in range(BLOCKS):
        now = next_block(where_, now)
        firsts = jnp.where(cols >= now, now, firsts)
    return firsts, jnp.where(cols >= where_[1], where_[1], -where_[0]), begin


def joined_rows(rim, own, target):
    target[: rim.shape[0], :] = rim[...]
    target[rim.shape[0] :, :] = own[...]


def local_mask(tile, first):
    rows = lax.broadcasted_iota(jnp.int32, (REACH, TILE), 0) + (tile * TILE - 2 * BLOCK)
    cols = lax.broadcasted_iota(jnp.int32, (1, TILE), 1) + tile * TILE
    return (rows >= first) & (rows <= cols)


def context_at(now):
    return pl.multiple_of((now + 2 * BLOCK) // CTX * CTX, CTX)


def context_mask(start, now, first, opening):
    rows = lax.broadcasted_iota(jnp.int32, (TILE, TILE), 0) + (start - 2 * BLOCK - CTX)
    low = jnp.where(first == now, jnp.maximum(now - CTX, opening), 1 << 28)
    return (rows >= low) & (rows < now)


def lanes_of(head):
    return slice(head * HD, (head + 1) * HD)


def attend_kernel(
    starts,
    sizes,
    query,
    key_own,
    value_own,
    context_own,
    key_rim,
    value_rim,
    context_rim,
    out,
    fine,
    level,
    key,
    value,
    context,
    value_t,
    context_t,
):
    where_ = block_facts(starts, sizes, query.shape[0])
    joined_rows(key_rim, key_own, key)
    joined_rows(value_rim, value_own, value)
    joined_rows(context_rim, context_own, context)
    heads = query.shape[1] // HD
    turn(value, value_t)
    turn(context, context_t)

    def one_tile(tile, _):
        here = pl.ds(pl.multiple_of(tile * TILE, TILE), TILE)
        rows = [query[here, lanes_of(head)] for head in range(heads)]
        firsts, openings, begin = block_rows(where_, tile)

        def score(near, at, head, mask):
            return jnp.where(mask, across(near[at, lanes_of(head)], rows[head]) * FACTOR2, LOWEST)

        def peak(found):
            return jnp.max(found, axis=0, keepdims=True)

        def gather(prob, values_t, at, head):
            low = prob.astype(jnp.bfloat16)
            return (
                jnp.sum(prob, axis=0, keepdims=True),
                jnp.sum(low.astype(jnp.float32), axis=0, keepdims=True),
                times(values_t[lanes_of(head), at], low),
            )

        near_at = pl.ds(pl.multiple_of(tile * TILE, TILE), REACH)
        far_at = pl.ds(context_at(begin), TILE)
        near_mask = local_mask(tile, firsts)
        far_mask = context_mask(context_at(begin), begin, firsts, openings)
        carry = []
        for head in range(heads):
            near = score(key, near_at, head, near_mask)
            far = score(context, far_at, head, far_mask)
            top = jnp.maximum(peak(near), peak(far))
            one = gather(jnp.exp2(near - top), value_t, near_at, head)
            two = gather(jnp.exp2(far - top), context_t, far_at, head)
            carry.append((top,) + tuple(a + b for a, b in zip(one, two)))

        def earlier(state):
            now, carry = state
            start = context_at(now)
            at = pl.ds(start, TILE)
            mask = context_mask(start, now, firsts, openings)
            found = []
            for head in range(heads):
                top, mass, low_mass, total = carry[head]
                far = score(context, at, head, mask)
                new_top = jnp.maximum(top, peak(far))
                shrink = jnp.exp2(top - new_top)
                more = gather(jnp.exp2(far - new_top), context_t, at, head)
                found.append(
                    (new_top,)
                    + tuple(a * shrink + b for a, b in zip((mass, low_mass, total), more))
                )
            return next_block(where_, now), tuple(found)

        _, carry = lax.while_loop(
            lambda state: state[0] < (tile + 1) * TILE,
            earlier,
            (next_block(where_, begin), tuple(carry)),
        )
        for head in range(heads):
            top, mass, low_mass, total = carry[head]
            done = (total / low_mass).T
            fine[here, lanes_of(head)] = done
            out[here, lanes_of(head)] = done.astype(out.dtype)
            level[head, tile] = top + jnp.log2(mass)
        return 0

    lax.fori_loop(0, query.shape[0] // TILE, one_tile, 0)


def attend_back_kernel(
    starts,
    sizes,
    query,
    key_own,
    value_own,
    context_own,
    key_rim,
    value_rim,
    context_rim,
    attended,
    grad,
    level,
    back_query,
    back_key_rim,
    back_value_rim,
    back_context_rim,
    back_key,
    back_value,
    back_context,
    key,
    value,
    context,
    key_t,
    context_t,
    key_sum,
    value_sum,
    context_sum,
):
    where_ = block_facts(starts, sizes, query.shape[0])
    joined_rows(key_rim, key_own, key)
    joined_rows(value_rim, value_own, value)
    joined_rows(context_rim, context_own, context)
    heads = query.shape[1] // HD
    turn(key, key_t)
    turn(context, context_t)
    key_sum[...] = jnp.zeros_like(key_sum)
    value_sum[...] = jnp.zeros_like(value_sum)
    context_sum[...] = jnp.zeros_like(context_sum)

    def one_tile(tile, _):
        here = pl.ds(pl.multiple_of(tile * TILE, TILE), TILE)
        rows = [query[here, lanes_of(head)] for head in range(heads)]
        grads = [grad[here, lanes_of(head)] for head in range(heads)]
        firsts, openings, begin = block_rows(where_, tile)
        levels = [level[head, tile] for head in range(heads)]
        centres = []
        for head in range(heads):
            joint = grads[head].astype(jnp.float32) * attended[here, lanes_of(head)]
            centres.append(jnp.sum(joint.T, axis=0, keepdims=True))

        def slopes(keys, values, at, head, mask):
            found = across(keys[at, lanes_of(head)], rows[head]) * FACTOR2 - levels[head]
            prob = jnp.exp2(jnp.where(mask, found, LOWEST))
            drive = across(values[at, lanes_of(head)], grads[head])
            slope = prob * (drive - centres[head])
            return prob.astype(jnp.bfloat16), slope.astype(jnp.bfloat16)

        def earlier(state):
            now, totals = state
            start = context_at(now)
            at = pl.ds(start, TILE)
            mask = context_mask(start, now, firsts, openings)
            found = []
            for h in range(heads):
                prob, slope = slopes(context, context, at, h, mask)
                context_sum[at, lanes_of(h)] += FACTOR * times(slope, rows[h]) + times(
                    prob, grads[h]
                )
                found.append(totals[h] + times(context_t[lanes_of(h), at], slope))
            return next_block(where_, now), tuple(found)

        at = pl.ds(pl.multiple_of(tile * TILE, TILE), REACH)
        mask = local_mask(tile, firsts)
        totals = []
        for h in range(heads):
            prob, slope = slopes(key, value, at, h, mask)
            key_sum[at, lanes_of(h)] += times(slope, rows[h])
            value_sum[at, lanes_of(h)] += times(prob, grads[h])
            totals.append(times(key_t[lanes_of(h), at], slope))
        state = earlier((begin, tuple(totals)))
        _, totals = lax.while_loop(lambda state: state[0] < (tile + 1) * TILE, earlier, state)
        for head in range(heads):
            back_query[here, lanes_of(head)] = (FACTOR * totals[head]).T.astype(back_query.dtype)
        return 0

    lax.fori_loop(0, query.shape[0] // TILE, one_tile, 0)
    window = 2 * BLOCK
    back_key_rim[...] = (FACTOR * key_sum[:window, :]).astype(back_key_rim.dtype)
    back_value_rim[...] = value_sum[:window, :].astype(back_value_rim.dtype)
    back_context_rim[...] = context_sum[: window + CTX, :].astype(back_context_rim.dtype)
    back_key[...] = FACTOR * key_sum[window:, :]
    back_value[...] = value_sum[window:, :]
    back_context[...] = context_sum[window + CTX :, :]


VMEM = pl.BlockSpec(memory_space=pltpu.VMEM)


def attend(starts, sizes, query, key, value, context, rims):
    rows, width = query.shape
    heads, tiles = width // HD, rows // TILE
    near, far = rows + rims[0].shape[0], rows + rims[2].shape[0]
    low = lambda *shape: pltpu.VMEM(shape, jnp.bfloat16)
    return pl.pallas_call(
        attend_kernel,
        in_specs=[SCALARS] * 2 + [VMEM] * 7,
        out_specs=[VMEM] * 3,
        out_shape=(
            jax.ShapeDtypeStruct((rows, width), jnp.bfloat16),
            jax.ShapeDtypeStruct((rows, width), jnp.float32),
            jax.ShapeDtypeStruct((heads, tiles, 1, TILE), jnp.float32),
        ),
        scratch_shapes=[
            low(near, width),
            low(near, width),
            low(far, width),
            low(width, near),
            low(width, far),
        ],
        compiler_params=wide(),
        name="attend",
    )(starts, sizes, query, key, value, context, *rims)


def attend_back(starts, sizes, query, key, value, context, rims, attended, grad, level):
    rows, width = query.shape
    near, far = rows + rims[0].shape[0], rows + rims[2].shape[0]
    low = lambda count: jax.ShapeDtypeStruct((count, width), jnp.bfloat16)
    full = lambda count: jax.ShapeDtypeStruct((count, width), jnp.float32)
    lows = lambda *shape: pltpu.VMEM(shape, jnp.bfloat16)
    fulls = lambda *shape: pltpu.VMEM(shape, jnp.float32)
    return pl.pallas_call(
        attend_back_kernel,
        in_specs=[SCALARS] * 2 + [VMEM] * 10,
        out_specs=[VMEM] * 7,
        out_shape=(
            low(rows),
            low(near - rows),
            low(near - rows),
            low(far - rows),
            full(rows),
            full(rows),
            full(rows),
        ),
        scratch_shapes=[
            lows(near, width),
            lows(near, width),
            lows(far, width),
            lows(width, near),
            lows(width, far),
            fulls(near, width),
            fulls(near, width),
            fulls(far, width),
        ],
        compiler_params=wide(),
        name="attend_back",
    )(starts, sizes, query, key, value, context, *rims, attended, grad, level)


MESH = pl.DeviceIdType.MESH
ROWS = 512


def bits_of(count):
    return count.bit_length() - 1


def mesh_bits():
    found = []
    tok, head = lax.axis_index("tok"), lax.axis_index("head")
    for axis in ("head", "tok"):
        for level in range(bits_of(lax.axis_size(axis))):
            at = head if axis == "head" else tok
            bit = (at // (1 << level)) % 2
            other = at + (1 - 2 * bit) * (1 << level)
            found.append((bit, (tok, other) if axis == "head" else (other, head)))
    return found


def greet(partners):
    barrier = pltpu.get_barrier_semaphore()
    for partner in partners:
        pl.semaphore_signal(barrier, inc=1, device_id=partner, device_id_type=MESH)
    pl.semaphore_wait(barrier, len(partners))


def halving_orders(bits):
    rest = list(range(4, bits))
    return [[0, 1, 3, 2] + rest, [0, 2, 1, 3] + rest, [0, 3, 2, 1] + rest]


def slot_of(block, order):
    place = 0
    for bit in order:
        place = place * 2 + (block // (1 << bit)) % 2
    return place


def unpack_refs(function, sizes):
    def kernel(*refs):
        grouped, at = [], 0
        for size in sizes:
            grouped.append(refs[at] if size == 0 else refs[at : at + max(size, 0)])
            at += 1 if size == 0 else max(size, 0)
        function(*grouped)

    return kernel


class Halver:
    def __init__(self, pieces, stages, arrivals, sems, ladder):
        self.now, self.stages, self.arrivals, self.ladder = list(pieces), stages, arrivals, ladder
        self.sems, self.steps = sems, len(ladder)
        self.orders = halving_orders(self.steps)
        self.sent, self.flying = [], {}

    def half(self, stage):
        return 1 << (self.steps - 1 - stage)

    def send(self, number, stage):
        bit, partner = self.ladder[self.orders[number][stage]]
        at = number * len(self.stages) + self.stages.index(stage)
        half = self.half(stage)
        copy = pltpu.make_async_remote_copy(
            src_ref=self.now[number].at[pl.ds((1 - bit) * half, half)],
            dst_ref=self.arrivals[at],
            send_sem=self.sems.at[0, at],
            recv_sem=self.sems.at[1, at],
            device_id=partner,
            device_id_type=MESH,
        )
        copy.start()
        self.sent.append(copy)
        self.flying[number] = (copy, self.arrivals[at], bit * half)

    def absorb(self, number, stage, into=None):
        copy, arrival, keep = self.flying[number]
        copy.wait_recv()
        before = self.now[number]
        target = arrival if into is None else into

        def add(i, _):
            target[i] = before[keep + i] + arrival[i]
            return 0

        lax.fori_loop(0, self.half(stage), add, 0)
        self.now[number] = target

    def last(self, number, stage):
        copy, arrival, keep = self.flying[number]
        copy.wait_recv()
        return self.now[number][keep].astype(jnp.float32) + arrival[0].astype(jnp.float32)

    def step(self, stage, into=None):
        for number in range(len(self.now)):
            self.absorb(number, stage, None if into is None else into[number])
            if into is None:
                self.send(number, stage + 1)

    def begin(self):
        for number in range(len(self.now)):
            self.send(number, self.stages[0])

    def drain(self):
        for copy in self.sent:
            copy.wait_send()


def halver_scratch(pieces, stages, devices):
    steps = bits_of(devices)
    buffers = [
        pltpu.VMEM((1 << (steps - 1 - stage), block, width), jnp.bfloat16)
        for block, width in pieces
        for stage in stages
    ]
    sems = pltpu.SemaphoreType.DMA((2, max(len(buffers), 1)))
    return buffers, len(buffers) or -1, sems


def left_over(pieces, stages, devices):
    slots = 1 << (bits_of(devices) - 1 - stages[-1])
    return [jax.ShapeDtypeStruct((slots, block, width), jnp.bfloat16) for block, width in pieces]


def fill(left, right, start, stop, target, column, order):
    block = target.shape[1]
    each = ROWS // block
    for low in range(start, stop, ROWS):
        high = min(low + ROWS, stop)
        to = column + low - start

        def some_rows(chunk, _):
            at = pl.ds(pl.multiple_of(chunk * ROWS, ROWS), ROWS)
            found = lax.dot_general(
                left[:, at],
                right[:, low:high],
                (((0,), (0,)), ((), ())),
                preferred_element_type=jnp.float32,
            ).astype(jnp.bfloat16)
            for inner in range(each):
                target[slot_of(chunk * each + inner, order), :, to : to + high - low] = found[
                    inner * block : (inner + 1) * block
                ]
            return 0

        lax.fori_loop(0, left.shape[1] // ROWS, some_rows, 0)


def stage_groups(devices):
    steps = bits_of(devices)
    return [0, 1], list(range(2, steps - 1)), [steps - 1]


DOWN_PARTS = (256, 384, 384)
UP_PARTS = (
    ((0, 0, 1792),),
    ((0, 1792, 3328),),
    ((0, 3328, 4096), (1, 0, 1024)),
)
UP_WIDTHS = (1792, 1536, 1792)


def products_apart(lefts, rights):
    return [
        lax.psum_scatter(product_left(left, right), ("tok", "head"), scatter_dimension=0, tiled=True)
        for left, right in zip(lefts, rights)
    ]


def tok_peers():
    count, here = lax.axis_size("tok"), lax.axis_index("tok")
    head = lax.axis_index("head")
    return [
        ((lax.rem(here + step, count), head), lax.rem(here + count - step, count))
        for step in range(1, count)
    ]


def share(mine, every, send_sems, recv_sems, place, peers):
    copies = []
    for step, (target, _) in enumerate(peers):
        copy = pltpu.make_async_remote_copy(
            src_ref=mine,
            dst_ref=every.at[place],
            send_sem=send_sems.at[step],
            recv_sem=recv_sems.at[step],
            device_id=target,
            device_id_type=MESH,
        )
        copy.start()
        copies.append(copy)
    return copies


TABLES = 6


def every_step(length, second, back, body, carry):
    begins = lax.broadcasted_iota(jnp.int32, (SUB, HD), 0) * length - second

    def some(block, now):
        for inner in range(UNROLL):
            t = block * UNROLL + inner
            at = length - 1 - t if back else t
            now = body(at, now, jnp.where(begins == -at, 0.0, 1.0))
        return now

    return lax.fori_loop(0, length // UNROLL, some, carry)


def kept(second, begin, end):
    return jnp.where((second >= begin) & (second < end), 0.0, 1.0)


def table_rows(tables):
    return [tables.at[pl.ds(number * NS, NS)] for number in range(TABLES)] + [
        tables.at[pl.ds(TABLES * NS, 1)]
    ]


def recurrence_kernel(
    seq_starts,
    feed_rows,
    key,
    value,
    tables,
    context,
    key_rim,
    value_rim,
    context_rim,
    rows,
    total,
    ends,
    mine,
    every,
    share_sends,
    share_recvs,
    rim_sems,
):
    here, count = lax.axis_index("tok"), every.shape[0]
    peers = tok_peers()
    greet([target for target, _ in peers])
    decay, mix, chunk_decay, _, span_decay, _, skip = table_rows(tables)
    length = feed_rows.shape[0] // SUB
    span = feed_rows.shape[0]
    second = seq_starts[1] - here * span
    keep = [kept(second, chunk * length, (chunk + 1) * length) for chunk in range(SUB)]
    groups = feed_rows.shape[1] // HD
    zero = jnp.zeros((SUB, HD), jnp.float32)

    def rim(source, target, number):
        copy = pltpu.make_async_remote_copy(
            src_ref=source,
            dst_ref=target,
            send_sem=rim_sems.at[0, number],
            recv_sem=rim_sems.at[1, number],
            device_id=peers[0][0],
            device_id_type=MESH,
        )

        @pl.when(here < count - 1)
        def _():
            copy.start()

        return copy

    @pl.when(here == 0)
    def _():
        for target in (key_rim, value_rim, context_rim):
            target[...] = jnp.zeros_like(target)

    for group in range(groups):
        lanes = slice(group * HD, (group + 1) * HD)
        rows[group] = feed_rows[:, lanes].astype(jnp.float32)
        factors = [spread(decay[:, lanes], n) for n in range(NS)]

        def end_step(t, states, live):
            drive = rows[group, pl.ds(t, SUB, stride=length), :]
            return tuple(s * live * f + drive for s, f in zip(states, factors))

        done = every_step(length, second, False, end_step, (zero,) * NS)
        for n in range(NS):
            ends[n, :, lanes] = done[n]
    factor = chunk_decay[...]
    now = ends[:, 0, :]
    for chunk in range(1, SUB):
        now = keep[chunk] * (factor * now) + ends[:, chunk, :]
    mine[...] = now
    every[here] = now
    copies = share(mine, every, share_sends, share_recvs, here, peers)
    window = key_rim.shape[0]
    sent = [
        rim(key.at[pl.ds(span - window, window)], key_rim, 0),
        rim(value.at[pl.ds(span - window, window)], value_rim, 1),
    ]
    for copy in copies:
        copy.wait()
    over = span_decay[...]
    now = jnp.zeros_like(over)
    for place in range(count - 1):
        whole = kept(seq_starts[1], place * span, (place + 1) * span)
        now = jnp.where(place < here, whole * (over * now) + every[place], now)
    for chunk in range(SUB):
        own = ends[:, chunk, :]
        ends[:, chunk, :] = now
        now = keep[chunk] * (factor * now) + own

    window = context_rim.shape[0]
    for group in range(groups):
        lanes = slice(group * HD, (group + 1) * HD)
        factors = [spread(decay[:, lanes], n) for n in range(NS)]
        mixes = [spread(mix[:, lanes], n) for n in range(NS)]
        direct = spread(skip[:, lanes], 0)

        def out_step(t, states, live):
            at = pl.ds(t, SUB, stride=length)
            drive = rows[group, at, :]
            states = tuple(s * live * f + drive for s, f in zip(states, factors))
            parts = [state * weight for state, weight in zip(states, mixes)] + [direct * drive]
            while len(parts) > 1:
                parts = [a + b for a, b in zip(parts[::2], parts[1::2])] + (
                    [parts[-1]] if len(parts) % 2 else []
                )
            total[group, at, :] = parts[0]
            return states

        every_step(
            length, second, False, out_step, tuple(ends[n, :, lanes] for n in range(NS))
        )
        context[:, lanes] = total[group].astype(context.dtype)
        sent.append(
            rim(
                context.at[pl.ds(span - window, window), pl.ds(group * HD, HD)],
                context_rim.at[:, pl.ds(group * HD, HD)],
                2 + group,
            )
        )
    @pl.when(here > 0)
    def _():
        for copy in sent:
            copy.wait_recv()

    @pl.when(here < count - 1)
    def _():
        for copy in sent:
            copy.wait_send()


def recurrence(seq_starts, feed_rows, key, value, tables, collective_id):
    span, width = feed_rows.shape
    toks, groups = lax.axis_size("tok"), width // HD
    low = lambda count: jax.ShapeDtypeStruct((count, width), jnp.bfloat16)
    fulls = lambda *shape: pltpu.VMEM(shape, jnp.float32)
    sems = lambda *shape: pltpu.SemaphoreType.DMA(shape)
    window = 2 * BLOCK
    found = pl.pallas_call(
        recurrence_kernel,
        in_specs=[SCALARS] + [VMEM] * 4,
        out_specs=[VMEM] * 4,
        out_shape=[low(span), low(window), low(window), low(window + CTX)],
        scratch_shapes=[
            fulls(groups, span, HD),
            fulls(groups, span, HD),
            fulls(NS, SUB, width),
            fulls(NS, width),
            fulls(toks, NS, width),
            sems(toks - 1),
            sems(toks - 1),
            sems(2, 2 + groups),
        ],
        compiler_params=pltpu.CompilerParams(
            collective_id=collective_id, has_side_effects=True, vmem_limit_bytes=32 * MIB
        ),
        name="recurrence",
    )(seq_starts, feed_rows, key, value, tables)
    return found[0], found[1:]


def recurrence_back_kernel(
    stages,
    seq_starts,
    slope,
    feed_rows,
    tables,
    lefts,
    rights,
    down_in,
    back,
    sums,
    lag_sums,
    skip_sum,
    down_out,
    up_out,
    slopes,
    rows,
    total,
    ends,
    lags,
    mine,
    every,
    share_sends,
    share_recvs,
    down_arrivals,
    down_sems,
    grads,
    up_arrivals,
    up_sems,
):
    here, count = lax.axis_index("tok"), every.shape[0]
    peers = tok_peers()
    ladder = mesh_bits()
    heads = bits_of(lax.axis_size("head"))
    greet([target for target, _ in peers] + [partner for _, partner in ladder[:heads]])

    down_stages = stages[1] + stages[2]
    down = Halver(down_in, down_stages, down_arrivals, down_sems, ladder)
    down.begin()
    decay, mix, chunk_decay, chunk_slope, span_decay, span_slope, skip = table_rows(tables)
    span = slope.shape[0]
    length = span // SUB
    second = seq_starts[1] - here * span
    keep = [kept(second, chunk * length, (chunk + 1) * length) for chunk in range(SUB)]
    groups = slope.shape[1] // HD
    zero = jnp.zeros((SUB, HD), jnp.float32)
    for group in range(groups):
        lanes = slice(group * HD, (group + 1) * HD)
        slopes[group] = slope[:, lanes]
        rows[group] = feed_rows[:, lanes].astype(jnp.float32)
        total[group] = slope[:, lanes] * skip[:, lanes]
        skip_sum[:, lanes] = jnp.sum(slopes[group] * rows[group], axis=0, keepdims=True)
        factors = [spread(decay[:, lanes], n) for n in range(NS)]

        def end_step(t, carry, live):
            drive = slopes[group, pl.ds(t, SUB, stride=length), :]
            adjoint, lag = carry[:NS], carry[NS:]
            lag = [(a * f + b) * live for a, f, b in zip(lag, factors, adjoint)]
            adjoint = [(a * f + drive) * live for a, f in zip(adjoint, factors)]
            return tuple(adjoint) + tuple(lag)

        done = every_step(length, second, True, end_step, (zero,) * (2 * NS))
        for n in range(NS):
            ends[n, :, lanes] = done[n]
            lags[n, :, lanes] = done[NS + n]

    factor, bend = chunk_decay[...], chunk_slope[...]
    now, late = ends[:, SUB - 1, :], lags[:, SUB - 1, :]
    for chunk in reversed(range(SUB - 1)):
        late = keep[chunk] * (factor * late + bend * now) + lags[:, chunk, :]
        now = keep[chunk] * (factor * now) + ends[:, chunk, :]
    mine[0] = now
    mine[1] = late
    every[here, 0] = now
    every[here, 1] = late
    copies = share(mine, every, share_sends, share_recvs, here, peers)
    up = Halver(grads, stages[0], up_arrivals, up_sems, ladder)
    for number, parts in enumerate(UP_PARTS if grads else ()):
        column = 0
        for pair, start, stop in parts:
            fill(
                lefts[pair], rights[pair], start, stop, grads[number], column, up.orders[number]
            )
            column += stop - start
        up.send(number, stages[0][0])

    for copy in copies:
        copy.wait()
    for stage in down_stages[:-2]:
        down.step(stage)
    up.step(stages[0][0])
    over, over_slope = span_decay[...], span_slope[...]
    now, late = jnp.zeros_like(over), jnp.zeros_like(over)
    for place in reversed(range(1, count)):
        reached = place > here
        whole = kept(seq_starts[1], place * span, (place + 1) * span)
        late = jnp.where(reached, whole * (over * late + over_slope * now) + every[place, 1], late)
        now = jnp.where(reached, whole * (over * now) + every[place, 0], now)
    for chunk in reversed(range(SUB)):
        own, own_late = ends[:, chunk, :], lags[:, chunk, :]
        ends[:, chunk, :] = now
        lags[:, chunk, :] = late
        late = keep[chunk] * (factor * late + bend * now) + own_late
        now = keep[chunk] * (factor * now) + own

    for group in range(groups):
        lanes = slice(group * HD, (group + 1) * HD)
        for base in range(0, NS, HALF):
            factors = [spread(decay[:, lanes], base + n) for n in range(HALF)]
            mixes = [spread(mix[:, lanes], base + n) for n in range(HALF)]

            def out_step(t, carry, live):
                at = pl.ds(t, SUB, stride=length)
                drive, source = slopes[group, at, :], rows[group, at, :]
                adjoint, lag = carry[:HALF], carry[HALF : 2 * HALF]
                direct, late_sum = carry[2 * HALF : 3 * HALF], carry[3 * HALF :]
                lag = [a * f + b for a, f, b in zip(lag, factors, adjoint)]
                adjoint = [a * f + drive for a, f in zip(adjoint, factors)]
                direct = [a + b * source for a, b in zip(direct, adjoint)]
                late_sum = [a + b * source for a, b in zip(late_sum, lag)]
                parts = [a * b for a, b in zip(adjoint, mixes)]
                while len(parts) > 1:
                    parts = [a + b for a, b in zip(parts[::2], parts[1::2])]
                total[group, at, :] = total[group, at, :] + parts[0]
                lag = [a * live for a in lag]
                adjoint = [a * live for a in adjoint]
                return tuple(adjoint) + tuple(lag) + tuple(direct) + tuple(late_sum)

            if group == 1 and base == 0:
                down.step(down_stages[-2])
            first = tuple(ends[base + n, :, lanes] for n in range(HALF)) + tuple(
                lags[base + n, :, lanes] for n in range(HALF)
            )
            done = every_step(length, second, True, out_step, first + (zero,) * (2 * HALF))
            for n in range(HALF):
                sums[base + n : base + n + 1, lanes] = jnp.sum(
                    done[2 * HALF + n], axis=0, keepdims=True
                )
                lag_sums[base + n : base + n + 1, lanes] = jnp.sum(
                    done[3 * HALF + n], axis=0, keepdims=True
                )
        back[:, lanes] = total[group].astype(back.dtype)
    column = 0
    for number, piece in enumerate(down_in):
        width = piece.shape[2]
        down_out[:, column : column + width] = down.last(number, down_stages[-1])
        column += width
    up.step(stages[0][1], up_out)
    down.drain()
    up.drain()


def recurrence_back(
    seq_starts, slope, feed_rows, tables, lefts, rights, down, collective_id
):
    span, width = feed_rows.shape
    toks = lax.axis_size("tok")
    devices = toks * lax.axis_size("head")
    stages = stage_groups(devices)
    block = lefts[0].shape[1] // devices
    apart, up_pieces = None, [(block, part) for part in UP_WIDTHS]
    if block < 16:
        apart = products_apart(lefts, rights)
        lefts, rights, up_pieces = [], [], []
    down_pieces = [piece.shape[1:] for piece in down]
    down_buffers, down_count, down_sems = halver_scratch(down_pieces, stages[1] + stages[2], devices)
    up_buffers, up_count, up_sems = halver_scratch(up_pieces, stages[0], devices)
    down_width = sum(piece[1] for piece in down_pieces)
    up_shapes = left_over(up_pieces, stages[0], devices)
    full = lambda *shape: jax.ShapeDtypeStruct(shape, jnp.float32)
    fulls = lambda *shape: pltpu.VMEM(shape, jnp.float32)
    sems = lambda *shape: pltpu.SemaphoreType.DMA(shape)
    groups = width // HD
    scratch = [
        fulls(groups, span, HD),
        fulls(groups, span, HD),
        fulls(groups, span, HD),
        fulls(NS, SUB, width),
        fulls(NS, SUB, width),
        fulls(2, NS, width),
        fulls(toks, 2, NS, width),
        sems(toks - 1),
        sems(toks - 1),
    ]
    scratch += down_buffers + [down_sems]
    scratch += [pltpu.VMEM((devices,) + piece, jnp.bfloat16) for piece in up_pieces]
    scratch += up_buffers + [up_sems]
    pairs, ups, downs = len(lefts) or -1, len(up_pieces) or -1, len(down)
    sizes = [0] * 4 + [pairs, pairs, downs] + [0] * 4 + [0, ups] + [0] * 9
    sizes += [down_count, 0, ups, up_count, 0]
    found = pl.pallas_call(
        unpack_refs(functools.partial(recurrence_back_kernel, stages), sizes),
        in_specs=[SCALARS] + [VMEM] * (3 + 2 * len(lefts) + downs),
        out_specs=[VMEM] * (5 + len(up_shapes)),
        out_shape=[
            jax.ShapeDtypeStruct((span, width), jnp.bfloat16),
            full(NS, width),
            full(NS, width),
            full(1, width),
        ]
        + [full(down_pieces[0][0], down_width)]
        + up_shapes,
        scratch_shapes=scratch,
        compiler_params=pltpu.CompilerParams(
            collective_id=collective_id, has_side_effects=True, vmem_limit_bytes=60 * MIB
        ),
        name="recurrence_back",
    )(
        seq_starts,
        slope,
        feed_rows,
        tables,
        *lefts,
        *rights,
        *down,
    )
    return tuple(found[:4]) + (found[4], found[5:], apart)


def row_norm(rows, gain, bias):
    rows = rows.astype(jnp.float32)
    centred = rows - jnp.mean(rows, axis=-1, keepdims=True)
    spread_ = jnp.mean(centred * centred, axis=-1, keepdims=True)
    return (centred * lax.rsqrt(spread_ + epsilon) * gain + bias).astype(jnp.bfloat16)


PIECE = 128


def head_forward_kernel(
    tokens,
    gain,
    bias,
    w_query,
    w_key,
    w_value,
    hid,
    query,
    key,
    value,
    feed_rows,
    weights,
    gathered,
    send_sems,
    recv_sems,
    load_sems,
):
    tok, head = lax.axis_index("tok"), lax.axis_index("head")
    near = head + 1 - 2 * lax.rem(head, 2)
    far = head + 2 - 4 * (head // 2)
    across_ = near + 2 - 4 * (near // 2)
    greet([(tok, near), (tok, far)])
    rows = tokens.shape[0]
    pieces = rows // PIECE
    width = query.shape[1]
    columns_ = pl.ds(pl.multiple_of(head * width, HD), width)
    loads = [
        pltpu.make_async_copy(
            whole.at[:, columns_], weights.at[:, pl.ds(kind * width, width)], load_sems.at[kind]
        )
        for kind, whole in enumerate((w_query, w_key, w_value))
    ]
    for load in loads:
        load.start()

    def copy(source, owner, target, number):
        return pltpu.make_async_remote_copy(
            src_ref=source,
            dst_ref=gathered.at[owner, pl.ds(number % pieces * PIECE, PIECE)],
            send_sem=send_sems.at[number],
            recv_sem=recv_sems.at[number],
            device_id=(tok, target),
            device_id_type=MESH,
        )

    def own(number):
        return tokens.at[pl.ds(number * PIECE, PIECE)]

    over = [copy(own(i), head, far, i) for i in range(pieces)]
    beside = [copy(own(i), head, near, pieces + i) for i in range(pieces)]
    for one in over + beside:
        one.start()

    def work(found, owner, number):
        at = pl.ds(pl.multiple_of(owner * rows + number * PIECE, PIECE), PIECE)
        low = row_norm(found, gain[...], bias[...])
        hid[at, :] = low
        feed_rows[at, :] = hid[at, columns_]
        mixed = jnp.dot(low, weights[...], preferred_element_type=jnp.float32).astype(
            jnp.bfloat16
        )
        query[at, :] = mixed[:, :width]
        key[at, :] = mixed[:, width : 2 * width]
        value[at, :] = mixed[:, 2 * width :]

    def block(owner, number):
        return gathered[owner, number * PIECE : (number + 1) * PIECE, :]

    for load in loads:
        load.wait()
    for i in range(pieces):
        work(tokens[i * PIECE : (i + 1) * PIECE, :], head, i)
    for i in range(pieces):
        beside[i].wait_recv()
        work(block(near, i), near, i)
    passed = []
    for i in range(pieces):
        over[i].wait_recv()
        one = copy(
            gathered.at[far, pl.ds(i * PIECE, PIECE)], far, near, 2 * pieces + i
        )
        one.start()
        passed.append(one)
        work(block(far, i), far, i)
    for i in range(pieces):
        passed[i].wait_recv()
        work(block(across_, i), across_, i)
    for one in over + beside + passed:
        one.wait_send()


def head_forward(tokens, gain, bias, w_query, w_key, w_value, collective_id):
    rows, depth = tokens.shape
    heads = lax.axis_size("head")
    span, width = rows * heads, w_query.shape[1] // heads
    low = lambda count: jax.ShapeDtypeStruct((span, count), jnp.bfloat16)
    return pl.pallas_call(
        head_forward_kernel,
        in_specs=[VMEM] * 3 + [pl.BlockSpec(memory_space=pl.ANY)] * 3,
        out_specs=[VMEM] * 6,
        out_shape=[
            low(depth),
            low(width),
            low(width),
            low(width),
            low(width),
            jax.ShapeDtypeStruct((depth, 3 * width), jnp.bfloat16),
        ],
        scratch_shapes=[
            pltpu.VMEM((heads, rows, depth), jnp.bfloat16),
            pltpu.SemaphoreType.DMA((3 * (rows // PIECE),)),
            pltpu.SemaphoreType.DMA((3 * (rows // PIECE),)),
            pltpu.SemaphoreType.DMA((3,)),
        ],
        compiler_params=pltpu.CompilerParams(
            collective_id=collective_id, has_side_effects=True, vmem_limit_bytes=60 * MIB
        ),
        name="head_forward",
    )(tokens, gain, bias, w_query, w_key, w_value)


def head_backward_kernel(
    stages,
    back_query,
    back_key,
    back_value,
    back_feed,
    hid,
    weights,
    tokens,
    gain,
    grad_middle,
    sums,
    lag_sums,
    skip_sum,
    vectors,
    grad_up_bias,
    up_in,
    input_grad,
    grad_weights,
    row_sum,
    vector_sum,
    up_out,
    total,
    parts,
    near_in,
    far_in,
    products,
    arrived,
    shares,
    head_sems,
    tok_sends,
    tok_recvs,
    share_sends,
    share_recvs,
    every_row,
    row_sends,
    row_recvs,
    vector_parts,
    every_vector,
    tok_sum,
    head_sums,
    vector_sems,
    swap_sems,
    up_arrivals,
    up_sems,
):
    tok, head = lax.axis_index("tok"), lax.axis_index("head")
    heads, toks = lax.axis_size("head"), lax.axis_size("tok")
    near = head + 1 - 2 * lax.rem(head, 2)
    far = head + 2 - 4 * (head // 2)
    across_ = near + 2 - 4 * (near // 2)
    head_peers = [lax.rem(head + step, heads) for step in range(1, heads)]
    ladder = mesh_bits()[bits_of(heads) :]
    peers = tok_peers()
    greet([(tok, other) for other in head_peers] + [target for target, _ in peers])
    rows = input_grad.shape[0]
    states = sums.shape[0]
    every_row[tok] = jnp.zeros_like(every_row[tok])
    every_row[tok, :states] = sums[...]
    every_row[tok, states : 2 * states] = lag_sums[...]
    every_row[tok, 2 * states : 2 * states + 1] = skip_sum[...]
    row_copies = share(every_row.at[tok], every_row, row_sends, row_recvs, tok, peers)
    width = back_query.shape[1]
    columns_ = pl.ds(pl.multiple_of(head * width, HD), width)

    def block_of(owner):
        return pl.ds(pl.multiple_of(owner * rows, PIECE), rows)

    def partial(owner):
        at = block_of(owner)
        found = across(back_query[at, :], weights[:, :width])
        found += across(back_key[at, :], weights[:, width : 2 * width])
        found += across(back_value[at, :], weights[:, 2 * width :])
        total[...] = found
        total[:, columns_] += back_feed[at, :].astype(jnp.float32)

    def copy(source, target, device, number):
        one = pltpu.make_async_remote_copy(
            src_ref=source,
            dst_ref=target,
            send_sem=head_sems.at[0, number],
            recv_sem=head_sems.at[1, number],
            device_id=(tok, device),
            device_id_type=MESH,
        )
        one.start()
        return one

    up_stages = stages[1] + stages[2]
    up = Halver(up_in, up_stages, up_arrivals, up_sems, mesh_bits())
    up.begin()
    partial(across_)
    parts[0] = total[...].astype(jnp.bfloat16)
    first = copy(parts.at[0], near_in.at[0], near, 0)
    partial(near)
    parts[1] = total[...].astype(jnp.bfloat16)
    second = copy(parts.at[1], near_in.at[1], near, 1)
    partial(far)
    first.wait_recv()
    parts[2] = (total[...] + near_in[0].astype(jnp.float32)).astype(jnp.bfloat16)
    third = copy(parts.at[2], far_in, far, 2)

    steps = len(ladder)
    orders = [list(range(steps)), [1, 0] + list(range(2, steps))]
    each = products[0].shape[1]
    half_width = products[0].shape[2]
    depth = hid.shape[1]
    base = [0, 0]
    sent = []

    def forward(number, stage):
        bit, partner = ladder[orders[number][stage]]
        half = 1 << (steps - 1 - stage)
        one = pltpu.make_async_remote_copy(
            src_ref=products[number].at[pl.ds(base[number] + (1 - bit) * half, half)],
            dst_ref=arrived[number * steps + stage],
            send_sem=tok_sends.at[number, stage],
            recv_sem=tok_recvs.at[number, stage],
            device_id=partner,
            device_id_type=MESH,
        )
        one.start()
        sent.append(one)
        base[number] = base[number] + bit * half
        return one

    def joined(at, number):
        if number == 0:
            return jnp.concatenate([back_query[at, :], back_key[at, : half_width - width]], axis=1)
        return jnp.concatenate([back_key[at, half_width - width :], back_value[at, :]], axis=1)

    everything = pl.ds(0, hid.shape[0])
    flying = []
    for number in range(2):
        right = joined(everything, number)
        for start in range(0, depth, TILE):
            found = lax.dot_general(
                hid[:, start : start + TILE],
                right,
                (((0,), (0,)), ((), ())),
                preferred_element_type=jnp.float32,
            ).astype(jnp.bfloat16)
            for inner in range(TILE // each):
                products[number][slot_of(start // each + inner, orders[number])] = found[
                    inner * each : (inner + 1) * each
                ]
        flying.append(forward(number, 0))

    partial(head)
    up.step(up_stages[0])
    second.wait_recv()
    total[...] += near_in[1].astype(jnp.float32)

    done = []
    for stage in range(steps):
        for number in range(2):
            flying[number].wait_recv()
            arrival = arrived[number * steps + stage]
            half = 1 << (steps - 1 - stage)
            if stage == steps - 1:
                done.append(
                    products[number][base[number]].astype(jnp.float32)
                    + arrival[0].astype(jnp.float32)
                )
            else:
                for i in range(half):
                    products[number][base[number] + i] = (
                        products[number][base[number] + i] + arrival[i]
                    )
                flying[number] = forward(number, stage + 1)
        if stage == 0:
            for later in up_stages[1:-1]:
                up.step(later)
        if stage == steps - 2:
            third.wait_recv()
            back = total[...] + far_in[...].astype(jnp.float32)
            found = tokens[...].astype(jnp.float32)
            centred = found - jnp.mean(found, axis=-1, keepdims=True)
            scale = lax.rsqrt(jnp.mean(centred * centred, axis=-1, keepdims=True) + epsilon)
            shaped = centred * scale
            lists = [jnp.sum(back * shaped, axis=0, keepdims=True), jnp.sum(back, axis=0, keepdims=True)]
            lists += [vectors[i : i + 1, :] for i in range(3)]
            part = depth // toks
            for place in range(toks):
                for i, row in enumerate(lists):
                    vector_parts[place, i : i + 1, :part] = row[:, place * part : (place + 1) * part]
                for i in range(grad_up_bias.shape[1] // depth):
                    start = place * part * (grad_up_bias.shape[1] // depth) + i * part
                    vector_parts[place, len(lists) + i : len(lists) + i + 1, :part] = grad_up_bias[
                        :, start : start + part
                    ]
            every_vector[tok] = vector_parts[tok]
            vector_copies = []
            for step, (target, _) in enumerate(peers):
                one = pltpu.make_async_remote_copy(
                    src_ref=vector_parts.at[target[0]],
                    dst_ref=every_vector.at[tok],
                    send_sem=vector_sems.at[0, step],
                    recv_sem=vector_sems.at[1, step],
                    device_id=target,
                    device_id_type=MESH,
                )
                one.start()
                vector_copies.append(one)
            back = back * gain[...]
            back = back - jnp.mean(back, axis=-1, keepdims=True)
            back = back - shaped * jnp.mean(back * shaped, axis=-1, keepdims=True)
            input_grad[...] = grad_middle[...] + back * scale
    small = each // heads
    ready, landed = shares
    for other in range(heads):
        for number in range(2):
            ready[other, :, number * half_width : (number + 1) * half_width] = done[number][
                other * small : (other + 1) * small
            ]
    landed[head] = ready[head]
    swaps = []
    for step, other in enumerate(head_peers):
        one = pltpu.make_async_remote_copy(
            src_ref=ready.at[other],
            dst_ref=landed.at[head],
            send_sem=share_sends.at[step],
            recv_sem=share_recvs.at[step],
            device_id=(tok, other),
            device_id_type=MESH,
        )
        one.start()
        swaps.append(one)

    for one in row_copies + vector_copies:
        one.wait_recv()
    row_sum[...] = jnp.sum(every_row[...], axis=0)
    tok_sum[...] = jnp.sum(every_vector[...], axis=0)
    head_sums[head] = tok_sum[...]
    head_copies = []
    for step, other in enumerate(head_peers):
        one = pltpu.make_async_remote_copy(
            src_ref=tok_sum,
            dst_ref=head_sums.at[head],
            send_sem=swap_sems.at[0, step],
            recv_sem=swap_sems.at[1, step],
            device_id=(tok, other),
            device_id_type=MESH,
        )
        one.start()
        head_copies.append(one)
    for one in swaps:
        one.wait()
    for other in range(heads):
        for kind in range(3):
            grad_weights[kind][:, other * width : (other + 1) * width] = landed[
                other, :, kind * width : (kind + 1) * width
            ]
    for one in head_copies:
        one.wait_recv()
    vector_sum[...] = jnp.sum(head_sums[...], axis=0)
    for number in range(len(up_in)):
        found, column = up.last(number, up_stages[-1]), 0
        for pair, start, stop in UP_PARTS[number]:
            up_out[pair][:, start:stop] = found[:, column : column + stop - start]
            column += stop - start
    up.drain()
    for one in sent + [first, second, third] + row_copies + vector_copies + head_copies:
        one.wait_send()


def head_backward(
    back_query,
    back_key,
    back_value,
    back_feed,
    hid,
    weights,
    tokens,
    gain,
    grad_middle,
    sums,
    lag_sums,
    skip_sum,
    vectors,
    grad_up_bias,
    up,
    collective_id,
):
    span, width = back_query.shape
    depth = hid.shape[1]
    heads, toks = lax.axis_size("head"), lax.axis_size("tok")
    rows, each = span // heads, depth // toks
    steps, half_width = bits_of(toks), 3 * width // 2
    devices = heads * toks
    stages = stage_groups(devices)
    up_pieces = [piece.shape[1:] for piece in up]
    up_buffers, up_count, up_sems = halver_scratch(up_pieces, stages[1] + stages[2], devices)
    outs = []
    for pair in range(2 if up else 0):
        stop = max(part[2] for parts in UP_PARTS for part in parts if part[0] == pair)
        outs.append(jax.ShapeDtypeStruct((up_pieces[0][0], stop), jnp.float32))
    states = sums.shape[0]
    states += -states % SUB
    row_count = 2 * states + SUB
    part = (16, max(depth // toks, HD))
    ups = len(up) or -1
    low = lambda *shape: pltpu.VMEM(shape, jnp.bfloat16)
    full = lambda *shape: pltpu.VMEM(shape, jnp.float32)
    sems = lambda *shape: pltpu.SemaphoreType.DMA(shape)
    sizes = [0] * 14 + [ups, 0, 3, 0, 0, len(outs) or -1] + [0] * 4 + [2, 2 * steps, 2]
    sizes += [0] * 5 + [0] * 9 + [up_count, 0]
    found = pl.pallas_call(
        unpack_refs(functools.partial(head_backward_kernel, stages), sizes),
        in_specs=[VMEM] * (14 + len(up)),
        out_specs=[VMEM] * (6 + len(outs)),
        out_shape=[
            jax.ShapeDtypeStruct((rows, depth), jnp.float32),
        ]
        + [jax.ShapeDtypeStruct((each // heads, depth), jnp.float32)] * 3
        + [
            jax.ShapeDtypeStruct((row_count, width), jnp.float32),
            jax.ShapeDtypeStruct(part, jnp.float32),
        ]
        + outs,
        scratch_shapes=[
            full(rows, depth),
            low(3, rows, depth),
            low(2, rows, depth),
            low(rows, depth),
        ]
        + [low(toks, each, half_width)] * 2
        + [low(1 << (steps - 1 - stage), each, half_width) for stage in range(steps)] * 2
        + [full(heads, each // heads, 3 * width)] * 2
        + [sems(2, 3), sems(2, steps), sems(2, steps), sems(heads - 1), sems(heads - 1)]
        + [full(toks, row_count, width), sems(toks - 1), sems(toks - 1)]
        + [full(toks, *part), full(toks, *part), full(*part), full(heads, *part)]
        + [sems(2, toks - 1), sems(2, heads - 1)]
        + up_buffers
        + [up_sems],
        compiler_params=pltpu.CompilerParams(
            collective_id=collective_id, has_side_effects=True, vmem_limit_bytes=58 * MIB
        ),
        name="head_backward",
    )(
        back_query,
        back_key,
        back_value,
        back_feed,
        hid,
        weights,
        tokens,
        gain,
        grad_middle,
        sums,
        lag_sums,
        skip_sum,
        vectors,
        grad_up_bias,
        *up,
    )
    return found[0], found[1:4], found[4], found[5], found[6:]


CHUNK = 512
ROOT = math.sqrt(2.0 / math.pi)
CUBIC = 0.044715


def feed_kernel(
    stages,
    attended,
    tokens,
    out_grad,
    gain,
    bias,
    up_bias,
    down_bias,
    w_output,
    w_up,
    w_down,
    layer_out,
    grad_middle,
    normed,
    grad_before,
    joined,
    grad_branch,
    grad_att,
    down_left,
    vectors,
    grad_up_bias,
    output_w,
    up_w,
    down_w,
    split,
    active,
    bend,
    shape,
    down_sum,
    back_sum,
    grad_split,
    grads,
    arrivals,
    weight_sems,
    down_sems,
    head_sems,
    halver_sems,
):
    tok, head = lax.axis_index("tok"), lax.axis_index("head")
    heads = lax.axis_size("head")
    rows, width = tokens.shape[0], attended.shape[1]
    hidden = up_w.shape[1]
    loads = [
        pltpu.make_async_copy(source, target, weight_sems.at[number])
        for number, (source, target) in enumerate(
            ((w_output, output_w), (w_up, up_w))
        )
    ]

    def down_load(chunk):
        slot = lax.rem(chunk, 2)
        return pltpu.make_async_copy(
            w_down.at[pl.ds(pl.multiple_of(chunk * CHUNK, CHUNK), CHUNK)],
            down_w.at[slot],
            down_sems.at[slot],
        )

    for load in loads:
        load.start()
    for chunk in range(2):
        down_load(chunk).start()
    peers = [lax.rem(head + step, heads) for step in range(1, heads)]
    ladder = mesh_bits()
    greet([(tok, other) for other in peers] + [p for _, p in ladder[bits_of(heads) :]])

    def block_of(owner):
        return pl.ds(pl.multiple_of(owner * rows, PIECE), rows)

    def swap(source_of, target, kind):
        found = []
        for step, other in enumerate(peers):
            copy = pltpu.make_async_remote_copy(
                src_ref=source_of(other),
                dst_ref=target,
                send_sem=head_sems.at[kind, 0, step],
                recv_sem=head_sems.at[kind, 1, step],
                device_id=(tok, other),
                device_id_type=MESH,
            )
            copy.start()
            found.append(copy)
        return found

    first = swap(lambda other: attended.at[block_of(other)], split.at[head], 0)
    split[head] = attended[block_of(head), :]
    loads[0].wait()
    for copy in first:
        copy.wait_recv()
    total = tokens[...].astype(jnp.float32)
    for owner in range(heads):
        at = slice(owner * width, (owner + 1) * width)
        joined[:, at] = split[owner]
        total += jnp.dot(split[owner], output_w[at, :], preferred_element_type=jnp.float32)
    grad_middle[...] = total
    centred = total - jnp.mean(total, axis=-1, keepdims=True)
    scale = lax.rsqrt(jnp.mean(centred * centred, axis=-1, keepdims=True) + epsilon)
    shape[...] = centred * scale
    normed[...] = (centred * scale * gain[...] + bias[...]).astype(jnp.bfloat16)

    loads[1].wait()
    block = grads[0].shape[1]
    halver = Halver(grads, stages, arrivals, halver_sems, ladder)

    def up_chunk(chunk, _):
        at = pl.ds(pl.multiple_of(chunk * CHUNK, CHUNK), CHUNK)
        before = jnp.dot(normed[...], up_w[:, at], preferred_element_type=jnp.float32)
        before += up_bias[:, at]
        square = before * before
        bent = jnp.tanh(ROOT * before * (1.0 + CUBIC * square))
        half = 0.5 * (1.0 + bent)
        low = (before * half).astype(jnp.bfloat16)
        active[:, at] = low
        bend[:, at] = half + (0.5 * ROOT) * before * (1.0 - bent * bent) * (
            1.0 + (3.0 * CUBIC) * square
        )
        found = lax.dot_general(
            low, out_grad[...], (((0,), (0,)), ((), ())), preferred_element_type=jnp.float32
        ).astype(jnp.bfloat16)
        for inner in range(CHUNK // block):
            some = found[inner * block : (inner + 1) * block]
            at = 0
            for grad, order, part in zip(grads, halver.orders, DOWN_PARTS):
                grad[slot_of(chunk * (CHUNK // block) + inner, order)] = some[:, at : at + part]
                at += part
        return 0

    lax.fori_loop(0, hidden // CHUNK, up_chunk, 0)
    halver.begin()
    down_sum[...] = jnp.zeros_like(down_sum)
    back_sum[...] = jnp.zeros_like(back_sum)

    def down_chunk(chunk, _):
        at = pl.ds(pl.multiple_of(chunk * CHUNK, CHUNK), CHUNK)
        down_load(chunk).wait()
        some = down_w.at[lax.rem(chunk, 2)]
        low = (across(out_grad[...], some[...]) * bend[:, at]).astype(jnp.bfloat16)
        grad_before[:, at] = low
        grad_up_bias[:, at] = jnp.sum(low.astype(jnp.float32), axis=0, keepdims=True)
        down_sum[...] += jnp.dot(
            active[:, at], some[...], preferred_element_type=jnp.float32
        )
        back_sum[...] += across(low, up_w[:, at])

        @pl.when(chunk + 2 < hidden // CHUNK)
        def _():
            down_load(chunk + 2).start()

        return 0

    groups = 4
    each = hidden // CHUNK // groups
    for group in range(groups):
        lax.fori_loop(group * each, (group + 1) * each, down_chunk, 0)
        if group == groups - 2:
            halver.step(stages[0])

    layer_out[...] = (grad_middle[...] + down_sum[...] + down_bias[...]).astype(jnp.bfloat16)
    back = back_sum[...]
    shaped = shape[...]
    vectors[0:1, :] = jnp.sum(back * shaped, axis=0, keepdims=True)
    vectors[1:2, :] = jnp.sum(back, axis=0, keepdims=True)
    top = out_grad[...].astype(jnp.float32)
    vectors[2:3, :] = jnp.sum(top, axis=0, keepdims=True)
    back = back * gain[...]
    back = back - jnp.mean(back, axis=-1, keepdims=True)
    back = back - shaped * jnp.mean(back * shaped, axis=-1, keepdims=True)
    total = grad_middle[...]
    centred = total - jnp.mean(total, axis=-1, keepdims=True)
    scale = lax.rsqrt(jnp.mean(centred * centred, axis=-1, keepdims=True) + epsilon)
    top = top + back * scale
    grad_middle[...] = top
    low = top.astype(jnp.bfloat16)
    grad_branch[...] = low
    for owner in range(heads):
        at = slice(owner * width, (owner + 1) * width)
        grad_split[owner] = across(low, output_w[at, :]).astype(jnp.bfloat16)
    second = swap(lambda other: grad_split.at[other], grad_att.at[block_of(head)], 1)
    grad_att[block_of(head), :] = grad_split[head]
    halver.step(stages[1], down_left)
    for copy in second:
        copy.wait_recv()
    halver.drain()
    for copy in first + second:
        copy.wait_send()


def feed(
    attended,
    tokens,
    out_grad,
    gain,
    bias,
    up_bias,
    down_bias,
    w_output,
    w_up,
    w_down,
    collective_id,
):
    rows, depth = tokens.shape
    span, width = attended.shape
    hidden = w_up.shape[1]
    heads = lax.axis_size("head")
    devices = heads * lax.axis_size("tok")
    block = hidden // devices
    stages = stage_groups(devices)[0]
    pieces = [(block, part) for part in DOWN_PARTS]
    buffers, buffer_count, halver_sems = halver_scratch(pieces, stages, devices)
    low = lambda *shape: jax.ShapeDtypeStruct(shape, jnp.bfloat16)
    full = lambda *shape: jax.ShapeDtypeStruct(shape, jnp.float32)
    any_ = pl.BlockSpec(memory_space=pl.ANY)
    sems = lambda *shape: pltpu.SemaphoreType.DMA(shape)
    lows = lambda *shape: pltpu.VMEM(shape, jnp.bfloat16)
    fulls = lambda *shape: pltpu.VMEM(shape, jnp.float32)
    scratch = [
        lows(depth, depth),
        lows(depth, hidden),
        lows(2, CHUNK, depth),
        lows(heads, rows, width),
        lows(rows, hidden),
        fulls(rows, hidden),
        fulls(rows, depth),
        fulls(rows, depth),
        fulls(rows, depth),
        lows(heads, rows, width),
    ]
    scratch += [lows(devices, block, part) for part in DOWN_PARTS] + buffers
    scratch += [sems(2), sems(2), sems(2, 2, heads - 1), halver_sems]
    count = len(pieces)
    sizes = [0] * 17 + [count] + [0] * 12 + [count, buffer_count] + [0] * 4
    outs = [
        low(rows, depth),
        full(rows, depth),
        low(rows, depth),
        low(rows, hidden),
        low(rows, depth),
        low(rows, depth),
        low(span, width),
    ]
    outs += left_over(pieces, stages, devices) + [full(SUB, depth), full(1, hidden)]
    return pl.pallas_call(
        unpack_refs(functools.partial(feed_kernel, stages), sizes),
        in_specs=[VMEM] * 7 + [any_] * 3,
        out_specs=[VMEM] * len(outs),
        out_shape=outs,
        scratch_shapes=scratch,
        compiler_params=pltpu.CompilerParams(
            collective_id=collective_id, has_side_effects=True, vmem_limit_bytes=60 * MIB
        ),
        name="feed",
    )(
        attended, tokens, out_grad, gain, bias, up_bias, down_bias, w_output, w_up, w_down
    )


def layer_norm(row_block, gain, bias):
    centre = jnp.mean(row_block, axis=-1, keepdims=True)
    centred = row_block - centre
    spread = jnp.mean(centred * centred, axis=-1, keepdims=True)
    return centred * lax.rsqrt(spread + epsilon) * gain + bias


def product(left, right):
    return jnp.dot(left, right, preferred_element_type=jnp.float32)


def product_left(left, right):
    return lax.dot_general(
        left, right, (((0,), (0,)), ((), ())), preferred_element_type=jnp.float32
    )


def product_right(left, right):
    return lax.dot_general(
        left, right, (((1,), (1,)), ((), ())), preferred_element_type=jnp.float32
    )


def shifted(shard, axis, by):
    devices = lax.axis_size(axis)
    pairs = [(i, i + by) for i in range(devices) if 0 <= i + by < devices]
    return lax.ppermute(shard, axis, pairs)


def per_device(
    tokens_in,
    seq_starts,
    block_sizes,
    norm1_gain,
    norm1_bias,
    w_query,
    w_key,
    w_value,
    w_output,
    ssm_rate,
    ssm_input,
    ssm_output,
    ssm_skip,
    norm2_gain,
    norm2_bias,
    w_up,
    up_bias,
    w_down,
    down_bias,
    out_grad,
):
    tok_rows = tokens_in.shape[0]
    pieces = lax.axis_size("tok")
    span = tok_rows * lax.axis_size("head")
    total_len = span * pieces
    window = 2 * BLOCK
    length = span // SUB

    hid, query_h, key_h, value_h, hidden_h, w_own = head_forward(
        tokens_in, norm1_gain[None, :], norm1_bias[None, :], w_query, w_key, w_value, 6
    )

    rate = ssm_rate.T / total_len
    drive_in, read_out = ssm_input.T, ssm_output.T
    decay = jnp.exp(-rate)
    gain = jnp.sqrt(-jnp.expm1(-2.0 * rate))
    driving = gain * drive_in
    mix = read_out * driving
    tables = jnp.concatenate(
        [
            decay,
            mix,
            jnp.exp(-rate * length),
            length * jnp.exp(-rate * (length - 1)),
            jnp.exp(-rate * span),
            span * jnp.exp(-rate * (span - 1)),
            jnp.broadcast_to(ssm_skip[None, :], (SUB, ssm_skip.shape[0])),
        ],
        axis=0,
    )
    context, rims = recurrence(seq_starts, hidden_h, key_h, value_h, tables, 1)
    attended, attended_fine, level = attend(seq_starts, block_sizes, query_h, key_h, value_h, context, rims)
    (
        layer_out,
        grad_middle,
        normed_low,
        grad_before_low,
        joined,
        grad_branch,
        grad_att,
        *down,
        vectors,
        grad_up_bias,
    ) = feed(
        attended,
        tokens_in,
        out_grad,
        norm2_gain[None, :],
        norm2_bias[None, :],
        up_bias[None, :],
        down_bias[None, :],
        w_output,
        w_up,
        w_down,
        7,
    )

    back_query_h, key_rim, value_rim, near_rim, back_key_h, back_value_h, back_context = attend_back(
        seq_starts, block_sizes, query_h, key_h, value_h, context, rims, attended_fine, grad_att, level
    )
    near_rim = shifted(near_rim, "tok", -1).astype(jnp.float32)
    rims = shifted(jnp.stack([key_rim, value_rim]), "tok", -1).astype(jnp.float32)
    back_context = back_context.at[span - window - CTX :].add(near_rim)
    back_key_h = back_key_h.at[span - window :].add(rims[0]).astype(jnp.bfloat16)
    back_value_h = back_value_h.at[span - window :].add(rims[1]).astype(jnp.bfloat16)

    back_feed_h, sums, lag_sums, skip_sum, out_w_down, up, apart = recurrence_back(
        seq_starts,
        back_context,
        hidden_h,
        tables,
        [normed_low, joined],
        [grad_before_low, grad_branch],
        down,
        2,
    )
    input_grad, out_w_heads, summed, packed, up = head_backward(
        back_query_h,
        back_key_h,
        back_value_h,
        back_feed_h,
        hid,
        w_own,
        tokens_in,
        norm1_gain[None, :],
        grad_middle,
        sums,
        lag_sums,
        skip_sum,
        vectors,
        grad_up_bias,
        up,
        4,
    )
    heads, head = lax.axis_size("head"), lax.axis_index("head")
    part = norm1_gain.shape[0] // pieces
    more = up_bias.shape[0] // norm1_gain.shape[0]
    short = lax.dynamic_slice_in_dim(packed[:5], head * (part // heads), part // heads, 1)
    out_up_bias = lax.dynamic_slice_in_dim(
        packed[5 : 5 + more, :part].reshape(-1), head * (more * part // heads), more * part // heads
    )
    out_w_up, out_w_output = up if apart is None else apart
    sums, lag_sums, skip_sum = summed[:NS], summed[NS : 2 * NS], summed[2 * NS]
    grad_ssm_output = (driving * sums).T
    grad_driving = read_out * sums
    grad_ssm_input = (gain * grad_driving).T
    grad_ssm_rate = (
        grad_driving * drive_in * jnp.exp(-2.0 * rate) / gain - mix * lag_sums * decay
    ).T / total_len

    return (
        layer_out,
        input_grad,
        short[0],
        short[1],
        out_w_heads[0],
        out_w_heads[1],
        out_w_heads[2],
        out_w_output,
        grad_ssm_rate,
        grad_ssm_input,
        grad_ssm_output,
        skip_sum,
        short[2],
        short[3],
        out_w_up,
        out_up_bias,
        out_w_down,
        short[4],
    )


def solution(mesh):
    return jax.shard_map(
        per_device,
        mesh=mesh,
        in_specs=(
            P(("tok", "head"), None),
            P(),
            P(),
            P(),
            P(),
            P(),
            P(),
            P(),
            P(),
            P("head", None),
            P("head", None),
            P("head", None),
            P("head"),
            P(),
            P(),
            P(),
            P(),
            P(),
            P(),
            P(("tok", "head"), None),
        ),
        out_specs=(
            P(("tok", "head"), None),
            P(("tok", "head"), None),
            P(("tok", "head")),
            P(("tok", "head")),
            P(("tok", "head"), None),
            P(("tok", "head"), None),
            P(("tok", "head"), None),
            P(("tok", "head"), None),
            P("head", None),
            P("head", None),
            P("head", None),
            P("head"),
            P(("tok", "head")),
            P(("tok", "head")),
            P(("tok", "head"), None),
            P(("tok", "head")),
            P(("tok", "head"), None),
            P(("tok", "head")),
        ),
        check_vma=False,
    )
```

```python
import functools
import math

import jax
import jax.numpy as jnp
from jax import lax
from jax.experimental import pallas as pl
from jax.experimental.pallas import tpu as pltpu
from jax.sharding import PartitionSpec as P

epsilon = 1e-05
HD = 128
CTX = 128
BLOCK = 256
NS = 16
SUB = 8
UNROLL = 8
HALF = 8
TILE = 256
MIB = 1 << 20
LOWEST = -1e30
FACTOR = HD ** (-0.5)
FACTOR2 = FACTOR * math.log2(math.e)


def spread(table, n):
    return jnp.broadcast_to(table[n : n + 1, :], (SUB, table.shape[1]))


SCALARS = pl.BlockSpec(memory_space=pltpu.SMEM)


def wide(limit=48):
    return pltpu.CompilerParams(vmem_limit_bytes=limit * MIB)


def across(left, right):
    return lax.dot_general(
        left, right, (((1,), (1,)), ((), ())), preferred_element_type=jnp.float32
    )


def times(left, right):
    return lax.dot_general(
        left, right, (((1,), (0,)), ((), ())), preferred_element_type=jnp.float32
    )


def turn(source, target):
    for at in range(0, source.shape[0], TILE):
        size = min(TILE, source.shape[0] - at)
        piece = source[at : at + size, :].astype(jnp.float32)
        target[:, at : at + size] = piece.T.astype(target.dtype)


def next_block(where_, now):
    second = where_[1]
    length = jnp.where(now >= second, where_[3], where_[2])
    after = now + length
    return jnp.where((now < second) & (after > second), second, after)


REACH = 2 * BLOCK + TILE
BLOCKS = 4


def block_facts(starts, sizes, span):
    anchor = lax.axis_index("tok") * span
    return anchor, starts[1] - anchor, sizes[0], sizes[1]


def block_begin(where_, at):
    opening = jnp.where(at >= where_[1], where_[1], -where_[0])
    length = jnp.where(at >= where_[1], where_[3], where_[2])
    return opening + lax.div(at - opening, length) * length


def block_rows(where_, tile):
    cols = lax.broadcasted_iota(jnp.int32, (1, TILE), 1) + tile * TILE
    begin = block_begin(where_, tile * TILE)
    now, firsts = begin, jnp.zeros_like(cols) + begin
    for _ in range(BLOCKS):
        now = next_block(where_, now)
        firsts = jnp.where(cols >= now, now, firsts)
    return firsts, jnp.where(cols >= where_[1], where_[1], -where_[0]), begin


def joined_rows(rim, own, target):
    target[: rim.shape[0], :] = rim[...]
    target[rim.shape[0] :, :] = own[...]


def local_mask(tile, first):
    rows = lax.broadcasted_iota(jnp.int32, (REACH, TILE), 0) + (tile * TILE - 2 * BLOCK)
    cols = lax.broadcasted_iota(jnp.int32, (1, TILE), 1) + tile * TILE
    return (rows >= first) & (rows <= cols)


def context_at(now):
    return pl.multiple_of((now + 2 * BLOCK) // CTX * CTX, CTX)


def context_mask(start, now, first, opening):
    rows = lax.broadcasted_iota(jnp.int32, (TILE, TILE), 0) + (start - 2 * BLOCK - CTX)
    low = jnp.where(first == now, jnp.maximum(now - CTX, opening), 1 << 28)
    return (rows >= low) & (rows < now)


def lanes_of(head):
    return slice(head * HD, (head + 1) * HD)


def attend_kernel(
    starts,
    sizes,
    query,
    key_own,
    value_own,
    context_own,
    key_rim,
    value_rim,
    context_rim,
    out,
    fine,
    level,
    key,
    value,
    context,
    value_t,
    context_t,
):
    where_ = block_facts(starts, sizes, query.shape[0])
    joined_rows(key_rim, key_own, key)
    joined_rows(value_rim, value_own, value)
    joined_rows(context_rim, context_own, context)
    heads = query.shape[1] // HD
    turn(value, value_t)
    turn(context, context_t)

    def one_tile(tile, _):
        here = pl.ds(pl.multiple_of(tile * TILE, TILE), TILE)
        rows = [query[here, lanes_of(head)] for head in range(heads)]
        firsts, openings, begin = block_rows(where_, tile)

        def score(near, at, head, mask):
            return jnp.where(mask, across(near[at, lanes_of(head)], rows[head]) * FACTOR2, LOWEST)

        def peak(found):
            return jnp.max(found, axis=0, keepdims=True)

        def gather(prob, values_t, at, head):
            low = prob.astype(jnp.bfloat16)
            return (
                jnp.sum(prob, axis=0, keepdims=True),
                jnp.sum(low.astype(jnp.float32), axis=0, keepdims=True),
                times(values_t[lanes_of(head), at], low),
            )

        near_at = pl.ds(pl.multiple_of(tile * TILE, TILE), REACH)
        far_at = pl.ds(context_at(begin), TILE)
        near_mask = local_mask(tile, firsts)
        far_mask = context_mask(context_at(begin), begin, firsts, openings)
        carry = []
        for head in range(heads):
            near = score(key, near_at, head, near_mask)
            far = score(context, far_at, head, far_mask)
            top = jnp.maximum(peak(near), peak(far))
            one = gather(jnp.exp2(near - top), value_t, near_at, head)
            two = gather(jnp.exp2(far - top), context_t, far_at, head)
            carry.append((top,) + tuple(a + b for a, b in zip(one, two)))

        def earlier(state):
            now, carry = state
            start = context_at(now)
            at = pl.ds(start, TILE)
            mask = context_mask(start, now, firsts, openings)
            found = []
            for head in range(heads):
                top, mass, low_mass, total = carry[head]
                far = score(context, at, head, mask)
                new_top = jnp.maximum(top, peak(far))
                shrink = jnp.exp2(top - new_top)
                more = gather(jnp.exp2(far - new_top), context_t, at, head)
                found.append(
                    (new_top,)
                    + tuple(a * shrink + b for a, b in zip((mass, low_mass, total), more))
                )
            return next_block(where_, now), tuple(found)

        _, carry = lax.while_loop(
            lambda state: state[0] < (tile + 1) * TILE,
            earlier,
            (next_block(where_, begin), tuple(carry)),
        )
        for head in range(heads):
            top, mass, low_mass, total = carry[head]
            done = (total / low_mass).T
            fine[here, lanes_of(head)] = done
            out[here, lanes_of(head)] = done.astype(out.dtype)
            level[head, tile] = top + jnp.log2(mass)
        return 0

    lax.fori_loop(0, query.shape[0] // TILE, one_tile, 0)


def attend_back_kernel(
    starts,
    sizes,
    query,
    key_own,
    value_own,
    context_own,
    key_rim,
    value_rim,
    context_rim,
    attended,
    grad,
    level,
    back_query,
    back_key_rim,
    back_value_rim,
    back_context_rim,
    back_key,
    back_value,
    back_context,
    key,
    value,
    context,
    key_t,
    context_t,
    key_sum,
    value_sum,
    context_sum,
):
    where_ = block_facts(starts, sizes, query.shape[0])
    joined_rows(key_rim, key_own, key)
    joined_rows(value_rim, value_own, value)
    joined_rows(context_rim, context_own, context)
    heads = query.shape[1] // HD
    turn(key, key_t)
    turn(context, context_t)
    key_sum[...] = jnp.zeros_like(key_sum)
    value_sum[...] = jnp.zeros_like(value_sum)
    context_sum[...] = jnp.zeros_like(context_sum)

    def one_tile(tile, _):
        here = pl.ds(pl.multiple_of(tile * TILE, TILE), TILE)
        rows = [query[here, lanes_of(head)] for head in range(heads)]
        grads = [grad[here, lanes_of(head)] for head in range(heads)]
        firsts, openings, begin = block_rows(where_, tile)
        levels = [level[head, tile] for head in range(heads)]
        centres = []
        for head in range(heads):
            joint = grads[head].astype(jnp.float32) * attended[here, lanes_of(head)]
            centres.append(jnp.sum(joint.T, axis=0, keepdims=True))

        def slopes(keys, values, at, head, mask):
            found = across(keys[at, lanes_of(head)], rows[head]) * FACTOR2 - levels[head]
            prob = jnp.exp2(jnp.where(mask, found, LOWEST))
            drive = across(values[at, lanes_of(head)], grads[head])
            slope = prob * (drive - centres[head])
            return prob.astype(jnp.bfloat16), slope.astype(jnp.bfloat16)

        def earlier(state):
            now, totals = state
            start = context_at(now)
            at = pl.ds(start, TILE)
            mask = context_mask(start, now, firsts, openings)
            found = []
            for h in range(heads):
                prob, slope = slopes(context, context, at, h, mask)
                context_sum[at, lanes_of(h)] += FACTOR * times(slope, rows[h]) + times(
                    prob, grads[h]
                )
                found.append(totals[h] + times(context_t[lanes_of(h), at], slope))
            return next_block(where_, now), tuple(found)

        at = pl.ds(pl.multiple_of(tile * TILE, TILE), REACH)
        mask = local_mask(tile, firsts)
        totals = []
        for h in range(heads):
            prob, slope = slopes(key, value, at, h, mask)
            key_sum[at, lanes_of(h)] += times(slope, rows[h])
            value_sum[at, lanes_of(h)] += times(prob, grads[h])
            totals.append(times(key_t[lanes_of(h), at], slope))
        state = earlier((begin, tuple(totals)))
        _, totals = lax.while_loop(lambda state: state[0] < (tile + 1) * TILE, earlier, state)
        for head in range(heads):
            back_query[here, lanes_of(head)] = (FACTOR * totals[head]).T.astype(back_query.dtype)
        return 0

    lax.fori_loop(0, query.shape[0] // TILE, one_tile, 0)
    window = 2 * BLOCK
    back_key_rim[...] = (FACTOR * key_sum[:window, :]).astype(back_key_rim.dtype)
    back_value_rim[...] = value_sum[:window, :].astype(back_value_rim.dtype)
    back_context_rim[...] = context_sum[: window + CTX, :].astype(back_context_rim.dtype)
    back_key[...] = FACTOR * key_sum[window:, :]
    back_value[...] = value_sum[window:, :]
    back_context[...] = context_sum[window + CTX :, :]


VMEM = pl.BlockSpec(memory_space=pltpu.VMEM)


def attend(starts, sizes, query, key, value, context, rims):
    rows, width = query.shape
    heads, tiles = width // HD, rows // TILE
    near, far = rows + rims[0].shape[0], rows + rims[2].shape[0]
    low = lambda *shape: pltpu.VMEM(shape, jnp.bfloat16)
    return pl.pallas_call(
        attend_kernel,
        in_specs=[SCALARS] * 2 + [VMEM] * 7,
        out_specs=[VMEM] * 3,
        out_shape=(
            jax.ShapeDtypeStruct((rows, width), jnp.bfloat16),
            jax.ShapeDtypeStruct((rows, width), jnp.float32),
            jax.ShapeDtypeStruct((heads, tiles, 1, TILE), jnp.float32),
        ),
        scratch_shapes=[
            low(near, width),
            low(near, width),
            low(far, width),
            low(width, near),
            low(width, far),
        ],
        compiler_params=wide(60),
        name="attend",
    )(starts, sizes, query, key, value, context, *rims)


def attend_back(starts, sizes, query, key, value, context, rims, attended, grad, level):
    rows, width = query.shape
    near, far = rows + rims[0].shape[0], rows + rims[2].shape[0]
    low = lambda count: jax.ShapeDtypeStruct((count, width), jnp.bfloat16)
    full = lambda count: jax.ShapeDtypeStruct((count, width), jnp.float32)
    lows = lambda *shape: pltpu.VMEM(shape, jnp.bfloat16)
    fulls = lambda *shape: pltpu.VMEM(shape, jnp.float32)
    return pl.pallas_call(
        attend_back_kernel,
        in_specs=[SCALARS] * 2 + [VMEM] * 10,
        out_specs=[VMEM] * 7,
        out_shape=(
            low(rows),
            low(near - rows),
            low(near - rows),
            low(far - rows),
            full(rows),
            full(rows),
            full(rows),
        ),
        scratch_shapes=[
            lows(near, width),
            lows(near, width),
            lows(far, width),
            lows(width, near),
            lows(width, far),
            fulls(near, width),
            fulls(near, width),
            fulls(far, width),
        ],
        compiler_params=wide(60),
        name="attend_back",
    )(starts, sizes, query, key, value, context, *rims, attended, grad, level)


MESH = pl.DeviceIdType.MESH
ROWS = 1024


def bits_of(count):
    return count.bit_length() - 1


def mesh_bits():
    found = []
    tok, head = lax.axis_index("tok"), lax.axis_index("head")
    for axis in ("head", "tok"):
        for level in range(bits_of(lax.axis_size(axis))):
            at = head if axis == "head" else tok
            bit = (at // (1 << level)) % 2
            other = at + (1 - 2 * bit) * (1 << level)
            found.append((bit, (tok, other) if axis == "head" else (other, head)))
    return found


def greet(partners):
    barrier = pltpu.get_barrier_semaphore()
    for partner in partners:
        pl.semaphore_signal(barrier, inc=1, device_id=partner, device_id_type=MESH)
    pl.semaphore_wait(barrier, len(partners))


def halving_orders(bits):
    rest = list(range(4, bits))
    return [
        [0, 1, 2, 3] + rest,
        [0, 2, 1, 3] + rest,
        [0, 3, 2, 1] + rest,
        [0, 3, 1, 2] + rest,
        [0, 2, 3, 1] + rest,
    ]


def slot_of(block, order):
    place = 0
    for bit in order:
        place = place * 2 + (block // (1 << bit)) % 2
    return place


def unpack_refs(function, sizes):
    def kernel(*refs):
        grouped, at = [], 0
        for size in sizes:
            grouped.append(refs[at] if size == 0 else refs[at : at + max(size, 0)])
            at += 1 if size == 0 else max(size, 0)
        function(*grouped)

    return kernel


class Halver:
    def __init__(self, pieces, stages, arrivals, sems, ladder, orders):
        self.now, self.stages, self.arrivals, self.ladder = list(pieces), stages, arrivals, ladder
        self.sems, self.steps = sems, len(ladder)
        self.orders = [halving_orders(self.steps)[order] for order in orders]
        self.sent, self.flying, self.doing = [], {}, {}

    def half(self, stage):
        return 1 << (self.steps - 1 - stage)

    def send(self, number, stage):
        bit, partner = self.ladder[self.orders[number][stage]]
        at = number * len(self.stages) + self.stages.index(stage)
        half = self.half(stage)
        copy = pltpu.make_async_remote_copy(
            src_ref=self.now[number].at[pl.ds((1 - bit) * half, half)],
            dst_ref=self.arrivals[at],
            send_sem=self.sems.at[0, at],
            recv_sem=self.sems.at[1, at],
            device_id=partner,
            device_id_type=MESH,
        )
        copy.start()
        self.sent.append(copy)
        self.flying[number] = (copy, self.arrivals[at], bit * half)
        self.doing[number] = stage

    def absorb(self, number, stage, into=None):
        copy, arrival, keep = self.flying[number]
        copy.wait_recv()
        before = self.now[number]
        target = arrival if into is None else into

        def add(i, _):
            target[i] = before[keep + i] + arrival[i]
            return 0

        lax.fori_loop(0, self.half(stage), add, 0)
        self.now[number] = target

    def part(self, number, stage, keep, leave):
        copy, arrival, base = self.flying[number]
        copy.wait_recv()
        before, half = self.now[number], self.half(stage + 1)
        bit = self.ladder[self.orders[number][stage + 1]][0]
        for at, target in ((bit * half, keep), ((1 - bit) * half, leave)):

            def add(i, _):
                target[i] = before[base + at + i] + arrival[at + i]
                return 0

            lax.fori_loop(0, half, add, 0)

    def last(self, number):
        while self.doing[number] != self.stages[-1]:
            self.advance(number)
        copy, arrival, keep = self.flying[number]
        copy.wait_recv()
        return self.now[number][keep].astype(jnp.float32) + arrival[0].astype(jnp.float32)

    def step(self, stage, into=None):
        for number in range(len(self.now)):
            self.absorb(number, stage, None if into is None else into[number])
            if into is None:
                self.send(number, stage + 1)

    def advance(self, number):
        stage = self.doing[number]
        if stage != self.stages[-1]:
            self.absorb(number, stage)
            self.send(number, stage + 1)

    def begin(self):
        for number in range(len(self.now)):
            self.send(number, self.stages[0])

    def drain(self):
        for copy in self.sent:
            copy.wait_send()


def halver_scratch(pieces, stages, devices):
    steps = bits_of(devices)
    buffers = [
        pltpu.VMEM((1 << (steps - 1 - stage), block, width), jnp.bfloat16)
        for block, width in pieces
        for stage in stages
    ]
    sems = pltpu.SemaphoreType.DMA((2, max(len(buffers), 1)))
    return buffers, len(buffers) or -1, sems


def left_over(pieces, stages, devices):
    slots = 1 << (bits_of(devices) - 1 - stages[-1])
    return [jax.ShapeDtypeStruct((slots, block, width), jnp.bfloat16) for block, width in pieces]


def fill(left, right, start, stop, target, column, order):
    block = target.shape[1]
    each = ROWS // block
    for low in range(start, stop, ROWS):
        high = min(low + ROWS, stop)
        to = column + low - start

        def some_rows(chunk, _):
            at = pl.ds(pl.multiple_of(chunk * ROWS, ROWS), ROWS)
            found = lax.dot_general(
                left[:, at],
                right[:, low:high],
                (((0,), (0,)), ((), ())),
                preferred_element_type=jnp.float32,
            ).astype(jnp.bfloat16)
            for inner in range(each):
                target[slot_of(chunk * each + inner, order), :, to : to + high - low] = found[
                    inner * block : (inner + 1) * block
                ]
            return 0

        lax.fori_loop(0, left.shape[1] // ROWS, some_rows, 0)


def stage_groups(devices):
    steps = bits_of(devices)
    return [0, 1], list(range(2, steps - 1)), [steps - 1]


DOWN_PARTS = (256, 384, 384)
DOWN_ORDERS = (0, 1, 3)
UP_ORDERS = (0, 4, 3)


def swapped(shard, bit):
    heads = bits_of(lax.axis_size("head"))
    axis, level = ("head", bit) if bit < heads else ("tok", bit - heads)
    pairs = [(i, i ^ (1 << level)) for i in range(lax.axis_size(axis))]
    return lax.ppermute(shard, axis, pairs)


UP_PARTS = (((0, 0, 2304),), ((0, 2304, 3840),), ((0, 3840, 4096), (1, 0, 1024)))
UP_WIDTHS = (2304, 1536, 1280)


def products_apart(lefts, rights):
    return [
        lax.psum_scatter(product_left(left, right), ("tok", "head"), scatter_dimension=0, tiled=True)
        for left, right in zip(lefts, rights)
    ]


def tok_peers():
    count, here = lax.axis_size("tok"), lax.axis_index("tok")
    head = lax.axis_index("head")
    return [
        ((lax.rem(here + step, count), head), lax.rem(here + count - step, count))
        for step in range(1, count)
    ]


def share(mine, every, send_sems, recv_sems, place, peers):
    copies = []
    for step, (target, _) in enumerate(peers):
        copy = pltpu.make_async_remote_copy(
            src_ref=mine,
            dst_ref=every.at[place],
            send_sem=send_sems.at[step],
            recv_sem=recv_sems.at[step],
            device_id=target,
            device_id_type=MESH,
        )
        copy.start()
        copies.append(copy)
    return copies


def row_norm(rows, gain, bias):
    rows = rows.astype(jnp.float32)
    centred = rows - jnp.mean(rows, axis=-1, keepdims=True)
    spread_ = jnp.mean(centred * centred, axis=-1, keepdims=True)
    return (centred * lax.rsqrt(spread_ + epsilon) * gain + bias).astype(jnp.bfloat16)


PIECE = 128


def head_backward_kernel(
    stages,
    back_query,
    back_key,
    back_value,
    back_feed,
    hid,
    weights,
    tokens,
    gain,
    grad_middle,
    sums,
    lag_sums,
    skip_sum,
    vectors,
    grad_up_bias,
    up_in,
    input_grad,
    grad_weights,
    row_sum,
    vector_sum,
    up_out,
    total,
    parts,
    near_in,
    far_in,
    products,
    arrived,
    shares,
    head_sems,
    tok_sends,
    tok_recvs,
    share_sends,
    share_recvs,
    every_row,
    row_sends,
    row_recvs,
    vector_parts,
    every_vector,
    tok_sum,
    head_sums,
    vector_sems,
    swap_sems,
    up_arrivals,
    up_sems,
):
    tok, head = lax.axis_index("tok"), lax.axis_index("head")
    heads, toks = lax.axis_size("head"), lax.axis_size("tok")
    near = head + 1 - 2 * lax.rem(head, 2)
    far = head + 2 - 4 * (head // 2)
    across_ = near + 2 - 4 * (near // 2)
    head_peers = [lax.rem(head + step, heads) for step in range(1, heads)]
    ladder = mesh_bits()[bits_of(heads) :]
    peers = tok_peers()
    greet([(tok, other) for other in head_peers] + [target for target, _ in peers])
    rows = input_grad.shape[0]
    states = sums.shape[0]
    every_row[tok] = jnp.zeros_like(every_row[tok])
    every_row[tok, :states] = sums[...]
    every_row[tok, states : 2 * states] = lag_sums[...]
    every_row[tok, 2 * states : 2 * states + 1] = skip_sum[...]
    row_copies = share(every_row.at[tok], every_row, row_sends, row_recvs, tok, peers)
    width = back_query.shape[1]
    columns_ = pl.ds(pl.multiple_of(head * width, HD), width)

    def block_of(owner):
        return pl.ds(pl.multiple_of(owner * rows, PIECE), rows)

    def partial(owner):
        at = block_of(owner)
        found = across(back_query[at, :], weights[:, :width])
        found += across(back_key[at, :], weights[:, width : 2 * width])
        found += across(back_value[at, :], weights[:, 2 * width :])
        total[...] = found
        total[:, columns_] += back_feed[at, :].astype(jnp.float32)

    def copy(source, target, device, number):
        one = pltpu.make_async_remote_copy(
            src_ref=source,
            dst_ref=target,
            send_sem=head_sems.at[0, number],
            recv_sem=head_sems.at[1, number],
            device_id=(tok, device),
            device_id_type=MESH,
        )
        one.start()
        return one

    up_stages = stages[1] + stages[2]
    up = Halver(up_in, up_stages, up_arrivals, up_sems, mesh_bits(), UP_ORDERS)
    up.begin()
    partial(across_)
    parts[0] = total[...].astype(jnp.bfloat16)
    first = copy(parts.at[0], near_in.at[0], near, 0)
    partial(near)
    parts[1] = total[...].astype(jnp.bfloat16)
    second = copy(parts.at[1], near_in.at[1], near, 1)
    partial(far)
    first.wait_recv()
    parts[2] = (total[...] + near_in[0].astype(jnp.float32)).astype(jnp.bfloat16)
    third = copy(parts.at[2], far_in, far, 2)

    steps = len(ladder)
    orders = [list(range(steps)), [1, 0] + list(range(2, steps))]
    each = products[0].shape[1]
    half_width = products[0].shape[2]
    depth = hid.shape[1]
    base = [0, 0]
    sent = []

    def forward(number, stage):
        bit, partner = ladder[orders[number][stage]]
        half = 1 << (steps - 1 - stage)
        one = pltpu.make_async_remote_copy(
            src_ref=products[number].at[pl.ds(base[number] + (1 - bit) * half, half)],
            dst_ref=arrived[number * steps + stage],
            send_sem=tok_sends.at[number, stage],
            recv_sem=tok_recvs.at[number, stage],
            device_id=partner,
            device_id_type=MESH,
        )
        one.start()
        sent.append(one)
        base[number] = base[number] + bit * half
        return one

    def joined(at, number):
        if number == 0:
            return jnp.concatenate([back_query[at, :], back_key[at, : half_width - width]], axis=1)
        return jnp.concatenate([back_key[at, half_width - width :], back_value[at, :]], axis=1)

    everything = pl.ds(0, hid.shape[0])
    flying = []
    for number in range(2):
        right = joined(everything, number)
        for start in range(0, depth, TILE):
            found = lax.dot_general(
                hid[:, start : start + TILE],
                right,
                (((0,), (0,)), ((), ())),
                preferred_element_type=jnp.float32,
            ).astype(jnp.bfloat16)
            for inner in range(TILE // each):
                products[number][slot_of(start // each + inner, orders[number])] = found[
                    inner * each : (inner + 1) * each
                ]
        flying.append(forward(number, 0))

    for number in (1, 2, 0) if up_in else ():
        up.advance(number)
    partial(head)
    second.wait_recv()
    total[...] += near_in[1].astype(jnp.float32)

    done = []
    for stage in range(steps):
        for number in range(2):
            flying[number].wait_recv()
            arrival = arrived[number * steps + stage]
            half = 1 << (steps - 1 - stage)
            if stage == steps - 1:
                done.append(
                    products[number][base[number]].astype(jnp.float32)
                    + arrival[0].astype(jnp.float32)
                )
            else:
                for i in range(half):
                    products[number][base[number] + i] = (
                        products[number][base[number] + i] + arrival[i]
                    )
                flying[number] = forward(number, stage + 1)
        for number in ((2, 1), (0,), ())[min(stage, 2)] if up_in else ():
            up.advance(number)
        if stage == steps - 2:
            third.wait_recv()
            back = total[...] + far_in[...].astype(jnp.float32)
            found = tokens[...].astype(jnp.float32)
            centred = found - jnp.mean(found, axis=-1, keepdims=True)
            scale = lax.rsqrt(jnp.mean(centred * centred, axis=-1, keepdims=True) + epsilon)
            shaped = centred * scale
            lists = [jnp.sum(back * shaped, axis=0, keepdims=True), jnp.sum(back, axis=0, keepdims=True)]
            lists += [vectors[i : i + 1, :] for i in range(3)]
            part = depth // toks
            for place in range(toks):
                for i, row in enumerate(lists):
                    vector_parts[place, i : i + 1, :part] = row[:, place * part : (place + 1) * part]
                for i in range(grad_up_bias.shape[1] // depth):
                    start = place * part * (grad_up_bias.shape[1] // depth) + i * part
                    vector_parts[place, len(lists) + i : len(lists) + i + 1, :part] = grad_up_bias[
                        :, start : start + part
                    ]
            every_vector[tok] = vector_parts[tok]
            vector_copies = []
            for step, (target, _) in enumerate(peers):
                one = pltpu.make_async_remote_copy(
                    src_ref=vector_parts.at[target[0]],
                    dst_ref=every_vector.at[tok],
                    send_sem=vector_sems.at[0, step],
                    recv_sem=vector_sems.at[1, step],
                    device_id=target,
                    device_id_type=MESH,
                )
                one.start()
                vector_copies.append(one)
            back = back * gain[...]
            back = back - jnp.mean(back, axis=-1, keepdims=True)
            back = back - shaped * jnp.mean(back * shaped, axis=-1, keepdims=True)
            input_grad[...] = grad_middle[...] + back * scale
    small = each // heads
    ready, landed = shares
    for other in range(heads):
        for number in range(2):
            ready[other, :, number * half_width : (number + 1) * half_width] = done[number][
                other * small : (other + 1) * small
            ]
    landed[head] = ready[head]
    swaps = []
    for step, other in enumerate(head_peers):
        one = pltpu.make_async_remote_copy(
            src_ref=ready.at[other],
            dst_ref=landed.at[head],
            send_sem=share_sends.at[step],
            recv_sem=share_recvs.at[step],
            device_id=(tok, other),
            device_id_type=MESH,
        )
        one.start()
        swaps.append(one)

    for one in row_copies + vector_copies:
        one.wait_recv()
    row_sum[...] = jnp.sum(every_row[...], axis=0)
    tok_sum[...] = jnp.sum(every_vector[...], axis=0)
    head_sums[head] = tok_sum[...]
    head_copies = []
    for step, other in enumerate(head_peers):
        one = pltpu.make_async_remote_copy(
            src_ref=tok_sum,
            dst_ref=head_sums.at[head],
            send_sem=swap_sems.at[0, step],
            recv_sem=swap_sems.at[1, step],
            device_id=(tok, other),
            device_id_type=MESH,
        )
        one.start()
        head_copies.append(one)
    for one in swaps:
        one.wait()
    for other in range(heads):
        for kind in range(3):
            grad_weights[kind][:, other * width : (other + 1) * width] = landed[
                other, :, kind * width : (kind + 1) * width
            ]
    for one in head_copies:
        one.wait_recv()
    vector_sum[...] = jnp.sum(head_sums[...], axis=0)
    for number in range(len(up_in)):
        found, column = up.last(number), 0
        for pair, start, stop in UP_PARTS[number]:
            up_out[pair][:, start:stop] = found[:, column : column + stop - start]
            column += stop - start
    up.drain()
    for one in sent + [first, second, third] + row_copies + vector_copies + head_copies:
        one.wait_send()


def head_backward(
    back_query,
    back_key,
    back_value,
    back_feed,
    hid,
    weights,
    tokens,
    gain,
    grad_middle,
    sums,
    lag_sums,
    skip_sum,
    vectors,
    grad_up_bias,
    up,
    collective_id,
):
    span, width = back_query.shape
    depth = hid.shape[1]
    heads, toks = lax.axis_size("head"), lax.axis_size("tok")
    rows, each = span // heads, depth // toks
    steps, half_width = bits_of(toks), 3 * width // 2
    devices = heads * toks
    stages = stage_groups(devices)
    up_pieces = [piece.shape[1:] for piece in up]
    up_buffers, up_count, up_sems = halver_scratch(up_pieces, stages[1] + stages[2], devices)
    outs = []
    for pair in range(2 if up else 0):
        stop = max(part[2] for parts in UP_PARTS for part in parts if part[0] == pair)
        outs.append(jax.ShapeDtypeStruct((up_pieces[0][0], stop), jnp.float32))
    states = sums.shape[0]
    states += -states % SUB
    row_count = 2 * states + SUB
    part = (16, max(depth // toks, HD))
    ups = len(up) or -1
    low = lambda *shape: pltpu.VMEM(shape, jnp.bfloat16)
    full = lambda *shape: pltpu.VMEM(shape, jnp.float32)
    sems = lambda *shape: pltpu.SemaphoreType.DMA(shape)
    sizes = [0] * 14 + [ups, 0, 3, 0, 0, len(outs) or -1] + [0] * 4 + [2, 2 * steps, 2]
    sizes += [0] * 5 + [0] * 9 + [up_count, 0]
    found = pl.pallas_call(
        unpack_refs(functools.partial(head_backward_kernel, stages), sizes),
        in_specs=[VMEM] * (14 + len(up)),
        out_specs=[VMEM] * (6 + len(outs)),
        out_shape=[
            jax.ShapeDtypeStruct((rows, depth), jnp.float32),
        ]
        + [jax.ShapeDtypeStruct((each // heads, depth), jnp.float32)] * 3
        + [
            jax.ShapeDtypeStruct((row_count, width), jnp.float32),
            jax.ShapeDtypeStruct(part, jnp.float32),
        ]
        + outs,
        scratch_shapes=[
            full(rows, depth),
            low(3, rows, depth),
            low(2, rows, depth),
            low(rows, depth),
        ]
        + [low(toks, each, half_width)] * 2
        + [low(1 << (steps - 1 - stage), each, half_width) for stage in range(steps)] * 2
        + [full(heads, each // heads, 3 * width)] * 2
        + [sems(2, 3), sems(2, steps), sems(2, steps), sems(heads - 1), sems(heads - 1)]
        + [full(toks, row_count, width), sems(toks - 1), sems(toks - 1)]
        + [full(toks, *part), full(toks, *part), full(*part), full(heads, *part)]
        + [sems(2, toks - 1), sems(2, heads - 1)]
        + up_buffers
        + [up_sems],
        compiler_params=pltpu.CompilerParams(
            collective_id=collective_id, has_side_effects=True, vmem_limit_bytes=58 * MIB
        ),
        name="head_backward",
    )(
        back_query,
        back_key,
        back_value,
        back_feed,
        hid,
        weights,
        tokens,
        gain,
        grad_middle,
        sums,
        lag_sums,
        skip_sum,
        vectors,
        grad_up_bias,
        *up,
    )
    return found[0], found[1:4], found[4], found[5], found[6:]


def every_step(length, second, back, body, carry):
    begins = lax.broadcasted_iota(jnp.int32, (SUB, HD), 0) * length - second

    def some(block, now):
        for inner in range(UNROLL):
            t = block * UNROLL + inner
            at = length - 1 - t if back else t
            now = body(at, now, jnp.where(begins == -at, 0.0, 1.0))
        return now

    return lax.fori_loop(0, length // UNROLL, some, carry)


def kept(second, begin, end):
    return jnp.where((second >= begin) & (second < end), 0.0, 1.0)


def decay_tables(rate, span):
    length = span // SUB
    return (
        jnp.exp(-rate),
        jnp.exp(-rate * length),
        length * jnp.exp(-rate * (length - 1)),
        jnp.exp(-rate * span),
        span * jnp.exp(-rate * (span - 1)),
    )


def front_kernel(
    seq_starts,
    tokens,
    gain,
    bias,
    rate,
    mix,
    skip,
    w_query,
    w_key,
    w_value,
    hid,
    query,
    key,
    value,
    feed_rows,
    weights,
    context,
    key_rim,
    value_rim,
    context_rim,
    gathered,
    drives,
    total,
    ends,
    mine,
    every,
    send_sems,
    recv_sems,
    load_sems,
    share_sends,
    share_recvs,
    rim_sems,
):
    tok, head = lax.axis_index("tok"), lax.axis_index("head")
    near = head + 1 - 2 * lax.rem(head, 2)
    far = head + 2 - 4 * (head // 2)
    across_ = near + 2 - 4 * (near // 2)
    peers = tok_peers()
    greet([(tok, near), (tok, far)] + [target for target, _ in peers])
    rows = tokens.shape[0]
    pieces = rows // PIECE
    width = query.shape[1]
    columns_ = pl.ds(pl.multiple_of(head * width, HD), width)
    loads = [
        pltpu.make_async_copy(
            whole.at[:, columns_], weights.at[:, pl.ds(kind * width, width)], load_sems.at[kind]
        )
        for kind, whole in enumerate((w_query, w_key, w_value))
    ]
    for load in loads:
        load.start()

    def copy(source, owner, target, number):
        return pltpu.make_async_remote_copy(
            src_ref=source,
            dst_ref=gathered.at[owner, pl.ds(number % pieces * PIECE, PIECE)],
            send_sem=send_sems.at[number],
            recv_sem=recv_sems.at[number],
            device_id=(tok, target),
            device_id_type=MESH,
        )

    def own(number):
        return tokens.at[pl.ds(number * PIECE, PIECE)]

    afar = [copy(own(i), head, far, i) for i in range(pieces)]
    beside = [copy(own(i), head, near, pieces + i) for i in range(pieces)]
    for one in afar + beside:
        one.start()

    def work(found, owner, number):
        at = pl.ds(pl.multiple_of(owner * rows + number * PIECE, PIECE), PIECE)
        low = row_norm(found, gain[...], bias[...])
        hid[at, :] = low
        feed_rows[at, :] = hid[at, columns_]
        mixed = jnp.dot(low, weights[...], preferred_element_type=jnp.float32).astype(
            jnp.bfloat16
        )
        query[at, :] = mixed[:, :width]
        key[at, :] = mixed[:, width : 2 * width]
        value[at, :] = mixed[:, 2 * width :]

    def block(owner, number):
        return gathered[owner, number * PIECE : (number + 1) * PIECE, :]

    for load in loads:
        load.wait()
    for i in range(pieces):
        work(tokens[i * PIECE : (i + 1) * PIECE, :], head, i)
    for i in range(pieces):
        beside[i].wait_recv()
        work(block(near, i), near, i)
    passed = []
    for i in range(pieces):
        afar[i].wait_recv()
        one = copy(
            gathered.at[far, pl.ds(i * PIECE, PIECE)], far, near, 2 * pieces + i
        )
        one.start()
        passed.append(one)
        work(block(far, i), far, i)
    for i in range(pieces):
        passed[i].wait_recv()
        work(block(across_, i), across_, i)

    here, count = tok, every.shape[0]
    decay, chunk_decay, _, span_decay, _ = decay_tables(rate[...], feed_rows.shape[0])
    length = feed_rows.shape[0] // SUB
    span = feed_rows.shape[0]
    second = seq_starts[1] - here * span
    keep = [kept(second, chunk * length, (chunk + 1) * length) for chunk in range(SUB)]
    groups = feed_rows.shape[1] // HD
    zero = jnp.zeros((SUB, HD), jnp.float32)

    def rim(source, target, number):
        copy = pltpu.make_async_remote_copy(
            src_ref=source,
            dst_ref=target,
            send_sem=rim_sems.at[0, number],
            recv_sem=rim_sems.at[1, number],
            device_id=peers[0][0],
            device_id_type=MESH,
        )

        @pl.when(here < count - 1)
        def _():
            copy.start()

        return copy

    @pl.when(here == 0)
    def _():
        for target in (key_rim, value_rim, context_rim):
            target[...] = jnp.zeros_like(target)

    for group in range(groups):
        lanes = slice(group * HD, (group + 1) * HD)
        drives[group] = feed_rows[:, lanes].astype(jnp.float32)
        factors = [spread(decay[:, lanes], n) for n in range(NS)]

        def end_step(t, states, live):
            drive = drives[group, pl.ds(t, SUB, stride=length), :]
            return tuple(s * live * f + drive for s, f in zip(states, factors))

        done = every_step(length, second, False, end_step, (zero,) * NS)
        for n in range(NS):
            ends[n, :, lanes] = done[n]
    now = ends[:, 0, :]
    for chunk in range(1, SUB):
        now = keep[chunk] * (chunk_decay * now) + ends[:, chunk, :]
    mine[...] = now
    every[here] = now
    copies = share(mine, every, share_sends, share_recvs, here, peers)
    window = key_rim.shape[0]
    sent = [
        rim(key.at[pl.ds(span - window, window)], key_rim, 0),
        rim(value.at[pl.ds(span - window, window)], value_rim, 1),
    ]
    for copy in copies:
        copy.wait()
    now = jnp.zeros_like(span_decay)
    for place in range(count - 1):
        whole = kept(seq_starts[1], place * span, (place + 1) * span)
        now = jnp.where(place < here, whole * (span_decay * now) + every[place], now)
    for chunk in range(SUB):
        own = ends[:, chunk, :]
        ends[:, chunk, :] = now
        now = keep[chunk] * (chunk_decay * now) + own

    window = context_rim.shape[0]
    for group in range(groups):
        lanes = slice(group * HD, (group + 1) * HD)
        factors = [spread(decay[:, lanes], n) for n in range(NS)]
        mixes = [spread(mix[:, lanes], n) for n in range(NS)]
        direct = spread(skip[:, lanes], 0)

        def out_step(t, states, live):
            at = pl.ds(t, SUB, stride=length)
            drive = drives[group, at, :]
            states = tuple(s * live * f + drive for s, f in zip(states, factors))
            parts = [state * weight for state, weight in zip(states, mixes)] + [direct * drive]
            while len(parts) > 1:
                parts = [a + b for a, b in zip(parts[::2], parts[1::2])] + (
                    [parts[-1]] if len(parts) % 2 else []
                )
            total[group, at, :] = parts[0]
            return states

        every_step(
            length, second, False, out_step, tuple(ends[n, :, lanes] for n in range(NS))
        )
        context[:, lanes] = total[group].astype(context.dtype)
        sent.append(
            rim(
                context.at[pl.ds(span - window, window), pl.ds(group * HD, HD)],
                context_rim.at[:, pl.ds(group * HD, HD)],
                2 + group,
            )
        )
    @pl.when(here > 0)
    def _():
        for copy in sent:
            copy.wait_recv()

    @pl.when(here < count - 1)
    def _():
        for copy in sent:
            copy.wait_send()

    for one in afar + beside + passed:
        one.wait_send()


def front(seq_starts, tokens, gain, bias, rate, mix, skip, w_query, w_key, w_value, collective_id):
    rows, depth = tokens.shape
    heads, toks = lax.axis_size("head"), lax.axis_size("tok")
    span, width = rows * heads, w_query.shape[1] // heads
    groups, window = width // HD, 2 * BLOCK
    low = lambda count: jax.ShapeDtypeStruct((span, count), jnp.bfloat16)
    rim = lambda count: jax.ShapeDtypeStruct((count, width), jnp.bfloat16)
    fulls = lambda *shape: pltpu.VMEM(shape, jnp.float32)
    sems = lambda *shape: pltpu.SemaphoreType.DMA(shape)
    found = pl.pallas_call(
        front_kernel,
        in_specs=[SCALARS] + [VMEM] * 6 + [pl.BlockSpec(memory_space=pl.ANY)] * 3,
        out_specs=[VMEM] * 10,
        out_shape=[
            low(depth),
            low(width),
            low(width),
            low(width),
            low(width),
            jax.ShapeDtypeStruct((depth, 3 * width), jnp.bfloat16),
            low(width),
            rim(window),
            rim(window),
            rim(window + CTX),
        ],
        scratch_shapes=[
            pltpu.VMEM((heads, rows, depth), jnp.bfloat16),
            fulls(groups, span, HD),
            fulls(groups, span, HD),
            fulls(NS, SUB, width),
            fulls(NS, width),
            fulls(toks, NS, width),
            sems(3 * (rows // PIECE)),
            sems(3 * (rows // PIECE)),
            sems(3),
            sems(toks - 1),
            sems(toks - 1),
            sems(2, 2 + groups),
        ],
        compiler_params=pltpu.CompilerParams(
            collective_id=collective_id, has_side_effects=True, vmem_limit_bytes=60 * MIB
        ),
        name="front",
    )(seq_starts, tokens, gain, bias, rate, mix, skip, w_query, w_key, w_value)
    return tuple(found[:7]) + (found[7:],)


def recurrence_back_kernel(
    stages,
    seq_starts,
    slope,
    feed_rows,
    rate,
    mix,
    skip,
    key_sum,
    value_sum,
    key_rim,
    value_rim,
    context_rim,
    lefts,
    rights,
    down_keep,
    down_come,
    back_key,
    back_value,
    back,
    sums,
    lag_sums,
    skip_sum,
    down_out,
    up_out,
    slopes,
    rows,
    total,
    ends,
    lags,
    mine,
    every,
    share_sends,
    share_recvs,
    key_in,
    value_in,
    context_in,
    rim_sems,
    down_now,
    down_arrivals,
    down_sems,
    grads,
    up_arrivals,
    up_sems,
):
    here, count = lax.axis_index("tok"), every.shape[0]
    peers = tok_peers()
    ladder = mesh_bits()
    heads = bits_of(lax.axis_size("head"))
    greet([target for target, _ in peers] + [partner for _, partner in ladder[:heads]])

    rims = []
    for number, (source, target) in enumerate(
        ((context_rim, context_in), (key_rim, key_in), (value_rim, value_in))
    ):
        rims.append(
            pltpu.make_async_remote_copy(
                src_ref=source,
                dst_ref=target,
                send_sem=rim_sems.at[0, number],
                recv_sem=rim_sems.at[1, number],
                device_id=peers[-1][0],
                device_id_type=MESH,
            )
        )

    @pl.when(here == count - 1)
    def _():
        for target in (context_in, key_in, value_in):
            target[...] = jnp.zeros_like(target)

    @pl.when(here > 0)
    def _():
        for copy in rims:
            copy.start()

    down_stages = stages[1] + stages[2]
    down = Halver(down_now, down_stages, down_arrivals, down_sems, ladder, DOWN_ORDERS)
    for number in (1, 2, 0):
        down_now[number][...] = down_keep[number][...] + down_come[number][...]
        if number:
            down.send(number, down_stages[0])
    up = Halver(grads, stages[0], up_arrivals, up_sems, ladder, UP_ORDERS)
    for number, parts in enumerate(UP_PARTS if grads else ()):
        column = 0
        for pair, start, stop in parts:
            fill(
                lefts[pair], rights[pair], start, stop, grads[number], column, up.orders[number]
            )
            column += stop - start
        up.send(number, stages[0][0])
    if grads:
        up.absorb(0, stages[0][0])
        up.send(0, stages[0][1])

    @pl.when(here < count - 1)
    def _():
        rims[0].wait_recv()

    span = slope.shape[0]
    decay, factor, bend, over, over_slope = decay_tables(rate[...], span)
    length = span // SUB
    second = seq_starts[1] - here * span
    keep = [kept(second, chunk * length, (chunk + 1) * length) for chunk in range(SUB)]
    groups = slope.shape[1] // HD
    zero = jnp.zeros((SUB, HD), jnp.float32)
    for group in range(groups):
        lanes = slice(group * HD, (group + 1) * HD)
        slopes[group] = slope[:, lanes]
        slopes[group, span - context_in.shape[0] :, :] += context_in[:, lanes].astype(jnp.float32)
        rows[group] = feed_rows[:, lanes].astype(jnp.float32)
        total[group] = slopes[group] * skip[:, lanes]
        skip_sum[:, lanes] = jnp.sum(slopes[group] * rows[group], axis=0, keepdims=True)
        factors = [spread(decay[:, lanes], n) for n in range(NS)]

        def end_step(t, carry, live):
            drive = slopes[group, pl.ds(t, SUB, stride=length), :]
            adjoint, lag = carry[:NS], carry[NS:]
            lag = [(a * f + b) * live for a, f, b in zip(lag, factors, adjoint)]
            adjoint = [(a * f + drive) * live for a, f in zip(adjoint, factors)]
            return tuple(adjoint) + tuple(lag)

        done = every_step(length, second, True, end_step, (zero,) * (2 * NS))
        for n in range(NS):
            ends[n, :, lanes] = done[n]
            lags[n, :, lanes] = done[NS + n]

    now, late = ends[:, SUB - 1, :], lags[:, SUB - 1, :]
    for chunk in reversed(range(SUB - 1)):
        late = keep[chunk] * (factor * late + bend * now) + lags[:, chunk, :]
        now = keep[chunk] * (factor * now) + ends[:, chunk, :]
    mine[0] = now
    mine[1] = late
    every[here, 0] = now
    every[here, 1] = late
    copies = share(mine, every, share_sends, share_recvs, here, peers)

    down.send(0, down_stages[0])
    down.advance(1)
    down.advance(2)
    for number in range(1, len(grads)):
        up.absorb(number, stages[0][0])
        up.send(number, stages[0][1])
    for copy in copies:
        copy.wait()
    now, late = jnp.zeros_like(over), jnp.zeros_like(over)
    for place in reversed(range(1, count)):
        reached = place > here
        whole = kept(seq_starts[1], place * span, (place + 1) * span)
        late = jnp.where(reached, whole * (over * late + over_slope * now) + every[place, 1], late)
        now = jnp.where(reached, whole * (over * now) + every[place, 0], now)
    for chunk in reversed(range(SUB)):
        own, own_late = ends[:, chunk, :], lags[:, chunk, :]
        ends[:, chunk, :] = now
        lags[:, chunk, :] = late
        late = keep[chunk] * (factor * late + bend * now) + own_late
        now = keep[chunk] * (factor * now) + own

    for group in range(groups):
        lanes = slice(group * HD, (group + 1) * HD)
        for base in range(0, NS, HALF):
            factors = [spread(decay[:, lanes], base + n) for n in range(HALF)]
            mixes = [spread(mix[:, lanes], base + n) for n in range(HALF)]

            def out_step(t, carry, live):
                at = pl.ds(t, SUB, stride=length)
                drive, source = slopes[group, at, :], rows[group, at, :]
                adjoint, lag = carry[:HALF], carry[HALF : 2 * HALF]
                direct, late_sum = carry[2 * HALF : 3 * HALF], carry[3 * HALF :]
                lag = [a * f + b for a, f, b in zip(lag, factors, adjoint)]
                adjoint = [a * f + drive for a, f in zip(adjoint, factors)]
                direct = [a + b * source for a, b in zip(direct, adjoint)]
                late_sum = [a + b * source for a, b in zip(late_sum, lag)]
                parts = [a * b for a, b in zip(adjoint, mixes)]
                while len(parts) > 1:
                    parts = [a + b for a, b in zip(parts[::2], parts[1::2])]
                total[group, at, :] = total[group, at, :] + parts[0]
                lag = [a * live for a in lag]
                adjoint = [a * live for a in adjoint]
                return tuple(adjoint) + tuple(lag) + tuple(direct) + tuple(late_sum)

            if group == 0 and base > 0:
                down.advance(0)
                down.advance(1)
                down.advance(2)
            if group == 1 and base == 0:
                down.advance(0)
            first = tuple(ends[base + n, :, lanes] for n in range(HALF)) + tuple(
                lags[base + n, :, lanes] for n in range(HALF)
            )
            done = every_step(length, second, True, out_step, first + (zero,) * (2 * HALF))
            for n in range(HALF):
                sums[base + n : base + n + 1, lanes] = jnp.sum(
                    done[2 * HALF + n], axis=0, keepdims=True
                )
                lag_sums[base + n : base + n + 1, lanes] = jnp.sum(
                    done[3 * HALF + n], axis=0, keepdims=True
                )
        back[:, lanes] = total[group].astype(back.dtype)
    finished = [down.last(number) for number in range(len(down_now))]
    column = 0
    for piece in finished:
        down_out[:, column : column + piece.shape[1]] = piece
        column += piece.shape[1]

    @pl.when(here < count - 1)
    def _():
        rims[1].wait_recv()
        rims[2].wait_recv()

    inner = span - key_in.shape[0]
    for source, more, target in (
        (key_sum, key_in, back_key),
        (value_sum, value_in, back_value),
    ):
        target[:inner, :] = source[:inner, :].astype(target.dtype)
        target[inner:, :] = (source[inner:, :] + more[...].astype(jnp.float32)).astype(
            target.dtype
        )
    up.step(stages[0][1], up_out)
    down.drain()
    up.drain()

    @pl.when(here > 0)
    def _():
        for copy in rims:
            copy.wait_send()


def recurrence_back(
    seq_starts, slope, feed_rows, rate, mix, skip, sums, rims, lefts, rights, down, collective_id
):
    span, width = feed_rows.shape
    toks = lax.axis_size("tok")
    devices = toks * lax.axis_size("head")
    stages = stage_groups(devices)
    block = lefts[0].shape[1] // devices
    apart, up_pieces = None, [(block, part) for part in UP_WIDTHS]
    if block < 16:
        apart = products_apart(lefts, rights)
        lefts, rights, up_pieces = [], [], []
    keep, come = down
    down_pieces = [piece.shape[1:] for piece in keep]
    late = stages[1] + stages[2]
    down_buffers, down_count, down_sems = halver_scratch(down_pieces, late, devices)
    up_buffers, up_count, up_sems = halver_scratch(up_pieces, stages[0], devices)
    down_width = sum(piece[1] for piece in down_pieces)
    up_shapes = left_over(up_pieces, stages[0], devices)
    full = lambda *shape: jax.ShapeDtypeStruct(shape, jnp.float32)
    fulls = lambda *shape: pltpu.VMEM(shape, jnp.float32)
    sems = lambda *shape: pltpu.SemaphoreType.DMA(shape)
    groups = width // HD
    scratch = [
        fulls(groups, span, HD),
        fulls(groups, span, HD),
        fulls(groups, span, HD),
        fulls(NS, SUB, width),
        fulls(NS, SUB, width),
        fulls(2, NS, width),
        fulls(toks, 2, NS, width),
        sems(toks - 1),
        sems(toks - 1),
    ]
    low = lambda count: jax.ShapeDtypeStruct((count, width), jnp.bfloat16)
    scratch += [pltpu.VMEM(rims[k].shape, jnp.bfloat16) for k in (0, 1, 2)]
    scratch += [sems(2, 3)] + [pltpu.VMEM(piece.shape, jnp.bfloat16) for piece in keep]
    scratch += down_buffers + [down_sems]
    scratch += [pltpu.VMEM((devices,) + piece, jnp.bfloat16) for piece in up_pieces]
    scratch += up_buffers + [up_sems]
    pairs, ups, downs = len(lefts) or -1, len(up_pieces) or -1, len(keep)
    sizes = [0] * 11 + [pairs, pairs, downs, downs] + [0] * 6 + [0, ups] + [0] * 9
    sizes += [0] * 4 + [downs, down_count, 0, ups, up_count, 0]
    found = pl.pallas_call(
        unpack_refs(functools.partial(recurrence_back_kernel, stages), sizes),
        in_specs=[SCALARS] + [VMEM] * (10 + 2 * len(lefts) + 2 * downs),
        out_specs=[VMEM] * (7 + len(up_shapes)),
        out_shape=[
            low(span),
            low(span),
            low(span),
            full(NS, width),
            full(NS, width),
            full(1, width),
        ]
        + [full(down_pieces[0][0], down_width)]
        + up_shapes,
        scratch_shapes=scratch,
        compiler_params=pltpu.CompilerParams(
            collective_id=collective_id, has_side_effects=True, vmem_limit_bytes=60 * MIB
        ),
        name="recurrence_back",
    )(
        seq_starts,
        slope,
        feed_rows,
        rate,
        mix,
        skip,
        *sums,
        *rims,
        *lefts,
        *rights,
        *keep,
        *come,
    )
    return tuple(found[:6]) + (found[6], found[7:], apart)


CHUNK = 1024
UP_CHUNK = 512
ROOT = math.sqrt(2.0 / math.pi)
CUBIC = 0.044715


def feed_kernel(
    stages,
    attended,
    tokens,
    out_grad,
    gain,
    bias,
    up_bias,
    down_bias,
    w_output,
    w_up,
    w_down,
    layer_out,
    grad_middle,
    normed,
    grad_before,
    joined,
    grad_branch,
    grad_att,
    down_left,
    vectors,
    grad_up_bias,
    output_w,
    up_w,
    down_w,
    split,
    active,
    bend,
    drive,
    shape,
    down_sum,
    back_sum,
    grad_split,
    grads,
    arrivals,
    weight_sems,
    down_sems,
    head_sems,
    halver_sems,
):
    tok, head = lax.axis_index("tok"), lax.axis_index("head")
    heads = lax.axis_size("head")
    rows, width = tokens.shape[0], attended.shape[1]
    hidden = up_w.shape[1]
    loads = [
        pltpu.make_async_copy(source, target, weight_sems.at[number])
        for number, (source, target) in enumerate(
            ((w_output, output_w), (w_up, up_w))
        )
    ]

    def down_load(chunk):
        slot = lax.rem(chunk, 2)
        return pltpu.make_async_copy(
            w_down.at[pl.ds(pl.multiple_of(chunk * CHUNK, CHUNK), CHUNK)],
            down_w.at[slot],
            down_sems.at[slot],
        )

    for load in loads:
        load.start()
    for chunk in range(2):
        down_load(chunk).start()
    peers = [lax.rem(head + step, heads) for step in range(1, heads)]
    ladder = mesh_bits()
    greet([(tok, other) for other in peers] + [p for _, p in ladder[bits_of(heads) :]])

    def block_of(owner):
        return pl.ds(pl.multiple_of(owner * rows, PIECE), rows)

    def swap(source_of, target, kind):
        found = []
        for step, other in enumerate(peers):
            copy = pltpu.make_async_remote_copy(
                src_ref=source_of(other),
                dst_ref=target,
                send_sem=head_sems.at[kind, 0, step],
                recv_sem=head_sems.at[kind, 1, step],
                device_id=(tok, other),
                device_id_type=MESH,
            )
            copy.start()
            found.append(copy)
        return found

    def drive_chunk(chunk, _):
        at = pl.ds(pl.multiple_of(chunk * CHUNK, CHUNK), CHUNK)
        down_load(chunk).wait()
        drive[:, at] = across(out_grad[...], down_w[lax.rem(chunk, 2)]).astype(jnp.bfloat16)
        down_load(lax.rem(chunk + 2, chunks)).start()
        return 0

    chunks = hidden // CHUNK
    first = swap(lambda other: attended.at[block_of(other)], split.at[head], 0)
    split[head] = attended[block_of(head), :]
    lax.fori_loop(0, chunks, drive_chunk, 0)
    loads[0].wait()
    for copy in first:
        copy.wait_recv()
    total = tokens[...].astype(jnp.float32)
    for owner in range(heads):
        at = slice(owner * width, (owner + 1) * width)
        joined[:, at] = split[owner]
        total += jnp.dot(split[owner], output_w[at, :], preferred_element_type=jnp.float32)
    grad_middle[...] = total
    centred = total - jnp.mean(total, axis=-1, keepdims=True)
    scale = lax.rsqrt(jnp.mean(centred * centred, axis=-1, keepdims=True) + epsilon)
    shape[...] = centred * scale
    normed[...] = (centred * scale * gain[...] + bias[...]).astype(jnp.bfloat16)

    loads[1].wait()

    def up_chunk(chunk, _):
        at = pl.ds(pl.multiple_of(chunk * UP_CHUNK, UP_CHUNK), UP_CHUNK)
        before = jnp.dot(normed[...], up_w[:, at], preferred_element_type=jnp.float32)
        before += up_bias[:, at]
        square = before * before
        bent = jnp.tanh(ROOT * before * (1.0 + CUBIC * square))
        half = 0.5 * (1.0 + bent)
        active[:, at] = (before * half).astype(jnp.bfloat16)
        bend[:, at] = half + (0.5 * ROOT) * before * (1.0 - bent * bent) * (
            1.0 + (3.0 * CUBIC) * square
        )
        return 0

    lax.fori_loop(0, hidden // UP_CHUNK, up_chunk, 0)
    halver = Halver(grads, stages, arrivals, halver_sems, ladder, DOWN_ORDERS)
    starts = [sum(DOWN_PARTS[:k]) for k in range(len(DOWN_PARTS) + 1)]
    for k, order in enumerate(halver.orders):
        fill(active, out_grad, starts[k], starts[k + 1], grads[k], 0, order)
        halver.send(k, stages[0])

    back_sum[...] = jnp.zeros_like(back_sum)

    def back_chunk(chunk, _):
        at = pl.ds(pl.multiple_of(chunk * CHUNK, CHUNK), CHUNK)
        low = (drive[:, at].astype(jnp.float32) * bend[:, at]).astype(jnp.bfloat16)
        grad_before[:, at] = low
        grad_up_bias[:, at] = jnp.sum(low.astype(jnp.float32), axis=0, keepdims=True)
        back_sum[...] += across(low, up_w[:, at])
        return 0

    lax.fori_loop(0, chunks, back_chunk, 0)
    back = back_sum[...]
    shaped = shape[...]
    vectors[0:1, :] = jnp.sum(back * shaped, axis=0, keepdims=True)
    vectors[1:2, :] = jnp.sum(back, axis=0, keepdims=True)
    top = out_grad[...].astype(jnp.float32)
    vectors[2:3, :] = jnp.sum(top, axis=0, keepdims=True)
    back = back * gain[...]
    back = back - jnp.mean(back, axis=-1, keepdims=True)
    back = back - shaped * jnp.mean(back * shaped, axis=-1, keepdims=True)
    total = grad_middle[...]
    centred = total - jnp.mean(total, axis=-1, keepdims=True)
    scale = lax.rsqrt(jnp.mean(centred * centred, axis=-1, keepdims=True) + epsilon)
    down_sum[...] = total + down_bias[...]
    top = top + back * scale
    grad_middle[...] = top
    low = top.astype(jnp.bfloat16)
    grad_branch[...] = low
    for owner in range(heads):
        at = slice(owner * width, (owner + 1) * width)
        grad_split[owner] = across(low, output_w[at, :]).astype(jnp.bfloat16)
    second = swap(lambda other: grad_split.at[other], grad_att.at[block_of(head)], 1)
    grad_att[block_of(head), :] = grad_split[head]

    def down_chunk(chunk, _):
        at = pl.ds(pl.multiple_of(chunk * CHUNK, CHUNK), CHUNK)
        down_load(chunk).wait()
        down_sum[...] += jnp.dot(
            active[:, at], down_w[lax.rem(chunk, 2)], preferred_element_type=jnp.float32
        )

        @pl.when(chunk + 2 < chunks)
        def _():
            down_load(chunk + 2).start()

        return 0

    for k in range(len(grads)):
        halver.part(k, stages[0], down_left[2 * k], down_left[2 * k + 1])
    lax.fori_loop(0, chunks, down_chunk, 0)
    layer_out[...] = down_sum[...].astype(jnp.bfloat16)
    for copy in second:
        copy.wait_recv()
    halver.drain()
    for copy in first + second:
        copy.wait_send()


def feed(
    attended,
    tokens,
    out_grad,
    gain,
    bias,
    up_bias,
    down_bias,
    w_output,
    w_up,
    w_down,
    collective_id,
):
    rows, depth = tokens.shape
    span, width = attended.shape
    hidden = w_up.shape[1]
    heads = lax.axis_size("head")
    devices = heads * lax.axis_size("tok")
    block = hidden // devices
    stages = stage_groups(devices)[0][:1]
    pieces = [(block, part) for part in DOWN_PARTS]
    buffers, buffer_count, halver_sems = halver_scratch(pieces, stages, devices)
    low = lambda *shape: jax.ShapeDtypeStruct(shape, jnp.bfloat16)
    full = lambda *shape: jax.ShapeDtypeStruct(shape, jnp.float32)
    any_ = pl.BlockSpec(memory_space=pl.ANY)
    sems = lambda *shape: pltpu.SemaphoreType.DMA(shape)
    lows = lambda *shape: pltpu.VMEM(shape, jnp.bfloat16)
    fulls = lambda *shape: pltpu.VMEM(shape, jnp.float32)
    scratch = [
        lows(depth, depth),
        lows(depth, hidden),
        lows(2, CHUNK, depth),
        lows(heads, rows, width),
        lows(rows, hidden),
        fulls(rows, hidden),
        lows(rows, hidden),
        fulls(rows, depth),
        fulls(rows, depth),
        fulls(rows, depth),
        lows(heads, rows, width),
    ]
    scratch += [lows(devices, block, part) for part in DOWN_PARTS]
    scratch += buffers
    scratch += [sems(2), sems(2), sems(2, 2, heads - 1), halver_sems]
    count = len(pieces)
    sizes = [0] * 17 + [2 * count] + [0] * 13 + [count, buffer_count] + [0] * 4
    outs = [
        low(rows, depth),
        full(rows, depth),
        low(rows, depth),
        low(rows, hidden),
        low(rows, depth),
        low(rows, depth),
        low(span, width),
    ]
    outs += left_over([piece for piece in pieces for _ in (0, 1)], [1], devices)
    outs += [full(SUB, depth), full(1, hidden)]
    return pl.pallas_call(
        unpack_refs(functools.partial(feed_kernel, stages), sizes),
        in_specs=[VMEM] * 7 + [any_] * 3,
        out_specs=[VMEM] * len(outs),
        out_shape=outs,
        scratch_shapes=scratch,
        compiler_params=pltpu.CompilerParams(
            collective_id=collective_id, has_side_effects=True, vmem_limit_bytes=63 * MIB
        ),
        name="feed",
    )(
        attended, tokens, out_grad, gain, bias, up_bias, down_bias, w_output, w_up, w_down
    )


def layer_norm(row_block, gain, bias):
    centre = jnp.mean(row_block, axis=-1, keepdims=True)
    centred = row_block - centre
    spread = jnp.mean(centred * centred, axis=-1, keepdims=True)
    return centred * lax.rsqrt(spread + epsilon) * gain + bias


def product(left, right):
    return jnp.dot(left, right, preferred_element_type=jnp.float32)


def product_left(left, right):
    return lax.dot_general(
        left, right, (((0,), (0,)), ((), ())), preferred_element_type=jnp.float32
    )


def product_right(left, right):
    return lax.dot_general(
        left, right, (((1,), (1,)), ((), ())), preferred_element_type=jnp.float32
    )


def per_device(
    tokens_in,
    seq_starts,
    block_sizes,
    norm1_gain,
    norm1_bias,
    w_query,
    w_key,
    w_value,
    w_output,
    ssm_rate,
    ssm_input,
    ssm_output,
    ssm_skip,
    norm2_gain,
    norm2_bias,
    w_up,
    up_bias,
    w_down,
    down_bias,
    out_grad,
):
    tok_rows = tokens_in.shape[0]
    pieces = lax.axis_size("tok")
    span = tok_rows * lax.axis_size("head")
    total_len = span * pieces

    rate = ssm_rate.T / total_len
    drive_in, read_out = ssm_input.T, ssm_output.T
    decay = jnp.exp(-rate)
    gain = jnp.sqrt(-jnp.expm1(-2.0 * rate))
    driving = gain * drive_in
    mix = read_out * driving
    skip = ssm_skip[None, :]
    hid, query_h, key_h, value_h, hidden_h, w_own, context, rims = front(
        seq_starts,
        tokens_in,
        norm1_gain[None, :],
        norm1_bias[None, :],
        rate,
        mix,
        skip,
        w_query,
        w_key,
        w_value,
        6,
    )
    attended, attended_fine, level = attend(seq_starts, block_sizes, query_h, key_h, value_h, context, rims)
    (
        layer_out,
        grad_middle,
        normed_low,
        grad_before_low,
        joined,
        grad_branch,
        grad_att,
        *down,
        vectors,
        grad_up_bias,
    ) = feed(
        attended,
        tokens_in,
        out_grad,
        norm2_gain[None, :],
        norm2_bias[None, :],
        up_bias[None, :],
        down_bias[None, :],
        w_output,
        w_up,
        w_down,
        7,
    )
    orders = halving_orders(bits_of(pieces * lax.axis_size("head")))
    come = [
        swapped(leave, orders[order][1]) for leave, order in zip(down[1::2], DOWN_ORDERS)
    ]

    back_query_h, key_rim, value_rim, near_rim, back_key_h, back_value_h, back_context = attend_back(
        seq_starts, block_sizes, query_h, key_h, value_h, context, rims, attended_fine, grad_att, level
    )
    (
        back_key_h,
        back_value_h,
        back_feed_h,
        sums,
        lag_sums,
        skip_sum,
        out_w_down,
        up,
        apart,
    ) = recurrence_back(
        seq_starts,
        back_context,
        hidden_h,
        rate,
        mix,
        skip,
        [back_key_h, back_value_h],
        [key_rim, value_rim, near_rim],
        [normed_low, joined],
        [grad_before_low, grad_branch],
        (down[::2], come),
        2,
    )
    input_grad, out_w_heads, summed, packed, up = head_backward(
        back_query_h,
        back_key_h,
        back_value_h,
        back_feed_h,
        hid,
        w_own,
        tokens_in,
        norm1_gain[None, :],
        grad_middle,
        sums,
        lag_sums,
        skip_sum,
        vectors,
        grad_up_bias,
        up,
        4,
    )
    heads, head = lax.axis_size("head"), lax.axis_index("head")
    part = norm1_gain.shape[0] // pieces
    more = up_bias.shape[0] // norm1_gain.shape[0]
    short = lax.dynamic_slice_in_dim(packed[:5], head * (part // heads), part // heads, 1)
    out_up_bias = lax.dynamic_slice_in_dim(
        packed[5 : 5 + more, :part].reshape(-1), head * (more * part // heads), more * part // heads
    )
    out_w_up, out_w_output = up if apart is None else apart
    sums, lag_sums, skip_sum = summed[:NS], summed[NS : 2 * NS], summed[2 * NS]
    grad_ssm_output = (driving * sums).T
    grad_driving = read_out * sums
    grad_ssm_input = (gain * grad_driving).T
    grad_ssm_rate = (
        grad_driving * drive_in * jnp.exp(-2.0 * rate) / gain - mix * lag_sums * decay
    ).T / total_len

    return (
        layer_out,
        input_grad,
        short[0],
        short[1],
        out_w_heads[0],
        out_w_heads[1],
        out_w_heads[2],
        out_w_output,
        grad_ssm_rate,
        grad_ssm_input,
        grad_ssm_output,
        skip_sum,
        short[2],
        short[3],
        out_w_up,
        out_up_bias,
        out_w_down,
        short[4],
    )


def solution(mesh):
    return jax.shard_map(
        per_device,
        mesh=mesh,
        in_specs=(
            P(("tok", "head"), None),
            P(),
            P(),
            P(),
            P(),
            P(),
            P(),
            P(),
            P(),
            P("head", None),
            P("head", None),
            P("head", None),
            P("head"),
            P(),
            P(),
            P(),
            P(),
            P(),
            P(),
            P(("tok", "head"), None),
        ),
        out_specs=(
            P(("tok", "head"), None),
            P(("tok", "head"), None),
            P(("tok", "head")),
            P(("tok", "head")),
            P(("tok", "head"), None),
            P(("tok", "head"), None),
            P(("tok", "head"), None),
            P(("tok", "head"), None),
            P("head", None),
            P("head", None),
            P("head", None),
            P("head"),
            P(("tok", "head")),
            P(("tok", "head")),
            P(("tok", "head"), None),
            P(("tok", "head")),
            P(("tok", "head"), None),
            P(("tok", "head")),
        ),
        check_vma=False,
    )
```

```python
import functools
import math

import jax
import jax.numpy as jnp
from jax import lax
from jax.experimental import pallas as pl
from jax.experimental.pallas import tpu as pltpu
from jax.sharding import PartitionSpec as P

epsilon = 1e-05
HD = 128
CTX = 128
BLOCK = 256
NS = 16
SUB = 8
UNROLL = 8
HALF = 8
TILE = 256
MIB = 1 << 20
LOWEST = -1e30
FACTOR = HD ** (-0.5)
FACTOR2 = FACTOR * math.log2(math.e)


def spread(table, n):
    return jnp.broadcast_to(table[n : n + 1, :], (SUB, table.shape[1]))


SCALARS = pl.BlockSpec(memory_space=pltpu.SMEM)


def wide(limit=48):
    return pltpu.CompilerParams(vmem_limit_bytes=limit * MIB)


def across(left, right):
    return lax.dot_general(
        left, right, (((1,), (1,)), ((), ())), preferred_element_type=jnp.float32
    )


def times(left, right):
    return lax.dot_general(
        left, right, (((1,), (0,)), ((), ())), preferred_element_type=jnp.float32
    )


def turn(source, target):
    for at in range(0, source.shape[0], TILE):
        size = min(TILE, source.shape[0] - at)
        piece = source[at : at + size, :].astype(jnp.float32)
        target[:, at : at + size] = piece.T.astype(target.dtype)


def next_block(where_, now):
    second = where_[1]
    length = jnp.where(now >= second, where_[3], where_[2])
    after = now + length
    return jnp.where((now < second) & (after > second), second, after)


REACH = 2 * BLOCK + TILE
BLOCKS = 4


def block_facts(starts, sizes, span):
    anchor = lax.axis_index("tok") * span
    return anchor, starts[1] - anchor, sizes[0], sizes[1]


def block_begin(where_, at):
    opening = jnp.where(at >= where_[1], where_[1], -where_[0])
    length = jnp.where(at >= where_[1], where_[3], where_[2])
    return opening + lax.div(at - opening, length) * length


def block_rows(where_, tile):
    cols = lax.broadcasted_iota(jnp.int32, (1, TILE), 1) + tile * TILE
    begin = block_begin(where_, tile * TILE)
    now, firsts = begin, jnp.zeros_like(cols) + begin
    for _ in range(BLOCKS):
        now = next_block(where_, now)
        firsts = jnp.where(cols >= now, now, firsts)
    return firsts, jnp.where(cols >= where_[1], where_[1], -where_[0]), begin


def joined_rows(rim, own, target):
    target[: rim.shape[0], :] = rim[...]
    target[rim.shape[0] :, :] = own[...]


def local_mask(tile, first):
    rows = lax.broadcasted_iota(jnp.int32, (REACH, TILE), 0) + (tile * TILE - 2 * BLOCK)
    cols = lax.broadcasted_iota(jnp.int32, (1, TILE), 1) + tile * TILE
    return (rows >= first) & (rows <= cols)


def context_at(now):
    return pl.multiple_of((now + 2 * BLOCK) // CTX * CTX, CTX)


def context_mask(start, now, first, opening):
    rows = lax.broadcasted_iota(jnp.int32, (TILE, TILE), 0) + (start - 2 * BLOCK - CTX)
    low = jnp.where(first == now, jnp.maximum(now - CTX, opening), 1 << 28)
    return (rows >= low) & (rows < now)


def lanes_of(head):
    return slice(head * HD, (head + 1) * HD)


def attend_kernel(
    starts,
    sizes,
    query,
    key_own,
    value_own,
    context_own,
    key_rim,
    value_rim,
    context_rim,
    out,
    fine,
    level,
    key,
    value,
    context,
    value_t,
    context_t,
):
    where_ = block_facts(starts, sizes, query.shape[0])
    joined_rows(key_rim, key_own, key)
    joined_rows(value_rim, value_own, value)
    joined_rows(context_rim, context_own, context)
    heads = query.shape[1] // HD
    turn(value, value_t)
    turn(context, context_t)

    def one_tile(tile, _):
        here = pl.ds(pl.multiple_of(tile * TILE, TILE), TILE)
        rows = [query[here, lanes_of(head)] for head in range(heads)]
        firsts, openings, begin = block_rows(where_, tile)

        def score(near, at, head, mask):
            return jnp.where(mask, across(near[at, lanes_of(head)], rows[head]) * FACTOR2, LOWEST)

        def peak(found):
            return jnp.max(found, axis=0, keepdims=True)

        def gather(prob, values_t, at, head):
            low = prob.astype(jnp.bfloat16)
            return (
                jnp.sum(prob, axis=0, keepdims=True),
                jnp.sum(low.astype(jnp.float32), axis=0, keepdims=True),
                times(values_t[lanes_of(head), at], low),
            )

        near_at = pl.ds(pl.multiple_of(tile * TILE, TILE), REACH)
        far_at = pl.ds(context_at(begin), TILE)
        near_mask = local_mask(tile, firsts)
        far_mask = context_mask(context_at(begin), begin, firsts, openings)
        carry = []
        for head in range(heads):
            near = score(key, near_at, head, near_mask)
            far = score(context, far_at, head, far_mask)
            top = jnp.maximum(peak(near), peak(far))
            one = gather(jnp.exp2(near - top), value_t, near_at, head)
            two = gather(jnp.exp2(far - top), context_t, far_at, head)
            carry.append((top,) + tuple(a + b for a, b in zip(one, two)))

        def earlier(state):
            now, carry = state
            start = context_at(now)
            at = pl.ds(start, TILE)
            mask = context_mask(start, now, firsts, openings)
            found = []
            for head in range(heads):
                top, mass, low_mass, total = carry[head]
                far = score(context, at, head, mask)
                new_top = jnp.maximum(top, peak(far))
                shrink = jnp.exp2(top - new_top)
                more = gather(jnp.exp2(far - new_top), context_t, at, head)
                found.append(
                    (new_top,)
                    + tuple(a * shrink + b for a, b in zip((mass, low_mass, total), more))
                )
            return next_block(where_, now), tuple(found)

        _, carry = lax.while_loop(
            lambda state: state[0] < (tile + 1) * TILE,
            earlier,
            (next_block(where_, begin), tuple(carry)),
        )
        for head in range(heads):
            top, mass, low_mass, total = carry[head]
            done = (total / low_mass).T
            fine[here, lanes_of(head)] = done
            out[here, lanes_of(head)] = done.astype(out.dtype)
            level[head, tile] = top + jnp.log2(mass)
        return 0

    lax.fori_loop(0, query.shape[0] // TILE, one_tile, 0)


def attend_back_kernel(
    starts,
    sizes,
    query,
    key_own,
    value_own,
    context_own,
    key_rim,
    value_rim,
    context_rim,
    attended,
    grad,
    level,
    back_query,
    back_key_rim,
    back_value_rim,
    back_context_rim,
    back_key,
    back_value,
    back_context,
    key,
    value,
    context,
    key_t,
    context_t,
    key_sum,
    value_sum,
    context_sum,
):
    where_ = block_facts(starts, sizes, query.shape[0])
    joined_rows(key_rim, key_own, key)
    joined_rows(value_rim, value_own, value)
    joined_rows(context_rim, context_own, context)
    heads = query.shape[1] // HD
    turn(key, key_t)
    turn(context, context_t)
    key_sum[...] = jnp.zeros_like(key_sum)
    value_sum[...] = jnp.zeros_like(value_sum)
    context_sum[...] = jnp.zeros_like(context_sum)

    def one_tile(tile, _):
        here = pl.ds(pl.multiple_of(tile * TILE, TILE), TILE)
        rows = [query[here, lanes_of(head)] for head in range(heads)]
        grads = [grad[here, lanes_of(head)] for head in range(heads)]
        firsts, openings, begin = block_rows(where_, tile)
        levels = [level[head, tile] for head in range(heads)]
        centres = []
        for head in range(heads):
            joint = grads[head].astype(jnp.float32) * attended[here, lanes_of(head)]
            centres.append(jnp.sum(joint.T, axis=0, keepdims=True))

        def slopes(keys, values, at, head, mask):
            found = across(keys[at, lanes_of(head)], rows[head]) * FACTOR2 - levels[head]
            prob = jnp.exp2(jnp.where(mask, found, LOWEST))
            drive = across(values[at, lanes_of(head)], grads[head])
            slope = prob * (drive - centres[head])
            return prob.astype(jnp.bfloat16), slope.astype(jnp.bfloat16)

        def earlier(state):
            now, totals = state
            start = context_at(now)
            at = pl.ds(start, TILE)
            mask = context_mask(start, now, firsts, openings)
            found = []
            for h in range(heads):
                prob, slope = slopes(context, context, at, h, mask)
                context_sum[at, lanes_of(h)] += FACTOR * times(slope, rows[h]) + times(
                    prob, grads[h]
                )
                found.append(totals[h] + times(context_t[lanes_of(h), at], slope))
            return next_block(where_, now), tuple(found)

        at = pl.ds(pl.multiple_of(tile * TILE, TILE), REACH)
        mask = local_mask(tile, firsts)
        totals = []
        for h in range(heads):
            prob, slope = slopes(key, value, at, h, mask)
            key_sum[at, lanes_of(h)] += times(slope, rows[h])
            value_sum[at, lanes_of(h)] += times(prob, grads[h])
            totals.append(times(key_t[lanes_of(h), at], slope))
        state = earlier((begin, tuple(totals)))
        _, totals = lax.while_loop(lambda state: state[0] < (tile + 1) * TILE, earlier, state)
        for head in range(heads):
            back_query[here, lanes_of(head)] = (FACTOR * totals[head]).T.astype(back_query.dtype)
        return 0

    lax.fori_loop(0, query.shape[0] // TILE, one_tile, 0)
    window = 2 * BLOCK
    back_key_rim[...] = (FACTOR * key_sum[:window, :]).astype(back_key_rim.dtype)
    back_value_rim[...] = value_sum[:window, :].astype(back_value_rim.dtype)
    back_context_rim[...] = context_sum[: window + CTX, :].astype(back_context_rim.dtype)
    back_key[...] = FACTOR * key_sum[window:, :]
    back_value[...] = value_sum[window:, :]
    back_context[...] = context_sum[window + CTX :, :]


VMEM = pl.BlockSpec(memory_space=pltpu.VMEM)


def attend(starts, sizes, query, key, value, context, rims):
    rows, width = query.shape
    heads, tiles = width // HD, rows // TILE
    near, far = rows + rims[0].shape[0], rows + rims[2].shape[0]
    low = lambda *shape: pltpu.VMEM(shape, jnp.bfloat16)
    return pl.pallas_call(
        attend_kernel,
        in_specs=[SCALARS] * 2 + [VMEM] * 7,
        out_specs=[VMEM] * 3,
        out_shape=(
            jax.ShapeDtypeStruct((rows, width), jnp.bfloat16),
            jax.ShapeDtypeStruct((rows, width), jnp.float32),
            jax.ShapeDtypeStruct((heads, tiles, 1, TILE), jnp.float32),
        ),
        scratch_shapes=[
            low(near, width),
            low(near, width),
            low(far, width),
            low(width, near),
            low(width, far),
        ],
        compiler_params=wide(60),
        name="attend",
    )(starts, sizes, query, key, value, context, *rims)


def attend_back(starts, sizes, query, key, value, context, rims, attended, grad, level):
    rows, width = query.shape
    near, far = rows + rims[0].shape[0], rows + rims[2].shape[0]
    low = lambda count: jax.ShapeDtypeStruct((count, width), jnp.bfloat16)
    full = lambda count: jax.ShapeDtypeStruct((count, width), jnp.float32)
    lows = lambda *shape: pltpu.VMEM(shape, jnp.bfloat16)
    fulls = lambda *shape: pltpu.VMEM(shape, jnp.float32)
    return pl.pallas_call(
        attend_back_kernel,
        in_specs=[SCALARS] * 2 + [VMEM] * 10,
        out_specs=[VMEM] * 7,
        out_shape=(
            low(rows),
            low(near - rows),
            low(near - rows),
            low(far - rows),
            full(rows),
            full(rows),
            full(rows),
        ),
        scratch_shapes=[
            lows(near, width),
            lows(near, width),
            lows(far, width),
            lows(width, near),
            lows(width, far),
            fulls(near, width),
            fulls(near, width),
            fulls(far, width),
        ],
        compiler_params=wide(60),
        name="attend_back",
    )(starts, sizes, query, key, value, context, *rims, attended, grad, level)


MESH = pl.DeviceIdType.MESH
ROWS = 1024


def bits_of(count):
    return count.bit_length() - 1


def mesh_bits():
    found = []
    tok, head = lax.axis_index("tok"), lax.axis_index("head")
    for axis in ("head", "tok"):
        for level in range(bits_of(lax.axis_size(axis))):
            at = head if axis == "head" else tok
            bit = (at // (1 << level)) % 2
            other = at + (1 - 2 * bit) * (1 << level)
            found.append((bit, (tok, other) if axis == "head" else (other, head)))
    return found


def greet(partners):
    barrier = pltpu.get_barrier_semaphore()
    for partner in partners:
        pl.semaphore_signal(barrier, inc=1, device_id=partner, device_id_type=MESH)
    pl.semaphore_wait(barrier, len(partners))


def halving_orders(bits):
    rest = list(range(4, bits))
    return [
        [0, 1, 2, 3] + rest,
        [0, 2, 1, 3] + rest,
        [0, 3, 2, 1] + rest,
        [0, 3, 1, 2] + rest,
        [0, 2, 3, 1] + rest,
    ]


def slot_of(block, order):
    place = 0
    for bit in order:
        place = place * 2 + (block // (1 << bit)) % 2
    return place


def unpack_refs(function, sizes):
    def kernel(*refs):
        grouped, at = [], 0
        for size in sizes:
            grouped.append(refs[at] if size == 0 else refs[at : at + max(size, 0)])
            at += 1 if size == 0 else max(size, 0)
        function(*grouped)

    return kernel


class Halver:
    def __init__(self, pieces, stages, arrivals, sems, ladder, orders):
        self.now, self.stages, self.arrivals, self.ladder = list(pieces), stages, arrivals, ladder
        self.sems, self.steps = sems, len(ladder)
        self.orders = [halving_orders(self.steps)[order] for order in orders]
        self.sent, self.flying, self.doing = [], {}, {}

    def half(self, stage):
        return 1 << (self.steps - 1 - stage)

    def send(self, number, stage):
        bit, partner = self.ladder[self.orders[number][stage]]
        at = number * len(self.stages) + self.stages.index(stage)
        half = self.half(stage)
        copy = pltpu.make_async_remote_copy(
            src_ref=self.now[number].at[pl.ds((1 - bit) * half, half)],
            dst_ref=self.arrivals[at],
            send_sem=self.sems.at[0, at],
            recv_sem=self.sems.at[1, at],
            device_id=partner,
            device_id_type=MESH,
        )
        copy.start()
        self.sent.append(copy)
        self.flying[number] = (copy, self.arrivals[at], bit * half)
        self.doing[number] = stage

    def absorb(self, number, stage, into=None):
        copy, arrival, keep = self.flying[number]
        copy.wait_recv()
        before = self.now[number]
        target = arrival if into is None else into

        def add(i, _):
            target[i] = before[keep + i] + arrival[i]
            return 0

        lax.fori_loop(0, self.half(stage), add, 0)
        self.now[number] = target

    def part(self, number, stage, keep, leave):
        copy, arrival, base = self.flying[number]
        copy.wait_recv()
        before, half = self.now[number], self.half(stage + 1)
        bit = self.ladder[self.orders[number][stage + 1]][0]
        for at, target in ((bit * half, keep), ((1 - bit) * half, leave)):

            def add(i, _):
                target[i] = before[base + at + i] + arrival[at + i]
                return 0

            lax.fori_loop(0, half, add, 0)

    def last(self, number):
        while self.doing[number] != self.stages[-1]:
            self.advance(number)
        copy, arrival, keep = self.flying[number]
        copy.wait_recv()
        return self.now[number][keep].astype(jnp.float32) + arrival[0].astype(jnp.float32)

    def step(self, stage, into=None):
        for number in range(len(self.now)):
            self.absorb(number, stage, None if into is None else into[number])
            if into is None:
                self.send(number, stage + 1)

    def advance(self, number):
        stage = self.doing[number]
        if stage != self.stages[-1]:
            self.absorb(number, stage)
            self.send(number, stage + 1)

    def begin(self):
        for number in range(len(self.now)):
            self.send(number, self.stages[0])

    def drain(self):
        for copy in self.sent:
            copy.wait_send()


def halver_scratch(pieces, stages, devices):
    steps = bits_of(devices)
    buffers = [
        pltpu.VMEM((1 << (steps - 1 - stage), block, width), jnp.bfloat16)
        for block, width in pieces
        for stage in stages
    ]
    sems = pltpu.SemaphoreType.DMA((2, max(len(buffers), 1)))
    return buffers, len(buffers) or -1, sems


def left_over(pieces, stages, devices):
    slots = 1 << (bits_of(devices) - 1 - stages[-1])
    return [jax.ShapeDtypeStruct((slots, block, width), jnp.bfloat16) for block, width in pieces]


def fill(left, right, start, stop, target, column, order):
    block = target.shape[1]
    each = ROWS // block
    for low in range(start, stop, ROWS):
        high = min(low + ROWS, stop)
        to = column + low - start

        def some_rows(chunk, _):
            at = pl.ds(pl.multiple_of(chunk * ROWS, ROWS), ROWS)
            found = lax.dot_general(
                left[:, at],
                right[:, low:high],
                (((0,), (0,)), ((), ())),
                preferred_element_type=jnp.float32,
            ).astype(jnp.bfloat16)
            for inner in range(each):
                target[slot_of(chunk * each + inner, order), :, to : to + high - low] = found[
                    inner * block : (inner + 1) * block
                ]
            return 0

        lax.fori_loop(0, left.shape[1] // ROWS, some_rows, 0)


def stage_groups(devices):
    steps = bits_of(devices)
    return [0, 1], list(range(2, steps - 1)), [steps - 1]


DOWN_PARTS = (256, 384, 384)
DOWN_ORDERS = (0, 1, 3)
UP_ORDERS = (0, 1, 3)


def swapped(shard, bit):
    heads = bits_of(lax.axis_size("head"))
    axis, level = ("head", bit) if bit < heads else ("tok", bit - heads)
    pairs = [(i, i ^ (1 << level)) for i in range(lax.axis_size(axis))]
    return lax.ppermute(shard, axis, pairs)


UP_PARTS = (((0, 0, 2560),), ((0, 2560, 4096), (1, 0, 256)), ((1, 256, 1024),))
UP_WIDTHS = (2560, 1792, 768)


def products_apart(lefts, rights):
    return [
        lax.psum_scatter(product_left(left, right), ("tok", "head"), scatter_dimension=0, tiled=True)
        for left, right in zip(lefts, rights)
    ]


def tok_peers():
    count, here = lax.axis_size("tok"), lax.axis_index("tok")
    head = lax.axis_index("head")
    return [
        ((lax.rem(here + step, count), head), lax.rem(here + count - step, count))
        for step in range(1, count)
    ]


def share(mine, every, send_sems, recv_sems, place, peers):
    copies = []
    for step, (target, _) in enumerate(peers):
        copy = pltpu.make_async_remote_copy(
            src_ref=mine,
            dst_ref=every.at[place],
            send_sem=send_sems.at[step],
            recv_sem=recv_sems.at[step],
            device_id=target,
            device_id_type=MESH,
        )
        copy.start()
        copies.append(copy)
    return copies


def row_norm(rows, gain, bias):
    rows = rows.astype(jnp.float32)
    centred = rows - jnp.mean(rows, axis=-1, keepdims=True)
    spread_ = jnp.mean(centred * centred, axis=-1, keepdims=True)
    return (centred * lax.rsqrt(spread_ + epsilon) * gain + bias).astype(jnp.bfloat16)


PIECE = 128


def head_backward_kernel(
    stages,
    back_query,
    back_key,
    back_value,
    back_feed,
    hid,
    weights,
    tokens,
    gain,
    grad_middle,
    sums,
    lag_sums,
    skip_sum,
    vectors,
    grad_up_bias,
    up_in,
    input_grad,
    grad_weights,
    row_sum,
    vector_sum,
    up_out,
    total,
    parts,
    near_in,
    far_in,
    products,
    arrived,
    shares,
    head_sems,
    tok_sends,
    tok_recvs,
    share_sends,
    share_recvs,
    every_row,
    row_sends,
    row_recvs,
    vector_parts,
    every_vector,
    tok_sum,
    head_sums,
    vector_sems,
    swap_sems,
    up_arrivals,
    up_sems,
):
    tok, head = lax.axis_index("tok"), lax.axis_index("head")
    heads, toks = lax.axis_size("head"), lax.axis_size("tok")
    near = head + 1 - 2 * lax.rem(head, 2)
    far = head + 2 - 4 * (head // 2)
    across_ = near + 2 - 4 * (near // 2)
    head_peers = [lax.rem(head + step, heads) for step in range(1, heads)]
    ladder = mesh_bits()[bits_of(heads) :]
    peers = tok_peers()
    greet([(tok, other) for other in head_peers] + [target for target, _ in peers])
    rows = input_grad.shape[0]
    states = sums.shape[0]
    every_row[tok] = jnp.zeros_like(every_row[tok])
    every_row[tok, :states] = sums[...]
    every_row[tok, states : 2 * states] = lag_sums[...]
    every_row[tok, 2 * states : 2 * states + 1] = skip_sum[...]
    row_copies = share(every_row.at[tok], every_row, row_sends, row_recvs, tok, peers)
    width = back_query.shape[1]
    columns_ = pl.ds(pl.multiple_of(head * width, HD), width)

    def block_of(owner):
        return pl.ds(pl.multiple_of(owner * rows, PIECE), rows)

    def partial(owner):
        at = block_of(owner)
        found = across(back_query[at, :], weights[:, :width])
        found += across(back_key[at, :], weights[:, width : 2 * width])
        found += across(back_value[at, :], weights[:, 2 * width :])
        total[...] = found
        total[:, columns_] += back_feed[at, :].astype(jnp.float32)

    def copy(source, target, device, number):
        one = pltpu.make_async_remote_copy(
            src_ref=source,
            dst_ref=target,
            send_sem=head_sems.at[0, number],
            recv_sem=head_sems.at[1, number],
            device_id=(tok, device),
            device_id_type=MESH,
        )
        one.start()
        return one

    up_stages = stages[1] + stages[2]
    up = Halver(up_in, up_stages, up_arrivals, up_sems, mesh_bits(), UP_ORDERS)
    up.begin()
    steps = len(ladder)
    orders = [[1, 0] + list(range(2, steps)), list(range(steps))]
    each = products[0].shape[1]
    half_width = products[0].shape[2]
    depth = hid.shape[1]
    base = [0, 0]
    sent = []

    def forward(number, stage):
        bit, partner = ladder[orders[number][stage]]
        half = 1 << (steps - 1 - stage)
        one = pltpu.make_async_remote_copy(
            src_ref=products[number].at[pl.ds(base[number] + (1 - bit) * half, half)],
            dst_ref=arrived[number * steps + stage],
            send_sem=tok_sends.at[number, stage],
            recv_sem=tok_recvs.at[number, stage],
            device_id=partner,
            device_id_type=MESH,
        )
        one.start()
        sent.append(one)
        base[number] = base[number] + bit * half
        return one

    def joined(at, number):
        if number == 0:
            return jnp.concatenate([back_query[at, :], back_key[at, : half_width - width]], axis=1)
        return jnp.concatenate([back_key[at, half_width - width :], back_value[at, :]], axis=1)

    everything = pl.ds(0, hid.shape[0])
    flying = []
    for number in range(2):
        right = joined(everything, number)
        for start in range(0, depth, 512):
            found = lax.dot_general(
                hid[:, start : start + 512],
                right,
                (((0,), (0,)), ((), ())),
                preferred_element_type=jnp.float32,
            ).astype(jnp.bfloat16)
            for inner in range(512 // each):
                products[number][slot_of(start // each + inner, orders[number])] = found[
                    inner * each : (inner + 1) * each
                ]
        flying.append(forward(number, 0))

    partial(across_)
    parts[0] = total[...].astype(jnp.bfloat16)
    first = copy(parts.at[0], near_in.at[0], near, 0)
    partial(near)
    parts[1] = total[...].astype(jnp.bfloat16)
    second = copy(parts.at[1], near_in.at[1], near, 1)
    partial(far)
    first.wait_recv()
    parts[2] = (total[...] + near_in[0].astype(jnp.float32)).astype(jnp.bfloat16)
    third = copy(parts.at[2], far_in, far, 2)
    if up_in:
        up.advance(1)
        up.advance(2)
        up.advance(0)

    partial(head)
    second.wait_recv()
    if up_in:
        up.advance(1)
        up.advance(1)
        up.advance(2)
        up.advance(0)
    total[...] += near_in[1].astype(jnp.float32)

    done = []
    for stage in range(steps):
        for number in range(2):
            flying[number].wait_recv()
            arrival = arrived[number * steps + stage]
            half = 1 << (steps - 1 - stage)
            if stage == steps - 1:
                done.append(
                    products[number][base[number]].astype(jnp.float32)
                    + arrival[0].astype(jnp.float32)
                )
            else:
                for i in range(half):
                    products[number][base[number] + i] = (
                        products[number][base[number] + i] + arrival[i]
                    )
                flying[number] = forward(number, stage + 1)
        if stage == steps - 2:
            third.wait_recv()
            back = total[...] + far_in[...].astype(jnp.float32)
            found = tokens[...].astype(jnp.float32)
            centred = found - jnp.mean(found, axis=-1, keepdims=True)
            scale = lax.rsqrt(jnp.mean(centred * centred, axis=-1, keepdims=True) + epsilon)
            shaped = centred * scale
            lists = [jnp.sum(back * shaped, axis=0, keepdims=True), jnp.sum(back, axis=0, keepdims=True)]
            lists += [vectors[i : i + 1, :] for i in range(3)]
            part = depth // toks
            for place in range(toks):
                for i, row in enumerate(lists):
                    vector_parts[place, i : i + 1, :part] = row[:, place * part : (place + 1) * part]
                for i in range(grad_up_bias.shape[1] // depth):
                    start = place * part * (grad_up_bias.shape[1] // depth) + i * part
                    vector_parts[place, len(lists) + i : len(lists) + i + 1, :part] = grad_up_bias[
                        :, start : start + part
                    ]
            every_vector[tok] = vector_parts[tok]
            vector_copies = []
            for step, (target, _) in enumerate(peers):
                one = pltpu.make_async_remote_copy(
                    src_ref=vector_parts.at[target[0]],
                    dst_ref=every_vector.at[tok],
                    send_sem=vector_sems.at[0, step],
                    recv_sem=vector_sems.at[1, step],
                    device_id=target,
                    device_id_type=MESH,
                )
                one.start()
                vector_copies.append(one)
            back = back * gain[...]
            back = back - jnp.mean(back, axis=-1, keepdims=True)
            back = back - shaped * jnp.mean(back * shaped, axis=-1, keepdims=True)
            input_grad[...] = grad_middle[...] + back * scale
    small = each // heads
    ready, landed = shares
    for other in range(heads):
        for number in range(2):
            ready[other, :, number * half_width : (number + 1) * half_width] = done[number][
                other * small : (other + 1) * small
            ].astype(ready.dtype)
    landed[head] = ready[head]
    swaps = []
    for step, other in enumerate(head_peers):
        one = pltpu.make_async_remote_copy(
            src_ref=ready.at[other],
            dst_ref=landed.at[head],
            send_sem=share_sends.at[step],
            recv_sem=share_recvs.at[step],
            device_id=(tok, other),
            device_id_type=MESH,
        )
        one.start()
        swaps.append(one)

    for one in row_copies + vector_copies:
        one.wait_recv()
    row_sum[...] = jnp.sum(every_row[...], axis=0)
    tok_sum[...] = jnp.sum(every_vector[...], axis=0)
    head_sums[head] = tok_sum[...]
    head_copies = []
    for step, other in enumerate(head_peers):
        one = pltpu.make_async_remote_copy(
            src_ref=tok_sum,
            dst_ref=head_sums.at[head],
            send_sem=swap_sems.at[0, step],
            recv_sem=swap_sems.at[1, step],
            device_id=(tok, other),
            device_id_type=MESH,
        )
        one.start()
        head_copies.append(one)
    for one in swaps:
        one.wait()
    for other in range(heads):
        for kind in range(3):
            grad_weights[kind][:, other * width : (other + 1) * width] = landed[
                other, :, kind * width : (kind + 1) * width
            ].astype(jnp.float32)
    for one in head_copies:
        one.wait_recv()
    vector_sum[...] = jnp.sum(head_sums[...], axis=0)
    for number in range(len(up_in)):
        found, column = up.last(number), 0
        for pair, start, stop in UP_PARTS[number]:
            up_out[pair][:, start:stop] = found[:, column : column + stop - start]
            column += stop - start
    up.drain()
    for one in sent + [first, second, third] + row_copies + vector_copies + head_copies:
        one.wait_send()


def head_backward(
    back_query,
    back_key,
    back_value,
    back_feed,
    hid,
    weights,
    tokens,
    gain,
    grad_middle,
    sums,
    lag_sums,
    skip_sum,
    vectors,
    grad_up_bias,
    up,
    collective_id,
):
    span, width = back_query.shape
    depth = hid.shape[1]
    heads, toks = lax.axis_size("head"), lax.axis_size("tok")
    rows, each = span // heads, depth // toks
    steps, half_width = bits_of(toks), 3 * width // 2
    swap_kind = jnp.bfloat16 if each // heads % 16 == 0 else jnp.float32
    devices = heads * toks
    stages = stage_groups(devices)
    up_pieces = [piece.shape[1:] for piece in up]
    up_buffers, up_count, up_sems = halver_scratch(up_pieces, stages[1] + stages[2], devices)
    outs = []
    for pair in range(2 if up else 0):
        stop = max(part[2] for parts in UP_PARTS for part in parts if part[0] == pair)
        outs.append(jax.ShapeDtypeStruct((up_pieces[0][0], stop), jnp.float32))
    states = sums.shape[0]
    states += -states % SUB
    row_count = 2 * states + SUB
    part = (16, max(depth // toks, HD))
    ups = len(up) or -1
    low = lambda *shape: pltpu.VMEM(shape, jnp.bfloat16)
    full = lambda *shape: pltpu.VMEM(shape, jnp.float32)
    sems = lambda *shape: pltpu.SemaphoreType.DMA(shape)
    sizes = [0] * 14 + [ups, 0, 3, 0, 0, len(outs) or -1] + [0] * 4 + [2, 2 * steps, 2]
    sizes += [0] * 5 + [0] * 9 + [up_count, 0]
    found = pl.pallas_call(
        unpack_refs(functools.partial(head_backward_kernel, stages), sizes),
        in_specs=[VMEM] * (14 + len(up)),
        out_specs=[VMEM] * (6 + len(outs)),
        out_shape=[
            jax.ShapeDtypeStruct((rows, depth), jnp.float32),
        ]
        + [jax.ShapeDtypeStruct((each // heads, depth), jnp.float32)] * 3
        + [
            jax.ShapeDtypeStruct((row_count, width), jnp.float32),
            jax.ShapeDtypeStruct(part, jnp.float32),
        ]
        + outs,
        scratch_shapes=[
            full(rows, depth),
            low(3, rows, depth),
            low(2, rows, depth),
            low(rows, depth),
        ]
        + [low(toks, each, half_width)] * 2
        + [low(1 << (steps - 1 - stage), each, half_width) for stage in range(steps)] * 2
        + [pltpu.VMEM((heads, each // heads, 3 * width), swap_kind)] * 2
        + [sems(2, 3), sems(2, steps), sems(2, steps), sems(heads - 1), sems(heads - 1)]
        + [full(toks, row_count, width), sems(toks - 1), sems(toks - 1)]
        + [full(toks, *part), full(toks, *part), full(*part), full(heads, *part)]
        + [sems(2, toks - 1), sems(2, heads - 1)]
        + up_buffers
        + [up_sems],
        compiler_params=pltpu.CompilerParams(
            collective_id=collective_id, has_side_effects=True, vmem_limit_bytes=58 * MIB
        ),
        name="head_backward",
    )(
        back_query,
        back_key,
        back_value,
        back_feed,
        hid,
        weights,
        tokens,
        gain,
        grad_middle,
        sums,
        lag_sums,
        skip_sum,
        vectors,
        grad_up_bias,
        *up,
    )
    return found[0], found[1:4], found[4], found[5], found[6:]


def every_step(length, second, back, body, carry):
    begins = lax.broadcasted_iota(jnp.int32, (SUB, HD), 0) * length - second

    def some(block, now):
        for inner in range(UNROLL):
            t = block * UNROLL + inner
            at = length - 1 - t if back else t
            now = body(at, now, jnp.where(begins == -at, 0.0, 1.0))
        return now

    return lax.fori_loop(0, length // UNROLL, some, carry)


def kept(second, begin, end):
    return jnp.where((second >= begin) & (second < end), 0.0, 1.0)


def decay_tables(rate, span):
    length = span // SUB
    return (
        jnp.exp(-rate),
        jnp.exp(-rate * length),
        length * jnp.exp(-rate * (length - 1)),
        jnp.exp(-rate * span),
        span * jnp.exp(-rate * (span - 1)),
    )


def front_kernel(
    seq_starts,
    tokens,
    gain,
    bias,
    rate,
    mix,
    skip,
    w_query,
    w_key,
    w_value,
    hid,
    query,
    key,
    value,
    feed_rows,
    weights,
    context,
    key_rim,
    value_rim,
    context_rim,
    gathered,
    drives,
    total,
    ends,
    mine,
    every,
    send_sems,
    recv_sems,
    load_sems,
    share_sends,
    share_recvs,
    rim_sems,
):
    tok, head = lax.axis_index("tok"), lax.axis_index("head")
    near = head + 1 - 2 * lax.rem(head, 2)
    far = head + 2 - 4 * (head // 2)
    across_ = near + 2 - 4 * (near // 2)
    peers = tok_peers()
    greet([(tok, near), (tok, far)] + [target for target, _ in peers])
    rows = tokens.shape[0]
    pieces = rows // PIECE
    width = query.shape[1]
    columns_ = pl.ds(pl.multiple_of(head * width, HD), width)
    loads = [
        pltpu.make_async_copy(
            whole.at[:, columns_], weights.at[:, pl.ds(kind * width, width)], load_sems.at[kind]
        )
        for kind, whole in enumerate((w_query, w_key, w_value))
    ]
    for load in loads:
        load.start()

    def copy(source, owner, target, number):
        return pltpu.make_async_remote_copy(
            src_ref=source,
            dst_ref=gathered.at[owner, pl.ds(number % pieces * PIECE, PIECE)],
            send_sem=send_sems.at[number],
            recv_sem=recv_sems.at[number],
            device_id=(tok, target),
            device_id_type=MESH,
        )

    def own(number):
        return tokens.at[pl.ds(number * PIECE, PIECE)]

    afar = [copy(own(i), head, far, i) for i in range(pieces)]
    beside = [copy(own(i), head, near, pieces + i) for i in range(pieces)]
    for one in afar + beside:
        one.start()

    def work(found, owner, number):
        at = pl.ds(pl.multiple_of(owner * rows + number * PIECE, PIECE), PIECE)
        low = row_norm(found, gain[...], bias[...])
        hid[at, :] = low
        feed_rows[at, :] = hid[at, columns_]
        mixed = jnp.dot(low, weights[...], preferred_element_type=jnp.float32).astype(
            jnp.bfloat16
        )
        query[at, :] = mixed[:, :width]
        key[at, :] = mixed[:, width : 2 * width]
        value[at, :] = mixed[:, 2 * width :]

    def block(owner, number):
        return gathered[owner, number * PIECE : (number + 1) * PIECE, :]

    for load in loads:
        load.wait()
    for i in range(pieces):
        work(tokens[i * PIECE : (i + 1) * PIECE, :], head, i)
    for i in range(pieces):
        beside[i].wait_recv()
        work(block(near, i), near, i)
    passed = []
    for i in range(pieces):
        afar[i].wait_recv()
        one = copy(
            gathered.at[far, pl.ds(i * PIECE, PIECE)], far, near, 2 * pieces + i
        )
        one.start()
        passed.append(one)
        work(block(far, i), far, i)
    for i in range(pieces):
        passed[i].wait_recv()
        work(block(across_, i), across_, i)

    here, count = tok, every.shape[0]
    decay, chunk_decay, _, span_decay, _ = decay_tables(rate[...], feed_rows.shape[0])
    length = feed_rows.shape[0] // SUB
    span = feed_rows.shape[0]
    second = seq_starts[1] - here * span
    keep = [kept(second, chunk * length, (chunk + 1) * length) for chunk in range(SUB)]
    groups = feed_rows.shape[1] // HD
    zero = jnp.zeros((SUB, HD), jnp.float32)

    def rim(source, target, number):
        copy = pltpu.make_async_remote_copy(
            src_ref=source,
            dst_ref=target,
            send_sem=rim_sems.at[0, number],
            recv_sem=rim_sems.at[1, number],
            device_id=peers[0][0],
            device_id_type=MESH,
        )

        @pl.when(here < count - 1)
        def _():
            copy.start()

        return copy

    @pl.when(here == 0)
    def _():
        for target in (key_rim, value_rim, context_rim):
            target[...] = jnp.zeros_like(target)

    window = key_rim.shape[0]
    sent = [rim(key.at[pl.ds(span - window, window)], key_rim, 0)]
    for group in range(groups):
        lanes = slice(group * HD, (group + 1) * HD)
        drives[group] = feed_rows[:, lanes].astype(jnp.float32)
        factors = [spread(decay[:, lanes], n) for n in range(NS)]

        def end_step(t, states, live):
            drive = drives[group, pl.ds(t, SUB, stride=length), :]
            return tuple(s * live * f + drive for s, f in zip(states, factors))

        done = every_step(length, second, False, end_step, (zero,) * NS)
        for n in range(NS):
            ends[n, :, lanes] = done[n]
    now = ends[:, 0, :]
    for chunk in range(1, SUB):
        now = keep[chunk] * (chunk_decay * now) + ends[:, chunk, :]
    mine[...] = now
    every[here] = now
    copies = share(mine, every, share_sends, share_recvs, here, peers)
    sent.append(rim(value.at[pl.ds(span - window, window)], value_rim, 1))
    for copy in copies:
        copy.wait()
    now = jnp.zeros_like(span_decay)
    for place in range(count - 1):
        whole = kept(seq_starts[1], place * span, (place + 1) * span)
        now = jnp.where(place < here, whole * (span_decay * now) + every[place], now)
    for chunk in range(SUB):
        own = ends[:, chunk, :]
        ends[:, chunk, :] = now
        now = keep[chunk] * (chunk_decay * now) + own

    window = context_rim.shape[0]
    for group in range(groups):
        lanes = slice(group * HD, (group + 1) * HD)
        factors = [spread(decay[:, lanes], n) for n in range(NS)]
        mixes = [spread(mix[:, lanes], n) for n in range(NS)]
        direct = spread(skip[:, lanes], 0)

        def out_step(t, states, live):
            at = pl.ds(t, SUB, stride=length)
            drive = drives[group, at, :]
            states = tuple(s * live * f + drive for s, f in zip(states, factors))
            parts = [state * weight for state, weight in zip(states, mixes)] + [direct * drive]
            while len(parts) > 1:
                parts = [a + b for a, b in zip(parts[::2], parts[1::2])] + (
                    [parts[-1]] if len(parts) % 2 else []
                )
            total[group, at, :] = parts[0]
            return states

        every_step(
            length, second, False, out_step, tuple(ends[n, :, lanes] for n in range(NS))
        )
        context[:, lanes] = total[group].astype(context.dtype)
        sent.append(
            rim(
                context.at[pl.ds(span - window, window), pl.ds(group * HD, HD)],
                context_rim.at[:, pl.ds(group * HD, HD)],
                2 + group,
            )
        )
    @pl.when(here > 0)
    def _():
        for copy in sent:
            copy.wait_recv()

    @pl.when(here < count - 1)
    def _():
        for copy in sent:
            copy.wait_send()

    for one in afar + beside + passed:
        one.wait_send()


def front(seq_starts, tokens, gain, bias, rate, mix, skip, w_query, w_key, w_value, collective_id):
    rows, depth = tokens.shape
    heads, toks = lax.axis_size("head"), lax.axis_size("tok")
    span, width = rows * heads, w_query.shape[1] // heads
    groups, window = width // HD, 2 * BLOCK
    low = lambda count: jax.ShapeDtypeStruct((span, count), jnp.bfloat16)
    rim = lambda count: jax.ShapeDtypeStruct((count, width), jnp.bfloat16)
    fulls = lambda *shape: pltpu.VMEM(shape, jnp.float32)
    sems = lambda *shape: pltpu.SemaphoreType.DMA(shape)
    found = pl.pallas_call(
        front_kernel,
        in_specs=[SCALARS] + [VMEM] * 6 + [pl.BlockSpec(memory_space=pl.ANY)] * 3,
        out_specs=[VMEM] * 10,
        out_shape=[
            low(depth),
            low(width),
            low(width),
            low(width),
            low(width),
            jax.ShapeDtypeStruct((depth, 3 * width), jnp.bfloat16),
            low(width),
            rim(window),
            rim(window),
            rim(window + CTX),
        ],
        scratch_shapes=[
            pltpu.VMEM((heads, rows, depth), jnp.bfloat16),
            fulls(groups, span, HD),
            fulls(groups, span, HD),
            fulls(NS, SUB, width),
            fulls(NS, width),
            fulls(toks, NS, width),
            sems(3 * (rows // PIECE)),
            sems(3 * (rows // PIECE)),
            sems(3),
            sems(toks - 1),
            sems(toks - 1),
            sems(2, 2 + groups),
        ],
        compiler_params=pltpu.CompilerParams(
            collective_id=collective_id, has_side_effects=True, vmem_limit_bytes=60 * MIB
        ),
        name="front",
    )(seq_starts, tokens, gain, bias, rate, mix, skip, w_query, w_key, w_value)
    return tuple(found[:7]) + (found[7:],)


def recurrence_back_kernel(
    stages,
    seq_starts,
    slope,
    feed_rows,
    rate,
    mix,
    skip,
    key_sum,
    value_sum,
    key_rim,
    value_rim,
    context_rim,
    lefts,
    rights,
    down_keep,
    down_come,
    back_key,
    back_value,
    back,
    sums,
    lag_sums,
    skip_sum,
    down_out,
    up_out,
    slopes,
    rows,
    total,
    ends,
    lags,
    mine,
    every,
    share_sends,
    share_recvs,
    key_in,
    value_in,
    context_in,
    rim_sems,
    down_now,
    down_arrivals,
    down_sems,
    grads,
    up_arrivals,
    up_sems,
):
    here, count = lax.axis_index("tok"), every.shape[0]
    peers = tok_peers()
    ladder = mesh_bits()
    heads = bits_of(lax.axis_size("head"))
    greet([target for target, _ in peers] + [partner for _, partner in ladder[:heads]])

    rims = []
    for number, (source, target) in enumerate(
        ((context_rim, context_in), (key_rim, key_in), (value_rim, value_in))
    ):
        rims.append(
            pltpu.make_async_remote_copy(
                src_ref=source,
                dst_ref=target,
                send_sem=rim_sems.at[0, number],
                recv_sem=rim_sems.at[1, number],
                device_id=peers[-1][0],
                device_id_type=MESH,
            )
        )

    @pl.when(here == count - 1)
    def _():
        for target in (context_in, key_in, value_in):
            target[...] = jnp.zeros_like(target)

    @pl.when(here > 0)
    def _():
        for copy in rims:
            copy.start()

    down_stages = stages[1] + stages[2]
    down = Halver(down_now, down_stages, down_arrivals, down_sems, ladder, DOWN_ORDERS)
    for number in (1, 2, 0):
        down_now[number][...] = down_keep[number][...] + down_come[number][...]
        if number:
            down.send(number, down_stages[0])
    up = Halver(grads, stages[0], up_arrivals, up_sems, ladder, UP_ORDERS)
    for number, parts in enumerate(UP_PARTS if grads else ()):
        column = 0
        for pair, start, stop in parts:
            fill(
                lefts[pair], rights[pair], start, stop, grads[number], column, up.orders[number]
            )
            column += stop - start
        up.send(number, stages[0][0])
    if grads:
        up.absorb(0, stages[0][0])
        up.send(0, stages[0][1])

    @pl.when(here < count - 1)
    def _():
        rims[0].wait_recv()

    span = slope.shape[0]
    decay, factor, bend, over, over_slope = decay_tables(rate[...], span)
    length = span // SUB
    second = seq_starts[1] - here * span
    keep = [kept(second, chunk * length, (chunk + 1) * length) for chunk in range(SUB)]
    groups = slope.shape[1] // HD
    zero = jnp.zeros((SUB, HD), jnp.float32)
    for group in range(groups):
        lanes = slice(group * HD, (group + 1) * HD)
        slopes[group] = slope[:, lanes]
        slopes[group, span - context_in.shape[0] :, :] += context_in[:, lanes].astype(jnp.float32)
        rows[group] = feed_rows[:, lanes].astype(jnp.float32)
        total[group] = slopes[group] * skip[:, lanes]
        skip_sum[:, lanes] = jnp.sum(slopes[group] * rows[group], axis=0, keepdims=True)
        factors = [spread(decay[:, lanes], n) for n in range(NS)]

        def end_step(t, carry, live):
            drive = slopes[group, pl.ds(t, SUB, stride=length), :]
            adjoint, lag = carry[:NS], carry[NS:]
            lag = [(a * f + b) * live for a, f, b in zip(lag, factors, adjoint)]
            adjoint = [(a * f + drive) * live for a, f in zip(adjoint, factors)]
            return tuple(adjoint) + tuple(lag)

        done = every_step(length, second, True, end_step, (zero,) * (2 * NS))
        for n in range(NS):
            ends[n, :, lanes] = done[n]
            lags[n, :, lanes] = done[NS + n]

    now, late = ends[:, SUB - 1, :], lags[:, SUB - 1, :]
    for chunk in reversed(range(SUB - 1)):
        late = keep[chunk] * (factor * late + bend * now) + lags[:, chunk, :]
        now = keep[chunk] * (factor * now) + ends[:, chunk, :]
    mine[0] = now
    mine[1] = late
    every[here, 0] = now
    every[here, 1] = late
    copies = share(mine, every, share_sends, share_recvs, here, peers)

    down.send(0, down_stages[0])
    down.advance(1)
    down.advance(2)
    for number in range(1, len(grads)):
        up.absorb(number, stages[0][0])
        up.send(number, stages[0][1])
    for copy in copies:
        copy.wait()
    now, late = jnp.zeros_like(over), jnp.zeros_like(over)
    for place in reversed(range(1, count)):
        reached = place > here
        whole = kept(seq_starts[1], place * span, (place + 1) * span)
        late = jnp.where(reached, whole * (over * late + over_slope * now) + every[place, 1], late)
        now = jnp.where(reached, whole * (over * now) + every[place, 0], now)
    for chunk in reversed(range(SUB)):
        own, own_late = ends[:, chunk, :], lags[:, chunk, :]
        ends[:, chunk, :] = now
        lags[:, chunk, :] = late
        late = keep[chunk] * (factor * late + bend * now) + own_late
        now = keep[chunk] * (factor * now) + own

    for group in range(groups):
        lanes = slice(group * HD, (group + 1) * HD)
        for base in range(0, NS, HALF):
            factors = [spread(decay[:, lanes], base + n) for n in range(HALF)]
            mixes = [spread(mix[:, lanes], base + n) for n in range(HALF)]

            def out_step(t, carry, live):
                at = pl.ds(t, SUB, stride=length)
                drive, source = slopes[group, at, :], rows[group, at, :]
                adjoint, lag = carry[:HALF], carry[HALF : 2 * HALF]
                direct, late_sum = carry[2 * HALF : 3 * HALF], carry[3 * HALF :]
                lag = [a * f + b for a, f, b in zip(lag, factors, adjoint)]
                adjoint = [a * f + drive for a, f in zip(adjoint, factors)]
                direct = [a + b * source for a, b in zip(direct, adjoint)]
                late_sum = [a + b * source for a, b in zip(late_sum, lag)]
                parts = [a * b for a, b in zip(adjoint, mixes)]
                while len(parts) > 1:
                    parts = [a + b for a, b in zip(parts[::2], parts[1::2])]
                total[group, at, :] = total[group, at, :] + parts[0]
                lag = [a * live for a in lag]
                adjoint = [a * live for a in adjoint]
                return tuple(adjoint) + tuple(lag) + tuple(direct) + tuple(late_sum)

            if group == 0 and base > 0:
                down.advance(0)
                down.advance(1)
                down.advance(2)
            if group == 1 and base == 0:
                down.advance(0)
            first = tuple(ends[base + n, :, lanes] for n in range(HALF)) + tuple(
                lags[base + n, :, lanes] for n in range(HALF)
            )
            done = every_step(length, second, True, out_step, first + (zero,) * (2 * HALF))
            for n in range(HALF):
                sums[base + n : base + n + 1, lanes] = jnp.sum(
                    done[2 * HALF + n], axis=0, keepdims=True
                )
                lag_sums[base + n : base + n + 1, lanes] = jnp.sum(
                    done[3 * HALF + n], axis=0, keepdims=True
                )
        back[:, lanes] = total[group].astype(back.dtype)
    finished = [down.last(number) for number in range(len(down_now))]
    column = 0
    for piece in finished:
        down_out[:, column : column + piece.shape[1]] = piece
        column += piece.shape[1]

    @pl.when(here < count - 1)
    def _():
        rims[1].wait_recv()
        rims[2].wait_recv()

    inner = span - key_in.shape[0]
    for source, more, target in (
        (key_sum, key_in, back_key),
        (value_sum, value_in, back_value),
    ):
        target[:inner, :] = source[:inner, :].astype(target.dtype)
        target[inner:, :] = (source[inner:, :] + more[...].astype(jnp.float32)).astype(
            target.dtype
        )
    up.step(stages[0][1], up_out)
    down.drain()
    up.drain()

    @pl.when(here > 0)
    def _():
        for copy in rims:
            copy.wait_send()


def recurrence_back(
    seq_starts, slope, feed_rows, rate, mix, skip, sums, rims, lefts, rights, down, collective_id
):
    span, width = feed_rows.shape
    toks = lax.axis_size("tok")
    devices = toks * lax.axis_size("head")
    stages = stage_groups(devices)
    block = lefts[0].shape[1] // devices
    apart, up_pieces = None, [(block, part) for part in UP_WIDTHS]
    if block < 16:
        apart = products_apart(lefts, rights)
        lefts, rights, up_pieces = [], [], []
    keep, come = down
    down_pieces = [piece.shape[1:] for piece in keep]
    late = stages[1] + stages[2]
    down_buffers, down_count, down_sems = halver_scratch(down_pieces, late, devices)
    up_buffers, up_count, up_sems = halver_scratch(up_pieces, stages[0], devices)
    down_width = sum(piece[1] for piece in down_pieces)
    up_shapes = left_over(up_pieces, stages[0], devices)
    full = lambda *shape: jax.ShapeDtypeStruct(shape, jnp.float32)
    fulls = lambda *shape: pltpu.VMEM(shape, jnp.float32)
    sems = lambda *shape: pltpu.SemaphoreType.DMA(shape)
    groups = width // HD
    scratch = [
        fulls(groups, span, HD),
        fulls(groups, span, HD),
        fulls(groups, span, HD),
        fulls(NS, SUB, width),
        fulls(NS, SUB, width),
        fulls(2, NS, width),
        fulls(toks, 2, NS, width),
        sems(toks - 1),
        sems(toks - 1),
    ]
    low = lambda count: jax.ShapeDtypeStruct((count, width), jnp.bfloat16)
    scratch += [pltpu.VMEM(rims[k].shape, jnp.bfloat16) for k in (0, 1, 2)]
    scratch += [sems(2, 3)] + [pltpu.VMEM(piece.shape, jnp.bfloat16) for piece in keep]
    scratch += down_buffers + [down_sems]
    scratch += [pltpu.VMEM((devices,) + piece, jnp.bfloat16) for piece in up_pieces]
    scratch += up_buffers + [up_sems]
    pairs, ups, downs = len(lefts) or -1, len(up_pieces) or -1, len(keep)
    sizes = [0] * 11 + [pairs, pairs, downs, downs] + [0] * 6 + [0, ups] + [0] * 9
    sizes += [0] * 4 + [downs, down_count, 0, ups, up_count, 0]
    found = pl.pallas_call(
        unpack_refs(functools.partial(recurrence_back_kernel, stages), sizes),
        in_specs=[SCALARS] + [VMEM] * (10 + 2 * len(lefts) + 2 * downs),
        out_specs=[VMEM] * (7 + len(up_shapes)),
        out_shape=[
            low(span),
            low(span),
            low(span),
            full(NS, width),
            full(NS, width),
            full(1, width),
        ]
        + [full(down_pieces[0][0], down_width)]
        + up_shapes,
        scratch_shapes=scratch,
        compiler_params=pltpu.CompilerParams(
            collective_id=collective_id, has_side_effects=True, vmem_limit_bytes=60 * MIB
        ),
        name="recurrence_back",
    )(
        seq_starts,
        slope,
        feed_rows,
        rate,
        mix,
        skip,
        *sums,
        *rims,
        *lefts,
        *rights,
        *keep,
        *come,
    )
    return tuple(found[:6]) + (found[6], found[7:], apart)


CHUNK = 1024
UP_CHUNK = 512
ROOT = math.sqrt(2.0 / math.pi)
CUBIC = 0.044715


def feed_kernel(
    stages,
    attended,
    tokens,
    out_grad,
    gain,
    bias,
    up_bias,
    down_bias,
    w_output,
    w_up,
    w_down,
    layer_out,
    grad_middle,
    normed,
    grad_before,
    joined,
    grad_branch,
    grad_att,
    down_left,
    vectors,
    grad_up_bias,
    output_w,
    up_w,
    down_w,
    split,
    active,
    bend,
    drive,
    shape,
    down_sum,
    back_sum,
    grad_split,
    grads,
    arrivals,
    weight_sems,
    down_sems,
    head_sems,
    halver_sems,
):
    tok, head = lax.axis_index("tok"), lax.axis_index("head")
    heads = lax.axis_size("head")
    rows, width = tokens.shape[0], attended.shape[1]
    hidden = up_w.shape[1]
    loads = [
        pltpu.make_async_copy(source, target, weight_sems.at[number])
        for number, (source, target) in enumerate(
            ((w_output, output_w), (w_up, up_w))
        )
    ]

    def down_load(chunk):
        slot = lax.rem(chunk, 2)
        return pltpu.make_async_copy(
            w_down.at[pl.ds(pl.multiple_of(chunk * CHUNK, CHUNK), CHUNK)],
            down_w.at[slot],
            down_sems.at[slot],
        )

    for load in loads:
        load.start()
    for chunk in range(2):
        down_load(chunk).start()
    peers = [lax.rem(head + step, heads) for step in range(1, heads)]
    ladder = mesh_bits()
    greet([(tok, other) for other in peers] + [p for _, p in ladder[bits_of(heads) :]])

    def block_of(owner):
        return pl.ds(pl.multiple_of(owner * rows, PIECE), rows)

    def swap(source_of, target, kind):
        found = []
        for step, other in enumerate(peers):
            copy = pltpu.make_async_remote_copy(
                src_ref=source_of(other),
                dst_ref=target,
                send_sem=head_sems.at[kind, 0, step],
                recv_sem=head_sems.at[kind, 1, step],
                device_id=(tok, other),
                device_id_type=MESH,
            )
            copy.start()
            found.append(copy)
        return found

    def drive_chunk(chunk, _):
        at = pl.ds(pl.multiple_of(chunk * CHUNK, CHUNK), CHUNK)
        down_load(chunk).wait()
        drive[:, at] = across(out_grad[...], down_w[lax.rem(chunk, 2)]).astype(jnp.bfloat16)
        down_load(lax.rem(chunk + 2, chunks)).start()
        return 0

    chunks = hidden // CHUNK
    first = swap(lambda other: attended.at[block_of(other)], split.at[head], 0)
    split[head] = attended[block_of(head), :]
    lax.fori_loop(0, chunks, drive_chunk, 0)
    loads[0].wait()
    for copy in first:
        copy.wait_recv()
    total = tokens[...].astype(jnp.float32)
    for owner in range(heads):
        at = slice(owner * width, (owner + 1) * width)
        joined[:, at] = split[owner]
        total += jnp.dot(split[owner], output_w[at, :], preferred_element_type=jnp.float32)
    grad_middle[...] = total
    centred = total - jnp.mean(total, axis=-1, keepdims=True)
    scale = lax.rsqrt(jnp.mean(centred * centred, axis=-1, keepdims=True) + epsilon)
    shape[...] = centred * scale
    normed[...] = (centred * scale * gain[...] + bias[...]).astype(jnp.bfloat16)

    loads[1].wait()

    def up_chunk(chunk, _):
        at = pl.ds(pl.multiple_of(chunk * UP_CHUNK, UP_CHUNK), UP_CHUNK)
        before = jnp.dot(normed[...], up_w[:, at], preferred_element_type=jnp.float32)
        before += up_bias[:, at]
        square = before * before
        bent = jnp.tanh(ROOT * before * (1.0 + CUBIC * square))
        half = 0.5 * (1.0 + bent)
        active[:, at] = (before * half).astype(jnp.bfloat16)
        bend[:, at] = half + (0.5 * ROOT) * before * (1.0 - bent * bent) * (
            1.0 + (3.0 * CUBIC) * square
        )
        return 0

    lax.fori_loop(0, hidden // UP_CHUNK, up_chunk, 0)
    halver = Halver(grads, stages, arrivals, halver_sems, ladder, DOWN_ORDERS)
    starts = [sum(DOWN_PARTS[:k]) for k in range(len(DOWN_PARTS) + 1)]
    for k, order in enumerate(halver.orders):
        fill(active, out_grad, starts[k], starts[k + 1], grads[k], 0, order)
        halver.send(k, stages[0])

    back_sum[...] = jnp.zeros_like(back_sum)

    def back_chunk(chunk, _):
        at = pl.ds(pl.multiple_of(chunk * CHUNK, CHUNK), CHUNK)
        low = (drive[:, at].astype(jnp.float32) * bend[:, at]).astype(jnp.bfloat16)
        grad_before[:, at] = low
        grad_up_bias[:, at] = jnp.sum(low.astype(jnp.float32), axis=0, keepdims=True)
        back_sum[...] += across(low, up_w[:, at])
        return 0

    lax.fori_loop(0, chunks, back_chunk, 0)
    back = back_sum[...]
    shaped = shape[...]
    vectors[0:1, :] = jnp.sum(back * shaped, axis=0, keepdims=True)
    vectors[1:2, :] = jnp.sum(back, axis=0, keepdims=True)
    top = out_grad[...].astype(jnp.float32)
    vectors[2:3, :] = jnp.sum(top, axis=0, keepdims=True)
    back = back * gain[...]
    back = back - jnp.mean(back, axis=-1, keepdims=True)
    back = back - shaped * jnp.mean(back * shaped, axis=-1, keepdims=True)
    total = grad_middle[...]
    centred = total - jnp.mean(total, axis=-1, keepdims=True)
    scale = lax.rsqrt(jnp.mean(centred * centred, axis=-1, keepdims=True) + epsilon)
    down_sum[...] = total + down_bias[...]
    top = top + back * scale
    grad_middle[...] = top
    low = top.astype(jnp.bfloat16)
    grad_branch[...] = low
    for owner in range(heads):
        at = slice(owner * width, (owner + 1) * width)
        grad_split[owner] = across(low, output_w[at, :]).astype(jnp.bfloat16)
    second = swap(lambda other: grad_split.at[other], grad_att.at[block_of(head)], 1)
    grad_att[block_of(head), :] = grad_split[head]

    def down_chunk(chunk, _):
        at = pl.ds(pl.multiple_of(chunk * CHUNK, CHUNK), CHUNK)
        down_load(chunk).wait()
        down_sum[...] += jnp.dot(
            active[:, at], down_w[lax.rem(chunk, 2)], preferred_element_type=jnp.float32
        )

        @pl.when(chunk + 2 < chunks)
        def _():
            down_load(chunk + 2).start()

        return 0

    for k in range(len(grads)):
        halver.part(k, stages[0], down_left[2 * k], down_left[2 * k + 1])
    lax.fori_loop(0, chunks, down_chunk, 0)
    layer_out[...] = down_sum[...].astype(jnp.bfloat16)
    for copy in second:
        copy.wait_recv()
    halver.drain()
    for copy in first + second:
        copy.wait_send()


def feed(
    attended,
    tokens,
    out_grad,
    gain,
    bias,
    up_bias,
    down_bias,
    w_output,
    w_up,
    w_down,
    collective_id,
):
    rows, depth = tokens.shape
    span, width = attended.shape
    hidden = w_up.shape[1]
    heads = lax.axis_size("head")
    devices = heads * lax.axis_size("tok")
    block = hidden // devices
    stages = stage_groups(devices)[0][:1]
    pieces = [(block, part) for part in DOWN_PARTS]
    buffers, buffer_count, halver_sems = halver_scratch(pieces, stages, devices)
    low = lambda *shape: jax.ShapeDtypeStruct(shape, jnp.bfloat16)
    full = lambda *shape: jax.ShapeDtypeStruct(shape, jnp.float32)
    any_ = pl.BlockSpec(memory_space=pl.ANY)
    sems = lambda *shape: pltpu.SemaphoreType.DMA(shape)
    lows = lambda *shape: pltpu.VMEM(shape, jnp.bfloat16)
    fulls = lambda *shape: pltpu.VMEM(shape, jnp.float32)
    scratch = [
        lows(depth, depth),
        lows(depth, hidden),
        lows(2, CHUNK, depth),
        lows(heads, rows, width),
        lows(rows, hidden),
        fulls(rows, hidden),
        lows(rows, hidden),
        fulls(rows, depth),
        fulls(rows, depth),
        fulls(rows, depth),
        lows(heads, rows, width),
    ]
    scratch += [lows(devices, block, part) for part in DOWN_PARTS]
    scratch += buffers
    scratch += [sems(2), sems(2), sems(2, 2, heads - 1), halver_sems]
    count = len(pieces)
    sizes = [0] * 17 + [2 * count] + [0] * 13 + [count, buffer_count] + [0] * 4
    outs = [
        low(rows, depth),
        full(rows, depth),
        low(rows, depth),
        low(rows, hidden),
        low(rows, depth),
        low(rows, depth),
        low(span, width),
    ]
    outs += left_over([piece for piece in pieces for _ in (0, 1)], [1], devices)
    outs += [full(SUB, depth), full(1, hidden)]
    return pl.pallas_call(
        unpack_refs(functools.partial(feed_kernel, stages), sizes),
        in_specs=[VMEM] * 7 + [any_] * 3,
        out_specs=[VMEM] * len(outs),
        out_shape=outs,
        scratch_shapes=scratch,
        compiler_params=pltpu.CompilerParams(
            collective_id=collective_id, has_side_effects=True, vmem_limit_bytes=63 * MIB
        ),
        name="feed",
    )(
        attended, tokens, out_grad, gain, bias, up_bias, down_bias, w_output, w_up, w_down
    )


def layer_norm(row_block, gain, bias):
    centre = jnp.mean(row_block, axis=-1, keepdims=True)
    centred = row_block - centre
    spread = jnp.mean(centred * centred, axis=-1, keepdims=True)
    return centred * lax.rsqrt(spread + epsilon) * gain + bias


def product(left, right):
    return jnp.dot(left, right, preferred_element_type=jnp.float32)


def product_left(left, right):
    return lax.dot_general(
        left, right, (((0,), (0,)), ((), ())), preferred_element_type=jnp.float32
    )


def product_right(left, right):
    return lax.dot_general(
        left, right, (((1,), (1,)), ((), ())), preferred_element_type=jnp.float32
    )


def per_device(
    tokens_in,
    seq_starts,
    block_sizes,
    norm1_gain,
    norm1_bias,
    w_query,
    w_key,
    w_value,
    w_output,
    ssm_rate,
    ssm_input,
    ssm_output,
    ssm_skip,
    norm2_gain,
    norm2_bias,
    w_up,
    up_bias,
    w_down,
    down_bias,
    out_grad,
):
    tok_rows = tokens_in.shape[0]
    pieces = lax.axis_size("tok")
    span = tok_rows * lax.axis_size("head")
    total_len = span * pieces

    rate = ssm_rate.T / total_len
    drive_in, read_out = ssm_input.T, ssm_output.T
    decay = jnp.exp(-rate)
    gain = jnp.sqrt(-jnp.expm1(-2.0 * rate))
    driving = gain * drive_in
    mix = read_out * driving
    skip = ssm_skip[None, :]
    hid, query_h, key_h, value_h, hidden_h, w_own, context, rims = front(
        seq_starts,
        tokens_in,
        norm1_gain[None, :],
        norm1_bias[None, :],
        rate,
        mix,
        skip,
        w_query,
        w_key,
        w_value,
        6,
    )
    attended, attended_fine, level = attend(seq_starts, block_sizes, query_h, key_h, value_h, context, rims)
    (
        layer_out,
        grad_middle,
        normed_low,
        grad_before_low,
        joined,
        grad_branch,
        grad_att,
        *down,
        vectors,
        grad_up_bias,
    ) = feed(
        attended,
        tokens_in,
        out_grad,
        norm2_gain[None, :],
        norm2_bias[None, :],
        up_bias[None, :],
        down_bias[None, :],
        w_output,
        w_up,
        w_down,
        7,
    )
    orders = halving_orders(bits_of(pieces * lax.axis_size("head")))
    come = [
        swapped(leave, orders[order][1]) for leave, order in zip(down[1::2], DOWN_ORDERS)
    ]

    back_query_h, key_rim, value_rim, near_rim, back_key_h, back_value_h, back_context = attend_back(
        seq_starts, block_sizes, query_h, key_h, value_h, context, rims, attended_fine, grad_att, level
    )
    (
        back_key_h,
        back_value_h,
        back_feed_h,
        sums,
        lag_sums,
        skip_sum,
        out_w_down,
        up,
        apart,
    ) = recurrence_back(
        seq_starts,
        back_context,
        hidden_h,
        rate,
        mix,
        skip,
        [back_key_h, back_value_h],
        [key_rim, value_rim, near_rim],
        [normed_low, joined],
        [grad_before_low, grad_branch],
        (down[::2], come),
        2,
    )
    input_grad, out_w_heads, summed, packed, up = head_backward(
        back_query_h,
        back_key_h,
        back_value_h,
        back_feed_h,
        hid,
        w_own,
        tokens_in,
        norm1_gain[None, :],
        grad_middle,
        sums,
        lag_sums,
        skip_sum,
        vectors,
        grad_up_bias,
        up,
        4,
    )
    heads, head = lax.axis_size("head"), lax.axis_index("head")
    part = norm1_gain.shape[0] // pieces
    more = up_bias.shape[0] // norm1_gain.shape[0]
    short = lax.dynamic_slice_in_dim(packed[:5], head * (part // heads), part // heads, 1)
    out_up_bias = lax.dynamic_slice_in_dim(
        packed[5 : 5 + more, :part].reshape(-1), head * (more * part // heads), more * part // heads
    )
    out_w_up, out_w_output = up if apart is None else apart
    sums, lag_sums, skip_sum = summed[:NS], summed[NS : 2 * NS], summed[2 * NS]
    grad_ssm_output = (driving * sums).T
    grad_driving = read_out * sums
    grad_ssm_input = (gain * grad_driving).T
    grad_ssm_rate = (
        grad_driving * drive_in * jnp.exp(-2.0 * rate) / gain - mix * lag_sums * decay
    ).T / total_len

    return (
        layer_out,
        input_grad,
        short[0],
        short[1],
        out_w_heads[0],
        out_w_heads[1],
        out_w_heads[2],
        out_w_output,
        grad_ssm_rate,
        grad_ssm_input,
        grad_ssm_output,
        skip_sum,
        short[2],
        short[3],
        out_w_up,
        out_up_bias,
        out_w_down,
        short[4],
    )


def solution(mesh):
    return jax.shard_map(
        per_device,
        mesh=mesh,
        in_specs=(
            P(("tok", "head"), None),
            P(),
            P(),
            P(),
            P(),
            P(),
            P(),
            P(),
            P(),
            P("head", None),
            P("head", None),
            P("head", None),
            P("head"),
            P(),
            P(),
            P(),
            P(),
            P(),
            P(),
            P(("tok", "head"), None),
        ),
        out_specs=(
            P(("tok", "head"), None),
            P(("tok", "head"), None),
            P(("tok", "head")),
            P(("tok", "head")),
            P(("tok", "head"), None),
            P(("tok", "head"), None),
            P(("tok", "head"), None),
            P(("tok", "head"), None),
            P("head", None),
            P("head", None),
            P("head", None),
            P("head"),
            P(("tok", "head")),
            P(("tok", "head")),
            P(("tok", "head"), None),
            P(("tok", "head")),
            P(("tok", "head"), None),
            P(("tok", "head")),
        ),
        check_vma=False,
    )
```

```python
import functools
import math

import jax
import jax.numpy as jnp
from jax import lax
from jax.experimental import pallas as pl
from jax.experimental.pallas import tpu as pltpu
from jax.sharding import PartitionSpec as P

epsilon = 1e-05
HD = 128
CTX = 128
BLOCK = 256
NS = 16
SUB = 8
UNROLL = 8
HALF = 8
TILE = 256
MIB = 1 << 20
LOWEST = -1e30
FACTOR = HD ** (-0.5)
FACTOR2 = FACTOR * math.log2(math.e)


def spread(table, n):
    return jnp.broadcast_to(table[n : n + 1, :], (SUB, table.shape[1]))


SCALARS = pl.BlockSpec(memory_space=pltpu.SMEM)


def wide(limit=48):
    return pltpu.CompilerParams(vmem_limit_bytes=limit * MIB)


def across(left, right):
    return lax.dot_general(
        left, right, (((1,), (1,)), ((), ())), preferred_element_type=jnp.float32
    )


def times(left, right):
    return lax.dot_general(
        left, right, (((1,), (0,)), ((), ())), preferred_element_type=jnp.float32
    )


def turn(source, target):
    for at in range(0, source.shape[0], TILE):
        size = min(TILE, source.shape[0] - at)
        piece = source[at : at + size, :].astype(jnp.float32)
        target[:, at : at + size] = piece.T.astype(target.dtype)


def next_block(where_, now):
    second = where_[1]
    length = jnp.where(now >= second, where_[3], where_[2])
    after = now + length
    return jnp.where((now < second) & (after > second), second, after)


REACH = 2 * BLOCK + TILE
BLOCKS = 4


def block_facts(starts, sizes, span):
    anchor = lax.axis_index("tok") * span
    return anchor, starts[1] - anchor, sizes[0], sizes[1]


def block_begin(where_, at):
    opening = jnp.where(at >= where_[1], where_[1], -where_[0])
    length = jnp.where(at >= where_[1], where_[3], where_[2])
    return opening + lax.div(at - opening, length) * length


def block_rows(where_, tile):
    cols = lax.broadcasted_iota(jnp.int32, (1, TILE), 1) + tile * TILE
    begin = block_begin(where_, tile * TILE)
    now, firsts = begin, jnp.zeros_like(cols) + begin
    for _ in range(BLOCKS):
        now = next_block(where_, now)
        firsts = jnp.where(cols >= now, now, firsts)
    return firsts, jnp.where(cols >= where_[1], where_[1], -where_[0]), begin


def joined_rows(rim, own, target):
    target[: rim.shape[0], :] = rim[...]
    target[rim.shape[0] :, :] = own[...]


def local_mask(tile, first):
    rows = lax.broadcasted_iota(jnp.int32, (REACH, TILE), 0) + (tile * TILE - 2 * BLOCK)
    cols = lax.broadcasted_iota(jnp.int32, (1, TILE), 1) + tile * TILE
    return (rows >= first) & (rows <= cols)


def context_at(now):
    return pl.multiple_of((now + 2 * BLOCK) // CTX * CTX, CTX)


def context_mask(start, now, first, opening):
    rows = lax.broadcasted_iota(jnp.int32, (TILE, TILE), 0) + (start - 2 * BLOCK - CTX)
    low = jnp.where(first == now, jnp.maximum(now - CTX, opening), 1 << 28)
    return (rows >= low) & (rows < now)


def lanes_of(head):
    return slice(head * HD, (head + 1) * HD)


def attend_kernel(
    starts,
    sizes,
    query,
    key_own,
    value_own,
    context_own,
    key_rim,
    value_rim,
    context_rim,
    out,
    fine,
    level,
    key,
    value,
    context,
    value_t,
    context_t,
):
    where_ = block_facts(starts, sizes, query.shape[0])
    joined_rows(key_rim, key_own, key)
    joined_rows(value_rim, value_own, value)
    joined_rows(context_rim, context_own, context)
    heads = query.shape[1] // HD
    turn(value, value_t)
    turn(context, context_t)

    def one_tile(tile, _):
        here = pl.ds(pl.multiple_of(tile * TILE, TILE), TILE)
        rows = [query[here, lanes_of(head)] for head in range(heads)]
        firsts, openings, begin = block_rows(where_, tile)

        def score(near, at, head, mask):
            return jnp.where(mask, across(near[at, lanes_of(head)], rows[head]) * FACTOR2, LOWEST)

        def peak(found):
            return jnp.max(found, axis=0, keepdims=True)

        def gather(prob, values_t, at, head):
            low = prob.astype(jnp.bfloat16)
            return (
                jnp.sum(prob, axis=0, keepdims=True),
                jnp.sum(low.astype(jnp.float32), axis=0, keepdims=True),
                times(values_t[lanes_of(head), at], low),
            )

        near_at = pl.ds(pl.multiple_of(tile * TILE, TILE), REACH)
        far_at = pl.ds(context_at(begin), TILE)
        near_mask = local_mask(tile, firsts)
        far_mask = context_mask(context_at(begin), begin, firsts, openings)
        carry = []
        for head in range(heads):
            near = score(key, near_at, head, near_mask)
            far = score(context, far_at, head, far_mask)
            top = jnp.maximum(peak(near), peak(far))
            one = gather(jnp.exp2(near - top), value_t, near_at, head)
            two = gather(jnp.exp2(far - top), context_t, far_at, head)
            carry.append((top,) + tuple(a + b for a, b in zip(one, two)))

        def earlier(state):
            now, carry = state
            start = context_at(now)
            at = pl.ds(start, TILE)
            mask = context_mask(start, now, firsts, openings)
            found = []
            for head in range(heads):
                top, mass, low_mass, total = carry[head]
                far = score(context, at, head, mask)
                new_top = jnp.maximum(top, peak(far))
                shrink = jnp.exp2(top - new_top)
                more = gather(jnp.exp2(far - new_top), context_t, at, head)
                found.append(
                    (new_top,)
                    + tuple(a * shrink + b for a, b in zip((mass, low_mass, total), more))
                )
            return next_block(where_, now), tuple(found)

        _, carry = lax.while_loop(
            lambda state: state[0] < (tile + 1) * TILE,
            earlier,
            (next_block(where_, begin), tuple(carry)),
        )
        for head in range(heads):
            top, mass, low_mass, total = carry[head]
            done = (total / low_mass).T
            fine[here, lanes_of(head)] = done
            out[here, lanes_of(head)] = done.astype(out.dtype)
            level[head, tile] = top + jnp.log2(mass)
        return 0

    lax.fori_loop(0, query.shape[0] // TILE, one_tile, 0)


def attend_back_kernel(
    starts,
    sizes,
    query,
    key_own,
    value_own,
    context_own,
    key_rim,
    value_rim,
    context_rim,
    attended,
    grad,
    level,
    back_query,
    back_key_rim,
    back_value_rim,
    back_context_rim,
    back_key,
    back_value,
    back_context,
    key,
    value,
    context,
    key_t,
    context_t,
    key_sum,
    value_sum,
    context_sum,
):
    where_ = block_facts(starts, sizes, query.shape[0])
    joined_rows(key_rim, key_own, key)
    joined_rows(value_rim, value_own, value)
    joined_rows(context_rim, context_own, context)
    heads = query.shape[1] // HD
    turn(key, key_t)
    turn(context, context_t)
    key_sum[...] = jnp.zeros_like(key_sum)
    value_sum[...] = jnp.zeros_like(value_sum)
    context_sum[...] = jnp.zeros_like(context_sum)

    def one_tile(tile, _):
        here = pl.ds(pl.multiple_of(tile * TILE, TILE), TILE)
        rows = [query[here, lanes_of(head)] for head in range(heads)]
        grads = [grad[here, lanes_of(head)] for head in range(heads)]
        firsts, openings, begin = block_rows(where_, tile)
        levels = [level[head, tile] for head in range(heads)]
        centres = []
        for head in range(heads):
            joint = grads[head].astype(jnp.float32) * attended[here, lanes_of(head)]
            centres.append(jnp.sum(joint.T, axis=0, keepdims=True))

        def slopes(keys, values, at, head, mask):
            found = across(keys[at, lanes_of(head)], rows[head]) * FACTOR2 - levels[head]
            prob = jnp.exp2(jnp.where(mask, found, LOWEST))
            drive = across(values[at, lanes_of(head)], grads[head])
            slope = prob * (drive - centres[head])
            return prob.astype(jnp.bfloat16), slope.astype(jnp.bfloat16)

        def earlier(state):
            now, totals = state
            start = context_at(now)
            at = pl.ds(start, TILE)
            mask = context_mask(start, now, firsts, openings)
            found = []
            for h in range(heads):
                prob, slope = slopes(context, context, at, h, mask)
                context_sum[at, lanes_of(h)] += FACTOR * times(slope, rows[h]) + times(
                    prob, grads[h]
                )
                found.append(totals[h] + times(context_t[lanes_of(h), at], slope))
            return next_block(where_, now), tuple(found)

        at = pl.ds(pl.multiple_of(tile * TILE, TILE), REACH)
        mask = local_mask(tile, firsts)
        totals = []
        for h in range(heads):
            prob, slope = slopes(key, value, at, h, mask)
            key_sum[at, lanes_of(h)] += times(slope, rows[h])
            value_sum[at, lanes_of(h)] += times(prob, grads[h])
            totals.append(times(key_t[lanes_of(h), at], slope))
        state = earlier((begin, tuple(totals)))
        _, totals = lax.while_loop(lambda state: state[0] < (tile + 1) * TILE, earlier, state)
        for head in range(heads):
            back_query[here, lanes_of(head)] = (FACTOR * totals[head]).T.astype(back_query.dtype)
        return 0

    lax.fori_loop(0, query.shape[0] // TILE, one_tile, 0)
    window = 2 * BLOCK
    back_key_rim[...] = (FACTOR * key_sum[:window, :]).astype(back_key_rim.dtype)
    back_value_rim[...] = value_sum[:window, :].astype(back_value_rim.dtype)
    back_context_rim[...] = context_sum[: window + CTX, :].astype(back_context_rim.dtype)
    back_key[...] = FACTOR * key_sum[window:, :]
    back_value[...] = value_sum[window:, :]
    back_context[...] = context_sum[window + CTX :, :]


VMEM = pl.BlockSpec(memory_space=pltpu.VMEM)


def attend(starts, sizes, query, key, value, context, rims):
    rows, width = query.shape
    heads, tiles = width // HD, rows // TILE
    near, far = rows + rims[0].shape[0], rows + rims[2].shape[0]
    low = lambda *shape: pltpu.VMEM(shape, jnp.bfloat16)
    return pl.pallas_call(
        attend_kernel,
        in_specs=[SCALARS] * 2 + [VMEM] * 7,
        out_specs=[VMEM] * 3,
        out_shape=(
            jax.ShapeDtypeStruct((rows, width), jnp.bfloat16),
            jax.ShapeDtypeStruct((rows, width), jnp.float32),
            jax.ShapeDtypeStruct((heads, tiles, 1, TILE), jnp.float32),
        ),
        scratch_shapes=[
            low(near, width),
            low(near, width),
            low(far, width),
            low(width, near),
            low(width, far),
        ],
        compiler_params=wide(60),
        name="attend",
    )(starts, sizes, query, key, value, context, *rims)


def attend_back(starts, sizes, query, key, value, context, rims, attended, grad, level):
    rows, width = query.shape
    near, far = rows + rims[0].shape[0], rows + rims[2].shape[0]
    low = lambda count: jax.ShapeDtypeStruct((count, width), jnp.bfloat16)
    full = lambda count: jax.ShapeDtypeStruct((count, width), jnp.float32)
    lows = lambda *shape: pltpu.VMEM(shape, jnp.bfloat16)
    fulls = lambda *shape: pltpu.VMEM(shape, jnp.float32)
    return pl.pallas_call(
        attend_back_kernel,
        in_specs=[SCALARS] * 2 + [VMEM] * 10,
        out_specs=[VMEM] * 7,
        out_shape=(
            low(rows),
            low(near - rows),
            low(near - rows),
            low(far - rows),
            full(rows),
            full(rows),
            full(rows),
        ),
        scratch_shapes=[
            lows(near, width),
            lows(near, width),
            lows(far, width),
            lows(width, near),
            lows(width, far),
            fulls(near, width),
            fulls(near, width),
            fulls(far, width),
        ],
        compiler_params=wide(60),
        name="attend_back",
    )(starts, sizes, query, key, value, context, *rims, attended, grad, level)


MESH = pl.DeviceIdType.MESH
ROWS = 1024


def bits_of(count):
    return count.bit_length() - 1


def mesh_bits():
    found = []
    tok, head = lax.axis_index("tok"), lax.axis_index("head")
    for axis in ("head", "tok"):
        for level in range(bits_of(lax.axis_size(axis))):
            at = head if axis == "head" else tok
            bit = (at // (1 << level)) % 2
            other = at + (1 - 2 * bit) * (1 << level)
            found.append((bit, (tok, other) if axis == "head" else (other, head)))
    return found


def greet(partners):
    barrier = pltpu.get_barrier_semaphore()
    for partner in partners:
        pl.semaphore_signal(barrier, inc=1, device_id=partner, device_id_type=MESH)
    pl.semaphore_wait(barrier, len(partners))


def halving_orders(bits):
    rest = list(range(4, bits))
    return [
        [0, 1, 2, 3] + rest,
        [0, 2, 1, 3] + rest,
        [0, 3, 2, 1] + rest,
        [0, 3, 1, 2] + rest,
        [0, 2, 3, 1] + rest,
    ]


def slot_of(block, order):
    place = 0
    for bit in order:
        place = place * 2 + (block // (1 << bit)) % 2
    return place


def unpack_refs(function, sizes):
    def kernel(*refs):
        grouped, at = [], 0
        for size in sizes:
            grouped.append(refs[at] if size == 0 else refs[at : at + max(size, 0)])
            at += 1 if size == 0 else max(size, 0)
        function(*grouped)

    return kernel


class Halver:
    def __init__(self, pieces, stages, arrivals, sems, ladder, orders):
        self.now, self.stages, self.arrivals, self.ladder = list(pieces), stages, arrivals, ladder
        self.sems, self.steps = sems, len(ladder)
        self.orders = [halving_orders(self.steps)[order] for order in orders]
        self.sent, self.flying, self.doing = [], {}, {}

    def half(self, stage):
        return 1 << (self.steps - 1 - stage)

    def send(self, number, stage):
        bit, partner = self.ladder[self.orders[number][stage]]
        at = number * len(self.stages) + self.stages.index(stage)
        half = self.half(stage)
        copy = pltpu.make_async_remote_copy(
            src_ref=self.now[number].at[pl.ds((1 - bit) * half, half)],
            dst_ref=self.arrivals[at],
            send_sem=self.sems.at[0, at],
            recv_sem=self.sems.at[1, at],
            device_id=partner,
            device_id_type=MESH,
        )
        copy.start()
        self.sent.append(copy)
        self.flying[number] = (copy, self.arrivals[at], bit * half)
        self.doing[number] = stage

    def absorb(self, number, stage, into=None):
        copy, arrival, keep = self.flying[number]
        copy.wait_recv()
        before = self.now[number]
        target = arrival if into is None else into

        def add(i, _):
            target[i] = before[keep + i] + arrival[i]
            return 0

        lax.fori_loop(0, self.half(stage), add, 0)
        self.now[number] = target

    def part(self, number, stage, keep, leave):
        copy, arrival, base = self.flying[number]
        copy.wait_recv()
        before, half = self.now[number], self.half(stage + 1)
        bit = self.ladder[self.orders[number][stage + 1]][0]
        for at, target in ((bit * half, keep), ((1 - bit) * half, leave)):

            def add(i, _):
                target[i] = before[base + at + i] + arrival[at + i]
                return 0

            lax.fori_loop(0, half, add, 0)

    def last(self, number):
        while self.doing[number] != self.stages[-1]:
            self.advance(number)
        copy, arrival, keep = self.flying[number]
        copy.wait_recv()
        return self.now[number][keep].astype(jnp.float32) + arrival[0].astype(jnp.float32)

    def step(self, stage, into=None):
        for number in range(len(self.now)):
            self.absorb(number, stage, None if into is None else into[number])
            if into is None:
                self.send(number, stage + 1)

    def advance(self, number):
        stage = self.doing[number]
        if stage != self.stages[-1]:
            self.absorb(number, stage)
            self.send(number, stage + 1)

    def begin(self):
        for number in range(len(self.now)):
            self.send(number, self.stages[0])

    def drain(self):
        for copy in self.sent:
            copy.wait_send()


def halver_scratch(pieces, stages, devices):
    steps = bits_of(devices)
    buffers = [
        pltpu.VMEM((1 << (steps - 1 - stage), block, width), jnp.bfloat16)
        for block, width in pieces
        for stage in stages
    ]
    sems = pltpu.SemaphoreType.DMA((2, max(len(buffers), 1)))
    return buffers, len(buffers) or -1, sems


def left_over(pieces, stages, devices):
    slots = 1 << (bits_of(devices) - 1 - stages[-1])
    return [jax.ShapeDtypeStruct((slots, block, width), jnp.bfloat16) for block, width in pieces]


def fill(left, right, start, stop, target, column, order):
    block = target.shape[1]
    each = ROWS // block
    for low in range(start, stop, ROWS):
        high = min(low + ROWS, stop)
        to = column + low - start

        def some_rows(chunk, _):
            at = pl.ds(pl.multiple_of(chunk * ROWS, ROWS), ROWS)
            found = lax.dot_general(
                left[:, at],
                right[:, low:high],
                (((0,), (0,)), ((), ())),
                preferred_element_type=jnp.float32,
            ).astype(jnp.bfloat16)
            for inner in range(each):
                target[slot_of(chunk * each + inner, order), :, to : to + high - low] = found[
                    inner * block : (inner + 1) * block
                ]
            return 0

        lax.fori_loop(0, left.shape[1] // ROWS, some_rows, 0)


def stage_groups(devices):
    steps = bits_of(devices)
    return [0, 1], list(range(2, steps - 1)), [steps - 1]


DOWN_PARTS = (256, 384, 384)
DOWN_ORDERS = (0, 1, 3)
UP_ORDERS = (0, 1, 3)


def swapped(shard, bit):
    heads = bits_of(lax.axis_size("head"))
    axis, level = ("head", bit) if bit < heads else ("tok", bit - heads)
    pairs = [(i, i ^ (1 << level)) for i in range(lax.axis_size(axis))]
    return lax.ppermute(shard, axis, pairs)


UP_PARTS = (((0, 0, 2560),), ((0, 2560, 4096), (1, 0, 256)), ((1, 256, 1024),))
UP_WIDTHS = (2560, 1792, 768)


def products_apart(lefts, rights):
    return [
        lax.psum_scatter(product_left(left, right), ("tok", "head"), scatter_dimension=0, tiled=True)
        for left, right in zip(lefts, rights)
    ]


def tok_peers():
    count, here = lax.axis_size("tok"), lax.axis_index("tok")
    head = lax.axis_index("head")
    return [
        ((lax.rem(here + step, count), head), lax.rem(here + count - step, count))
        for step in range(1, count)
    ]


def share(mine, every, send_sems, recv_sems, place, peers):
    copies = []
    for step, (target, _) in enumerate(peers):
        copy = pltpu.make_async_remote_copy(
            src_ref=mine,
            dst_ref=every.at[place],
            send_sem=send_sems.at[step],
            recv_sem=recv_sems.at[step],
            device_id=target,
            device_id_type=MESH,
        )
        copy.start()
        copies.append(copy)
    return copies


def row_norm(rows, gain, bias):
    rows = rows.astype(jnp.float32)
    centred = rows - jnp.mean(rows, axis=-1, keepdims=True)
    spread_ = jnp.mean(centred * centred, axis=-1, keepdims=True)
    return (centred * lax.rsqrt(spread_ + epsilon) * gain + bias).astype(jnp.bfloat16)


PIECE = 128


def head_backward_kernel(
    stages,
    back_query,
    back_key,
    back_value,
    back_feed,
    hid,
    weights,
    tokens,
    gain,
    grad_middle,
    sums,
    lag_sums,
    skip_sum,
    vectors,
    grad_up_bias,
    up_in,
    input_grad,
    grad_weights,
    row_sum,
    vector_sum,
    up_out,
    total,
    parts,
    near_in,
    far_in,
    products,
    arrived,
    shares,
    head_sems,
    tok_sends,
    tok_recvs,
    share_sends,
    share_recvs,
    every_row,
    row_sends,
    row_recvs,
    vector_parts,
    every_vector,
    tok_sum,
    head_sums,
    vector_sems,
    swap_sems,
    up_arrivals,
    up_sems,
):
    tok, head = lax.axis_index("tok"), lax.axis_index("head")
    heads, toks = lax.axis_size("head"), lax.axis_size("tok")
    near = head + 1 - 2 * lax.rem(head, 2)
    far = head + 2 - 4 * (head // 2)
    across_ = near + 2 - 4 * (near // 2)
    head_peers = [lax.rem(head + step, heads) for step in range(1, heads)]
    ladder = mesh_bits()[bits_of(heads) :]
    peers = tok_peers()
    greet([(tok, other) for other in head_peers] + [target for target, _ in peers])
    rows = input_grad.shape[0]
    states = sums.shape[0]
    every_row[tok] = jnp.zeros_like(every_row[tok])
    every_row[tok, :states] = sums[...]
    every_row[tok, states : 2 * states] = lag_sums[...]
    every_row[tok, 2 * states : 2 * states + 1] = skip_sum[...]
    row_copies = share(every_row.at[tok], every_row, row_sends, row_recvs, tok, peers)
    width = back_query.shape[1]
    columns_ = pl.ds(pl.multiple_of(head * width, HD), width)

    def block_of(owner):
        return pl.ds(pl.multiple_of(owner * rows, PIECE), rows)

    def partial(owner):
        at = block_of(owner)
        found = across(back_query[at, :], weights[:, :width])
        found += across(back_key[at, :], weights[:, width : 2 * width])
        found += across(back_value[at, :], weights[:, 2 * width :])
        total[...] = found
        total[:, columns_] += back_feed[at, :].astype(jnp.float32)

    def copy(source, target, device, number):
        one = pltpu.make_async_remote_copy(
            src_ref=source,
            dst_ref=target,
            send_sem=head_sems.at[0, number],
            recv_sem=head_sems.at[1, number],
            device_id=(tok, device),
            device_id_type=MESH,
        )
        one.start()
        return one

    up_stages = stages[1] + stages[2]
    up = Halver(up_in, up_stages, up_arrivals, up_sems, mesh_bits(), UP_ORDERS)
    up.begin()
    steps = len(ladder)
    orders = [[1, 0] + list(range(2, steps)), list(range(steps))]
    each = products[0].shape[1]
    half_width = products[0].shape[2]
    depth = hid.shape[1]
    base = [0, 0]
    sent = []

    def forward(number, stage):
        bit, partner = ladder[orders[number][stage]]
        half = 1 << (steps - 1 - stage)
        one = pltpu.make_async_remote_copy(
            src_ref=products[number].at[pl.ds(base[number] + (1 - bit) * half, half)],
            dst_ref=arrived[number * steps + stage],
            send_sem=tok_sends.at[number, stage],
            recv_sem=tok_recvs.at[number, stage],
            device_id=partner,
            device_id_type=MESH,
        )
        one.start()
        sent.append(one)
        base[number] = base[number] + bit * half
        return one

    def joined(at, number):
        if number == 0:
            return jnp.concatenate([back_query[at, :], back_key[at, : half_width - width]], axis=1)
        return jnp.concatenate([back_key[at, half_width - width :], back_value[at, :]], axis=1)

    everything = pl.ds(0, hid.shape[0])
    flying = []
    for number in range(2):
        right = joined(everything, number)
        for start in range(0, depth, 512):
            found = lax.dot_general(
                hid[:, start : start + 512],
                right,
                (((0,), (0,)), ((), ())),
                preferred_element_type=jnp.float32,
            ).astype(jnp.bfloat16)
            for inner in range(512 // each):
                products[number][slot_of(start // each + inner, orders[number])] = found[
                    inner * each : (inner + 1) * each
                ]
        flying.append(forward(number, 0))

    partial(across_)
    parts[0] = total[...].astype(jnp.bfloat16)
    first = copy(parts.at[0], near_in.at[0], near, 0)
    partial(near)
    parts[1] = total[...].astype(jnp.bfloat16)
    second = copy(parts.at[1], near_in.at[1], near, 1)
    partial(far)
    first.wait_recv()
    parts[2] = (total[...] + near_in[0].astype(jnp.float32)).astype(jnp.bfloat16)
    third = copy(parts.at[2], far_in, far, 2)
    if up_in:
        up.advance(1)
        up.advance(2)
        up.advance(0)

    partial(head)
    second.wait_recv()
    if up_in:
        up.advance(1)
        up.advance(1)
        up.advance(2)
        up.advance(0)
    total[...] += near_in[1].astype(jnp.float32)

    done = []
    for stage in range(steps):
        for number in range(2):
            flying[number].wait_recv()
            arrival = arrived[number * steps + stage]
            half = 1 << (steps - 1 - stage)
            if stage == steps - 1:
                done.append(
                    products[number][base[number]].astype(jnp.float32)
                    + arrival[0].astype(jnp.float32)
                )
            else:
                for i in range(half):
                    products[number][base[number] + i] = (
                        products[number][base[number] + i] + arrival[i]
                    )
                flying[number] = forward(number, stage + 1)
        if stage == steps - 2:
            third.wait_recv()
            back = total[...] + far_in[...].astype(jnp.float32)
            found = tokens[...].astype(jnp.float32)
            centred = found - jnp.mean(found, axis=-1, keepdims=True)
            scale = lax.rsqrt(jnp.mean(centred * centred, axis=-1, keepdims=True) + epsilon)
            shaped = centred * scale
            lists = [jnp.sum(back * shaped, axis=0, keepdims=True), jnp.sum(back, axis=0, keepdims=True)]
            lists += [vectors[i : i + 1, :] for i in range(3)]
            part = depth // toks
            for place in range(toks):
                for i, row in enumerate(lists):
                    vector_parts[place, i : i + 1, :part] = row[:, place * part : (place + 1) * part]
                for i in range(grad_up_bias.shape[1] // depth):
                    start = place * part * (grad_up_bias.shape[1] // depth) + i * part
                    vector_parts[place, len(lists) + i : len(lists) + i + 1, :part] = grad_up_bias[
                        :, start : start + part
                    ]
            every_vector[tok] = vector_parts[tok]
            vector_copies = []
            for step, (target, _) in enumerate(peers):
                one = pltpu.make_async_remote_copy(
                    src_ref=vector_parts.at[target[0]],
                    dst_ref=every_vector.at[tok],
                    send_sem=vector_sems.at[0, step],
                    recv_sem=vector_sems.at[1, step],
                    device_id=target,
                    device_id_type=MESH,
                )
                one.start()
                vector_copies.append(one)
            back = back * gain[...]
            back = back - jnp.mean(back, axis=-1, keepdims=True)
            back = back - shaped * jnp.mean(back * shaped, axis=-1, keepdims=True)
            input_grad[...] = grad_middle[...] + back * scale
    small = each // heads
    ready, landed = shares
    for other in range(heads):
        for number in range(2):
            ready[other, :, number * half_width : (number + 1) * half_width] = done[number][
                other * small : (other + 1) * small
            ].astype(ready.dtype)
    landed[head] = ready[head]
    swaps = []
    for step, other in enumerate(head_peers):
        one = pltpu.make_async_remote_copy(
            src_ref=ready.at[other],
            dst_ref=landed.at[head],
            send_sem=share_sends.at[step],
            recv_sem=share_recvs.at[step],
            device_id=(tok, other),
            device_id_type=MESH,
        )
        one.start()
        swaps.append(one)

    for one in row_copies + vector_copies:
        one.wait_recv()
    row_sum[...] = jnp.sum(every_row[...], axis=0)
    tok_sum[...] = jnp.sum(every_vector[...], axis=0)
    head_sums[head] = tok_sum[...]
    head_copies = []
    for step, other in enumerate(head_peers):
        one = pltpu.make_async_remote_copy(
            src_ref=tok_sum,
            dst_ref=head_sums.at[head],
            send_sem=swap_sems.at[0, step],
            recv_sem=swap_sems.at[1, step],
            device_id=(tok, other),
            device_id_type=MESH,
        )
        one.start()
        head_copies.append(one)
    for one in swaps:
        one.wait()
    for other in range(heads):
        for kind in range(3):
            grad_weights[kind][:, other * width : (other + 1) * width] = landed[
                other, :, kind * width : (kind + 1) * width
            ].astype(jnp.float32)
    for one in head_copies:
        one.wait_recv()
    vector_sum[...] = jnp.sum(head_sums[...], axis=0)
    for number in range(len(up_in)):
        found, column = up.last(number), 0
        for pair, start, stop in UP_PARTS[number]:
            up_out[pair][:, start:stop] = found[:, column : column + stop - start]
            column += stop - start
    up.drain()
    for one in sent + [first, second, third] + row_copies + vector_copies + head_copies:
        one.wait_send()


def head_backward(
    back_query,
    back_key,
    back_value,
    back_feed,
    hid,
    weights,
    tokens,
    gain,
    grad_middle,
    sums,
    lag_sums,
    skip_sum,
    vectors,
    grad_up_bias,
    up,
    collective_id,
):
    span, width = back_query.shape
    depth = hid.shape[1]
    heads, toks = lax.axis_size("head"), lax.axis_size("tok")
    rows, each = span // heads, depth // toks
    steps, half_width = bits_of(toks), 3 * width // 2
    swap_kind = jnp.bfloat16 if each // heads % 16 == 0 else jnp.float32
    devices = heads * toks
    stages = stage_groups(devices)
    up_pieces = [piece.shape[1:] for piece in up]
    up_buffers, up_count, up_sems = halver_scratch(up_pieces, stages[1] + stages[2], devices)
    outs = []
    for pair in range(2 if up else 0):
        stop = max(part[2] for parts in UP_PARTS for part in parts if part[0] == pair)
        outs.append(jax.ShapeDtypeStruct((up_pieces[0][0], stop), jnp.float32))
    states = sums.shape[0]
    states += -states % SUB
    row_count = 2 * states + SUB
    part = (16, max(depth // toks, HD))
    ups = len(up) or -1
    low = lambda *shape: pltpu.VMEM(shape, jnp.bfloat16)
    full = lambda *shape: pltpu.VMEM(shape, jnp.float32)
    sems = lambda *shape: pltpu.SemaphoreType.DMA(shape)
    sizes = [0] * 14 + [ups, 0, 3, 0, 0, len(outs) or -1] + [0] * 4 + [2, 2 * steps, 2]
    sizes += [0] * 5 + [0] * 9 + [up_count, 0]
    found = pl.pallas_call(
        unpack_refs(functools.partial(head_backward_kernel, stages), sizes),
        in_specs=[VMEM] * (14 + len(up)),
        out_specs=[VMEM] * (6 + len(outs)),
        out_shape=[
            jax.ShapeDtypeStruct((rows, depth), jnp.float32),
        ]
        + [jax.ShapeDtypeStruct((each // heads, depth), jnp.float32)] * 3
        + [
            jax.ShapeDtypeStruct((row_count, width), jnp.float32),
            jax.ShapeDtypeStruct(part, jnp.float32),
        ]
        + outs,
        scratch_shapes=[
            full(rows, depth),
            low(3, rows, depth),
            low(2, rows, depth),
            low(rows, depth),
        ]
        + [low(toks, each, half_width)] * 2
        + [low(1 << (steps - 1 - stage), each, half_width) for stage in range(steps)] * 2
        + [pltpu.VMEM((heads, each // heads, 3 * width), swap_kind)] * 2
        + [sems(2, 3), sems(2, steps), sems(2, steps), sems(heads - 1), sems(heads - 1)]
        + [full(toks, row_count, width), sems(toks - 1), sems(toks - 1)]
        + [full(toks, *part), full(toks, *part), full(*part), full(heads, *part)]
        + [sems(2, toks - 1), sems(2, heads - 1)]
        + up_buffers
        + [up_sems],
        compiler_params=pltpu.CompilerParams(
            collective_id=collective_id, has_side_effects=True, vmem_limit_bytes=58 * MIB
        ),
        name="head_backward",
    )(
        back_query,
        back_key,
        back_value,
        back_feed,
        hid,
        weights,
        tokens,
        gain,
        grad_middle,
        sums,
        lag_sums,
        skip_sum,
        vectors,
        grad_up_bias,
        *up,
    )
    return found[0], found[1:4], found[4], found[5], found[6:]


def every_step(length, second, back, body, carry):
    begins = lax.broadcasted_iota(jnp.int32, (SUB, HD), 0) * length - second

    def some(block, now):
        for inner in range(UNROLL):
            t = block * UNROLL + inner
            at = length - 1 - t if back else t
            now = body(at, now, jnp.where(begins == -at, 0.0, 1.0))
        return now

    return lax.fori_loop(0, length // UNROLL, some, carry)


def kept(second, begin, end):
    return jnp.where((second >= begin) & (second < end), 0.0, 1.0)


def decay_tables(rate, span):
    length = span // SUB
    return (
        jnp.exp(-rate),
        jnp.exp(-rate * length),
        length * jnp.exp(-rate * (length - 1)),
        jnp.exp(-rate * span),
        span * jnp.exp(-rate * (span - 1)),
    )


def front_kernel(
    seq_starts,
    tokens,
    gain,
    bias,
    rate,
    mix,
    skip,
    w_query,
    w_key,
    w_value,
    hid,
    query,
    key,
    value,
    feed_rows,
    weights,
    context,
    key_rim,
    value_rim,
    context_rim,
    gathered,
    drives,
    total,
    ends,
    mine,
    every,
    send_sems,
    recv_sems,
    load_sems,
    share_sends,
    share_recvs,
    rim_sems,
):
    tok, head = lax.axis_index("tok"), lax.axis_index("head")
    near = head + 1 - 2 * lax.rem(head, 2)
    far = head + 2 - 4 * (head // 2)
    across_ = near + 2 - 4 * (near // 2)
    peers = tok_peers()
    greet([(tok, near), (tok, far)] + [target for target, _ in peers])
    rows = tokens.shape[0]
    pieces = rows // PIECE
    width = query.shape[1]
    columns_ = pl.ds(pl.multiple_of(head * width, HD), width)
    loads = [
        pltpu.make_async_copy(
            whole.at[:, columns_], weights.at[:, pl.ds(kind * width, width)], load_sems.at[kind]
        )
        for kind, whole in enumerate((w_query, w_key, w_value))
    ]
    for load in loads:
        load.start()

    def copy(source, owner, target, number):
        return pltpu.make_async_remote_copy(
            src_ref=source,
            dst_ref=gathered.at[owner, pl.ds(number % pieces * PIECE, PIECE)],
            send_sem=send_sems.at[number],
            recv_sem=recv_sems.at[number],
            device_id=(tok, target),
            device_id_type=MESH,
        )

    def own(number):
        return tokens.at[pl.ds(number * PIECE, PIECE)]

    afar = [copy(own(i), head, far, i) for i in range(pieces)]
    beside = [copy(own(i), head, near, pieces + i) for i in range(pieces)]
    for one in afar + beside:
        one.start()

    def work(found, owner, number):
        at = pl.ds(pl.multiple_of(owner * rows + number * PIECE, PIECE), PIECE)
        low = row_norm(found, gain[...], bias[...])
        hid[at, :] = low
        feed_rows[at, :] = hid[at, columns_]
        mixed = jnp.dot(low, weights[...], preferred_element_type=jnp.float32).astype(
            jnp.bfloat16
        )
        query[at, :] = mixed[:, :width]
        key[at, :] = mixed[:, width : 2 * width]
        value[at, :] = mixed[:, 2 * width :]

    def block(owner, number):
        return gathered[owner, number * PIECE : (number + 1) * PIECE, :]

    for load in loads:
        load.wait()
    for i in range(pieces):
        work(tokens[i * PIECE : (i + 1) * PIECE, :], head, i)
    for i in range(pieces):
        beside[i].wait_recv()
        work(block(near, i), near, i)
    passed = []
    for i in range(pieces):
        afar[i].wait_recv()
        one = copy(
            gathered.at[far, pl.ds(i * PIECE, PIECE)], far, near, 2 * pieces + i
        )
        one.start()
        passed.append(one)
        work(block(far, i), far, i)
    for i in range(pieces):
        passed[i].wait_recv()
        work(block(across_, i), across_, i)

    here, count = tok, every.shape[0]
    decay, chunk_decay, _, span_decay, _ = decay_tables(rate[...], feed_rows.shape[0])
    length = feed_rows.shape[0] // SUB
    span = feed_rows.shape[0]
    second = seq_starts[1] - here * span
    keep = [kept(second, chunk * length, (chunk + 1) * length) for chunk in range(SUB)]
    groups = feed_rows.shape[1] // HD
    zero = jnp.zeros((SUB, HD), jnp.float32)

    def rim(source, target, number):
        copy = pltpu.make_async_remote_copy(
            src_ref=source,
            dst_ref=target,
            send_sem=rim_sems.at[0, number],
            recv_sem=rim_sems.at[1, number],
            device_id=peers[0][0],
            device_id_type=MESH,
        )

        @pl.when(here < count - 1)
        def _():
            copy.start()

        return copy

    @pl.when(here == 0)
    def _():
        for target in (key_rim, value_rim, context_rim):
            target[...] = jnp.zeros_like(target)

    window = key_rim.shape[0]
    sent = [rim(key.at[pl.ds(span - window, window)], key_rim, 0)]
    for group in range(groups):
        lanes = slice(group * HD, (group + 1) * HD)
        drives[group] = feed_rows[:, lanes].astype(jnp.float32)
        factors = [spread(decay[:, lanes], n) for n in range(NS)]

        def end_step(t, states, live):
            drive = drives[group, pl.ds(t, SUB, stride=length), :]
            return tuple(s * live * f + drive for s, f in zip(states, factors))

        done = every_step(length, second, False, end_step, (zero,) * NS)
        for n in range(NS):
            ends[n, :, lanes] = done[n]
    now = ends[:, 0, :]
    for chunk in range(1, SUB):
        now = keep[chunk] * (chunk_decay * now) + ends[:, chunk, :]
    mine[...] = now
    every[here] = now
    copies = share(mine, every, share_sends, share_recvs, here, peers)
    sent.append(rim(value.at[pl.ds(span - window, window)], value_rim, 1))
    for copy in copies:
        copy.wait()
    now = jnp.zeros_like(span_decay)
    for place in range(count - 1):
        whole = kept(seq_starts[1], place * span, (place + 1) * span)
        now = jnp.where(place < here, whole * (span_decay * now) + every[place], now)
    for chunk in range(SUB):
        own = ends[:, chunk, :]
        ends[:, chunk, :] = now
        now = keep[chunk] * (chunk_decay * now) + own

    window = context_rim.shape[0]
    for group in range(groups):
        lanes = slice(group * HD, (group + 1) * HD)
        factors = [spread(decay[:, lanes], n) for n in range(NS)]
        mixes = [spread(mix[:, lanes], n) for n in range(NS)]
        direct = spread(skip[:, lanes], 0)

        def out_step(t, states, live):
            at = pl.ds(t, SUB, stride=length)
            drive = drives[group, at, :]
            states = tuple(s * live * f + drive for s, f in zip(states, factors))
            parts = [state * weight for state, weight in zip(states, mixes)] + [direct * drive]
            while len(parts) > 1:
                parts = [a + b for a, b in zip(parts[::2], parts[1::2])] + (
                    [parts[-1]] if len(parts) % 2 else []
                )
            total[group, at, :] = parts[0]
            return states

        every_step(
            length, second, False, out_step, tuple(ends[n, :, lanes] for n in range(NS))
        )
        context[:, lanes] = total[group].astype(context.dtype)
        sent.append(
            rim(
                context.at[pl.ds(span - window, window), pl.ds(group * HD, HD)],
                context_rim.at[:, pl.ds(group * HD, HD)],
                2 + group,
            )
        )
    @pl.when(here > 0)
    def _():
        for copy in sent:
            copy.wait_recv()

    @pl.when(here < count - 1)
    def _():
        for copy in sent:
            copy.wait_send()

    for one in afar + beside + passed:
        one.wait_send()


def front(seq_starts, tokens, gain, bias, rate, mix, skip, w_query, w_key, w_value, collective_id):
    rows, depth = tokens.shape
    heads, toks = lax.axis_size("head"), lax.axis_size("tok")
    span, width = rows * heads, w_query.shape[1] // heads
    groups, window = width // HD, 2 * BLOCK
    low = lambda count: jax.ShapeDtypeStruct((span, count), jnp.bfloat16)
    rim = lambda count: jax.ShapeDtypeStruct((count, width), jnp.bfloat16)
    fulls = lambda *shape: pltpu.VMEM(shape, jnp.float32)
    sems = lambda *shape: pltpu.SemaphoreType.DMA(shape)
    found = pl.pallas_call(
        front_kernel,
        in_specs=[SCALARS] + [VMEM] * 6 + [pl.BlockSpec(memory_space=pl.ANY)] * 3,
        out_specs=[VMEM] * 10,
        out_shape=[
            low(depth),
            low(width),
            low(width),
            low(width),
            low(width),
            jax.ShapeDtypeStruct((depth, 3 * width), jnp.bfloat16),
            low(width),
            rim(window),
            rim(window),
            rim(window + CTX),
        ],
        scratch_shapes=[
            pltpu.VMEM((heads, rows, depth), jnp.bfloat16),
            fulls(groups, span, HD),
            fulls(groups, span, HD),
            fulls(NS, SUB, width),
            fulls(NS, width),
            fulls(toks, NS, width),
            sems(3 * (rows // PIECE)),
            sems(3 * (rows // PIECE)),
            sems(3),
            sems(toks - 1),
            sems(toks - 1),
            sems(2, 2 + groups),
        ],
        compiler_params=pltpu.CompilerParams(
            collective_id=collective_id, has_side_effects=True, vmem_limit_bytes=60 * MIB
        ),
        name="front",
    )(seq_starts, tokens, gain, bias, rate, mix, skip, w_query, w_key, w_value)
    return tuple(found[:7]) + (found[7:],)


def recurrence_back_kernel(
    stages,
    seq_starts,
    slope,
    feed_rows,
    rate,
    mix,
    skip,
    key_sum,
    value_sum,
    key_rim,
    value_rim,
    context_rim,
    lefts,
    rights,
    down_keep,
    down_come,
    back_key,
    back_value,
    back,
    sums,
    lag_sums,
    skip_sum,
    down_out,
    up_out,
    slopes,
    rows,
    total,
    ends,
    lags,
    mine,
    every,
    share_sends,
    share_recvs,
    key_in,
    value_in,
    context_in,
    rim_sems,
    down_now,
    down_arrivals,
    down_sems,
    grads,
    up_arrivals,
    up_sems,
):
    here, count = lax.axis_index("tok"), every.shape[0]
    peers = tok_peers()
    ladder = mesh_bits()
    heads = bits_of(lax.axis_size("head"))
    greet([target for target, _ in peers] + [partner for _, partner in ladder[:heads]])

    rims = []
    for number, (source, target) in enumerate(
        ((context_rim, context_in), (key_rim, key_in), (value_rim, value_in))
    ):
        rims.append(
            pltpu.make_async_remote_copy(
                src_ref=source,
                dst_ref=target,
                send_sem=rim_sems.at[0, number],
                recv_sem=rim_sems.at[1, number],
                device_id=peers[-1][0],
                device_id_type=MESH,
            )
        )

    @pl.when(here == count - 1)
    def _():
        for target in (context_in, key_in, value_in):
            target[...] = jnp.zeros_like(target)

    @pl.when(here > 0)
    def _():
        for copy in rims:
            copy.start()

    down_stages = stages[1] + stages[2]
    down = Halver(down_now, down_stages, down_arrivals, down_sems, ladder, DOWN_ORDERS)
    for number in (1, 2, 0):
        down_now[number][...] = down_keep[number][...] + down_come[number][...]
        if number:
            down.send(number, down_stages[0])
    up = Halver(grads, stages[0], up_arrivals, up_sems, ladder, UP_ORDERS)
    for number, parts in enumerate(UP_PARTS if grads else ()):
        column = 0
        for pair, start, stop in parts:
            fill(
                lefts[pair], rights[pair], start, stop, grads[number], column, up.orders[number]
            )
            column += stop - start
        up.send(number, stages[0][0])
    if grads:
        up.absorb(0, stages[0][0])
        up.send(0, stages[0][1])

    @pl.when(here < count - 1)
    def _():
        rims[0].wait_recv()

    span = slope.shape[0]
    decay, factor, bend, over, over_slope = decay_tables(rate[...], span)
    length = span // SUB
    second = seq_starts[1] - here * span
    keep = [kept(second, chunk * length, (chunk + 1) * length) for chunk in range(SUB)]
    groups = slope.shape[1] // HD
    zero = jnp.zeros((SUB, HD), jnp.float32)
    for group in range(groups):
        lanes = slice(group * HD, (group + 1) * HD)
        slopes[group] = slope[:, lanes]
        slopes[group, span - context_in.shape[0] :, :] += context_in[:, lanes].astype(jnp.float32)
        rows[group] = feed_rows[:, lanes].astype(jnp.float32)
        total[group] = slopes[group] * skip[:, lanes]
        skip_sum[:, lanes] = jnp.sum(slopes[group] * rows[group], axis=0, keepdims=True)
        factors = [spread(decay[:, lanes], n) for n in range(NS)]

        def end_step(t, carry, live):
            drive = slopes[group, pl.ds(t, SUB, stride=length), :]
            adjoint, lag = carry[:NS], carry[NS:]
            lag = [(a * f + b) * live for a, f, b in zip(lag, factors, adjoint)]
            adjoint = [(a * f + drive) * live for a, f in zip(adjoint, factors)]
            return tuple(adjoint) + tuple(lag)

        done = every_step(length, second, True, end_step, (zero,) * (2 * NS))
        for n in range(NS):
            ends[n, :, lanes] = done[n]
            lags[n, :, lanes] = done[NS + n]

    now, late = ends[:, SUB - 1, :], lags[:, SUB - 1, :]
    for chunk in reversed(range(SUB - 1)):
        late = keep[chunk] * (factor * late + bend * now) + lags[:, chunk, :]
        now = keep[chunk] * (factor * now) + ends[:, chunk, :]
    mine[0] = now
    mine[1] = late
    every[here, 0] = now
    every[here, 1] = late
    copies = share(mine, every, share_sends, share_recvs, here, peers)

    down.send(0, down_stages[0])
    down.advance(1)
    down.advance(2)
    for number in range(1, len(grads)):
        up.absorb(number, stages[0][0])
        up.send(number, stages[0][1])
    for copy in copies:
        copy.wait()
    now, late = jnp.zeros_like(over), jnp.zeros_like(over)
    for place in reversed(range(1, count)):
        reached = place > here
        whole = kept(seq_starts[1], place * span, (place + 1) * span)
        late = jnp.where(reached, whole * (over * late + over_slope * now) + every[place, 1], late)
        now = jnp.where(reached, whole * (over * now) + every[place, 0], now)
    for chunk in reversed(range(SUB)):
        own, own_late = ends[:, chunk, :], lags[:, chunk, :]
        ends[:, chunk, :] = now
        lags[:, chunk, :] = late
        late = keep[chunk] * (factor * late + bend * now) + own_late
        now = keep[chunk] * (factor * now) + own

    for group in range(groups):
        lanes = slice(group * HD, (group + 1) * HD)
        for base in range(0, NS, HALF):
            factors = [spread(decay[:, lanes], base + n) for n in range(HALF)]
            mixes = [spread(mix[:, lanes], base + n) for n in range(HALF)]

            def out_step(t, carry, live):
                at = pl.ds(t, SUB, stride=length)
                drive, source = slopes[group, at, :], rows[group, at, :]
                adjoint, lag = carry[:HALF], carry[HALF : 2 * HALF]
                direct, late_sum = carry[2 * HALF : 3 * HALF], carry[3 * HALF :]
                lag = [a * f + b for a, f, b in zip(lag, factors, adjoint)]
                adjoint = [a * f + drive for a, f in zip(adjoint, factors)]
                direct = [a + b * source for a, b in zip(direct, adjoint)]
                late_sum = [a + b * source for a, b in zip(late_sum, lag)]
                parts = [a * b for a, b in zip(adjoint, mixes)]
                while len(parts) > 1:
                    parts = [a + b for a, b in zip(parts[::2], parts[1::2])]
                total[group, at, :] = total[group, at, :] + parts[0]
                lag = [a * live for a in lag]
                adjoint = [a * live for a in adjoint]
                return tuple(adjoint) + tuple(lag) + tuple(direct) + tuple(late_sum)

            if group == 0 and base > 0:
                down.advance(1)
                down.advance(2)
            if group == 1:
                down.advance(0)
            first = tuple(ends[base + n, :, lanes] for n in range(HALF)) + tuple(
                lags[base + n, :, lanes] for n in range(HALF)
            )
            done = every_step(length, second, True, out_step, first + (zero,) * (2 * HALF))
            for n in range(HALF):
                sums[base + n : base + n + 1, lanes] = jnp.sum(
                    done[2 * HALF + n], axis=0, keepdims=True
                )
                lag_sums[base + n : base + n + 1, lanes] = jnp.sum(
                    done[3 * HALF + n], axis=0, keepdims=True
                )
        back[:, lanes] = total[group].astype(back.dtype)
    finished = [down.last(number) for number in range(len(down_now))]
    column = 0
    for piece in finished:
        down_out[:, column : column + piece.shape[1]] = piece
        column += piece.shape[1]

    @pl.when(here < count - 1)
    def _():
        rims[1].wait_recv()
        rims[2].wait_recv()

    inner = span - key_in.shape[0]
    for source, more, target in (
        (key_sum, key_in, back_key),
        (value_sum, value_in, back_value),
    ):
        target[:inner, :] = source[:inner, :].astype(target.dtype)
        target[inner:, :] = (source[inner:, :] + more[...].astype(jnp.float32)).astype(
            target.dtype
        )
    up.step(stages[0][1], up_out)
    down.drain()
    up.drain()

    @pl.when(here > 0)
    def _():
        for copy in rims:
            copy.wait_send()


def recurrence_back(
    seq_starts, slope, feed_rows, rate, mix, skip, sums, rims, lefts, rights, down, collective_id
):
    span, width = feed_rows.shape
    toks = lax.axis_size("tok")
    devices = toks * lax.axis_size("head")
    stages = stage_groups(devices)
    block = lefts[0].shape[1] // devices
    apart, up_pieces = None, [(block, part) for part in UP_WIDTHS]
    if block < 16:
        apart = products_apart(lefts, rights)
        lefts, rights, up_pieces = [], [], []
    keep, come = down
    down_pieces = [piece.shape[1:] for piece in keep]
    late = stages[1] + stages[2]
    down_buffers, down_count, down_sems = halver_scratch(down_pieces, late, devices)
    up_buffers, up_count, up_sems = halver_scratch(up_pieces, stages[0], devices)
    down_width = sum(piece[1] for piece in down_pieces)
    up_shapes = left_over(up_pieces, stages[0], devices)
    full = lambda *shape: jax.ShapeDtypeStruct(shape, jnp.float32)
    fulls = lambda *shape: pltpu.VMEM(shape, jnp.float32)
    sems = lambda *shape: pltpu.SemaphoreType.DMA(shape)
    groups = width // HD
    scratch = [
        fulls(groups, span, HD),
        fulls(groups, span, HD),
        fulls(groups, span, HD),
        fulls(NS, SUB, width),
        fulls(NS, SUB, width),
        fulls(2, NS, width),
        fulls(toks, 2, NS, width),
        sems(toks - 1),
        sems(toks - 1),
    ]
    low = lambda count: jax.ShapeDtypeStruct((count, width), jnp.bfloat16)
    scratch += [pltpu.VMEM(rims[k].shape, jnp.bfloat16) for k in (0, 1, 2)]
    scratch += [sems(2, 3)] + [pltpu.VMEM(piece.shape, jnp.bfloat16) for piece in keep]
    scratch += down_buffers + [down_sems]
    scratch += [pltpu.VMEM((devices,) + piece, jnp.bfloat16) for piece in up_pieces]
    scratch += up_buffers + [up_sems]
    pairs, ups, downs = len(lefts) or -1, len(up_pieces) or -1, len(keep)
    sizes = [0] * 11 + [pairs, pairs, downs, downs] + [0] * 6 + [0, ups] + [0] * 9
    sizes += [0] * 4 + [downs, down_count, 0, ups, up_count, 0]
    found = pl.pallas_call(
        unpack_refs(functools.partial(recurrence_back_kernel, stages), sizes),
        in_specs=[SCALARS] + [VMEM] * (10 + 2 * len(lefts) + 2 * downs),
        out_specs=[VMEM] * (7 + len(up_shapes)),
        out_shape=[
            low(span),
            low(span),
            low(span),
            full(NS, width),
            full(NS, width),
            full(1, width),
        ]
        + [full(down_pieces[0][0], down_width)]
        + up_shapes,
        scratch_shapes=scratch,
        compiler_params=pltpu.CompilerParams(
            collective_id=collective_id, has_side_effects=True, vmem_limit_bytes=60 * MIB
        ),
        name="recurrence_back",
    )(
        seq_starts,
        slope,
        feed_rows,
        rate,
        mix,
        skip,
        *sums,
        *rims,
        *lefts,
        *rights,
        *keep,
        *come,
    )
    return tuple(found[:6]) + (found[6], found[7:], apart)


CHUNK = 1024
UP_CHUNK = 512
ROOT = math.sqrt(2.0 / math.pi)
CUBIC = 0.044715


def feed_kernel(
    stages,
    attended,
    tokens,
    out_grad,
    gain,
    bias,
    up_bias,
    down_bias,
    w_output,
    w_up,
    w_down,
    layer_out,
    grad_middle,
    normed,
    grad_before,
    joined,
    grad_branch,
    grad_att,
    down_left,
    vectors,
    grad_up_bias,
    output_w,
    up_w,
    down_w,
    split,
    active,
    bend,
    drive,
    shape,
    down_sum,
    back_sum,
    grad_split,
    grads,
    arrivals,
    weight_sems,
    down_sems,
    head_sems,
    halver_sems,
):
    tok, head = lax.axis_index("tok"), lax.axis_index("head")
    heads = lax.axis_size("head")
    rows, width = tokens.shape[0], attended.shape[1]
    hidden = up_w.shape[1]
    loads = [
        pltpu.make_async_copy(source, target, weight_sems.at[number])
        for number, (source, target) in enumerate(
            ((w_output, output_w), (w_up, up_w))
        )
    ]

    def down_load(chunk):
        slot = lax.rem(chunk, 2)
        return pltpu.make_async_copy(
            w_down.at[pl.ds(pl.multiple_of(chunk * CHUNK, CHUNK), CHUNK)],
            down_w.at[slot],
            down_sems.at[slot],
        )

    for load in loads:
        load.start()
    for chunk in range(2):
        down_load(chunk).start()
    peers = [lax.rem(head + step, heads) for step in range(1, heads)]
    ladder = mesh_bits()
    greet([(tok, other) for other in peers] + [p for _, p in ladder[bits_of(heads) :]])

    def block_of(owner):
        return pl.ds(pl.multiple_of(owner * rows, PIECE), rows)

    def swap(source_of, target, kind):
        found = []
        for step, other in enumerate(peers):
            copy = pltpu.make_async_remote_copy(
                src_ref=source_of(other),
                dst_ref=target,
                send_sem=head_sems.at[kind, 0, step],
                recv_sem=head_sems.at[kind, 1, step],
                device_id=(tok, other),
                device_id_type=MESH,
            )
            copy.start()
            found.append(copy)
        return found

    def drive_chunk(chunk, _):
        at = pl.ds(pl.multiple_of(chunk * CHUNK, CHUNK), CHUNK)
        down_load(chunk).wait()
        drive[:, at] = across(out_grad[...], down_w[lax.rem(chunk, 2)]).astype(jnp.bfloat16)
        down_load(lax.rem(chunk + 2, chunks)).start()
        return 0

    chunks = hidden // CHUNK
    first = swap(lambda other: attended.at[block_of(other)], split.at[head], 0)
    split[head] = attended[block_of(head), :]
    lax.fori_loop(0, chunks, drive_chunk, 0)
    loads[0].wait()
    for copy in first:
        copy.wait_recv()
    total = tokens[...].astype(jnp.float32)
    for owner in range(heads):
        at = slice(owner * width, (owner + 1) * width)
        joined[:, at] = split[owner]
        total += jnp.dot(split[owner], output_w[at, :], preferred_element_type=jnp.float32)
    grad_middle[...] = total
    centred = total - jnp.mean(total, axis=-1, keepdims=True)
    scale = lax.rsqrt(jnp.mean(centred * centred, axis=-1, keepdims=True) + epsilon)
    shape[...] = centred * scale
    normed[...] = (centred * scale * gain[...] + bias[...]).astype(jnp.bfloat16)

    loads[1].wait()

    def up_chunk(chunk, _):
        at = pl.ds(pl.multiple_of(chunk * UP_CHUNK, UP_CHUNK), UP_CHUNK)
        before = jnp.dot(normed[...], up_w[:, at], preferred_element_type=jnp.float32)
        before += up_bias[:, at]
        square = before * before
        bent = jnp.tanh(ROOT * before * (1.0 + CUBIC * square))
        half = 0.5 * (1.0 + bent)
        active[:, at] = (before * half).astype(jnp.bfloat16)
        bend[:, at] = half + (0.5 * ROOT) * before * (1.0 - bent * bent) * (
            1.0 + (3.0 * CUBIC) * square
        )
        return 0

    lax.fori_loop(0, hidden // UP_CHUNK, up_chunk, 0)
    halver = Halver(grads, stages, arrivals, halver_sems, ladder, DOWN_ORDERS)
    starts = [sum(DOWN_PARTS[:k]) for k in range(len(DOWN_PARTS) + 1)]
    for k, order in enumerate(halver.orders):
        fill(active, out_grad, starts[k], starts[k + 1], grads[k], 0, order)
        halver.send(k, stages[0])

    back_sum[...] = jnp.zeros_like(back_sum)

    def back_chunk(chunk, _):
        at = pl.ds(pl.multiple_of(chunk * CHUNK, CHUNK), CHUNK)
        low = (drive[:, at].astype(jnp.float32) * bend[:, at]).astype(jnp.bfloat16)
        grad_before[:, at] = low
        grad_up_bias[:, at] = jnp.sum(low.astype(jnp.float32), axis=0, keepdims=True)
        back_sum[...] += across(low, up_w[:, at])
        return 0

    lax.fori_loop(0, chunks, back_chunk, 0)
    back = back_sum[...]
    shaped = shape[...]
    vectors[0:1, :] = jnp.sum(back * shaped, axis=0, keepdims=True)
    vectors[1:2, :] = jnp.sum(back, axis=0, keepdims=True)
    top = out_grad[...].astype(jnp.float32)
    vectors[2:3, :] = jnp.sum(top, axis=0, keepdims=True)
    back = back * gain[...]
    back = back - jnp.mean(back, axis=-1, keepdims=True)
    back = back - shaped * jnp.mean(back * shaped, axis=-1, keepdims=True)
    total = grad_middle[...]
    centred = total - jnp.mean(total, axis=-1, keepdims=True)
    scale = lax.rsqrt(jnp.mean(centred * centred, axis=-1, keepdims=True) + epsilon)
    down_sum[...] = total + down_bias[...]
    top = top + back * scale
    grad_middle[...] = top
    low = top.astype(jnp.bfloat16)
    grad_branch[...] = low
    for owner in range(heads):
        at = slice(owner * width, (owner + 1) * width)
        grad_split[owner] = across(low, output_w[at, :]).astype(jnp.bfloat16)
    second = swap(lambda other: grad_split.at[other], grad_att.at[block_of(head)], 1)
    grad_att[block_of(head), :] = grad_split[head]

    def down_chunk(chunk, _):
        at = pl.ds(pl.multiple_of(chunk * CHUNK, CHUNK), CHUNK)
        down_load(chunk).wait()
        down_sum[...] += jnp.dot(
            active[:, at], down_w[lax.rem(chunk, 2)], preferred_element_type=jnp.float32
        )

        @pl.when(chunk + 2 < chunks)
        def _():
            down_load(chunk + 2).start()

        return 0

    for k in range(len(grads)):
        halver.part(k, stages[0], down_left[2 * k], down_left[2 * k + 1])
    lax.fori_loop(0, chunks, down_chunk, 0)
    layer_out[...] = down_sum[...].astype(jnp.bfloat16)
    for copy in second:
        copy.wait_recv()
    halver.drain()
    for copy in first + second:
        copy.wait_send()


def feed(
    attended,
    tokens,
    out_grad,
    gain,
    bias,
    up_bias,
    down_bias,
    w_output,
    w_up,
    w_down,
    collective_id,
):
    rows, depth = tokens.shape
    span, width = attended.shape
    hidden = w_up.shape[1]
    heads = lax.axis_size("head")
    devices = heads * lax.axis_size("tok")
    block = hidden // devices
    stages = stage_groups(devices)[0][:1]
    pieces = [(block, part) for part in DOWN_PARTS]
    buffers, buffer_count, halver_sems = halver_scratch(pieces, stages, devices)
    low = lambda *shape: jax.ShapeDtypeStruct(shape, jnp.bfloat16)
    full = lambda *shape: jax.ShapeDtypeStruct(shape, jnp.float32)
    any_ = pl.BlockSpec(memory_space=pl.ANY)
    sems = lambda *shape: pltpu.SemaphoreType.DMA(shape)
    lows = lambda *shape: pltpu.VMEM(shape, jnp.bfloat16)
    fulls = lambda *shape: pltpu.VMEM(shape, jnp.float32)
    scratch = [
        lows(depth, depth),
        lows(depth, hidden),
        lows(2, CHUNK, depth),
        lows(heads, rows, width),
        lows(rows, hidden),
        fulls(rows, hidden),
        lows(rows, hidden),
        fulls(rows, depth),
        fulls(rows, depth),
        fulls(rows, depth),
        lows(heads, rows, width),
    ]
    scratch += [lows(devices, block, part) for part in DOWN_PARTS]
    scratch += buffers
    scratch += [sems(2), sems(2), sems(2, 2, heads - 1), halver_sems]
    count = len(pieces)
    sizes = [0] * 17 + [2 * count] + [0] * 13 + [count, buffer_count] + [0] * 4
    outs = [
        low(rows, depth),
        full(rows, depth),
        low(rows, depth),
        low(rows, hidden),
        low(rows, depth),
        low(rows, depth),
        low(span, width),
    ]
    outs += left_over([piece for piece in pieces for _ in (0, 1)], [1], devices)
    outs += [full(SUB, depth), full(1, hidden)]
    return pl.pallas_call(
        unpack_refs(functools.partial(feed_kernel, stages), sizes),
        in_specs=[VMEM] * 7 + [any_] * 3,
        out_specs=[VMEM] * len(outs),
        out_shape=outs,
        scratch_shapes=scratch,
        compiler_params=pltpu.CompilerParams(
            collective_id=collective_id, has_side_effects=True, vmem_limit_bytes=63 * MIB
        ),
        name="feed",
    )(
        attended, tokens, out_grad, gain, bias, up_bias, down_bias, w_output, w_up, w_down
    )


def layer_norm(row_block, gain, bias):
    centre = jnp.mean(row_block, axis=-1, keepdims=True)
    centred = row_block - centre
    spread = jnp.mean(centred * centred, axis=-1, keepdims=True)
    return centred * lax.rsqrt(spread + epsilon) * gain + bias


def product(left, right):
    return jnp.dot(left, right, preferred_element_type=jnp.float32)


def product_left(left, right):
    return lax.dot_general(
        left, right, (((0,), (0,)), ((), ())), preferred_element_type=jnp.float32
    )


def product_right(left, right):
    return lax.dot_general(
        left, right, (((1,), (1,)), ((), ())), preferred_element_type=jnp.float32
    )


def per_device(
    tokens_in,
    seq_starts,
    block_sizes,
    norm1_gain,
    norm1_bias,
    w_query,
    w_key,
    w_value,
    w_output,
    ssm_rate,
    ssm_input,
    ssm_output,
    ssm_skip,
    norm2_gain,
    norm2_bias,
    w_up,
    up_bias,
    w_down,
    down_bias,
    out_grad,
):
    tok_rows = tokens_in.shape[0]
    pieces = lax.axis_size("tok")
    span = tok_rows * lax.axis_size("head")
    total_len = span * pieces

    rate = ssm_rate.T / total_len
    drive_in, read_out = ssm_input.T, ssm_output.T
    decay = jnp.exp(-rate)
    gain = jnp.sqrt(-jnp.expm1(-2.0 * rate))
    driving = gain * drive_in
    mix = read_out * driving
    skip = ssm_skip[None, :]
    hid, query_h, key_h, value_h, hidden_h, w_own, context, rims = front(
        seq_starts,
        tokens_in,
        norm1_gain[None, :],
        norm1_bias[None, :],
        rate,
        mix,
        skip,
        w_query,
        w_key,
        w_value,
        6,
    )
    attended, attended_fine, level = attend(seq_starts, block_sizes, query_h, key_h, value_h, context, rims)
    (
        layer_out,
        grad_middle,
        normed_low,
        grad_before_low,
        joined,
        grad_branch,
        grad_att,
        *down,
        vectors,
        grad_up_bias,
    ) = feed(
        attended,
        tokens_in,
        out_grad,
        norm2_gain[None, :],
        norm2_bias[None, :],
        up_bias[None, :],
        down_bias[None, :],
        w_output,
        w_up,
        w_down,
        7,
    )
    orders = halving_orders(bits_of(pieces * lax.axis_size("head")))
    come = [
        swapped(leave, orders[order][1]) for leave, order in zip(down[1::2], DOWN_ORDERS)
    ]

    back_query_h, key_rim, value_rim, near_rim, back_key_h, back_value_h, back_context = attend_back(
        seq_starts, block_sizes, query_h, key_h, value_h, context, rims, attended_fine, grad_att, level
    )
    (
        back_key_h,
        back_value_h,
        back_feed_h,
        sums,
        lag_sums,
        skip_sum,
        out_w_down,
        up,
        apart,
    ) = recurrence_back(
        seq_starts,
        back_context,
        hidden_h,
        rate,
        mix,
        skip,
        [back_key_h, back_value_h],
        [key_rim, value_rim, near_rim],
        [normed_low, joined],
        [grad_before_low, grad_branch],
        (down[::2], come),
        2,
    )
    input_grad, out_w_heads, summed, packed, up = head_backward(
        back_query_h,
        back_key_h,
        back_value_h,
        back_feed_h,
        hid,
        w_own,
        tokens_in,
        norm1_gain[None, :],
        grad_middle,
        sums,
        lag_sums,
        skip_sum,
        vectors,
        grad_up_bias,
        up,
        4,
    )
    heads, head = lax.axis_size("head"), lax.axis_index("head")
    part = norm1_gain.shape[0] // pieces
    more = up_bias.shape[0] // norm1_gain.shape[0]
    short = lax.dynamic_slice_in_dim(packed[:5], head * (part // heads), part // heads, 1)
    out_up_bias = lax.dynamic_slice_in_dim(
        packed[5 : 5 + more, :part].reshape(-1), head * (more * part // heads), more * part // heads
    )
    out_w_up, out_w_output = up if apart is None else apart
    sums, lag_sums, skip_sum = summed[:NS], summed[NS : 2 * NS], summed[2 * NS]
    grad_ssm_output = (driving * sums).T
    grad_driving = read_out * sums
    grad_ssm_input = (gain * grad_driving).T
    grad_ssm_rate = (
        grad_driving * drive_in * jnp.exp(-2.0 * rate) / gain - mix * lag_sums * decay
    ).T / total_len

    return (
        layer_out,
        input_grad,
        short[0],
        short[1],
        out_w_heads[0],
        out_w_heads[1],
        out_w_heads[2],
        out_w_output,
        grad_ssm_rate,
        grad_ssm_input,
        grad_ssm_output,
        skip_sum,
        short[2],
        short[3],
        out_w_up,
        out_up_bias,
        out_w_down,
        short[4],
    )


def solution(mesh):
    return jax.shard_map(
        per_device,
        mesh=mesh,
        in_specs=(
            P(("tok", "head"), None),
            P(),
            P(),
            P(),
            P(),
            P(),
            P(),
            P(),
            P(),
            P("head", None),
            P("head", None),
            P("head", None),
            P("head"),
            P(),
            P(),
            P(),
            P(),
            P(),
            P(),
            P(("tok", "head"), None),
        ),
        out_specs=(
            P(("tok", "head"), None),
            P(("tok", "head"), None),
            P(("tok", "head")),
            P(("tok", "head")),
            P(("tok", "head"), None),
            P(("tok", "head"), None),
            P(("tok", "head"), None),
            P(("tok", "head"), None),
            P("head", None),
            P("head", None),
            P("head", None),
            P("head"),
            P(("tok", "head")),
            P(("tok", "head")),
            P(("tok", "head"), None),
            P(("tok", "head")),
            P(("tok", "head"), None),
            P(("tok", "head")),
        ),
        check_vma=False,
    )
```
